32 devices in a mesh: expert: 16 (over z, y, x), tensor: 2 (over core).
Axes of the slice: x: 2, y: 2, z: 4, core: 2. Of those that a mesh axis runs over, the one named last changes fastest.
Arguments:
- tokens: bfloat16 [36864, 768], P(('expert', 'tensor')), may hold values from -6 to 6
- gains: float32 [768], replicated, may hold values from 0.5 to 1.5
- shifts: float32 [768], replicated, may hold values from -1 to 1
- projection: bfloat16 [768, 2304], replicated, may hold values from -0.21875 to 0.21875
- mixing: bfloat16 [768, 768], replicated, may hold values from -0.875 to 0.875
- factors: float32 [768], replicated, may hold values from 0.5 to 1.5
- biases: float32 [768], replicated, may hold values from -1 to 1
- centroids: bfloat16 [4, 768], replicated, may hold values from -0.15625 to 0.15625
- expanding: bfloat16 [16, 768, 768], P('expert', None, 'tensor'), may hold values from -0.21875 to 0.21875
- contracting: bfloat16 [16, 768, 768], P('expert', 'tensor'), may hold values from -0.21875 to 0.21875
- routes: int32 [36864, 1], P(('expert', 'tensor')), may hold values from 0 to 3; in each aligned block of 1152 rows (0 to 1151, 1152 to 2303, ...) at most 576 rows name the same one
- lengths: int32 [32, 4], P(('expert', 'tensor')), may hold values from 1 to 1024, 1152 in all within a row
- cotangent: bfloat16 [36864, 768], P(('expert', 'tensor')), may hold values from -6 to 6
Outputs:
- layer_output: bfloat16 [36864, 768], P(('expert', 'tensor'))
- balance: float32 [], replicated
- grad_tokens: float32 [36864, 768], P(('expert', 'tensor'))
- grad_gains: float32 [768], replicated
- grad_shifts: float32 [768], replicated
- grad_projection: float32 [768, 2304], replicated
- grad_mixing: float32 [768, 768], replicated
- grad_factors: float32 [768], replicated
- grad_biases: float32 [768], replicated
- grad_centroids: float32 [4, 768], replicated
- grad_expanding: float32 [16, 768, 768], P('expert', None, 'tensor')
- grad_contracting: float32 [16, 768, 768], P('expert', 'tensor')
The draws below stay inside these ranges and needn't reach their ends.
Inputs may be any that keep to these rules, and one draw needn't show every extreme that they name: `routes`: in each device's block of 1152 rows no expert is named more than 576 times, a bound that some block reaches. `lengths`: each row sums to 1152; its largest entry is 1024.
All inputs are finite; a program needn't handle non-finite values.
Results may differ from the reference program's by a relative error of at most 0.014.
Values may be sent and summed in bfloat16 or wider, within the bound.
A program may use at most 384 MiB of HBM per device.

```python
import math
import jax
import jax.numpy as jnp
import numpy as np
from jax import lax

D = 768
HEADS = 12
HEAD_DIM = 64
FF = 3072
SLABS = 4
MAXLEN = 1024
DOCS = 4
TOK_DEV = 1152
EXPERTS = 4
CAP = 576
PACKS = 32
TOKENS = 36864


def shard_levels(own_key, dims, shards, least, largest):
    factor_of = 1.0
    for axis_at, parts in shards:
        steps = jax.random.uniform(jax.random.fold_in(jax.random.fold_in(own_key, 6), axis_at), (parts,), jnp.float32, least / len(shards), largest / len(shards))
        factor_of = factor_of * jnp.repeat(jnp.exp(steps), dims[axis_at] // parts).reshape((-1,) + (1,) * (len(dims) - 1 - axis_at))
    return factor_of


def profile(number_of, total, bound, lean):
    portions = [(1 << 20) // math.isqrt(standing ** lean) + 1 for standing in range(2, number_of + 1)]
    surplus, counts = total - bound - (number_of - 1), [1] * (number_of - 1)
    while surplus > 0:
        candidates = [i for i in range(number_of - 1) if counts[i] < bound]
        pool, budget = sum([portions[i] for i in candidates]), surplus
        for i in candidates:
            more = min(bound - counts[i], max(1, budget * portions[i] // pool), surplus)
            counts[i] = counts[i] + more
            surplus = surplus - more
    return np.array([bound] + counts)


def uneven(rng, number_of, total, reach, lean):
    if number_of == 2:
        one = jax.random.randint(rng, (), max(1, total - reach), min(reach, total - 1) + 1)
        return jnp.stack([one, total - one])
    sizes = jnp.asarray(profile(number_of, total, reach, lean), jnp.int32)
    twos = (number_of - 1) // 2
    giver, receiver = sizes[1:1 + 2 * twos:2], sizes[2:2 + 2 * twos:2]
    room = jnp.minimum(giver - 1, reach - receiver)
    moved = jax.random.randint(jax.random.fold_in(rng, 1), (twos,), 0, 1 << 20) % (room + 1)
    sizes = sizes.at[1:1 + 2 * twos:2].set(giver - moved).at[2:2 + 2 * twos:2].set(receiver + moved)
    return sizes[jax.random.permutation(jax.random.fold_in(rng, 2), number_of)]


def deal_out(key, own, number, rows, amount, top, limit, skew):
    order = jax.random.permutation(key, amount)
    heavy_load, ordinary = shares(amount, rows * top, limit, skew, True), shares(amount, rows * top, limit, skew, False)
    places = jnp.arange(amount)

    def named(sizes, rotation):
        used = int((sizes > 0).sum())
        fixed = max(1, used // 4)
        shifted = fixed + (places - fixed + rotation * (used - fixed)) % max(1, amount - fixed)
        return jnp.zeros((amount,), jnp.int32).at[order[jnp.where(places < fixed, places, shifted)]].set(jnp.asarray(sizes, jnp.int32))

    sizes = jnp.where(number % 4 == 0, named(heavy_load, number // 4), named(ordinary, number - number // 4 - 1))
    mixed = jax.random.permutation(jax.random.fold_in(own, 3), amount)
    giver, receiver = mixed[0:amount // 2 * 2:2], mixed[1:amount // 2 * 2:2]
    margin = jnp.minimum(sizes[giver] - 1, limit - sizes[receiver]) // 2
    margin = jnp.where((giver == order[0]) | (receiver == order[0]) | (sizes[receiver] == 0), 0, jnp.maximum(margin, 0))
    shifted = jax.random.randint(jax.random.fold_in(own, 4), (amount // 2,), 0, 1 << 20) % (margin + 1)
    sizes = sizes.at[giver].add(-shifted).at[receiver].add(shifted)
    items = jnp.searchsorted(jnp.cumsum(sizes), jnp.arange(rows * top), side="right").astype(jnp.int32)
    listing = items.reshape(top, rows).T
    listing = listing[jax.random.permutation(jax.random.fold_in(own, 1), rows)]
    rotation = jax.random.randint(jax.random.fold_in(own, 2), (rows, 1), 0, top)
    return jnp.take_along_axis(listing, (jnp.arange(top)[None, :] + rotation) % top, axis=1)


def shares(count, total, most, lean, full):
    portions = [(1 << 20) // math.isqrt(rank ** lean) + 1 for rank in range(1, count + 1)]
    largest = most if full else min(most, max(-(-total // count), total * portions[0] // sum(portions)))
    least = 1 if total - largest >= count - 1 else 0
    given, rest = [largest] + [least] * (count - 1), total - largest - least * (count - 1)
    while rest > 0:
        movable = [i for i in range(1, count) if given[i] < largest] or [i for i in range(1, count) if given[i] < most]
        pool, remaining = sum([portions[i] for i in movable]), rest
        for i in movable:
            more = min(most - given[i], max(1, remaining * portions[i] // pool), rest)
            given[i] = given[i] + more
            rest = rest - more
    return np.array(given)


def centred(rng, dims, scale, most, shards=(), kind=jnp.bfloat16):
    drawn = scale * jax.random.normal(rng, dims, jnp.float32)
    if shards:
        drawn = drawn * shard_levels(rng, dims, shards, -0.22, 0.18)
    return jnp.clip(drawn, -most, most).astype(kind)


def setup_inputs(seed: int = 0) -> dict:
    key_list = jax.random.split(jax.random.key(seed), 14)
    tokens = centred(key_list[0], (TOKENS, D), 1.0, 6.0, ((0, 32),))
    gains = jnp.clip(1.0 + 0.1 * jax.random.normal(key_list[1], (D,), jnp.float32), 0.5, 1.5)
    shifts = centred(key_list[2], (D,), 0.2, 1.0, (), jnp.float32)
    projection = centred(key_list[3], (D, 3 * D), D ** -0.5, 0.21875)
    mixing = centred(key_list[4], (D, D), (D // 16) ** -0.5, 0.875)
    factors = jnp.clip(1.0 + 0.1 * jax.random.normal(key_list[5], (D,), jnp.float32), 0.5, 1.5)
    biases = centred(key_list[6], (D,), 0.2, 1.0, (), jnp.float32)
    centroids = centred(key_list[7], (EXPERTS, D), (2 * D) ** -0.5, 0.15625)
    expanding = centred(key_list[8], (EXPERTS * SLABS, D, FF // SLABS), D ** -0.5, 0.21875, ((0, 16), (2, 2)))
    contracting = centred(key_list[9], (EXPERTS * SLABS, FF // SLABS, D), (FF // 4) ** -0.5, 0.21875, ((0, 16), (1, 2)))
    routes_keys = jax.random.split(jax.random.fold_in(key_list[10], 1), TOKENS // TOK_DEV)
    routes_turns = jax.random.permutation(jax.random.fold_in(key_list[10], 3), TOKENS // TOK_DEV)
    routes = jax.vmap(lambda own, number: deal_out(jax.random.fold_in(key_list[10], 2), own, number, TOK_DEV, EXPERTS, 1, CAP, 1))(routes_keys, routes_turns).reshape((TOKENS, 1))
    lengths = jax.vmap(lambda own: uneven(own, DOCS, TOK_DEV, MAXLEN, 2))(jax.random.split(key_list[11], PACKS)).reshape((PACKS, DOCS)).astype(jnp.int32)
    cotangent = centred(key_list[12], (TOKENS, D), 1.0, 6.0, ((0, 32),))
    return dict(tokens=tokens, gains=gains, shifts=shifts, projection=projection, mixing=mixing, factors=factors, biases=biases, centroids=centroids, expanding=expanding, contracting=contracting, routes=routes, lengths=lengths, cotangent=cotangent)


highest = lax.Precision.HIGHEST

@jax.custom_vjp
def low(v):
    return lax.optimization_barrier(v.astype(jnp.bfloat16)).astype(jnp.float32)

@jax.custom_vjp
def low_back(v):
    return v

def low_keep(v):
    return (low(v), None)

def low_pass(kept, grad):
    return (grad,)

def back_keep(v):
    return (v, None)

def back_low(kept, grad):
    return (low(grad),)
low.defvjp(low_keep, low_pass)
low_back.defvjp(back_keep, back_low)

def norm_rows(values, gain, shift):
    centered = values - lax.optimization_barrier(jnp.mean(values, axis=1, keepdims=True))
    scale = lax.rsqrt(lax.optimization_barrier(jnp.mean(centered * centered, axis=1, keepdims=True)) + 1e-05)
    return centered * scale * gain + shift

def attend_block(item):
    joint, documents = item
    places = jnp.arange(TOK_DEV, dtype=jnp.int32)
    allowed = (places[:, None] >= places[None, :]) & (documents[:, None] == documents[None, :])
    heads = joint.reshape(TOK_DEV, 3, HEADS, HEAD_DIM)
    scores = jnp.einsum('qhd,khd->hqk', heads[:, 0], heads[:, 1], precision=highest) * HEAD_DIM ** (-0.5)
    scores = low_back(jnp.where(allowed[None], scores, -1000000000.0))
    probs = low(jax.nn.softmax(scores, axis=-1))
    mixed = jnp.einsum('hqk,khd->qhd', probs, heads[:, 2], precision=highest)
    return mixed.reshape(TOK_DEV, HEADS * HEAD_DIM)

def expert_block(item):
    gathered, upward, downward = item
    total = jnp.zeros((gathered.shape[0], D), jnp.float32)
    for block_index in range(SLABS):
        before = low_back(jnp.dot(low_back(gathered), upward[block_index], precision=highest))
        active = low(jax.nn.gelu(before, approximate=False))
        total = total + low(low_back(jnp.dot(active, downward[block_index], precision=highest)))
    return total

def reference(tokens, gains, shifts, projection, mixing, factors, biases, centroids, expanding, contracting, routes, lengths, cotangent):
    route = routes[:, 0]
    picks_int = (route[:, None] == jnp.arange(EXPERTS, dtype=jnp.int32)[None, :]).astype(jnp.int32)
    per_block = picks_int.reshape(PACKS, TOK_DEV, EXPERTS)
    ranks = lax.optimization_barrier(jnp.sum((jnp.cumsum(per_block, axis=1) - per_block) * per_block, axis=2)).reshape(TOKENS)
    column = jnp.arange(TOKENS, dtype=jnp.int32) // TOK_DEV * CAP + ranks
    ends = jnp.cumsum(lengths, axis=1)
    places = jnp.arange(TOK_DEV, dtype=jnp.int32)
    documents = lax.optimization_barrier(jnp.sum((places[None, :, None] >= ends[:, None, :]).astype(jnp.int32), axis=2))
    picks = picks_int.astype(jnp.float32)
    loads = lax.optimization_barrier(jnp.sum(picks, axis=0))
    average = TOKENS / EXPERTS
    spread = (loads - average) / average

    def forward(inputs, gains, shifts, projection, mixing, factors, biases, centroids, expanding, contracting):
        entry = low(norm_rows(inputs, gains, shifts))
        joint = low(low_back(jnp.dot(entry, projection, precision=highest)))
        blocks = joint.reshape(PACKS, TOK_DEV, 3 * D)
        mixed = lax.map(jax.checkpoint(attend_block), (blocks, documents)).reshape(TOKENS, D)
        mixed = low(low_back(mixed))
        residual = inputs + low_back(jnp.dot(mixed, mixing, precision=highest))
        normed = norm_rows(residual, factors, biases)
        sent = low(normed)
        chosen = jnp.dot(picks, centroids, precision=highest)
        gates = jax.nn.sigmoid(lax.optimization_barrier(jnp.sum(normed * chosen, axis=1)))
        buffer = jnp.zeros((EXPERTS, PACKS * CAP, D), sent.dtype).at[route, column].set(sent)
        upward = expanding.reshape(EXPERTS, SLABS, D, FF // SLABS)
        downward = contracting.reshape(EXPERTS, SLABS, FF // SLABS, D)
        produced = lax.map(jax.checkpoint(expert_block), (buffer, upward, downward))
        picked = produced[route, column]
        output = residual + gates[:, None] * picked
        balance = jnp.sum(jnp.dot(picks, spread, precision=highest) * gates) / TOKENS
        return (output, balance)
    floats = (tokens.astype(jnp.float32), gains.astype(jnp.float32), shifts.astype(jnp.float32), projection.astype(jnp.float32), mixing.astype(jnp.float32), factors.astype(jnp.float32), biases.astype(jnp.float32), centroids.astype(jnp.float32), expanding.astype(jnp.float32), contracting.astype(jnp.float32))
    primal, pullback = jax.vjp(forward, *floats)
    output, balance = primal
    grads = pullback((cotangent.astype(jnp.float32), jnp.ones_like(balance)))
    return (output.astype(jnp.bfloat16), balance, grads[0], grads[1], grads[2], grads[3], grads[4], grads[5], grads[6], grads[7], grads[8], grads[9])
```

```python
from functools import partial

import jax
import jax.numpy as jnp
from jax import lax
from jax.experimental import pallas as pl
from jax.experimental.pallas import tpu as pltpu
from jax.sharding import PartitionSpec as P

HEADS = 12


highest = lax.Precision.HIGHEST
epsilon = 1e-05


def running(values):
    places = jnp.arange(values.shape[0])
    return jnp.sum(jnp.where(places[:, None] >= places[None, :], values[None, :], 0), axis=1)


def earlier(picks):
    places = jnp.arange(picks.shape[0])
    before = (places[:, None] > places[None, :]).astype(jnp.bfloat16)
    return jnp.dot(
        before, picks.astype(jnp.bfloat16), preferred_element_type=jnp.float32
    ).astype(jnp.int32)


def norm_parts(values, gain, shift):
    centered = values - jnp.mean(values, axis=1, keepdims=True)
    scale = lax.rsqrt(jnp.mean(centered * centered, axis=1, keepdims=True) + epsilon)
    normal = centered * scale
    return (normal * gain + shift, normal, scale)


def norm_back(upstream, normal, scale, gain):
    scaled = upstream * gain
    inner = (
        scaled
        - jnp.mean(scaled, axis=1, keepdims=True)
        - normal * jnp.mean(scaled * normal, axis=1, keepdims=True)
    )
    return (inner * scale, jnp.sum(upstream * normal, axis=0), jnp.sum(upstream, axis=0))


def gelu_slope(values):
    return (
        0.5 * (1.0 + lax.erf(values * 0.7071067811865476))
        + values * jnp.exp(-0.5 * values * values) * 0.3989422804014327
    )


def expert_forward(gathered, upward, downward):
    before = jnp.dot(gathered, upward, preferred_element_type=jnp.float32)
    active = jax.nn.gelu(before, approximate=False).astype(jnp.bfloat16)
    return jnp.dot(active, downward, preferred_element_type=jnp.float32)


def expert_backward(gathered, incoming, upward, downward):
    before = jnp.dot(gathered, upward, preferred_element_type=jnp.float32)
    active = jax.nn.gelu(before, approximate=False).astype(jnp.bfloat16)
    down_grad = jnp.einsum("rf,rd->fd", active, incoming, preferred_element_type=jnp.float32)
    through = jnp.einsum("rd,fd->rf", incoming, downward, preferred_element_type=jnp.float32)
    hidden_grad = (through * gelu_slope(before)).astype(jnp.bfloat16)
    up_grad = jnp.einsum("rd,rf->df", gathered, hidden_grad, preferred_element_type=jnp.float32)
    return (up_grad, down_grad, hidden_grad)


def head_forward(allowed, item):
    query, keys, values = item
    factor = query.shape[1] ** (-0.5)
    scores = jnp.einsum("qd,kd->qk", query, keys, preferred_element_type=jnp.float32) * factor
    scores = jnp.where(allowed, scores, -1000000000.0)
    peak = jnp.max(scores, axis=1, keepdims=True)
    weights = jnp.exp(scores - peak)
    total = jnp.sum(weights, axis=1, keepdims=True)
    mixed = jnp.dot(
        (weights / total).astype(jnp.bfloat16), values, preferred_element_type=jnp.float32
    )
    return (mixed.astype(jnp.bfloat16), (peak + jnp.log(total))[:, 0])


def head_backward(allowed, item):
    query, keys, values, upstream, log_total = item
    factor = query.shape[1] ** (-0.5)
    scores = jnp.einsum("qd,kd->qk", query, keys, preferred_element_type=jnp.float32) * factor
    scores = jnp.where(allowed, scores, -1000000000.0)
    probs = jnp.exp(scores - log_total[:, None])
    value_grad = jnp.einsum(
        "qk,qd->kd", probs.astype(jnp.bfloat16), upstream, preferred_element_type=jnp.float32
    )
    prob_grad = jnp.einsum("qd,kd->qk", upstream, values, preferred_element_type=jnp.float32)
    inner = jnp.sum(prob_grad * probs, axis=1, keepdims=True)
    score_grad = (probs * (prob_grad - inner)).astype(jnp.bfloat16)
    query_grad = (
        jnp.einsum("qk,kd->qd", score_grad, keys, preferred_element_type=jnp.float32) * factor
    )
    key_grad = (
        jnp.einsum("qk,qd->kd", score_grad, query, preferred_element_type=jnp.float32) * factor
    )
    return (query_grad, key_grad, value_grad)


def moving_tokens(
    tokens,
    gains,
    shifts,
    projection,
    mixing,
    factors,
    biases,
    centroids,
    expanding,
    contracting,
    routes,
    lengths,
    cotangent,
):
    count, width = tokens.shape
    experts = centroids.shape[0]
    groups = lax.axis_size("expert")
    slab_count = groups // experts
    capacity = max(2, 2 * count // experts)
    total_tokens = count * groups * lax.axis_size("tensor")
    average = total_tokens / experts
    route = routes[:, 0]
    picks = route[:, None] == jnp.arange(experts, dtype=jnp.int32)[None, :]
    picks_int = picks.astype(jnp.int32)
    picks_float = picks.astype(jnp.float32)
    loads = lax.psum(jnp.sum(picks_float, axis=0), ("expert", "tensor"))
    spread = (loads - average) / average
    token_spread = jnp.sum(jnp.where(picks, spread[None, :], 0.0), axis=1)
    ranks = jnp.sum(earlier(picks) * picks_int, axis=1)
    slots = route * capacity + ranks
    places = jnp.arange(count, dtype=jnp.int32)
    documents = jnp.sum(
        (places[:, None] >= running(lengths[0])[None, :]).astype(jnp.int32), axis=1
    )
    allowed = (places[:, None] >= places[None, :]) & (documents[:, None] == documents[None, :])
    inputs = tokens.astype(jnp.float32)
    entry, entry_normal, entry_scale = norm_parts(inputs, gains, shifts)
    entry = entry.astype(jnp.bfloat16)
    joint = jnp.dot(entry, projection, preferred_element_type=jnp.float32).astype(jnp.bfloat16)
    heads = joint.reshape(count, 3, HEADS, width // HEADS).transpose(1, 2, 0, 3)
    mixed, log_total = lax.map(partial(head_forward, allowed), (heads[0], heads[1], heads[2]))
    mixed_rows = mixed.transpose(1, 0, 2).reshape(count, width)
    residual = inputs + jnp.dot(mixed_rows, mixing, preferred_element_type=jnp.float32)
    normed, mixer_normal, mixer_scale = norm_parts(residual, factors, biases)
    chosen = jnp.dot(picks.astype(jnp.bfloat16), centroids, preferred_element_type=jnp.float32)
    gates = jax.nn.sigmoid(jnp.sum(normed * chosen, axis=1))
    outgoing = (
        jnp.zeros((experts * capacity, width), jnp.bfloat16)
        .at[slots]
        .set(normed.astype(jnp.bfloat16))
    )
    copies = jnp.broadcast_to(
        outgoing.reshape(experts, 1, capacity, width), (experts, slab_count, capacity, width)
    ).reshape(groups, capacity, width)
    arrived = lax.all_to_all(copies, "expert", split_axis=0, concat_axis=0, tiled=True)
    sources = groups * capacity
    own_rows = arrived.reshape(sources, width)
    gathered = lax.all_gather(own_rows, "tensor", axis=0, tiled=True)
    produced = lax.psum_scatter(
        expert_forward(gathered, expanding[0], contracting[0]).astype(jnp.bfloat16),
        "tensor",
        scatter_dimension=0,
        tiled=True,
    )
    returned = lax.all_to_all(
        produced.reshape(arrived.shape), "expert", split_axis=0, concat_axis=0, tiled=True
    )
    combined = jnp.sum(
        returned.reshape(experts, slab_count, capacity, width).astype(jnp.float32), axis=1
    ).reshape(experts * capacity, width)
    picked = combined[slots]
    layer_output = (residual + gates[:, None] * picked).astype(jnp.bfloat16)
    balance_part = jnp.sum(token_spread * gates) / total_tokens
    upstream = cotangent.astype(jnp.float32)
    gate_grad = jnp.sum(upstream * picked, axis=1)
    logit_grad = (gate_grad + token_spread / total_tokens) * gates * (1.0 - gates)
    scaled_rows = (gates[:, None] * upstream).astype(jnp.bfloat16)
    grad_slots = jnp.zeros((experts * capacity, width), jnp.bfloat16).at[slots].set(scaled_rows)
    grad_copies = jnp.broadcast_to(
        grad_slots.reshape(experts, 1, capacity, width), (experts, slab_count, capacity, width)
    ).reshape(groups, capacity, width)
    incoming = lax.all_to_all(
        grad_copies, "expert", split_axis=0, concat_axis=0, tiled=True
    ).reshape(sources, width)
    incoming_pair = lax.all_gather(incoming, "tensor", axis=0, tiled=True)
    up_share, down_share, hidden_grad = expert_backward(
        gathered, incoming_pair, expanding[0], contracting[0]
    )
    back_rows = lax.psum_scatter(
        jnp.einsum(
            "rf,df->rd", hidden_grad, expanding[0], preferred_element_type=jnp.float32
        ).astype(jnp.bfloat16),
        "tensor",
        scatter_dimension=0,
        tiled=True,
    )
    back = lax.all_to_all(
        back_rows.reshape(arrived.shape), "expert", split_axis=0, concat_axis=0, tiled=True
    )
    back_sum = jnp.sum(
        back.reshape(experts, slab_count, capacity, width).astype(jnp.float32), axis=1
    ).reshape(experts * capacity, width)
    normed_grad = back_sum[slots] + logit_grad[:, None] * chosen
    centroid_grad = jnp.einsum(
        "te,td->ed", picks_float, logit_grad[:, None] * normed, precision=highest
    )
    mixer_back, factor_grad, bias_grad = norm_back(normed_grad, mixer_normal, mixer_scale, factors)
    residual_grad = upstream + mixer_back
    branch_grad = residual_grad.astype(jnp.bfloat16)
    mixing_grad = jnp.einsum(
        "td,te->de", mixed_rows, branch_grad, preferred_element_type=jnp.float32
    )
    mixed_grad = jnp.einsum(
        "te,de->td", branch_grad, mixing, preferred_element_type=jnp.float32
    ).astype(jnp.bfloat16)
    head_grads = mixed_grad.reshape(count, HEADS, width // HEADS).transpose(1, 0, 2)
    query_grad, key_grad, value_grad = lax.map(
        partial(head_backward, allowed), (heads[0], heads[1], heads[2], head_grads, log_total)
    )
    joint_grad = (
        jnp.stack((query_grad, key_grad, value_grad))
        .transpose(2, 0, 1, 3)
        .reshape(count, 3 * width)
        .astype(jnp.bfloat16)
    )
    projection_grad = jnp.einsum("td,te->de", entry, joint_grad, preferred_element_type=jnp.float32)
    entry_back = jnp.einsum("te,de->td", joint_grad, projection, preferred_element_type=jnp.float32)
    entry_input, gain_grad, shift_grad = norm_back(entry_back, entry_normal, entry_scale, gains)
    token_grad = residual_grad + entry_input
    summed = lax.psum(
        (
            gain_grad,
            shift_grad,
            projection_grad,
            mixing_grad,
            factor_grad,
            bias_grad,
            centroid_grad,
            balance_part,
        ),
        ("expert", "tensor"),
    )
    return (
        layer_output,
        summed[7],
        token_grad,
        summed[0],
        summed[1],
        summed[2],
        summed[3],
        summed[4],
        summed[5],
        summed[6],
        up_share[None],
        down_share[None],
    )


HALF_LOG = 1.4426950408889634
LN2 = 0.6931471805599453
NT = (((1,), (1,)), ((), ()))
TN = (((0,), (0,)), ((), ()))
VMEM_LIMIT = 60 * 1024 * 1024


def query_blocks(count):
    step = 256 if count > 256 else count
    return [(i, min(i + step, count)) for i in range(0, count, step)]


def document_starts(lengths_ref, places):
    starts = jnp.zeros_like(places)
    end = 0
    for d in range(lengths_ref.shape[0]):
        end = end + lengths_ref[d]
        starts = jnp.where(places >= end, end, starts)
    return starts


def attend_forward(joint, lengths):
    count, width = joint.shape[0], joint.shape[1] // 3
    pairs = width // 128
    factor = (width // HEADS) ** (-0.5) * HALF_LOG

    def kernel(lengths_ref, q_ref, k_ref, v_ref, o_ref, l_ref, bias_ref):
        @pl.when(pl.program_id(0) == 0)
        def _():
            rows = lax.broadcasted_iota(jnp.int32, (count, 1), 0)
            starts = document_starts(lengths_ref, rows)
            for s, e in query_blocks(count):
                column = lax.broadcasted_iota(jnp.int32, (count, e - s), 1) + s
                seen = (column <= rows) & (column >= starts)
                bias_ref[:, s:e] = jnp.where(seen, 0.0, -1e9)

        first = lax.broadcasted_iota(jnp.int32, (1, 128), 1) < 64
        for s, e in query_blocks(count):
            outs, logs = [], []
            for half in range(2):
                q = jnp.where(first == (half == 0), q_ref[s:e, :], jnp.bfloat16(0))
                scores = lax.dot_general(
                    q, k_ref[0:e, :], NT, preferred_element_type=jnp.float32
                )
                scores = scores * factor + bias_ref[s:e, 0:e]
                peak = jnp.max(scores, axis=1, keepdims=True)
                weights = jnp.exp2(scores - peak)
                total = jnp.sum(weights, axis=1, keepdims=True)
                mixed = jnp.dot(
                    weights.astype(jnp.bfloat16),
                    v_ref[0:e, :],
                    preferred_element_type=jnp.float32,
                )
                outs.append(mixed / total)
                logs.append(peak + jnp.log2(total))
            o_ref[s:e, :] = jnp.where(first, outs[0], outs[1]).astype(jnp.bfloat16)
            spread = jnp.transpose(jnp.where(first, logs[0], logs[1]))
            l_ref[0, 0:1, s:e] = spread[0:1, :]
            l_ref[0, 1:2, s:e] = spread[64:65, :]

    return pl.pallas_call(
        kernel,
        out_shape=(
            jax.ShapeDtypeStruct((count, width), jnp.bfloat16),
            jax.ShapeDtypeStruct((pairs, 2, count), jnp.float32),
        ),
        grid_spec=pltpu.PrefetchScalarGridSpec(
            num_scalar_prefetch=1,
            grid=(pairs,),
            in_specs=[
                pl.BlockSpec((count, 128), lambda p, _: (0, p)),
                pl.BlockSpec((count, 128), lambda p, _: (0, pairs + p)),
                pl.BlockSpec((count, 128), lambda p, _: (0, 2 * pairs + p)),
            ],
            out_specs=(
                pl.BlockSpec((count, 128), lambda p, _: (0, p)),
                pl.BlockSpec((1, 2, count), lambda p, _: (p, 0, 0)),
            ),
            scratch_shapes=[pltpu.VMEM((count, count), jnp.float32)],
        ),
        compiler_params=pltpu.CompilerParams(vmem_limit_bytes=VMEM_LIMIT),
        cost_estimate=pl.CostEstimate(
            flops=4 * count * count * width, bytes_accessed=8 * count * width, transcendentals=count * count * HEADS
        ),
    )(lengths, joint, joint, joint)


def attend_backward(joint, mixed, upstream, logs, lengths):
    count, width = joint.shape[0], joint.shape[1] // 3
    pairs = width // 128
    scale = (width // HEADS) ** (-0.5)
    factor = scale * HALF_LOG

    def kernel(
        lengths_ref, q_ref, k_ref, v_ref, o_ref, u_ref, l_ref, dq_ref, dk_ref, dv_ref, bias_ref, ka_ref, va_ref
    ):
        @pl.when(pl.program_id(0) == 0)
        def _():
            places = lax.broadcasted_iota(jnp.int32, (1, count), 1)
            starts = document_starts(lengths_ref, places)
            for s, e in query_blocks(count):
                row = lax.broadcasted_iota(jnp.int32, (e - s, count), 0) + s
                seen = (row <= places) & (row >= starts)
                bias_ref[s:e, :] = jnp.where(seen, 0.0, -1e9)

        first = lax.broadcasted_iota(jnp.int32, (1, 128), 1) < 64
        ka_ref[...] = jnp.zeros_like(ka_ref)
        va_ref[...] = jnp.zeros_like(va_ref)
        for s, e in query_blocks(count):
            both = jnp.transpose(
                u_ref[s:e, :].astype(jnp.float32) * o_ref[s:e, :].astype(jnp.float32)
            )
            found = []
            for half in range(2):
                mine = first == (half == 0)
                inner = jnp.sum(both[64 * half : 64 * half + 64, :], axis=0, keepdims=True)
                q = jnp.where(mine, q_ref[s:e, :], jnp.bfloat16(0))
                u = jnp.where(mine, u_ref[s:e, :], jnp.bfloat16(0))
                scores = lax.dot_general(
                    k_ref[0:e, :], q, NT, preferred_element_type=jnp.float32
                )
                probs = jnp.exp2(
                    scores * factor + bias_ref[0:e, s:e] - l_ref[0, half : half + 1, s:e]
                )
                prob_grad = lax.dot_general(
                    v_ref[0:e, :], u, NT, preferred_element_type=jnp.float32
                )
                score_grad = (probs * (prob_grad - inner)).astype(jnp.bfloat16)
                va_ref[0:e, :] += jnp.dot(
                    probs.astype(jnp.bfloat16), u, preferred_element_type=jnp.float32
                )
                ka_ref[0:e, :] += jnp.dot(score_grad, q, preferred_element_type=jnp.float32)
                found.append(
                    lax.dot_general(
                        score_grad, k_ref[0:e, :], TN, preferred_element_type=jnp.float32
                    )
                )
            dq_ref[s:e, :] = (jnp.where(first, found[0], found[1]) * scale).astype(jnp.bfloat16)
        dk_ref[...] = (ka_ref[...] * scale).astype(jnp.bfloat16)
        dv_ref[...] = va_ref[...].astype(jnp.bfloat16)

    column = lambda shift: pl.BlockSpec((count, 128), lambda p, _: (0, shift + p))
    return pl.pallas_call(
        kernel,
        out_shape=(jax.ShapeDtypeStruct((count, width), jnp.bfloat16),) * 3,
        grid_spec=pltpu.PrefetchScalarGridSpec(
            num_scalar_prefetch=1,
            grid=(pairs,),
            in_specs=[
                column(0),
                column(pairs),
                column(2 * pairs),
                column(0),
                column(0),
                pl.BlockSpec((1, 2, count), lambda p, _: (p, 0, 0)),
            ],
            out_specs=(column(0),) * 3,
            scratch_shapes=[
                pltpu.VMEM((count, count), jnp.float32),
                pltpu.VMEM((count, 128), jnp.float32),
                pltpu.VMEM((count, 128), jnp.float32),
            ],
        ),
        compiler_params=pltpu.CompilerParams(vmem_limit_bytes=VMEM_LIMIT),
        cost_estimate=pl.CostEstimate(
            flops=10 * count * count * width, bytes_accessed=16 * count * width, transcendentals=count * count * HEADS
        ),
    )(lengths, joint, joint, joint, mixed, upstream, logs)


TILE = 256
ALIGN = 16


def aligned_rows(count, experts):
    return -(-(count + experts * (ALIGN - 1)) // ALIGN) * ALIGN


def gelu_pair(values):
    bell = jnp.exp2(values * values * (-0.5 * HALF_LOG))
    near = 1.0 / (1.0 + (0.3275911 * 0.7071067811865476) * jnp.abs(values))
    series = 1.061405429 * 0.5 * near - 1.453152027 * 0.5
    series = series * near + 1.421413741 * 0.5
    series = series * near - 0.284496736 * 0.5
    series = series * near + 0.254829592 * 0.5
    tail = series * near * bell
    below = jnp.where(values >= 0.0, 1.0 - tail, tail)
    return values * below, below + values * bell * 0.3989422804014327


def expert_kernel_body(
    experts,
    sources,
    rows,
    limit,
    width,
    hidden,
    meta_ref,
    *refs,
):
    sent_refs, refs = refs[:sources], refs[sources:]
    cot_refs, refs = refs[:sources], refs[sources:]
    gate_refs, refs = refs[:sources], refs[sources:]
    near_refs, refs = refs[: 2 * experts - 1], refs[2 * experts - 1 :]
    far_refs, refs = refs[: 2 * experts - 1], refs[2 * experts - 1 :]
    back_outs, refs = refs[:sources], refs[sources:]
    made_outs, refs = refs[:sources], refs[sources:]
    dot_outs, refs = refs[:sources], refs[sources:]
    near_out, far_out = refs[:2]
    (x_ref, c_ref, g_ref, column_ref, up_ref, down_ref, gu_ref, gd_ref, pack_ref, zero_ref) = refs[2:12]
    weight_sem, row_sem, out_sem, grad_sem, zero_sem = refs[12:]
    half = hidden // 2
    own = meta_ref[0]

    def size_of(s, e):
        return meta_ref[1 + s * experts + e]

    source_at, joined_at, tiles = {}, {}, []
    first = []
    base = 0
    for s in range(sources):
        at = 0
        for e in range(experts):
            source_at[s, e] = at
            at = at + size_of(s, e)
        source_at[s, experts] = at
    for e in range(experts):
        first.append(base)
        at = base
        for s in range(sources):
            joined_at[s, e] = at
            at = at + size_of(s, e)
        number = (at - base + (TILE - 1)) // TILE
        tiles.append(number)
        base = base + number * TILE

    bits = [1 << b for b in range(limit.bit_length()) if ALIGN <= (1 << b)]

    def pieces(s, e):
        size = size_of(s, e)
        for i, piece in enumerate(bits):
            yield i, piece, (size & piece) != 0, size & (piece - 1)

    def move_in(s, e, act):
        for i, piece, taken, offset in pieces(s, e):
            @pl.when(taken)
            def _(i=i, piece=piece, offset=offset):
                src = pl.ds(pl.multiple_of(source_at[s, e] + offset, ALIGN), piece)
                dst = pl.ds(pl.multiple_of(joined_at[s, e] + offset, ALIGN), piece)
                k = s * experts + e
                act(pltpu.make_async_copy(sent_refs[s].at[src], x_ref.at[dst], row_sem.at[0, k, i]))
                act(pltpu.make_async_copy(cot_refs[s].at[src], c_ref.at[dst], row_sem.at[1, k, i]))

    def move_out(s, e, act):
        for i, piece, taken, offset in pieces(s, e):
            @pl.when(taken)
            def _(i=i, piece=piece, offset=offset):
                src = pl.ds(pl.multiple_of(source_at[s, e] + offset, ALIGN), piece)
                dst = pl.ds(pl.multiple_of(joined_at[s, e] + offset, ALIGN), piece)
                k = s * experts + e
                act(pltpu.make_async_copy(x_ref.at[dst], made_outs[s].at[src], out_sem.at[0, k, i]))
                act(pltpu.make_async_copy(c_ref.at[dst], back_outs[s].at[src], out_sem.at[1, k, i]))

    def move_weights(e, act):
        step = e - own
        for k in range(2 * experts - 1):
            @pl.when(step == k - (experts - 1))
            def _(k=k):
                for j, ref in enumerate((near_refs[k], far_refs[k])):
                    lanes = pl.ds(j * half, half)
                    act(pltpu.make_async_copy(ref.at[pl.ds(0, width)], up_ref.at[e, :, lanes], weight_sem.at[e, j, 0]))
                    for part in range(2):
                        act(
                            pltpu.make_async_copy(
                                ref.at[pl.ds(width + part * half, half)],
                                down_ref.at[e, lanes, pl.ds(part * half, half)],
                                weight_sem.at[e, j, 1 + part],
                            )
                        )

    zero_ref[...] = jnp.zeros_like(zero_ref)
    for e in range(experts):
        @pl.when(tiles[e] > 0)
        def _(e=e):
            last = pl.ds(pl.multiple_of(first[e] + (tiles[e] - 1) * TILE, TILE), TILE)
            x_ref[last, :] = jnp.zeros((TILE, width), jnp.bfloat16)
            c_ref[last, :] = jnp.zeros((TILE, width), jnp.bfloat16)
            g_ref[last, :] = jnp.zeros((TILE, 128), jnp.float32)

    for e in range(experts):
        move_weights(e, lambda copy: copy.start())
        for s in range(sources):
            move_in(s, e, lambda copy: copy.start())

    tail_chunks = rows // ALIGN

    def tail(s, act):
        def one(i, _):
            @pl.when(i * ALIGN >= source_at[s, experts])
            def _():
                dst = pl.ds(pl.multiple_of(i * ALIGN, ALIGN), ALIGN)
                act(pltpu.make_async_copy(zero_ref, made_outs[s].at[dst], zero_sem.at[0, s, i]))
                act(pltpu.make_async_copy(zero_ref, back_outs[s].at[dst], zero_sem.at[1, s, i]))
            return 0
        lax.fori_loop(tail_chunks - 5, tail_chunks, one, 0)

    for s in range(sources):
        tail(s, lambda copy: copy.start())

    for s in range(sources):
        column_ref[...] = jnp.broadcast_to(
            jnp.transpose(jnp.broadcast_to(gate_refs[s][0:1, :], (128, rows)))[:, 0:128], (rows, 128)
        )
        for e in range(experts):
            def one(i, _, s=s, e=e):
                src = pl.ds(pl.multiple_of(source_at[s, e] + i * ALIGN, ALIGN), ALIGN)
                dst = pl.ds(pl.multiple_of(joined_at[s, e] + i * ALIGN, ALIGN), ALIGN)
                g_ref[dst, :] = column_ref[src, :]
                return 0
            lax.fori_loop(0, size_of(s, e) // ALIGN, one, 0)

    for e in range(experts):
        move_weights(e, lambda copy: copy.wait())
        for s in range(sources):
            move_in(s, e, lambda copy: copy.wait())
        gu_ref[...] = jnp.zeros_like(gu_ref)
        gd_ref[...] = jnp.zeros_like(gd_ref)

        def tile(t, _, e=e):
            at = pl.ds(pl.multiple_of(first[e] + t * TILE, TILE), TILE)
            x, c, gate = x_ref[at, :], c_ref[at, :], g_ref[at, 0:1]
            before = jnp.dot(x, up_ref[e], preferred_element_type=jnp.float32)
            active, slope = gelu_pair(before)
            through = lax.dot_general(c, down_ref[e], NT, preferred_element_type=jnp.float32)
            grad = (through * (slope * gate)).astype(jnp.bfloat16)
            gated = (active * gate).astype(jnp.bfloat16)
            made = jnp.dot(active.astype(jnp.bfloat16), down_ref[e], preferred_element_type=jnp.float32)
            g_ref[at, :] = jnp.broadcast_to(
                jnp.sum(made * c.astype(jnp.float32), axis=1, keepdims=True), (TILE, 128)
            )
            gd_ref[...] += lax.dot_general(gated, c, TN, preferred_element_type=jnp.float32)
            gu_ref[...] += lax.dot_general(x, grad, TN, preferred_element_type=jnp.float32)
            back = lax.dot_general(grad, up_ref[e], NT, preferred_element_type=jnp.float32)
            x_ref[at, :] = made.astype(jnp.bfloat16)
            c_ref[at, :] = back.astype(jnp.bfloat16)
            return 0

        lax.fori_loop(0, tiles[e], tile, 0)
        for s in range(sources):
            move_out(s, e, lambda copy: copy.start())

        slot = e % 2
        grads = lambda e, slot: [
            pltpu.make_async_copy(pack_ref.at[slot, j], ref.at[e - own + experts - 1], grad_sem.at[slot, j])
            for j, ref in enumerate((near_out, far_out))
        ]
        if e >= 2:
            for copy in grads(e - 2, slot):
                copy.wait()
        for j in range(2):
            pack_ref[slot, j, 0:width, :] = gu_ref[:, j * half : (j + 1) * half].astype(jnp.bfloat16)
            for part in range(2):
                pack_ref[slot, j, width + part * half : width + (part + 1) * half, :] = gd_ref[
                    j * half : (j + 1) * half, part * half : (part + 1) * half
                ].astype(jnp.bfloat16)
        for copy in grads(e, slot):
            copy.start()

    for s in range(sources):
        for e in range(experts):
            def one(i, _, s=s, e=e):
                src = pl.ds(pl.multiple_of(source_at[s, e] + i * ALIGN, ALIGN), ALIGN)
                dst = pl.ds(pl.multiple_of(joined_at[s, e] + i * ALIGN, ALIGN), ALIGN)
                column_ref[src, :] = g_ref[dst, :]
                return 0
            lax.fori_loop(0, size_of(s, e) // ALIGN, one, 0)
        dot_outs[s][...] = jnp.transpose(column_ref[...])[0:8, :]

    for e in range(experts):
        for s in range(sources):
            move_out(s, e, lambda copy: copy.wait())
    for s in range(sources):
        tail(s, lambda copy: copy.wait())
    for e in range(max(0, experts - 2), experts):
        for copy in grads(e, e % 2):
            copy.wait()


def expert_stage(meta, sent, cot, gates, near, far, experts, limit):
    sources = len(sent)
    rows, width = sent[0].shape
    half = near[0].shape[1]
    hidden = 2 * half
    joined = -(-(sources * rows + experts * (TILE - 1)) // TILE) * TILE
    limit = -(-limit // ALIGN) * ALIGN
    pieces = limit.bit_length() - ALIGN.bit_length() + 1
    anywhere = pl.BlockSpec(memory_space=pl.ANY)
    local = pl.BlockSpec(memory_space=pltpu.VMEM)
    slots = 2 * experts - 1
    dma = pltpu.SemaphoreType.DMA
    outs = pl.pallas_call(
        partial(expert_kernel_body, experts, sources, rows, limit, width, hidden),
        out_shape=(
            [jax.ShapeDtypeStruct((rows, width), jnp.bfloat16)] * (2 * sources)
            + [jax.ShapeDtypeStruct((8, rows), jnp.float32)] * sources
            + [jax.ShapeDtypeStruct((slots,) + near[0].shape, jnp.bfloat16)] * 2
        ),
        in_specs=[pl.BlockSpec(memory_space=pltpu.SMEM)]
        + [anywhere] * (2 * sources)
        + [local] * sources
        + [anywhere] * (2 * slots),
        out_specs=[anywhere] * (2 * sources) + [local] * sources + [anywhere] * 2,
        scratch_shapes=[
            pltpu.VMEM((joined, width), jnp.bfloat16),
            pltpu.VMEM((joined, width), jnp.bfloat16),
            pltpu.VMEM((joined, 128), jnp.float32),
            pltpu.VMEM((rows, 128), jnp.float32),
            pltpu.VMEM((experts, width, hidden), jnp.bfloat16),
            pltpu.VMEM((experts, hidden, width), jnp.bfloat16),
            pltpu.VMEM((width, hidden), jnp.float32),
            pltpu.VMEM((hidden, width), jnp.float32),
            pltpu.VMEM((2, 2) + near[0].shape, jnp.bfloat16),
            pltpu.VMEM((ALIGN, width), jnp.bfloat16),
            dma((experts, 2, 3)),
            dma((2, sources * experts, pieces)),
            dma((2, sources * experts, pieces)),
            dma((2, 2)),
            dma((2, sources, rows // ALIGN)),
        ],
        compiler_params=pltpu.CompilerParams(vmem_limit_bytes=VMEM_LIMIT),
        cost_estimate=pl.CostEstimate(
            flops=12 * sources * rows * width * hidden, bytes_accessed=100_000_000, transcendentals=sources * rows * hidden
        ),
    )(meta, *sent, *cot, *gates, *near, *far)
    back, made, dots = outs[:sources], outs[sources : 2 * sources], outs[2 * sources : 3 * sources]
    return back, made, dots, outs[-2], outs[-1]


def swap(value, bit):
    groups = lax.axis_size("expert")
    return lax.ppermute(value, "expert", [(i, i ^ bit) for i in range(groups)])


def across(value):
    return lax.ppermute(value, "tensor", [(0, 1), (1, 0)])


def spread_out(value):
    other = swap(value, 2)
    return [value, across(value), other, across(other)]


def line(value, step, planes, slabs, least):
    pairs = []
    for i in range(planes * slabs):
        plane = i // slabs
        source = plane if step > 0 else planes - 1 - plane
        if source >= least and 0 <= plane + step < planes:
            pairs.append((i, i + step * slabs))
    return lax.ppermute(value, "expert", pairs)


def beside(value, planes, slabs, shift):
    pairs = [
        (i, i ^ 1) for i in range(planes * slabs) if 0 <= i // slabs + shift < planes
    ]
    return lax.ppermute(value, "expert", pairs)


def gather_weights(packed, planes, slabs):
    near = [None] * (2 * planes - 1)
    near[planes - 1] = packed
    for k in range(1, planes):
        near[planes - 1 - k] = line(near[planes - k], 1, planes, slabs, k - 1)
        near[planes - 1 + k] = line(near[planes - 2 + k], -1, planes, slabs, k - 1)
    far = [None] * (2 * planes - 1)
    for k in range(planes):
        for sign in (1, -1):
            if k or sign > 0:
                at = planes - 1 + sign * k
                far[at] = beside(near[at], planes, slabs, sign * k)
    return near, far


def reduce_weights(near, far, planes, slabs):
    sums = {}
    for k in range(planes - 1, -1, -1):
        for sign in (1, -1):
            if k or sign > 0:
                at = planes - 1 + sign * k
                came = beside(far[at], planes, slabs, sign * k)
                sums[sign * k] = near[at].astype(jnp.float32) + came.astype(jnp.float32)
    arrived = []
    for sign in (1, -1):
        came = None
        for k in range(planes - 1, 0, -1):
            total = sums[sign * k]
            if came is not None:
                total = total + came.astype(jnp.float32)
            pairs = [
                (i, i + sign * slabs)
                for i in range(planes * slabs)
                if 0 <= i // slabs + sign * k < planes
            ]
            came = lax.ppermute(total.astype(jnp.bfloat16), "expert", pairs)
        arrived.append(came.astype(jnp.float32))
    return sums[0] + arrived[0] + arrived[1]


def per_device(
    tokens,
    gains,
    shifts,
    projection,
    mixing,
    factors,
    biases,
    centroids,
    expanding,
    contracting,
    routes,
    lengths,
    cotangent,
):
    count, width = tokens.shape
    experts = centroids.shape[0]
    groups = lax.axis_size("expert")
    slabs = groups // experts
    half = expanding.shape[2]
    limit = 2 * count // experts
    total_tokens = count * groups * lax.axis_size("tensor")
    average = total_tokens / experts
    rows = aligned_rows(count, experts)
    me, core = lax.axis_index("expert"), lax.axis_index("tensor")

    packed = jnp.concatenate(
        (expanding[0], contracting[0, :, :half], contracting[0, :, half:]), axis=0
    )
    near, far = gather_weights(packed, experts, slabs)

    route = routes[:, 0]
    picks = route[:, None] == jnp.arange(experts, dtype=jnp.int32)[None, :]
    picks_int = picks.astype(jnp.int32)
    counts = jnp.sum(picks_int, axis=0)
    all_counts = lax.all_gather(counts, ("expert", "tensor"))
    loads = jnp.sum(all_counts, axis=0).astype(jnp.float32)
    spread = (loads - average) / average
    token_spread = jnp.sum(jnp.where(picks, spread[None, :], 0.0), axis=1)
    sizes = (all_counts + (ALIGN - 1)) // ALIGN * ALIGN
    mine = sizes[me * 2 + core]
    starts = running(mine) - mine
    ranks = earlier(picks)
    position = jnp.sum((ranks + starts[None, :]) * picks_int, axis=1)
    order = (jnp.arange(rows, dtype=jnp.int32)[:, None] == position[None, :]).astype(jnp.bfloat16)
    back_order = (position[:, None] == jnp.arange(rows, dtype=jnp.int32)[None, :]).astype(jnp.bfloat16)
    group = [me * 2 + core, me * 2 + 1 - core, (me ^ 2) * 2 + core, (me ^ 2) * 2 + 1 - core]
    meta = jnp.concatenate(
        [(me // slabs).astype(jnp.int32)[None]] + [sizes[g] for g in group]
    )
    sorted_cot = jnp.dot(order, cotangent, preferred_element_type=jnp.float32).astype(jnp.bfloat16)
    group_cot = spread_out(sorted_cot)

    inputs = tokens.astype(jnp.float32)
    entry, entry_normal, entry_scale = norm_parts(inputs, gains, shifts)
    entry = entry.astype(jnp.bfloat16)
    joint = jnp.dot(entry, projection, preferred_element_type=jnp.float32).astype(jnp.bfloat16)
    mixed_rows, logs = attend_forward(joint, lengths[0])
    residual = inputs + jnp.dot(mixed_rows, mixing, preferred_element_type=jnp.float32)
    normed, mixer_normal, mixer_scale = norm_parts(residual, factors, biases)
    chosen = jnp.dot(picks.astype(jnp.bfloat16), centroids, preferred_element_type=jnp.float32)
    gates = jax.nn.sigmoid(jnp.sum(normed * chosen, axis=1))
    sorted_sent = jnp.dot(
        order, normed.astype(jnp.bfloat16), preferred_element_type=jnp.float32
    ).astype(jnp.bfloat16)
    sorted_gates = jnp.sum(
        jnp.where(position[:, None] == jnp.arange(rows, dtype=jnp.int32)[None, :], gates[:, None], 0.0),
        axis=0,
    )
    group_gates = spread_out(jnp.broadcast_to(sorted_gates[None, :], (8, rows)))
    group_sent = spread_out(sorted_sent)
    back, made, dots, near_grads, far_grads = expert_stage(
        meta, group_sent, group_cot, group_gates, near, far, experts, limit
    )

    def collect(parts, narrow):
        own = parts[0].astype(jnp.float32) + across(parts[1]).astype(jnp.float32)
        other = parts[2].astype(jnp.float32) + across(parts[3]).astype(jnp.float32)
        return own, swap(other.astype(narrow), 2)

    def unsort(own, came):
        high = own.astype(jnp.bfloat16)
        return jnp.dot(
            back_order, high, preferred_element_type=jnp.float32
        ) + jnp.dot(back_order, came, preferred_element_type=jnp.float32)

    dot_own, dot_came = collect(dots, jnp.float32)
    gate_rows = (dot_own + dot_came)[0]
    gate_grad = jnp.sum(
        jnp.where(position[:, None] == jnp.arange(rows, dtype=jnp.int32)[None, :], gate_rows[None, :], 0.0),
        axis=1,
    )
    sent_grad = unsort(*collect(back, jnp.bfloat16))
    made_own, made_came = collect(made, jnp.bfloat16)
    up_down = reduce_weights(near_grads, far_grads, experts, slabs)

    upstream = cotangent.astype(jnp.float32)
    balance_part = jnp.sum(token_spread * gates) / total_tokens
    logit_grad = (gate_grad + token_spread / total_tokens) * gates * (1.0 - gates)
    normed_grad = sent_grad + logit_grad[:, None] * chosen
    centroid_grad = jnp.einsum(
        "te,td->ed", picks.astype(jnp.float32), logit_grad[:, None] * normed, precision=highest
    )
    mixer_back, factor_grad, bias_grad = norm_back(normed_grad, mixer_normal, mixer_scale, factors)
    residual_grad = upstream + mixer_back
    branch_grad = residual_grad.astype(jnp.bfloat16)
    mixing_grad = jnp.einsum(
        "td,te->de", mixed_rows, branch_grad, preferred_element_type=jnp.float32
    )
    mixed_grad = jnp.einsum(
        "te,de->td", branch_grad, mixing, preferred_element_type=jnp.float32
    ).astype(jnp.bfloat16)
    joint_grad = jnp.concatenate(
        attend_backward(joint, mixed_rows, mixed_grad, logs, lengths[0]), axis=1
    )
    projection_grad = jnp.einsum("td,te->de", entry, joint_grad, preferred_element_type=jnp.float32)
    entry_back = jnp.einsum("te,de->td", joint_grad, projection, preferred_element_type=jnp.float32)
    entry_input, gain_grad, shift_grad = norm_back(entry_back, entry_normal, entry_scale, gains)
    token_grad = residual_grad + entry_input
    layer_output = (residual + gates[:, None] * unsort(made_own, made_came)).astype(jnp.bfloat16)
    summed = lax.psum(
        (
            gain_grad,
            shift_grad,
            projection_grad,
            mixing_grad,
            factor_grad,
            bias_grad,
            centroid_grad,
            balance_part,
        ),
        ("expert", "tensor"),
    )
    return (
        layer_output,
        summed[7],
        token_grad,
        summed[0],
        summed[1],
        summed[2],
        summed[3],
        summed[4],
        summed[5],
        summed[6],
        up_down[:width][None],
        jnp.concatenate((up_down[width : width + half], up_down[width + half :]), axis=1)[None],
    )


def solution(mesh):
    placed = (
        P(("expert", "tensor"), None),
        P(),
        P(),
        P(),
        P(),
        P(),
        P(),
        P(),
        P("expert", None, "tensor"),
        P("expert", "tensor", None),
        P(("expert", "tensor"), None),
        P(("expert", "tensor"), None),
        P(("expert", "tensor"), None),
    )
    near = mesh.shape["expert"] == 16 and mesh.shape["tensor"] == 2
    return jax.shard_map(
        per_device if near else moving_tokens,
        mesh=mesh,
        in_specs=placed,
        out_specs=(
            P(("expert", "tensor"), None),
            P(),
            P(("expert", "tensor"), None),
            P(),
            P(),
            P(),
            P(),
            P(),
            P(),
            P(),
            P("expert", None, "tensor"),
            P("expert", "tensor", None),
        ),
        check_vma=False,
    )
```

```python
from functools import partial

import jax
import jax.numpy as jnp
from jax import lax
from jax.experimental import pallas as pl
from jax.experimental.pallas import tpu as pltpu
from jax.sharding import PartitionSpec as P

HEADS = 12


highest = lax.Precision.HIGHEST
epsilon = 1e-05


def running(values):
    places = jnp.arange(values.shape[0])
    return jnp.sum(jnp.where(places[:, None] >= places[None, :], values[None, :], 0), axis=1)


def earlier(picks):
    places = jnp.arange(picks.shape[0])
    before = (places[:, None] > places[None, :]).astype(jnp.bfloat16)
    return jnp.dot(
        before, picks.astype(jnp.bfloat16), preferred_element_type=jnp.float32
    ).astype(jnp.int32)


def norm_parts(values, gain, shift):
    centered = values - jnp.mean(values, axis=1, keepdims=True)
    scale = lax.rsqrt(jnp.mean(centered * centered, axis=1, keepdims=True) + epsilon)
    normal = centered * scale
    return (normal * gain + shift, normal, scale)


def norm_back(upstream, normal, scale, gain):
    scaled = upstream * gain
    inner = (
        scaled
        - jnp.mean(scaled, axis=1, keepdims=True)
        - normal * jnp.mean(scaled * normal, axis=1, keepdims=True)
    )
    return (inner * scale, jnp.sum(upstream * normal, axis=0), jnp.sum(upstream, axis=0))


def gelu_slope(values):
    return (
        0.5 * (1.0 + lax.erf(values * 0.7071067811865476))
        + values * jnp.exp(-0.5 * values * values) * 0.3989422804014327
    )


def expert_forward(gathered, upward, downward):
    before = jnp.dot(gathered, upward, preferred_element_type=jnp.float32)
    active = jax.nn.gelu(before, approximate=False).astype(jnp.bfloat16)
    return jnp.dot(active, downward, preferred_element_type=jnp.float32)


def expert_backward(gathered, incoming, upward, downward):
    before = jnp.dot(gathered, upward, preferred_element_type=jnp.float32)
    active = jax.nn.gelu(before, approximate=False).astype(jnp.bfloat16)
    down_grad = jnp.einsum("rf,rd->fd", active, incoming, preferred_element_type=jnp.float32)
    through = jnp.einsum("rd,fd->rf", incoming, downward, preferred_element_type=jnp.float32)
    hidden_grad = (through * gelu_slope(before)).astype(jnp.bfloat16)
    up_grad = jnp.einsum("rd,rf->df", gathered, hidden_grad, preferred_element_type=jnp.float32)
    return (up_grad, down_grad, hidden_grad)


def head_forward(allowed, item):
    query, keys, values = item
    factor = query.shape[1] ** (-0.5)
    scores = jnp.einsum("qd,kd->qk", query, keys, preferred_element_type=jnp.float32) * factor
    scores = jnp.where(allowed, scores, -1000000000.0)
    peak = jnp.max(scores, axis=1, keepdims=True)
    weights = jnp.exp(scores - peak)
    total = jnp.sum(weights, axis=1, keepdims=True)
    mixed = jnp.dot(
        (weights / total).astype(jnp.bfloat16), values, preferred_element_type=jnp.float32
    )
    return (mixed.astype(jnp.bfloat16), (peak + jnp.log(total))[:, 0])


def head_backward(allowed, item):
    query, keys, values, upstream, log_total = item
    factor = query.shape[1] ** (-0.5)
    scores = jnp.einsum("qd,kd->qk", query, keys, preferred_element_type=jnp.float32) * factor
    scores = jnp.where(allowed, scores, -1000000000.0)
    probs = jnp.exp(scores - log_total[:, None])
    value_grad = jnp.einsum(
        "qk,qd->kd", probs.astype(jnp.bfloat16), upstream, preferred_element_type=jnp.float32
    )
    prob_grad = jnp.einsum("qd,kd->qk", upstream, values, preferred_element_type=jnp.float32)
    inner = jnp.sum(prob_grad * probs, axis=1, keepdims=True)
    score_grad = (probs * (prob_grad - inner)).astype(jnp.bfloat16)
    query_grad = (
        jnp.einsum("qk,kd->qd", score_grad, keys, preferred_element_type=jnp.float32) * factor
    )
    key_grad = (
        jnp.einsum("qk,qd->kd", score_grad, query, preferred_element_type=jnp.float32) * factor
    )
    return (query_grad, key_grad, value_grad)


def moving_tokens(
    tokens,
    gains,
    shifts,
    projection,
    mixing,
    factors,
    biases,
    centroids,
    expanding,
    contracting,
    routes,
    lengths,
    cotangent,
):
    count, width = tokens.shape
    experts = centroids.shape[0]
    groups = lax.axis_size("expert")
    slab_count = groups // experts
    capacity = max(2, 2 * count // experts)
    total_tokens = count * groups * lax.axis_size("tensor")
    average = total_tokens / experts
    route = routes[:, 0]
    picks = route[:, None] == jnp.arange(experts, dtype=jnp.int32)[None, :]
    picks_int = picks.astype(jnp.int32)
    picks_float = picks.astype(jnp.float32)
    loads = lax.psum(jnp.sum(picks_float, axis=0), ("expert", "tensor"))
    spread = (loads - average) / average
    token_spread = jnp.sum(jnp.where(picks, spread[None, :], 0.0), axis=1)
    ranks = jnp.sum(earlier(picks) * picks_int, axis=1)
    slots = route * capacity + ranks
    places = jnp.arange(count, dtype=jnp.int32)
    documents = jnp.sum(
        (places[:, None] >= running(lengths[0])[None, :]).astype(jnp.int32), axis=1
    )
    allowed = (places[:, None] >= places[None, :]) & (documents[:, None] == documents[None, :])
    inputs = tokens.astype(jnp.float32)
    entry, entry_normal, entry_scale = norm_parts(inputs, gains, shifts)
    entry = entry.astype(jnp.bfloat16)
    joint = jnp.dot(entry, projection, preferred_element_type=jnp.float32).astype(jnp.bfloat16)
    heads = joint.reshape(count, 3, HEADS, width // HEADS).transpose(1, 2, 0, 3)
    mixed, log_total = lax.map(partial(head_forward, allowed), (heads[0], heads[1], heads[2]))
    mixed_rows = mixed.transpose(1, 0, 2).reshape(count, width)
    residual = inputs + jnp.dot(mixed_rows, mixing, preferred_element_type=jnp.float32)
    normed, mixer_normal, mixer_scale = norm_parts(residual, factors, biases)
    chosen = jnp.dot(picks.astype(jnp.bfloat16), centroids, preferred_element_type=jnp.float32)
    gates = jax.nn.sigmoid(jnp.sum(normed * chosen, axis=1))
    outgoing = (
        jnp.zeros((experts * capacity, width), jnp.bfloat16)
        .at[slots]
        .set(normed.astype(jnp.bfloat16))
    )
    copies = jnp.broadcast_to(
        outgoing.reshape(experts, 1, capacity, width), (experts, slab_count, capacity, width)
    ).reshape(groups, capacity, width)
    arrived = lax.all_to_all(copies, "expert", split_axis=0, concat_axis=0, tiled=True)
    sources = groups * capacity
    own_rows = arrived.reshape(sources, width)
    gathered = lax.all_gather(own_rows, "tensor", axis=0, tiled=True)
    produced = lax.psum_scatter(
        expert_forward(gathered, expanding[0], contracting[0]).astype(jnp.bfloat16),
        "tensor",
        scatter_dimension=0,
        tiled=True,
    )
    returned = lax.all_to_all(
        produced.reshape(arrived.shape), "expert", split_axis=0, concat_axis=0, tiled=True
    )
    combined = jnp.sum(
        returned.reshape(experts, slab_count, capacity, width).astype(jnp.float32), axis=1
    ).reshape(experts * capacity, width)
    picked = combined[slots]
    layer_output = (residual + gates[:, None] * picked).astype(jnp.bfloat16)
    balance_part = jnp.sum(token_spread * gates) / total_tokens
    upstream = cotangent.astype(jnp.float32)
    gate_grad = jnp.sum(upstream * picked, axis=1)
    logit_grad = (gate_grad + token_spread / total_tokens) * gates * (1.0 - gates)
    scaled_rows = (gates[:, None] * upstream).astype(jnp.bfloat16)
    grad_slots = jnp.zeros((experts * capacity, width), jnp.bfloat16).at[slots].set(scaled_rows)
    grad_copies = jnp.broadcast_to(
        grad_slots.reshape(experts, 1, capacity, width), (experts, slab_count, capacity, width)
    ).reshape(groups, capacity, width)
    incoming = lax.all_to_all(
        grad_copies, "expert", split_axis=0, concat_axis=0, tiled=True
    ).reshape(sources, width)
    incoming_pair = lax.all_gather(incoming, "tensor", axis=0, tiled=True)
    up_share, down_share, hidden_grad = expert_backward(
        gathered, incoming_pair, expanding[0], contracting[0]
    )
    back_rows = lax.psum_scatter(
        jnp.einsum(
            "rf,df->rd", hidden_grad, expanding[0], preferred_element_type=jnp.float32
        ).astype(jnp.bfloat16),
        "tensor",
        scatter_dimension=0,
        tiled=True,
    )
    back = lax.all_to_all(
        back_rows.reshape(arrived.shape), "expert", split_axis=0, concat_axis=0, tiled=True
    )
    back_sum = jnp.sum(
        back.reshape(experts, slab_count, capacity, width).astype(jnp.float32), axis=1
    ).reshape(experts * capacity, width)
    normed_grad = back_sum[slots] + logit_grad[:, None] * chosen
    centroid_grad = jnp.einsum(
        "te,td->ed", picks_float, logit_grad[:, None] * normed, precision=highest
    )
    mixer_back, factor_grad, bias_grad = norm_back(normed_grad, mixer_normal, mixer_scale, factors)
    residual_grad = upstream + mixer_back
    branch_grad = residual_grad.astype(jnp.bfloat16)
    mixing_grad = jnp.einsum(
        "td,te->de", mixed_rows, branch_grad, preferred_element_type=jnp.float32
    )
    mixed_grad = jnp.einsum(
        "te,de->td", branch_grad, mixing, preferred_element_type=jnp.float32
    ).astype(jnp.bfloat16)
    head_grads = mixed_grad.reshape(count, HEADS, width // HEADS).transpose(1, 0, 2)
    query_grad, key_grad, value_grad = lax.map(
        partial(head_backward, allowed), (heads[0], heads[1], heads[2], head_grads, log_total)
    )
    joint_grad = (
        jnp.stack((query_grad, key_grad, value_grad))
        .transpose(2, 0, 1, 3)
        .reshape(count, 3 * width)
        .astype(jnp.bfloat16)
    )
    projection_grad = jnp.einsum("td,te->de", entry, joint_grad, preferred_element_type=jnp.float32)
    entry_back = jnp.einsum("te,de->td", joint_grad, projection, preferred_element_type=jnp.float32)
    entry_input, gain_grad, shift_grad = norm_back(entry_back, entry_normal, entry_scale, gains)
    token_grad = residual_grad + entry_input
    summed = lax.psum(
        (
            gain_grad,
            shift_grad,
            projection_grad,
            mixing_grad,
            factor_grad,
            bias_grad,
            centroid_grad,
            balance_part,
        ),
        ("expert", "tensor"),
    )
    return (
        layer_output,
        summed[7],
        token_grad,
        summed[0],
        summed[1],
        summed[2],
        summed[3],
        summed[4],
        summed[5],
        summed[6],
        up_share[None],
        down_share[None],
    )


HALF_LOG = 1.4426950408889634
LN2 = 0.6931471805599453
NT = (((1,), (1,)), ((), ()))
TN = (((0,), (0,)), ((), ()))
VMEM_LIMIT = 60 * 1024 * 1024


def query_blocks(count):
    step = 256 if count > 256 else count
    return [(i, min(i + step, count)) for i in range(0, count, step)]


def document_starts(lengths_ref, places):
    starts = jnp.zeros_like(places)
    end = 0
    for d in range(lengths_ref.shape[0]):
        end = end + lengths_ref[d]
        starts = jnp.where(places >= end, end, starts)
    return starts


def attend_backward(joint, mixed, upstream, logs, lengths):
    count, width = joint.shape[0], joint.shape[1] // 3
    pairs = width // 128
    scale = (width // HEADS) ** (-0.5)
    factor = scale * HALF_LOG

    def kernel(
        lengths_ref, q_ref, k_ref, v_ref, o_ref, u_ref, l_ref, dq_ref, dk_ref, dv_ref, bias_ref, ka_ref, va_ref
    ):
        @pl.when(pl.program_id(0) == 0)
        def _():
            places = lax.broadcasted_iota(jnp.int32, (1, count), 1)
            starts = document_starts(lengths_ref, places)
            for s, e in query_blocks(count):
                row = lax.broadcasted_iota(jnp.int32, (e - s, count), 0) + s
                seen = (row <= places) & (row >= starts)
                bias_ref[s:e, :] = jnp.where(seen, 0.0, -1e9)

        first = lax.broadcasted_iota(jnp.int32, (1, 128), 1) < 64
        ka_ref[...] = jnp.zeros_like(ka_ref)
        va_ref[...] = jnp.zeros_like(va_ref)
        for s, e in query_blocks(count):
            both = jnp.transpose(
                u_ref[s:e, :].astype(jnp.float32) * o_ref[s:e, :].astype(jnp.float32)
            )
            found = []
            for half in range(2):
                mine = first == (half == 0)
                inner = jnp.sum(both[64 * half : 64 * half + 64, :], axis=0, keepdims=True)
                q = jnp.where(mine, q_ref[s:e, :], jnp.bfloat16(0))
                u = jnp.where(mine, u_ref[s:e, :], jnp.bfloat16(0))
                scores = lax.dot_general(
                    k_ref[0:e, :], q, NT, preferred_element_type=jnp.float32
                )
                probs = jnp.exp2(
                    scores * factor + bias_ref[0:e, s:e] - l_ref[0, half : half + 1, s:e]
                )
                prob_grad = lax.dot_general(
                    v_ref[0:e, :], u, NT, preferred_element_type=jnp.float32
                )
                score_grad = (probs * (prob_grad - inner)).astype(jnp.bfloat16)
                va_ref[0:e, :] += jnp.dot(
                    probs.astype(jnp.bfloat16), u, preferred_element_type=jnp.float32
                )
                ka_ref[0:e, :] += jnp.dot(score_grad, q, preferred_element_type=jnp.float32)
                found.append(
                    lax.dot_general(
                        score_grad, k_ref[0:e, :], TN, preferred_element_type=jnp.float32
                    )
                )
            dq_ref[s:e, :] = (jnp.where(first, found[0], found[1]) * scale).astype(jnp.bfloat16)
        dk_ref[...] = (ka_ref[...] * scale).astype(jnp.bfloat16)
        dv_ref[...] = va_ref[...].astype(jnp.bfloat16)

    column = lambda shift: pl.BlockSpec((count, 128), lambda p, _: (0, shift + p))
    return pl.pallas_call(
        kernel,
        out_shape=(jax.ShapeDtypeStruct((count, width), jnp.bfloat16),) * 3,
        grid_spec=pltpu.PrefetchScalarGridSpec(
            num_scalar_prefetch=1,
            grid=(pairs,),
            in_specs=[
                column(0),
                column(pairs),
                column(2 * pairs),
                column(0),
                column(0),
                pl.BlockSpec((1, 2, count), lambda p, _: (p, 0, 0)),
            ],
            out_specs=(column(0),) * 3,
            scratch_shapes=[
                pltpu.VMEM((count, count), jnp.float32),
                pltpu.VMEM((count, 128), jnp.float32),
                pltpu.VMEM((count, 128), jnp.float32),
            ],
        ),
        compiler_params=pltpu.CompilerParams(vmem_limit_bytes=VMEM_LIMIT),
        cost_estimate=pl.CostEstimate(
            flops=10 * count * count * width, bytes_accessed=16 * count * width, transcendentals=count * count * HEADS
        ),
    )(lengths, joint, joint, joint, mixed, upstream, logs)


MESH = pl.DeviceIdType.MESH


def neighbours(slabs):
    me, core = lax.axis_index("expert"), lax.axis_index("tensor")
    plane = lax.div(me, slabs)
    x = lax.rem(me, 2)
    y = lax.rem(lax.div(me, 2), 2)
    return me, core, plane, (me + 1 - 2 * x, core), (me + 2 - 4 * y, core), (me, 1 - core)


def greet(partners):
    barrier = pltpu.get_barrier_semaphore()
    number = 0
    for device, there in partners:
        @pl.when(there)
        def _(device=device):
            pl.semaphore_signal(barrier, inc=1, device_id=device, device_id_type=MESH)
        number = number + there.astype(jnp.int32)
    pl.semaphore_wait(barrier, number)


def score_bias(bias_ref, lengths_ref, count):
    places = lax.broadcasted_iota(jnp.int32, (1, count), 1)
    starts = document_starts(lengths_ref, places)
    for s, e in query_blocks(count):
        row = lax.broadcasted_iota(jnp.int32, (e - s, count), 0) + s
        seen = (row <= places) & (row >= starts)
        bias_ref[s:e, :] = jnp.where(seen, 0.0, -1e9)


def row_norm(values, gain, shift):
    centered = values - jnp.mean(values, axis=1, keepdims=True)
    scale = lax.rsqrt(jnp.mean(centered * centered, axis=1, keepdims=True) + epsilon)
    normal = centered * scale
    return normal * gain + shift, normal, scale


def chosen_rows(route, centroids_ref, experts):
    chosen = jnp.zeros((route.shape[0], centroids_ref.shape[1]), jnp.float32)
    for e in range(experts):
        chosen = jnp.where(route == e, centroids_ref[e : e + 1, :].astype(jnp.float32), chosen)
    return chosen


def front_kernel(
    planes,
    slabs,
    lengths_ref,
    tokens_ref,
    gains_ref,
    shifts_ref,
    projection_ref,
    mixing_ref,
    factors_ref,
    biases_ref,
    centroids_ref,
    route_row_ref,
    route_ref,
    cot_ref,
    up_ref,
    down_ref,
    entry_ref,
    joint_ref,
    mixed_ref,
    logs_ref,
    residual_ref,
    place_ref,
    loads_ref,
    sent_own,
    cot_own,
    gate_own,
    sent_others,
    cot_others,
    gate_others,
    up_near,
    up_far,
    down_near,
    down_far,
    bias_ref,
    order_ref,
    normed_ref,
    tally_ref,
    send_sem,
    recv_sem,
    local_sem,
):
    count, width = tokens_ref.shape
    experts = planes
    rows = sent_own.shape[0]
    half_rows = rows // 2
    pairs = width // 128
    factor = (width // HEADS) ** (-0.5) * HALF_LOG
    middle = planes - 1
    me, core, plane, beside_x, beside_y, beside_core = neighbours(slabs)
    hop_two = lax.rem(plane + 2, planes)
    hop_one = plane + 1 - 2 * lax.rem(plane, 2)
    here = lax.rem(me, slabs)
    always = plane >= 0
    greet(
        [
            (beside_x, always),
            (beside_y, always),
            (beside_core, always),
            ((hop_two * slabs + here, core), always),
            ((me + slabs, core), plane < planes - 1),
            ((me - slabs, core), plane > 0),
        ]
    )

    def remote(i, src, dst, device):
        return pltpu.make_async_remote_copy(
            src_ref=src, dst_ref=dst, send_sem=send_sem.at[i], recv_sem=recv_sem.at[i], device_id=device, device_id_type=MESH
        )

    owns, nears, fars = (up_ref, down_ref), (up_near, down_near), (up_far, down_far)
    stride = 2 * (planes - 1) + 2 * planes - 1

    def hop(kind, sign, r):
        src = owns[kind].at[0] if r == 1 else nears[kind].at[middle - sign * (r - 1)]
        i = kind * stride + (r - 1) * 2 + (sign > 0)
        return remote(i, src, nears[kind].at[middle - sign * r], (me + sign * slabs, core))

    def hop_sent(sign, r):
        ahead = plane if sign > 0 else planes - 1 - plane
        return (ahead >= r - 1) & (ahead < planes - 1)

    def hop_came(sign, r):
        ahead = plane if sign > 0 else planes - 1 - plane
        return ahead >= r

    def aside(kind, slot):
        src = owns[kind].at[0] if slot == middle else nears[kind].at[slot]
        i = kind * stride + 2 * (planes - 1) + slot
        return remote(i, src, fars[kind].at[slot], beside_x)

    def held(slot):
        at = plane + slot - middle
        return (at >= 0) & (at < planes)

    def own_weights(kind):
        return pltpu.make_async_copy(owns[kind].at[0], nears[kind].at[middle], local_sem.at[kind])

    for kind in range(2):
        for sign in (1, -1):
            @pl.when(hop_sent(sign, 1))
            def _(kind=kind, sign=sign):
                hop(kind, sign, 1).start()
        aside(kind, middle).start()
        own_weights(kind).start()

    def forward_weights(kind, r):
        for sign in (1, -1):
            slot = middle - sign * r

            @pl.when(hop_came(sign, r))
            def _(sign=sign, slot=slot):
                hop(kind, sign, r).wait_recv()
                aside(kind, slot).start()

            if r < planes - 1:
                @pl.when(hop_sent(sign, r + 1))
                def _(sign=sign):
                    hop(kind, sign, r + 1).start()

    base = 2 * stride

    def row_copy(which, part, piece):
        own, others = ((cot_own, cot_others), (sent_own, sent_others))[which]
        at = pl.ds(piece * half_rows, half_rows)
        i = base + which * 6 + part * 2 + piece
        if part == 0:
            return remote(i, own.at[at], others.at[1, at], beside_y)
        if part == 1:
            return remote(i, own.at[at], others.at[0, at], beside_core)
        return remote(i, others.at[1, at], others.at[2, at], beside_core)

    def gate_copy(part):
        i = base + 12 + part
        if part == 0:
            return remote(i, gate_own, gate_others.at[1], beside_y)
        if part == 1:
            return remote(i, gate_own, gate_others.at[0], beside_core)
        return remote(i, gate_others.at[1], gate_others.at[2], beside_core)

    rounds = [beside_core, beside_x, beside_y, (hop_one * slabs + here, core), (hop_two * slabs + here, core)]

    def tally(k):
        return remote(base + 15 + k, tally_ref.at[2 * k], tally_ref.at[2 * k + 1], rounds[k])

    def tally_step(k):
        tally(k).wait_recv()
        total = tally_ref[2 * k] + tally_ref[2 * k + 1]
        if k + 1 < len(rounds):
            tally_ref[2 * k + 2] = total
            tally(k + 1).start()
        else:
            loads_ref[...] = total

    number = lax.broadcasted_iota(jnp.int32, (8, count), 0)
    picks = jnp.where(number == route_row_ref[...], 1.0, 0.0)
    chunk = 128
    for s in range(0, count, chunk):
        row = lax.broadcasted_iota(jnp.int32, (chunk, count), 0) + s
        column = lax.broadcasted_iota(jnp.int32, (chunk, count), 1)
        order_ref[s : s + chunk, :] = jnp.where(row < column, 1.0, 0.0).astype(jnp.bfloat16)
    ranks = jnp.dot(picks.astype(jnp.bfloat16), order_ref[0:count, :], preferred_element_type=jnp.float32)
    counts = jnp.sum(picks, axis=1, keepdims=True)
    padded = jnp.ceil(counts * (1.0 / ALIGN)) * ALIGN
    place = jnp.zeros((1, count), jnp.float32)
    start = jnp.zeros((1, 1), jnp.float32)
    for e in range(experts):
        place = place + picks[e : e + 1, :] * (ranks[e : e + 1, :] + start)
        start = start + padded[e : e + 1, :]
    place_ref[...] = jnp.broadcast_to(place, (8, count))
    tally_ref[0] = jnp.broadcast_to(counts, (8, 128))
    tally(0).start()
    for s in range(0, rows, 64):
        row = lax.broadcasted_iota(jnp.int32, (64, count), 0) + s
        order_ref[s : s + 64, :] = jnp.where(row.astype(jnp.float32) == place, 1.0, 0.0).astype(jnp.bfloat16)

    def sort_rows(source_ref, to_ref, which):
        for piece in range(2):
            at = slice(piece * half_rows, (piece + 1) * half_rows)
            to_ref[at, :] = jnp.dot(
                order_ref[at, :], source_ref[...], preferred_element_type=jnp.float32
            ).astype(jnp.bfloat16)
            row_copy(which, 0, piece).start()
            row_copy(which, 1, piece).start()

    sort_rows(cot_ref, cot_own, 0)

    def project(i, _):
        at = pl.ds(pl.multiple_of(i * 192, 192), 192)
        entry, _, _ = row_norm(tokens_ref[at, :].astype(jnp.float32), gains_ref[...], shifts_ref[...])
        entry = entry.astype(jnp.bfloat16)
        entry_ref[at, :] = entry
        joint_ref[at, :] = jnp.dot(entry, projection_ref[...], preferred_element_type=jnp.float32).astype(jnp.bfloat16)
        return 0

    lax.fori_loop(0, count // 192, project, 0)
    score_bias(bias_ref, lengths_ref, count)
    forward_weights(0, 1)
    tally_step(0)

    first = lax.broadcasted_iota(jnp.int32, (1, 128), 1) < 64

    def attend(p, _):
        lanes = pl.ds(pl.multiple_of(p * 128, 128), 128)
        keys = pl.ds(pl.multiple_of(width + p * 128, 128), 128)
        values = pl.ds(pl.multiple_of(2 * width + p * 128, 128), 128)
        for s, e in query_blocks(count):
            outs = []
            for half in range(2):
                q = jnp.where(first == (half == 0), joint_ref[s:e, lanes], jnp.bfloat16(0))
                scores = lax.dot_general(joint_ref[0:e, keys], q, NT, preferred_element_type=jnp.float32)
                scores = scores * factor + bias_ref[0:e, s:e]
                peak = jnp.max(scores, axis=0, keepdims=True)
                weights = jnp.exp2(scores - peak)
                total = jnp.sum(weights, axis=0, keepdims=True)
                probs = (weights * (1.0 / total)).astype(jnp.bfloat16)
                outs.append(
                    lax.dot_general(probs, joint_ref[0:e, values], TN, preferred_element_type=jnp.float32)
                )
                logs_ref[p, half : half + 1, s:e] = peak + jnp.log2(total)
            mixed_ref[s:e, lanes] = jnp.where(first, outs[0], outs[1]).astype(jnp.bfloat16)

        @pl.when(p == 1)
        def _():
            forward_weights(1, 1)
            tally_step(1)

        @pl.when(p == 3)
        def _():
            forward_weights(0, 2)
            tally_step(2)

        @pl.when(p == 5)
        def _():
            for piece in range(2):
                row_copy(0, 0, piece).wait_recv()
                row_copy(0, 2, piece).start()
            forward_weights(1, 2)
            tally_step(3)

        return 0

    lax.fori_loop(0, pairs, attend, 0)

    lane = lax.broadcasted_iota(jnp.int32, (1, 128), 1)

    def mix(i, _):
        at = pl.ds(pl.multiple_of(i * 192, 192), 192)
        residual = tokens_ref[at, :].astype(jnp.float32) + jnp.dot(
            mixed_ref[at, :], mixing_ref[...], preferred_element_type=jnp.float32
        )
        residual_ref[at, :] = residual
        normed, _, _ = row_norm(residual, factors_ref[...], biases_ref[...])
        chosen = chosen_rows(route_ref[at, :], centroids_ref, experts)
        gate = 1.0 / (1.0 + jnp.exp(-jnp.sum(normed * chosen, axis=1, keepdims=True)))
        high = gate.astype(jnp.bfloat16).astype(jnp.float32)
        mid = (gate - high).astype(jnp.bfloat16).astype(jnp.float32)
        low = gate - high - mid
        parts = jnp.where(lane == 0, high, jnp.where(lane == 1, mid, jnp.where(lane == 2, low, 0.0)))
        normed_ref[at, 0:width] = normed.astype(jnp.bfloat16)
        normed_ref[at, width : width + 128] = parts.astype(jnp.bfloat16)
        return 0

    lax.fori_loop(0, count // 192, mix, 0)
    for piece in range(2):
        at = slice(piece * half_rows, (piece + 1) * half_rows)
        moved = jnp.dot(order_ref[at, :], normed_ref[...], preferred_element_type=jnp.float32)
        sent_own[at, :] = moved[:, 0:width].astype(jnp.bfloat16)
        row_copy(1, 0, piece).start()
        row_copy(1, 1, piece).start()
        bias_ref[at, 0:128] = jnp.broadcast_to(
            jnp.sum(moved[:, width : width + 128], axis=1, keepdims=True), (half_rows, 128)
        )
    gates = jnp.transpose(bias_ref[0:rows, 0:128])
    gate_own[0:1, :] = gates[0:1, :]
    gate_own[1:2, :] = jnp.zeros((1, rows), jnp.float32)
    for e in range(8):
        gate_own[1:2, e : e + 1] = padded[e : e + 1, :]
    gate_copy(0).start()
    gate_copy(1).start()

    for kind in range(2):
        forward_weights(kind, 3)
    gate_copy(0).wait_recv()
    gate_copy(2).start()
    tally_step(4)
    for piece in range(2):
        row_copy(1, 0, piece).wait_recv()
        row_copy(1, 2, piece).start()

    for which in range(2):
        for part in range(3):
            for piece in range(2):
                copy = row_copy(which, part, piece)
                copy.wait_send()
                if part:
                    copy.wait_recv()
    for part in range(3):
        gate_copy(part).wait_send()
        if part:
            gate_copy(part).wait_recv()
    for k in range(len(rounds)):
        tally(k).wait_send()
    for kind in range(2):
        own_weights(kind).wait()
        for r in range(1, planes):
            for sign in (1, -1):
                @pl.when(hop_sent(sign, r))
                def _(kind=kind, sign=sign, r=r):
                    hop(kind, sign, r).wait_send()
        for slot in range(2 * planes - 1):
            @pl.when(held(slot))
            def _(kind=kind, slot=slot):
                aside(kind, slot).wait()


def front_stage(
    tokens, gains, shifts, projection, mixing, factors, biases, centroids, expanding, contracting, route, lengths, cotangent, planes, slabs
):
    count, width = tokens.shape
    rows = aligned_rows(count, planes)
    pairs = width // 128
    slots = 2 * planes - 1
    bf16, f32 = jnp.bfloat16, jnp.float32
    shape = jax.ShapeDtypeStruct
    anywhere = pl.BlockSpec(memory_space=pl.ANY)
    local = pl.BlockSpec(memory_space=pltpu.VMEM)
    dma = pltpu.SemaphoreType.DMA
    copies = 2 * (2 * (planes - 1) + slots) + 12 + 3 + 5
    outs = [
        (shape((count, width), bf16), local),
        (shape((count, 3 * width), bf16), local),
        (shape((count, width), bf16), local),
        (shape((pairs, 2, count), f32), local),
        (shape((count, width), f32), local),
        (shape((8, count), f32), local),
        (shape((8, 128), f32), local),
        (shape((rows, width), bf16), local),
        (shape((rows, width), bf16), local),
        (shape((8, rows), f32), local),
        (shape((3, rows, width), bf16), anywhere),
        (shape((3, rows, width), bf16), anywhere),
        (shape((3, 8, rows), f32), anywhere),
        (shape((slots,) + expanding.shape[1:], bf16), anywhere),
        (shape((slots,) + expanding.shape[1:], bf16), anywhere),
        (shape((slots,) + contracting.shape[1:], bf16), anywhere),
        (shape((slots,) + contracting.shape[1:], bf16), anywhere),
    ]
    row = lambda v: v.reshape(1, -1)
    return pl.pallas_call(
        partial(front_kernel, planes, slabs),
        out_shape=[o[0] for o in outs],
        in_specs=[pl.BlockSpec(memory_space=pltpu.SMEM)] + [local] * 11 + [anywhere] * 2,
        out_specs=[o[1] for o in outs],
        scratch_shapes=[
            pltpu.VMEM((rows, count), f32),
            pltpu.VMEM((rows, count), bf16),
            pltpu.VMEM((count, width + 128), bf16),
            pltpu.VMEM((10, 8, 128), f32),
            dma((copies,)),
            dma((copies,)),
            dma((2,)),
        ],
        compiler_params=pltpu.CompilerParams(
            collective_id=0, has_side_effects=True, vmem_limit_bytes=VMEM_LIMIT
        ),
    )(
        lengths[0],
        tokens,
        row(gains),
        row(shifts),
        projection,
        mixing,
        row(factors),
        row(biases),
        jnp.pad(centroids, ((0, -centroids.shape[0] % 8), (0, 0))),
        row(route),
        route,
        cotangent,
        expanding,
        contracting,
    )


TILE = 256
ALIGN = 16


def aligned_rows(count, experts):
    return -(-(count + experts * (ALIGN - 1)) // ALIGN) * ALIGN


def gelu_pair(values):
    bell = jnp.exp2(values * values * (-0.5 * HALF_LOG))
    near = 1.0 / (1.0 + (0.3275911 * 0.7071067811865476) * jnp.abs(values))
    series = 1.061405429 * 0.5 * near - 1.453152027 * 0.5
    series = series * near + 1.421413741 * 0.5
    series = series * near - 0.284496736 * 0.5
    series = series * near + 0.254829592 * 0.5
    tail = series * near * bell
    below = jnp.where(values >= 0.0, 1.0 - tail, tail)
    return values * below, below + values * bell * 0.3989422804014327


def expert_kernel_body(
    experts,
    sources,
    rows,
    limit,
    width,
    hidden,
    meta_ref,
    *refs,
):
    sent_own, sent_others, cot_own, cot_others, gate_own, gate_others = refs[:6]
    up_near, up_far, down_near, down_far = refs[6:10]
    refs = refs[10:]
    sent_refs = [sent_own] + [sent_others.at[s] for s in range(sources - 1)]
    cot_refs = [cot_own] + [cot_others.at[s] for s in range(sources - 1)]
    gate_refs = [gate_own] + [gate_others.at[s] for s in range(sources - 1)]
    back_outs, refs = refs[:sources], refs[sources:]
    made_outs, refs = refs[:sources], refs[sources:]
    dot_outs, refs = refs[:sources], refs[sources:]
    near_out, far_out = refs[:2]
    (x_ref, c_ref, g_ref, column_ref, up_ref, down_ref, gu_ref, gd_ref, pack_ref, zero_ref) = refs[2:12]
    weight_sem, row_sem, out_sem, grad_sem, zero_sem = refs[12:]
    half = hidden // 2
    own = meta_ref[0]

    def size_of(s, e):
        return meta_ref[1 + s * experts + e]

    source_at, joined_at, tiles = {}, {}, []
    first = []
    base = 0
    for s in range(sources):
        at = 0
        for e in range(experts):
            source_at[s, e] = at
            at = at + size_of(s, e)
        source_at[s, experts] = at
    for e in range(experts):
        first.append(base)
        at = base
        for s in range(sources):
            joined_at[s, e] = at
            at = at + size_of(s, e)
        number = (at - base + (TILE - 1)) // TILE
        tiles.append(number)
        base = base + number * TILE

    bits = [1 << b for b in range(limit.bit_length()) if ALIGN <= (1 << b)]

    def pieces(s, e):
        size = size_of(s, e)
        for i, piece in enumerate(bits):
            yield i, piece, (size & piece) != 0, size & (piece - 1)

    def move_in(s, e, act):
        for i, piece, taken, offset in pieces(s, e):
            @pl.when(taken)
            def _(i=i, piece=piece, offset=offset):
                src = pl.ds(pl.multiple_of(source_at[s, e] + offset, ALIGN), piece)
                dst = pl.ds(pl.multiple_of(joined_at[s, e] + offset, ALIGN), piece)
                k = s * experts + e
                act(pltpu.make_async_copy(sent_refs[s].at[src], x_ref.at[dst], row_sem.at[0, k, i]))
                act(pltpu.make_async_copy(cot_refs[s].at[src], c_ref.at[dst], row_sem.at[1, k, i]))

    def move_out(s, e, act):
        for i, piece, taken, offset in pieces(s, e):
            @pl.when(taken)
            def _(i=i, piece=piece, offset=offset):
                src = pl.ds(pl.multiple_of(source_at[s, e] + offset, ALIGN), piece)
                dst = pl.ds(pl.multiple_of(joined_at[s, e] + offset, ALIGN), piece)
                k = s * experts + e
                act(pltpu.make_async_copy(x_ref.at[dst], made_outs[s].at[src], out_sem.at[0, k, i]))
                act(pltpu.make_async_copy(c_ref.at[dst], back_outs[s].at[src], out_sem.at[1, k, i]))

    def move_weights(e, act):
        slot = e - own + experts - 1
        for j, (ups, downs) in enumerate(((up_near, down_near), (up_far, down_far))):
            part = pl.ds(j * half, half)
            act(pltpu.make_async_copy(ups.at[slot], up_ref.at[e, :, part], weight_sem.at[e, j, 0]))
            act(pltpu.make_async_copy(downs.at[slot], down_ref.at[e, part], weight_sem.at[e, j, 1]))

    zero_ref[...] = jnp.zeros_like(zero_ref)
    for e in range(experts):
        @pl.when(tiles[e] > 0)
        def _(e=e):
            last = pl.ds(pl.multiple_of(first[e] + (tiles[e] - 1) * TILE, TILE), TILE)
            x_ref[last, :] = jnp.zeros((TILE, width), jnp.bfloat16)
            c_ref[last, :] = jnp.zeros((TILE, width), jnp.bfloat16)
            g_ref[last, :] = jnp.zeros((TILE, 128), jnp.float32)

    for e in range(experts):
        move_weights(e, lambda copy: copy.start())
        for s in range(sources):
            move_in(s, e, lambda copy: copy.start())

    tail_chunks = rows // ALIGN

    def tail(s, act):
        def one(i, _):
            @pl.when(i * ALIGN >= source_at[s, experts])
            def _():
                dst = pl.ds(pl.multiple_of(i * ALIGN, ALIGN), ALIGN)
                act(pltpu.make_async_copy(zero_ref, made_outs[s].at[dst], zero_sem.at[0, s, i]))
                act(pltpu.make_async_copy(zero_ref, back_outs[s].at[dst], zero_sem.at[1, s, i]))
            return 0
        lax.fori_loop(tail_chunks - 5, tail_chunks, one, 0)

    for s in range(sources):
        tail(s, lambda copy: copy.start())

    for s in range(sources):
        column_ref[...] = jnp.broadcast_to(
            jnp.transpose(jnp.broadcast_to(gate_refs[s][0:1, :], (128, rows)))[:, 0:128], (rows, 128)
        )
        for e in range(experts):
            def one(i, _, s=s, e=e):
                src = pl.ds(pl.multiple_of(source_at[s, e] + i * ALIGN, ALIGN), ALIGN)
                dst = pl.ds(pl.multiple_of(joined_at[s, e] + i * ALIGN, ALIGN), ALIGN)
                g_ref[dst, :] = column_ref[src, :]
                return 0
            lax.fori_loop(0, size_of(s, e) // ALIGN, one, 0)

    for e in range(experts):
        move_weights(e, lambda copy: copy.wait())
        for s in range(sources):
            move_in(s, e, lambda copy: copy.wait())
        gu_ref[...] = jnp.zeros_like(gu_ref)
        gd_ref[...] = jnp.zeros_like(gd_ref)

        def tile(t, _, e=e):
            at = pl.ds(pl.multiple_of(first[e] + t * TILE, TILE), TILE)
            x, c, gate = x_ref[at, :], c_ref[at, :], g_ref[at, 0:1]
            before = jnp.dot(x, up_ref[e], preferred_element_type=jnp.float32)
            active, slope = gelu_pair(before)
            through = lax.dot_general(c, down_ref[e], NT, preferred_element_type=jnp.float32)
            grad = (through * (slope * gate)).astype(jnp.bfloat16)
            gated = (active * gate).astype(jnp.bfloat16)
            made = jnp.dot(active.astype(jnp.bfloat16), down_ref[e], preferred_element_type=jnp.float32)
            g_ref[at, :] = jnp.broadcast_to(
                jnp.sum(made * c.astype(jnp.float32), axis=1, keepdims=True), (TILE, 128)
            )
            gd_ref[...] += lax.dot_general(gated, c, TN, preferred_element_type=jnp.float32)
            gu_ref[...] += lax.dot_general(x, grad, TN, preferred_element_type=jnp.float32)
            back = lax.dot_general(grad, up_ref[e], NT, preferred_element_type=jnp.float32)
            x_ref[at, :] = made.astype(jnp.bfloat16)
            c_ref[at, :] = back.astype(jnp.bfloat16)
            return 0

        lax.fori_loop(0, tiles[e], tile, 0)
        for s in range(sources):
            move_out(s, e, lambda copy: copy.start())

        slot = e % 2
        grads = lambda e, slot: [
            pltpu.make_async_copy(pack_ref.at[slot, j], ref.at[e - own + experts - 1], grad_sem.at[slot, j])
            for j, ref in enumerate((near_out, far_out))
        ]
        if e >= 2:
            for copy in grads(e - 2, slot):
                copy.wait()
        for j in range(2):
            pack_ref[slot, j, 0:width, :] = gu_ref[:, j * half : (j + 1) * half].astype(jnp.bfloat16)
            for part in range(2):
                pack_ref[slot, j, width + part * half : width + (part + 1) * half, :] = gd_ref[
                    j * half : (j + 1) * half, part * half : (part + 1) * half
                ].astype(jnp.bfloat16)
        for copy in grads(e, slot):
            copy.start()

    for s in range(sources):
        for e in range(experts):
            def one(i, _, s=s, e=e):
                src = pl.ds(pl.multiple_of(source_at[s, e] + i * ALIGN, ALIGN), ALIGN)
                dst = pl.ds(pl.multiple_of(joined_at[s, e] + i * ALIGN, ALIGN), ALIGN)
                column_ref[src, :] = g_ref[dst, :]
                return 0
            lax.fori_loop(0, size_of(s, e) // ALIGN, one, 0)
        dot_outs[s][...] = jnp.transpose(column_ref[...])[0:8, :]

    for e in range(experts):
        for s in range(sources):
            move_out(s, e, lambda copy: copy.wait())
    for s in range(sources):
        tail(s, lambda copy: copy.wait())
    for e in range(max(0, experts - 2), experts):
        for copy in grads(e, e % 2):
            copy.wait()


def expert_stage(meta, sent, cot, gates, weights, experts, limit):
    rows, width = sent[0].shape
    sources = 1 + sent[1].shape[0]
    half = weights[0].shape[2]
    hidden = 2 * half
    joined = -(-(sources * rows + experts * (TILE - 1)) // TILE) * TILE
    limit = -(-limit // ALIGN) * ALIGN
    pieces = limit.bit_length() - ALIGN.bit_length() + 1
    anywhere = pl.BlockSpec(memory_space=pl.ANY)
    local = pl.BlockSpec(memory_space=pltpu.VMEM)
    slots = 2 * experts - 1
    dma = pltpu.SemaphoreType.DMA
    packed = (width + hidden, half)
    outs = pl.pallas_call(
        partial(expert_kernel_body, experts, sources, rows, limit, width, hidden),
        out_shape=(
            [jax.ShapeDtypeStruct((rows, width), jnp.bfloat16)] * (2 * sources)
            + [jax.ShapeDtypeStruct((8, rows), jnp.float32)] * sources
            + [jax.ShapeDtypeStruct((slots,) + packed, jnp.bfloat16)] * 2
        ),
        in_specs=[pl.BlockSpec(memory_space=pltpu.SMEM)]
        + [anywhere] * 4
        + [local] * 2
        + [anywhere] * 4,
        out_specs=[anywhere] * (2 * sources) + [local] * sources + [anywhere] * 2,
        scratch_shapes=[
            pltpu.VMEM((joined, width), jnp.bfloat16),
            pltpu.VMEM((joined, width), jnp.bfloat16),
            pltpu.VMEM((joined, 128), jnp.float32),
            pltpu.VMEM((rows, 128), jnp.float32),
            pltpu.VMEM((experts, width, hidden), jnp.bfloat16),
            pltpu.VMEM((experts, hidden, width), jnp.bfloat16),
            pltpu.VMEM((width, hidden), jnp.float32),
            pltpu.VMEM((hidden, width), jnp.float32),
            pltpu.VMEM((2, 2) + packed, jnp.bfloat16),
            pltpu.VMEM((ALIGN, width), jnp.bfloat16),
            dma((experts, 2, 2)),
            dma((2, sources * experts, pieces)),
            dma((2, sources * experts, pieces)),
            dma((2, 2)),
            dma((2, sources, rows // ALIGN)),
        ],
        compiler_params=pltpu.CompilerParams(vmem_limit_bytes=VMEM_LIMIT),
        cost_estimate=pl.CostEstimate(
            flops=12 * sources * rows * width * hidden, bytes_accessed=100_000_000, transcendentals=sources * rows * hidden
        ),
    )(meta, *sent, *cot, *gates, *weights)
    back, made, dots = outs[:sources], outs[sources : 2 * sources], outs[2 * sources : 3 * sources]
    return back, made, dots, outs[-2], outs[-1]


def swap(value, bit):
    groups = lax.axis_size("expert")
    return lax.ppermute(value, "expert", [(i, i ^ bit) for i in range(groups)])


def across(value):
    return lax.ppermute(value, "tensor", [(0, 1), (1, 0)])


def beside(value, planes, slabs, shift):
    pairs = [
        (i, i ^ 1) for i in range(planes * slabs) if 0 <= i // slabs + shift < planes
    ]
    return lax.ppermute(value, "expert", pairs)


def reduce_weights(near, far, planes, slabs):
    sums = {}
    for k in range(planes - 1, -1, -1):
        for sign in (1, -1):
            if k or sign > 0:
                at = planes - 1 + sign * k
                came = beside(far[at], planes, slabs, sign * k)
                sums[sign * k] = near[at].astype(jnp.float32) + came.astype(jnp.float32)
    arrived = []
    for sign in (1, -1):
        came = None
        for k in range(planes - 1, 0, -1):
            total = sums[sign * k]
            if came is not None:
                total = total + came.astype(jnp.float32)
            pairs = [
                (i, i + sign * slabs)
                for i in range(planes * slabs)
                if 0 <= i // slabs + sign * k < planes
            ]
            came = lax.ppermute(total.astype(jnp.bfloat16), "expert", pairs)
        arrived.append(came.astype(jnp.float32))
    return sums[0] + arrived[0] + arrived[1]


def per_device(
    tokens,
    gains,
    shifts,
    projection,
    mixing,
    factors,
    biases,
    centroids,
    expanding,
    contracting,
    routes,
    lengths,
    cotangent,
):
    count, width = tokens.shape
    experts = centroids.shape[0]
    groups = lax.axis_size("expert")
    slabs = groups // experts
    half = expanding.shape[2]
    limit = 2 * count // experts
    total_tokens = count * groups * lax.axis_size("tensor")
    average = total_tokens / experts
    rows = aligned_rows(count, experts)
    me, core = lax.axis_index("expert"), lax.axis_index("tensor")

    route = routes[:, 0]
    picks = routes == jnp.arange(experts, dtype=jnp.int32)[None, :]
    entry, joint, mixed_rows, logs, residual, place, loads, sent_own, cot_own, gate_own, sent_others, cot_others, gate_others, *weights = front_stage(
        tokens, gains, shifts, projection, mixing, factors, biases, centroids, expanding, contracting, routes, lengths, cotangent, experts, slabs
    )
    spread = (loads[:experts, 0] - average) / average
    token_spread = jnp.sum(jnp.where(picks, spread[None, :], 0.0), axis=1)
    position = place[0].astype(jnp.int32)
    sizes = jnp.concatenate((gate_own[1:2, :experts], gate_others[:, 1, :experts]), axis=0)
    meta = jnp.concatenate(
        [(me // slabs).astype(jnp.int32)[None], sizes.reshape(-1).astype(jnp.int32)]
    )
    back_order = (position[:, None] == jnp.arange(rows, dtype=jnp.int32)[None, :]).astype(jnp.bfloat16)
    inputs = tokens.astype(jnp.float32)
    _, entry_normal, entry_scale = norm_parts(inputs, gains, shifts)
    normed, mixer_normal, mixer_scale = norm_parts(residual, factors, biases)
    chosen = jnp.dot(picks.astype(jnp.bfloat16), centroids, preferred_element_type=jnp.float32)
    gates = jax.nn.sigmoid(jnp.sum(normed * chosen, axis=1))
    back, made, dots, near_grads, far_grads = expert_stage(
        meta, (sent_own, sent_others), (cot_own, cot_others), (gate_own, gate_others), weights, experts, limit
    )

    def collect(parts, narrow):
        own = parts[0].astype(jnp.float32) + across(parts[1]).astype(jnp.float32)
        other = parts[2].astype(jnp.float32) + across(parts[3]).astype(jnp.float32)
        return own, swap(other.astype(narrow), 2)

    def unsort(own, came):
        high = own.astype(jnp.bfloat16)
        return jnp.dot(
            back_order, high, preferred_element_type=jnp.float32
        ) + jnp.dot(back_order, came, preferred_element_type=jnp.float32)

    dot_own, dot_came = collect(dots, jnp.float32)
    gate_rows = (dot_own + dot_came)[0]
    gate_grad = jnp.sum(
        jnp.where(position[:, None] == jnp.arange(rows, dtype=jnp.int32)[None, :], gate_rows[None, :], 0.0),
        axis=1,
    )
    sent_grad = unsort(*collect(back, jnp.bfloat16))
    made_own, made_came = collect(made, jnp.bfloat16)
    up_down = reduce_weights(near_grads, far_grads, experts, slabs)

    upstream = cotangent.astype(jnp.float32)
    balance_part = jnp.sum(token_spread * gates) / total_tokens
    logit_grad = (gate_grad + token_spread / total_tokens) * gates * (1.0 - gates)
    normed_grad = sent_grad + logit_grad[:, None] * chosen
    centroid_grad = jnp.einsum(
        "te,td->ed", picks.astype(jnp.float32), logit_grad[:, None] * normed, precision=highest
    )
    mixer_back, factor_grad, bias_grad = norm_back(normed_grad, mixer_normal, mixer_scale, factors)
    residual_grad = upstream + mixer_back
    branch_grad = residual_grad.astype(jnp.bfloat16)
    mixing_grad = jnp.einsum(
        "td,te->de", mixed_rows, branch_grad, preferred_element_type=jnp.float32
    )
    mixed_grad = jnp.einsum(
        "te,de->td", branch_grad, mixing, preferred_element_type=jnp.float32
    ).astype(jnp.bfloat16)
    joint_grad = jnp.concatenate(
        attend_backward(joint, mixed_rows, mixed_grad, logs, lengths[0]), axis=1
    )
    projection_grad = jnp.einsum("td,te->de", entry, joint_grad, preferred_element_type=jnp.float32)
    entry_back = jnp.einsum("te,de->td", joint_grad, projection, preferred_element_type=jnp.float32)
    entry_input, gain_grad, shift_grad = norm_back(entry_back, entry_normal, entry_scale, gains)
    token_grad = residual_grad + entry_input
    layer_output = (residual + gates[:, None] * unsort(made_own, made_came)).astype(jnp.bfloat16)
    summed = lax.psum(
        (
            gain_grad,
            shift_grad,
            projection_grad,
            mixing_grad,
            factor_grad,
            bias_grad,
            centroid_grad,
            balance_part,
        ),
        ("expert", "tensor"),
    )
    return (
        layer_output,
        summed[7],
        token_grad,
        summed[0],
        summed[1],
        summed[2],
        summed[3],
        summed[4],
        summed[5],
        summed[6],
        up_down[:width][None],
        jnp.concatenate((up_down[width : width + half], up_down[width + half :]), axis=1)[None],
    )


def solution(mesh):
    placed = (
        P(("expert", "tensor"), None),
        P(),
        P(),
        P(),
        P(),
        P(),
        P(),
        P(),
        P("expert", None, "tensor"),
        P("expert", "tensor", None),
        P(("expert", "tensor"), None),
        P(("expert", "tensor"), None),
        P(("expert", "tensor"), None),
    )
    near = mesh.shape["expert"] == 16 and mesh.shape["tensor"] == 2
    return jax.shard_map(
        per_device if near else moving_tokens,
        mesh=mesh,
        in_specs=placed,
        out_specs=(
            P(("expert", "tensor"), None),
            P(),
            P(("expert", "tensor"), None),
            P(),
            P(),
            P(),
            P(),
            P(),
            P(),
            P(),
            P("expert", None, "tensor"),
            P("expert", "tensor", None),
        ),
        check_vma=False,
    )
```

```python
from functools import partial

import jax
import jax.numpy as jnp
from jax import lax
from jax.experimental import pallas as pl
from jax.experimental.pallas import tpu as pltpu
from jax.sharding import PartitionSpec as P

HEADS = 12


highest = lax.Precision.HIGHEST
epsilon = 1e-05


def running(values):
    places = jnp.arange(values.shape[0])
    return jnp.sum(jnp.where(places[:, None] >= places[None, :], values[None, :], 0), axis=1)


def earlier(picks):
    places = jnp.arange(picks.shape[0])
    before = (places[:, None] > places[None, :]).astype(jnp.bfloat16)
    return jnp.dot(
        before, picks.astype(jnp.bfloat16), preferred_element_type=jnp.float32
    ).astype(jnp.int32)


def norm_parts(values, gain, shift):
    centered = values - jnp.mean(values, axis=1, keepdims=True)
    scale = lax.rsqrt(jnp.mean(centered * centered, axis=1, keepdims=True) + epsilon)
    normal = centered * scale
    return (normal * gain + shift, normal, scale)


def norm_back(upstream, normal, scale, gain):
    scaled = upstream * gain
    inner = (
        scaled
        - jnp.mean(scaled, axis=1, keepdims=True)
        - normal * jnp.mean(scaled * normal, axis=1, keepdims=True)
    )
    return (inner * scale, jnp.sum(upstream * normal, axis=0), jnp.sum(upstream, axis=0))


def gelu_slope(values):
    return (
        0.5 * (1.0 + lax.erf(values * 0.7071067811865476))
        + values * jnp.exp(-0.5 * values * values) * 0.3989422804014327
    )


def expert_forward(gathered, upward, downward):
    before = jnp.dot(gathered, upward, preferred_element_type=jnp.float32)
    active = jax.nn.gelu(before, approximate=False).astype(jnp.bfloat16)
    return jnp.dot(active, downward, preferred_element_type=jnp.float32)


def expert_backward(gathered, incoming, upward, downward):
    before = jnp.dot(gathered, upward, preferred_element_type=jnp.float32)
    active = jax.nn.gelu(before, approximate=False).astype(jnp.bfloat16)
    down_grad = jnp.einsum("rf,rd->fd", active, incoming, preferred_element_type=jnp.float32)
    through = jnp.einsum("rd,fd->rf", incoming, downward, preferred_element_type=jnp.float32)
    hidden_grad = (through * gelu_slope(before)).astype(jnp.bfloat16)
    up_grad = jnp.einsum("rd,rf->df", gathered, hidden_grad, preferred_element_type=jnp.float32)
    return (up_grad, down_grad, hidden_grad)


def head_forward(allowed, item):
    query, keys, values = item
    factor = query.shape[1] ** (-0.5)
    scores = jnp.einsum("qd,kd->qk", query, keys, preferred_element_type=jnp.float32) * factor
    scores = jnp.where(allowed, scores, -1000000000.0)
    peak = jnp.max(scores, axis=1, keepdims=True)
    weights = jnp.exp(scores - peak)
    total = jnp.sum(weights, axis=1, keepdims=True)
    mixed = jnp.dot(
        (weights / total).astype(jnp.bfloat16), values, preferred_element_type=jnp.float32
    )
    return (mixed.astype(jnp.bfloat16), (peak + jnp.log(total))[:, 0])


def head_backward(allowed, item):
    query, keys, values, upstream, log_total = item
    factor = query.shape[1] ** (-0.5)
    scores = jnp.einsum("qd,kd->qk", query, keys, preferred_element_type=jnp.float32) * factor
    scores = jnp.where(allowed, scores, -1000000000.0)
    probs = jnp.exp(scores - log_total[:, None])
    value_grad = jnp.einsum(
        "qk,qd->kd", probs.astype(jnp.bfloat16), upstream, preferred_element_type=jnp.float32
    )
    prob_grad = jnp.einsum("qd,kd->qk", upstream, values, preferred_element_type=jnp.float32)
    inner = jnp.sum(prob_grad * probs, axis=1, keepdims=True)
    score_grad = (probs * (prob_grad - inner)).astype(jnp.bfloat16)
    query_grad = (
        jnp.einsum("qk,kd->qd", score_grad, keys, preferred_element_type=jnp.float32) * factor
    )
    key_grad = (
        jnp.einsum("qk,qd->kd", score_grad, query, preferred_element_type=jnp.float32) * factor
    )
    return (query_grad, key_grad, value_grad)


def moving_tokens(
    tokens,
    gains,
    shifts,
    projection,
    mixing,
    factors,
    biases,
    centroids,
    expanding,
    contracting,
    routes,
    lengths,
    cotangent,
):
    count, width = tokens.shape
    experts = centroids.shape[0]
    groups = lax.axis_size("expert")
    slab_count = groups // experts
    capacity = max(2, 2 * count // experts)
    total_tokens = count * groups * lax.axis_size("tensor")
    average = total_tokens / experts
    route = routes[:, 0]
    picks = route[:, None] == jnp.arange(experts, dtype=jnp.int32)[None, :]
    picks_int = picks.astype(jnp.int32)
    picks_float = picks.astype(jnp.float32)
    loads = lax.psum(jnp.sum(picks_float, axis=0), ("expert", "tensor"))
    spread = (loads - average) / average
    token_spread = jnp.sum(jnp.where(picks, spread[None, :], 0.0), axis=1)
    ranks = jnp.sum(earlier(picks) * picks_int, axis=1)
    slots = route * capacity + ranks
    places = jnp.arange(count, dtype=jnp.int32)
    documents = jnp.sum(
        (places[:, None] >= running(lengths[0])[None, :]).astype(jnp.int32), axis=1
    )
    allowed = (places[:, None] >= places[None, :]) & (documents[:, None] == documents[None, :])
    inputs = tokens.astype(jnp.float32)
    entry, entry_normal, entry_scale = norm_parts(inputs, gains, shifts)
    entry = entry.astype(jnp.bfloat16)
    joint = jnp.dot(entry, projection, preferred_element_type=jnp.float32).astype(jnp.bfloat16)
    heads = joint.reshape(count, 3, HEADS, width // HEADS).transpose(1, 2, 0, 3)
    mixed, log_total = lax.map(partial(head_forward, allowed), (heads[0], heads[1], heads[2]))
    mixed_rows = mixed.transpose(1, 0, 2).reshape(count, width)
    residual = inputs + jnp.dot(mixed_rows, mixing, preferred_element_type=jnp.float32)
    normed, mixer_normal, mixer_scale = norm_parts(residual, factors, biases)
    chosen = jnp.dot(picks.astype(jnp.bfloat16), centroids, preferred_element_type=jnp.float32)
    gates = jax.nn.sigmoid(jnp.sum(normed * chosen, axis=1))
    outgoing = (
        jnp.zeros((experts * capacity, width), jnp.bfloat16)
        .at[slots]
        .set(normed.astype(jnp.bfloat16))
    )
    copies = jnp.broadcast_to(
        outgoing.reshape(experts, 1, capacity, width), (experts, slab_count, capacity, width)
    ).reshape(groups, capacity, width)
    arrived = lax.all_to_all(copies, "expert", split_axis=0, concat_axis=0, tiled=True)
    sources = groups * capacity
    own_rows = arrived.reshape(sources, width)
    gathered = lax.all_gather(own_rows, "tensor", axis=0, tiled=True)
    produced = lax.psum_scatter(
        expert_forward(gathered, expanding[0], contracting[0]).astype(jnp.bfloat16),
        "tensor",
        scatter_dimension=0,
        tiled=True,
    )
    returned = lax.all_to_all(
        produced.reshape(arrived.shape), "expert", split_axis=0, concat_axis=0, tiled=True
    )
    combined = jnp.sum(
        returned.reshape(experts, slab_count, capacity, width).astype(jnp.float32), axis=1
    ).reshape(experts * capacity, width)
    picked = combined[slots]
    layer_output = (residual + gates[:, None] * picked).astype(jnp.bfloat16)
    balance_part = jnp.sum(token_spread * gates) / total_tokens
    upstream = cotangent.astype(jnp.float32)
    gate_grad = jnp.sum(upstream * picked, axis=1)
    logit_grad = (gate_grad + token_spread / total_tokens) * gates * (1.0 - gates)
    scaled_rows = (gates[:, None] * upstream).astype(jnp.bfloat16)
    grad_slots = jnp.zeros((experts * capacity, width), jnp.bfloat16).at[slots].set(scaled_rows)
    grad_copies = jnp.broadcast_to(
        grad_slots.reshape(experts, 1, capacity, width), (experts, slab_count, capacity, width)
    ).reshape(groups, capacity, width)
    incoming = lax.all_to_all(
        grad_copies, "expert", split_axis=0, concat_axis=0, tiled=True
    ).reshape(sources, width)
    incoming_pair = lax.all_gather(incoming, "tensor", axis=0, tiled=True)
    up_share, down_share, hidden_grad = expert_backward(
        gathered, incoming_pair, expanding[0], contracting[0]
    )
    back_rows = lax.psum_scatter(
        jnp.einsum(
            "rf,df->rd", hidden_grad, expanding[0], preferred_element_type=jnp.float32
        ).astype(jnp.bfloat16),
        "tensor",
        scatter_dimension=0,
        tiled=True,
    )
    back = lax.all_to_all(
        back_rows.reshape(arrived.shape), "expert", split_axis=0, concat_axis=0, tiled=True
    )
    back_sum = jnp.sum(
        back.reshape(experts, slab_count, capacity, width).astype(jnp.float32), axis=1
    ).reshape(experts * capacity, width)
    normed_grad = back_sum[slots] + logit_grad[:, None] * chosen
    centroid_grad = jnp.einsum(
        "te,td->ed", picks_float, logit_grad[:, None] * normed, precision=highest
    )
    mixer_back, factor_grad, bias_grad = norm_back(normed_grad, mixer_normal, mixer_scale, factors)
    residual_grad = upstream + mixer_back
    branch_grad = residual_grad.astype(jnp.bfloat16)
    mixing_grad = jnp.einsum(
        "td,te->de", mixed_rows, branch_grad, preferred_element_type=jnp.float32
    )
    mixed_grad = jnp.einsum(
        "te,de->td", branch_grad, mixing, preferred_element_type=jnp.float32
    ).astype(jnp.bfloat16)
    head_grads = mixed_grad.reshape(count, HEADS, width // HEADS).transpose(1, 0, 2)
    query_grad, key_grad, value_grad = lax.map(
        partial(head_backward, allowed), (heads[0], heads[1], heads[2], head_grads, log_total)
    )
    joint_grad = (
        jnp.stack((query_grad, key_grad, value_grad))
        .transpose(2, 0, 1, 3)
        .reshape(count, 3 * width)
        .astype(jnp.bfloat16)
    )
    projection_grad = jnp.einsum("td,te->de", entry, joint_grad, preferred_element_type=jnp.float32)
    entry_back = jnp.einsum("te,de->td", joint_grad, projection, preferred_element_type=jnp.float32)
    entry_input, gain_grad, shift_grad = norm_back(entry_back, entry_normal, entry_scale, gains)
    token_grad = residual_grad + entry_input
    summed = lax.psum(
        (
            gain_grad,
            shift_grad,
            projection_grad,
            mixing_grad,
            factor_grad,
            bias_grad,
            centroid_grad,
            balance_part,
        ),
        ("expert", "tensor"),
    )
    return (
        layer_output,
        summed[7],
        token_grad,
        summed[0],
        summed[1],
        summed[2],
        summed[3],
        summed[4],
        summed[5],
        summed[6],
        up_share[None],
        down_share[None],
    )


HALF_LOG = 1.4426950408889634
LN2 = 0.6931471805599453
NT = (((1,), (1,)), ((), ()))
TN = (((0,), (0,)), ((), ()))
VMEM_LIMIT = 60 * 1024 * 1024


def query_blocks(count):
    step = 256 if count > 256 else count
    return [(i, min(i + step, count)) for i in range(0, count, step)]


def document_starts(lengths_ref, places):
    starts = jnp.zeros_like(places)
    end = 0
    for d in range(lengths_ref.shape[0]):
        end = end + lengths_ref[d]
        starts = jnp.where(places >= end, end, starts)
    return starts


MESH = pl.DeviceIdType.MESH


def neighbours(slabs):
    me, core = lax.axis_index("expert"), lax.axis_index("tensor")
    plane = lax.div(me, slabs)
    x = lax.rem(me, 2)
    y = lax.rem(lax.div(me, 2), 2)
    return me, core, plane, (me + 1 - 2 * x, core), (me + 2 - 4 * y, core), (me, 1 - core)


def greet(partners):
    barrier = pltpu.get_barrier_semaphore()
    number = 0
    for device, there in partners:
        @pl.when(there)
        def _(device=device):
            pl.semaphore_signal(barrier, inc=1, device_id=device, device_id_type=MESH)
        number = number + there.astype(jnp.int32)
    pl.semaphore_wait(barrier, number)


def score_bias(bias_ref, lengths_ref, count):
    places = lax.broadcasted_iota(jnp.int32, (1, count), 1)
    starts = document_starts(lengths_ref, places)
    for s, e in query_blocks(count):
        row = lax.broadcasted_iota(jnp.int32, (e - s, count), 0) + s
        seen = (row <= places) & (row >= starts)
        bias_ref[s:e, :] = jnp.where(seen, 0.0, -1e9)


def row_norm(values, gain, shift):
    centered = values - jnp.mean(values, axis=1, keepdims=True)
    scale = lax.rsqrt(jnp.mean(centered * centered, axis=1, keepdims=True) + epsilon)
    normal = centered * scale
    return normal * gain + shift, normal, scale


def chosen_rows(route, centroids_ref, experts):
    chosen = jnp.zeros((route.shape[0], centroids_ref.shape[1]), jnp.float32)
    for e in range(experts):
        chosen = jnp.where(route == e, centroids_ref[e : e + 1, :].astype(jnp.float32), chosen)
    return chosen


def front_kernel(
    planes,
    slabs,
    lengths_ref,
    tokens_ref,
    gains_ref,
    shifts_ref,
    projection_ref,
    mixing_ref,
    factors_ref,
    biases_ref,
    centroids_ref,
    route_row_ref,
    route_ref,
    cot_ref,
    up_ref,
    down_ref,
    flipped_ref,
    joint_ref,
    mixed_ref,
    logs_ref,
    residual_ref,
    place_ref,
    loads_ref,
    sent_own,
    cot_own,
    gate_own,
    sent_others,
    cot_others,
    gate_others,
    up_near,
    up_far,
    down_near,
    down_far,
    bias_ref,
    order_ref,
    normed_ref,
    tally_ref,
    send_sem,
    recv_sem,
    local_sem,
):
    count, width = tokens_ref.shape
    experts = planes
    rows = sent_own.shape[0]
    half_rows = rows // 2
    pairs = width // 128
    factor = (width // HEADS) ** (-0.5) * HALF_LOG
    middle = planes - 1
    me, core, plane, beside_x, beside_y, beside_core = neighbours(slabs)
    hop_two = lax.rem(plane + 2, planes)
    hop_one = plane + 1 - 2 * lax.rem(plane, 2)
    here = lax.rem(me, slabs)
    always = plane >= 0
    greet(
        [
            (beside_x, always),
            (beside_y, always),
            (beside_core, always),
            ((hop_two * slabs + here, core), always),
            ((me + slabs, core), plane < planes - 1),
            ((me - slabs, core), plane > 0),
        ]
    )

    def remote(i, src, dst, device):
        return pltpu.make_async_remote_copy(
            src_ref=src, dst_ref=dst, send_sem=send_sem.at[i], recv_sem=recv_sem.at[i], device_id=device, device_id_type=MESH
        )

    owns, nears, fars = (up_ref, down_ref), (up_near, down_near), (up_far, down_far)
    stride = 2 * (planes - 1) + 2 * planes - 1

    def hop(kind, sign, r):
        src = owns[kind].at[0] if r == 1 else nears[kind].at[middle - sign * (r - 1)]
        i = kind * stride + (r - 1) * 2 + (sign > 0)
        return remote(i, src, nears[kind].at[middle - sign * r], (me + sign * slabs, core))

    def hop_sent(sign, r):
        ahead = plane if sign > 0 else planes - 1 - plane
        return (ahead >= r - 1) & (ahead < planes - 1)

    def hop_came(sign, r):
        ahead = plane if sign > 0 else planes - 1 - plane
        return ahead >= r

    def aside(kind, slot):
        src = owns[kind].at[0] if slot == middle else nears[kind].at[slot]
        i = kind * stride + 2 * (planes - 1) + slot
        return remote(i, src, fars[kind].at[slot], beside_x)

    def held(slot):
        at = plane + slot - middle
        return (at >= 0) & (at < planes)

    def own_weights(kind):
        return pltpu.make_async_copy(owns[kind].at[0], nears[kind].at[middle], local_sem.at[kind])

    for kind in range(2):
        for sign in (1, -1):
            @pl.when(hop_sent(sign, 1))
            def _(kind=kind, sign=sign):
                hop(kind, sign, 1).start()
        aside(kind, middle).start()
        own_weights(kind).start()

    def forward_weights(kind, r):
        for sign in (1, -1):
            slot = middle - sign * r

            @pl.when(hop_came(sign, r))
            def _(sign=sign, slot=slot):
                hop(kind, sign, r).wait_recv()
                aside(kind, slot).start()

            if r < planes - 1:
                @pl.when(hop_sent(sign, r + 1))
                def _(sign=sign):
                    hop(kind, sign, r + 1).start()

    base = 2 * stride

    def row_copy(which, part, piece):
        own, others = ((cot_own, cot_others), (sent_own, sent_others))[which]
        at = pl.ds(piece * half_rows, half_rows)
        i = base + which * 6 + part * 2 + piece
        if part == 0:
            return remote(i, own.at[at], others.at[1, at], beside_y)
        if part == 1:
            return remote(i, own.at[at], others.at[0, at], beside_core)
        return remote(i, others.at[1, at], others.at[2, at], beside_core)

    def gate_copy(part):
        i = base + 12 + part
        if part == 0:
            return remote(i, gate_own, gate_others.at[1], beside_y)
        if part == 1:
            return remote(i, gate_own, gate_others.at[0], beside_core)
        return remote(i, gate_others.at[1], gate_others.at[2], beside_core)

    rounds = [beside_core, beside_x, beside_y, (hop_one * slabs + here, core), (hop_two * slabs + here, core)]

    def tally(k):
        return remote(base + 15 + k, tally_ref.at[2 * k], tally_ref.at[2 * k + 1], rounds[k])

    def tally_step(k):
        tally(k).wait_recv()
        total = tally_ref[2 * k] + tally_ref[2 * k + 1]
        if k + 1 < len(rounds):
            tally_ref[2 * k + 2] = total
            tally(k + 1).start()
        else:
            loads_ref[...] = total

    number = lax.broadcasted_iota(jnp.int32, (8, count), 0)
    picks = jnp.where(number == route_row_ref[...], 1.0, 0.0)
    chunk = 128
    for s in range(0, count, chunk):
        row = lax.broadcasted_iota(jnp.int32, (chunk, count), 0) + s
        column = lax.broadcasted_iota(jnp.int32, (chunk, count), 1)
        order_ref[s : s + chunk, :] = jnp.where(row < column, 1.0, 0.0).astype(jnp.bfloat16)
    ranks = jnp.dot(picks.astype(jnp.bfloat16), order_ref[0:count, :], preferred_element_type=jnp.float32)
    counts = jnp.sum(picks, axis=1, keepdims=True)
    padded = jnp.ceil(counts * (1.0 / ALIGN)) * ALIGN
    place = jnp.zeros((1, count), jnp.float32)
    start = jnp.zeros((1, 1), jnp.float32)
    for e in range(experts):
        place = place + picks[e : e + 1, :] * (ranks[e : e + 1, :] + start)
        start = start + padded[e : e + 1, :]
    place_ref[...] = jnp.broadcast_to(place, (8, count))
    tally_ref[0] = jnp.broadcast_to(counts, (8, 128))
    tally(0).start()
    for s in range(0, rows, 64):
        row = lax.broadcasted_iota(jnp.int32, (64, count), 0) + s
        order_ref[s : s + 64, :] = jnp.where(row.astype(jnp.float32) == place, 1.0, 0.0).astype(jnp.bfloat16)

    def sort_rows(source_ref, to_ref, which):
        for piece in range(2):
            at = slice(piece * half_rows, (piece + 1) * half_rows)
            to_ref[at, :] = jnp.dot(
                order_ref[at, :], source_ref[...], preferred_element_type=jnp.float32
            ).astype(jnp.bfloat16)
            row_copy(which, 0, piece).start()
            row_copy(which, 1, piece).start()

    sort_rows(cot_ref, cot_own, 0)

    def project(i, _):
        at = pl.ds(pl.multiple_of(i * 192, 192), 192)
        entry, _, _ = row_norm(tokens_ref[at, :].astype(jnp.float32), gains_ref[...], shifts_ref[...])
        entry = entry.astype(jnp.bfloat16)
        normed_ref[at, 0:width] = entry
        joint_ref[at, :] = jnp.dot(entry, projection_ref[...], preferred_element_type=jnp.float32).astype(jnp.bfloat16)
        return 0

    lax.fori_loop(0, count // 192, project, 0)
    for s in range(0, count, 384):
        flipped_ref[:, s : s + 384] = jnp.transpose(normed_ref[s : s + 384, 0:width])
    score_bias(bias_ref, lengths_ref, count)
    forward_weights(0, 1)
    tally_step(0)

    first = lax.broadcasted_iota(jnp.int32, (1, 128), 1) < 64

    def attend(p, _):
        lanes = pl.ds(pl.multiple_of(p * 128, 128), 128)
        keys = pl.ds(pl.multiple_of(width + p * 128, 128), 128)
        values = pl.ds(pl.multiple_of(2 * width + p * 128, 128), 128)
        for s, e in query_blocks(count):
            outs = []
            for half in range(2):
                q = jnp.where(first == (half == 0), joint_ref[s:e, lanes], jnp.bfloat16(0))
                scores = lax.dot_general(joint_ref[0:e, keys], q, NT, preferred_element_type=jnp.float32)
                scores = scores * factor + bias_ref[0:e, s:e]
                peak = jnp.max(scores, axis=0, keepdims=True)
                weights = jnp.exp2(scores - peak)
                total = jnp.sum(weights, axis=0, keepdims=True)
                probs = (weights * (1.0 / total)).astype(jnp.bfloat16)
                outs.append(
                    lax.dot_general(probs, joint_ref[0:e, values], TN, preferred_element_type=jnp.float32)
                )
                logs_ref[p, half : half + 1, s:e] = peak + jnp.log2(total)
            mixed_ref[s:e, lanes] = jnp.where(first, outs[0], outs[1]).astype(jnp.bfloat16)

        @pl.when(p == 1)
        def _():
            forward_weights(1, 1)
            tally_step(1)

        @pl.when(p == 3)
        def _():
            forward_weights(0, 2)
            tally_step(2)

        @pl.when(p == 5)
        def _():
            for piece in range(2):
                row_copy(0, 0, piece).wait_recv()
                row_copy(0, 2, piece).start()
            forward_weights(1, 2)
            tally_step(3)

        return 0

    lax.fori_loop(0, pairs, attend, 0)

    lane = lax.broadcasted_iota(jnp.int32, (1, 128), 1)

    def mix(i, _):
        at = pl.ds(pl.multiple_of(i * 192, 192), 192)
        residual = tokens_ref[at, :].astype(jnp.float32) + jnp.dot(
            mixed_ref[at, :], mixing_ref[...], preferred_element_type=jnp.float32
        )
        residual_ref[at, :] = residual
        normed, _, _ = row_norm(residual, factors_ref[...], biases_ref[...])
        chosen = chosen_rows(route_ref[at, :], centroids_ref, experts)
        gate = 1.0 / (1.0 + jnp.exp(-jnp.sum(normed * chosen, axis=1, keepdims=True)))
        high = gate.astype(jnp.bfloat16).astype(jnp.float32)
        mid = (gate - high).astype(jnp.bfloat16).astype(jnp.float32)
        low = gate - high - mid
        parts = jnp.where(lane == 0, high, jnp.where(lane == 1, mid, jnp.where(lane == 2, low, 0.0)))
        normed_ref[at, 0:width] = normed.astype(jnp.bfloat16)
        normed_ref[at, width : width + 128] = parts.astype(jnp.bfloat16)
        return 0

    lax.fori_loop(0, count // 192, mix, 0)
    for piece in range(2):
        at = slice(piece * half_rows, (piece + 1) * half_rows)
        moved = jnp.dot(order_ref[at, :], normed_ref[...], preferred_element_type=jnp.float32)
        sent_own[at, :] = moved[:, 0:width].astype(jnp.bfloat16)
        row_copy(1, 0, piece).start()
        row_copy(1, 1, piece).start()
        bias_ref[at, 0:128] = jnp.broadcast_to(
            jnp.sum(moved[:, width : width + 128], axis=1, keepdims=True), (half_rows, 128)
        )
    gates = jnp.transpose(bias_ref[0:rows, 0:128])
    gate_own[0:1, :] = gates[0:1, :]
    gate_own[1:2, :] = jnp.zeros((1, rows), jnp.float32)
    for e in range(8):
        gate_own[1:2, e : e + 1] = padded[e : e + 1, :]
    gate_copy(0).start()
    gate_copy(1).start()

    for kind in range(2):
        forward_weights(kind, 3)
    gate_copy(0).wait_recv()
    gate_copy(2).start()
    tally_step(4)
    for piece in range(2):
        row_copy(1, 0, piece).wait_recv()
        row_copy(1, 2, piece).start()

    for which in range(2):
        for part in range(3):
            for piece in range(2):
                copy = row_copy(which, part, piece)
                copy.wait_send()
                if part:
                    copy.wait_recv()
    for part in range(3):
        gate_copy(part).wait_send()
        if part:
            gate_copy(part).wait_recv()
    for k in range(len(rounds)):
        tally(k).wait_send()
    for kind in range(2):
        own_weights(kind).wait()
        for r in range(1, planes):
            for sign in (1, -1):
                @pl.when(hop_sent(sign, r))
                def _(kind=kind, sign=sign, r=r):
                    hop(kind, sign, r).wait_send()
        for slot in range(2 * planes - 1):
            @pl.when(held(slot))
            def _(kind=kind, slot=slot):
                aside(kind, slot).wait()


def front_stage(
    tokens, gains, shifts, projection, mixing, factors, biases, centroids, expanding, contracting, route, lengths, cotangent, planes, slabs
):
    count, width = tokens.shape
    rows = aligned_rows(count, planes)
    pairs = width // 128
    slots = 2 * planes - 1
    bf16, f32 = jnp.bfloat16, jnp.float32
    shape = jax.ShapeDtypeStruct
    anywhere = pl.BlockSpec(memory_space=pl.ANY)
    local = pl.BlockSpec(memory_space=pltpu.VMEM)
    dma = pltpu.SemaphoreType.DMA
    copies = 2 * (2 * (planes - 1) + slots) + 12 + 3 + 5
    outs = [
        (shape((width, count), bf16), local),
        (shape((count, 3 * width), bf16), local),
        (shape((count, width), bf16), local),
        (shape((pairs, 2, count), f32), local),
        (shape((count, width), f32), local),
        (shape((8, count), f32), local),
        (shape((8, 128), f32), local),
        (shape((rows, width), bf16), local),
        (shape((rows, width), bf16), local),
        (shape((8, rows), f32), local),
        (shape((3, rows, width), bf16), anywhere),
        (shape((3, rows, width), bf16), anywhere),
        (shape((3, 8, rows), f32), anywhere),
        (shape((slots,) + expanding.shape[1:], bf16), anywhere),
        (shape((slots,) + expanding.shape[1:], bf16), anywhere),
        (shape((slots,) + contracting.shape[1:], bf16), anywhere),
        (shape((slots,) + contracting.shape[1:], bf16), anywhere),
    ]
    row = lambda v: v.reshape(1, -1)
    return pl.pallas_call(
        partial(front_kernel, planes, slabs),
        out_shape=[o[0] for o in outs],
        in_specs=[pl.BlockSpec(memory_space=pltpu.SMEM)] + [local] * 11 + [anywhere] * 2,
        out_specs=[o[1] for o in outs],
        scratch_shapes=[
            pltpu.VMEM((rows, count), f32),
            pltpu.VMEM((rows, count), bf16),
            pltpu.VMEM((count, width + 128), bf16),
            pltpu.VMEM((10, 8, 128), f32),
            dma((copies,)),
            dma((copies,)),
            dma((2,)),
        ],
        compiler_params=pltpu.CompilerParams(
            collective_id=0, has_side_effects=True, vmem_limit_bytes=VMEM_LIMIT
        ),
    )(
        lengths[0],
        tokens,
        row(gains),
        row(shifts),
        projection,
        mixing,
        row(factors),
        row(biases),
        jnp.pad(centroids, ((0, -centroids.shape[0] % 8), (0, 0))),
        row(route),
        route,
        cotangent,
        expanding,
        contracting,
    )


STEP = 192


def rear_kernel(
    planes,
    slabs,
    total_tokens,
    lengths_ref,
    tokens_ref,
    gains_ref,
    projection_ref,
    mixing_ref,
    factors_ref,
    biases_ref,
    centroids_ref,
    route_ref,
    cot_ref,
    flipped_ref,
    joint_in,
    mixed_ref,
    logs_ref,
    residual_in,
    place_ref,
    loads_ref,
    dots_ref,
    back_all,
    made_all,
    near_all,
    far_all,
    layer_ref,
    token_ref,
    vector_ref,
    up_out,
    down_out,
    shared_out,
    core_land,
    y_land,
    x_land,
    z_land,
    joint_ref,
    residual_ref,
    bias_ref,
    upstream_ref,
    a_ref,
    b_ref,
    place_col,
    gate_col,
    dot_land,
    part_ref,
    stage_ref,
    own_ref,
    own_core,
    own_x,
    own_y,
    own_z,
    piece_ref,
    tally_ref,
    key_sums,
    send_sem,
    recv_sem,
    local_sem,
):
    count, width = tokens_ref.shape
    experts = planes
    rows = a_ref.shape[0]
    half_rows = rows // 2
    pairs = width // 128
    half = width // 2
    scale = (width // HEADS) ** (-0.5)
    factor = scale * HALF_LOG
    average = total_tokens / experts
    me, core, plane, beside_x, beside_y, beside_core = neighbours(slabs)
    x = lax.rem(me, 2)
    y = lax.rem(lax.div(me, 2), 2)
    here = lax.rem(me, slabs)
    diagonal = (beside_y[0], 1 - core)
    always = plane >= 0
    others = [(lax.rem(plane + d, planes) * slabs + here, core) for d in range(1, planes)]
    greet([(d, always) for d in [beside_x, beside_y, beside_core, diagonal] + others])
    ids = {}

    def remote(key, src, dst, device):
        i = ids.setdefault(key, len(ids))
        return pltpu.make_async_remote_copy(
            src_ref=src, dst_ref=dst, send_sem=send_sem.at[i], recv_sem=recv_sem.at[i], device_id=device, device_id_type=MESH
        )

    def fetch(i, src, dst):
        return pltpu.make_async_copy(src, dst, local_sem.at[i])

    loads = [fetch(0, joint_in, joint_ref), fetch(1, residual_in, residual_ref)]
    for copy in loads:
        copy.start()

    alls = (back_all, made_all)

    def to_core(which, second, piece):
        at = pl.ds(piece * half_rows, half_rows)
        return remote(
            ("core", which, second, piece), alls[which].at[1 + 2 * second, at], core_land.at[which, second, at], beside_core
        )

    def to_y(which, piece):
        at = pl.ds(piece * half_rows, half_rows)
        return remote(("y", which, piece), a_ref.at[at], y_land.at[which, at], beside_y)

    def dot_copy(k):
        return remote(("dot", k), dots_ref.at[1 + k], dot_land.at[k], (beside_core, beside_y, diagonal)[k])

    for which in range(2):
        for second in (1, 0):
            for piece in range(2):
                to_core(which, second, piece).start()
        if which == 0:
            for k in range(3):
                dot_copy(k).start()

    def target(sign, r):
        e = plane + sign * r
        return jnp.clip(e, 0, planes - 1), (e >= 0) & (e < planes)

    def share_x(sign, r):
        e, _ = target(sign, r)
        return remote(("x", sign, r), far_all.at[e], x_land.at[e], beside_x)

    def share_z(sign, r):
        return remote(
            ("z", sign, r),
            stage_ref.at[0 if sign > 0 else 1],
            z_land.at[0 if sign > 0 else 1, r - 1],
            (jnp.clip(me + sign * slabs, 0, planes * slabs - 1), core),
        )

    ways = [(s, r) for r in range(planes - 1, 0, -1) for s in (1, -1)] + [(1, 0)]
    for sign, r in ways:
        @pl.when(target(sign, r)[1])
        def _(sign=sign, r=r):
            share_x(sign, r).start()

    def add_pieces(into, sources, size, step):
        def one(i, _):
            at = pl.ds(pl.multiple_of(i * step, step), step)
            total = sources[0][at, :].astype(jnp.float32)
            for s in sources[1:]:
                total = total + s[at, :].astype(jnp.float32)
            into[at, :] = total.astype(into.dtype)
            return 0
        lax.fori_loop(0, size // step, one, 0)

    def share_step(sign, r):
        e, valid = target(sign, r)
        lane = 0 if sign > 0 else 1

        @pl.when(valid)
        def _():
            first = fetch(2, near_all.at[e], part_ref.at[0])
            first.start()
            share_x(sign, r).wait_recv()
            second = fetch(3, x_land.at[e], part_ref.at[1])
            second.start()
            if r < planes - 1:
                @pl.when(target(sign, r + 1)[1])
                def _():
                    share_z(sign, r + 1).wait_send()
            first.wait()
            second.wait()
            add_pieces(stage_ref.at[lane], [part_ref.at[0], part_ref.at[1]], part_ref.shape[1], 96)
            if r < planes - 1:
                @pl.when((plane - sign >= 0) & (plane - sign < planes))
                def _():
                    share_z(sign, r + 1).wait_recv()
                    third = fetch(2, z_land.at[lane, r], part_ref.at[0])
                    third.start()
                    third.wait()
                    add_pieces(stage_ref.at[lane], [stage_ref.at[lane], part_ref.at[0]], part_ref.shape[1], 96)
            share_z(sign, r).start()

    def share_end():
        share_x(1, 0).wait_recv()
        copies = [fetch(2, near_all.at[plane], part_ref.at[0]), fetch(3, x_land.at[plane], part_ref.at[1])]
        for copy in copies:
            copy.start()
        for copy in copies:
            copy.wait()

        def put(sources, more):
            def rows_of(i, _):
                at = pl.ds(pl.multiple_of(i * 96, 96), 96)
                total = sources[0][at, :].astype(jnp.float32)
                if len(sources) > 1:
                    total = total + sources[1][at, :].astype(jnp.float32)
                up_out[at, :] = up_out[at, :] + total if more else total
                return 0
            lax.fori_loop(0, width // 96, rows_of, 0)

            def columns_of(i, _):
                at = pl.ds(pl.multiple_of(i * 96, 96), 96)
                for part in range(2):
                    source_at = pl.ds(pl.multiple_of(width + part * half + i * 96, 32), 96)
                    total = sources[0][source_at, :].astype(jnp.float32)
                    if len(sources) > 1:
                        total = total + sources[1][source_at, :].astype(jnp.float32)
                    to = slice(part * half, (part + 1) * half)
                    down_out[at, to] = down_out[at, to] + total if more else total
                return 0
            lax.fori_loop(0, half // 96, columns_of, 0)

        put([part_ref.at[0], part_ref.at[1]], False)
        for sign in (1, -1):
            lane = 0 if sign > 0 else 1

            @pl.when((plane - sign >= 0) & (plane - sign < planes))
            def _(sign=sign, lane=lane):
                share_z(sign, 1).wait_recv()
                third = fetch(2, z_land.at[lane, 0], part_ref.at[0])
                third.start()
                third.wait()
                put([part_ref.at[0]], True)

    q1, q2, q3, q4 = width // 2, width // 4, width // 8, width // 16
    base1 = core * q1
    base2 = base1 + x * q2
    base3 = base2 + y * q3

    def spot(start, size):
        return pl.ds(pl.multiple_of(start, 16), size)

    def corner(p):
        return lax.div(p, 2) * q4, pl.multiple_of(lax.rem(p, 2) * half, 128)

    def sum_copy(c, stage, d=0):
        own = own_ref.at[c % 2]
        if stage == "core":
            return remote((c, stage), own.at[spot((1 - core) * q1, q1)], own_core.at[c], beside_core)
        if stage == "x":
            return remote((c, stage), own.at[spot(base1 + (1 - x) * q2, q2)], own_x.at[c], beside_x)
        if stage == "y":
            return remote((c, stage), own.at[spot(base2 + (1 - y) * q3, q3)], own_y.at[c], beside_y)
        if stage == "z":
            r, k = corner(lax.rem(plane + d, planes))
            return remote(
                (c, stage, d), own.at[spot(base3 + r, q4), pl.ds(k, half)], own_z.at[c, d - 1], others[d - 1]
            )
        out = shared_out.at[c]
        if stage == "zz":
            r, k = corner(plane)
            return remote(
                (c, stage, d), piece_ref.at[c], out.at[spot(base3 + r, q4), pl.ds(k, half)], others[d - 1]
            )
        if stage == "yy":
            at = spot(base3, q3)
            return remote((c, stage), out.at[at], out.at[at], beside_y)
        if stage == "xx":
            at = spot(base2, q2)
            return remote((c, stage), out.at[at], out.at[at], beside_x)
        at = spot(base1, q1)
        return remote((c, stage), out.at[at], out.at[at], beside_core)

    def add_rows(c, start, size, came, step):
        def one(i, _):
            at = pl.ds(pl.multiple_of(i * step, step), step)
            mine = spot(start + i * step, step)
            own_ref[c % 2, mine, :] = (
                own_ref[c % 2, mine, :].astype(jnp.float32) + came[c, at, :].astype(jnp.float32)
            ).astype(jnp.bfloat16)
            return 0
        lax.fori_loop(0, size // step, one, 0)

    def keep_piece(c):
        r, k = corner(plane)
        return fetch(4 + c, piece_ref.at[c], shared_out.at[c, spot(base3 + r, q4), pl.ds(k, half)])

    def sum_step(c, stage):
        if stage == 0:
            sum_copy(c, "core").start()
        elif stage == 1:
            sum_copy(c, "core").wait_recv()
            add_rows(c, base1, q1, own_core, 48)
            sum_copy(c, "x").start()
        elif stage == 2:
            sum_copy(c, "x").wait_recv()
            add_rows(c, base2, q2, own_x, 48)
            sum_copy(c, "y").start()
        elif stage == 3:
            sum_copy(c, "y").wait_recv()
            add_rows(c, base3, q3, own_y, 48)
            for d in range(1, planes):
                sum_copy(c, "z", d).start()
        elif stage == 4:
            r, k = corner(plane)
            total = own_ref[c % 2, spot(base3 + r, q4), pl.ds(k, half)].astype(jnp.float32)
            for d in range(1, planes):
                sum_copy(c, "z", d).wait_recv()
                total = total + own_z[c, d - 1].astype(jnp.float32)
            piece_ref[c] = total.astype(jnp.bfloat16)
            keep_piece(c).start()
            for d in range(1, planes):
                sum_copy(c, "zz", d).start()
        elif stage == 5:
            keep_piece(c).wait()
            for d in range(1, planes):
                sum_copy(c, "zz", d).wait_recv()
            sum_copy(c, "yy").start()
        elif stage == 6:
            sum_copy(c, "yy").wait_recv()
            sum_copy(c, "xx").start()
        elif stage == 7:
            sum_copy(c, "xx").wait_recv()
            sum_copy(c, "cc").start()
        else:
            sum_copy(c, "cc").wait_recv()

    def sum_sent(c):
        for stage in ("core", "x", "y"):
            sum_copy(c, stage).wait_send()
        for d in range(1, planes):
            sum_copy(c, "z", d).wait_send()

    def sum_for_y(which):
        for piece in range(2):
            at = pl.ds(piece * half_rows, half_rows)
            first = fetch(2, alls[which].at[2, at], a_ref.at[at])
            first.start()
            to_core(which, 1, piece).wait_recv()
            second = fetch(3, core_land.at[which, 1, at], b_ref.at[at])
            second.start()
            first.wait()
            second.wait()
            add_pieces(a_ref.at[at], [a_ref.at[at], b_ref.at[at]], half_rows, 32)
            to_y(which, piece).start()

    sum_for_y(0)
    place_col[...] = jnp.transpose(place_ref[...])
    score_bias(bias_ref, lengths_ref, count)
    for copy in loads:
        copy.wait()
    vector_ref[...] = jnp.zeros_like(vector_ref)
    number = lax.broadcasted_iota(jnp.int32, (1, rows), 1).astype(jnp.float32)

    def order_of(at):
        return jnp.where(place_col[at, 0:1] == number, 1.0, 0.0)

    def chunk_of(i):
        return pl.ds(pl.multiple_of(i * STEP, STEP), STEP)

    steps = count // STEP

    def unsort(buffer, act):
        def one(i, _):
            at = chunk_of(i)
            act(at, jnp.dot(order_of(at).astype(jnp.bfloat16), buffer[...], preferred_element_type=jnp.float32))
            return 0
        lax.fori_loop(0, steps, one, 0)

    def set_token(at, value):
        token_ref[at, :] = value

    def add_token(at, value):
        token_ref[at, :] += value

    own_back = fetch(2, back_all.at[0], b_ref)
    own_back.start()
    own_back.wait()
    unsort(b_ref, set_token)
    for piece in range(2):
        to_core(0, 0, piece).wait_recv()
    core_back = fetch(2, core_land.at[0, 0], b_ref)
    core_back.start()
    core_back.wait()
    unsort(b_ref, add_token)
    for sign in (1, -1):
        share_step(sign, planes - 1)
    for piece in range(2):
        to_y(0, piece).wait_recv()
    y_back = fetch(2, y_land.at[0], b_ref)
    y_back.start()
    y_back.wait()
    unsort(b_ref, add_token)
    for k in range(3):
        dot_copy(k).wait_recv()
    dots = dots_ref[0] + dot_land[0] + dot_land[1] + dot_land[2]
    dots = dots[0:1, :]

    def norm_step(i, _):
        at = chunk_of(i)
        normed, normal, spread_by = row_norm(residual_ref[at, :], factors_ref[...], biases_ref[...])
        route = route_ref[at, :]
        chosen = chosen_rows(route, centroids_ref, experts)
        gate = 1.0 / (1.0 + jnp.exp(-jnp.sum(normed * chosen, axis=1, keepdims=True)))
        gate_col[at, :] = jnp.broadcast_to(gate, (STEP, 128))
        gate_grad = jnp.sum(order_of(at) * dots, axis=1, keepdims=True)
        spread = jnp.zeros((STEP, 1), jnp.float32)
        for e in range(experts):
            spread = jnp.where(route == e, (loads_ref[e : e + 1, 0:1] - average) * (1.0 / average), spread)
        logit = (gate_grad + spread * (1.0 / total_tokens)) * gate * (1.0 - gate)
        above = token_ref[at, :] + logit * chosen
        pull = logit * normed
        vector_ref[2:3, :] += jnp.sum(above * normal, axis=0, keepdims=True)
        vector_ref[3:4, :] += jnp.sum(above, axis=0, keepdims=True)
        for e in range(experts):
            vector_ref[8 + e : 9 + e, :] += jnp.sum(jnp.where(route == e, pull, 0.0), axis=0, keepdims=True)
        vector_ref[4:5, :] += jnp.broadcast_to(
            jnp.sum(spread * gate, axis=0, keepdims=True) * (1.0 / total_tokens), (1, width)
        )
        scaled = above * factors_ref[...]
        inner = (
            scaled
            - jnp.mean(scaled, axis=1, keepdims=True)
            - normal * jnp.mean(scaled * normal, axis=1, keepdims=True)
        )
        grad = cot_ref[at, :].astype(jnp.float32) + inner * spread_by
        token_ref[at, :] = grad
        branch = grad.astype(jnp.bfloat16)
        layer_ref[at, :] = branch
        upstream_ref[at, :] = lax.dot_general(
            branch, mixing_ref[...], NT, preferred_element_type=jnp.float32
        ).astype(jnp.bfloat16)
        return 0

    lax.fori_loop(0, steps, norm_step, 0)
    own_ref[0] = lax.dot_general(
        mixed_ref[...], layer_ref[...], TN, preferred_element_type=jnp.float32
    ).astype(jnp.bfloat16)
    sum_step(0, 0)
    for piece in range(2):
        to_y(0, piece).wait_send()
    sum_for_y(1)

    first = lax.broadcasted_iota(jnp.int32, (1, 128), 1) < 64

    def attend(p, _):
        lanes = pl.ds(pl.multiple_of(p * 128, 128), 128)
        keys = pl.ds(pl.multiple_of(width + p * 128, 128), 128)
        values = pl.ds(pl.multiple_of(2 * width + p * 128, 128), 128)
        key_sum, value_sum = key_sums.at[0], key_sums.at[1]
        key_sum[...] = jnp.zeros_like(key_sum)
        value_sum[...] = jnp.zeros_like(value_sum)
        for s, e in query_blocks(count):
            both = jnp.transpose(
                upstream_ref[s:e, lanes].astype(jnp.float32) * mixed_ref[s:e, lanes].astype(jnp.float32)
            )
            found = []
            for h in range(2):
                mine = first == (h == 0)
                inner = jnp.sum(both[64 * h : 64 * h + 64, :], axis=0, keepdims=True)
                q = jnp.where(mine, joint_ref[s:e, lanes], jnp.bfloat16(0))
                u = jnp.where(mine, upstream_ref[s:e, lanes], jnp.bfloat16(0))
                scores = lax.dot_general(joint_ref[0:e, keys], q, NT, preferred_element_type=jnp.float32)
                probs = jnp.exp2(scores * factor + bias_ref[0:e, s:e] - logs_ref[p, h : h + 1, s:e])
                prob_grad = lax.dot_general(joint_ref[0:e, values], u, NT, preferred_element_type=jnp.float32)
                score_grad = (probs * (prob_grad - inner)).astype(jnp.bfloat16)
                value_sum[0:e, :] += jnp.dot(probs.astype(jnp.bfloat16), u, preferred_element_type=jnp.float32)
                key_sum[0:e, :] += jnp.dot(score_grad, q, preferred_element_type=jnp.float32)
                found.append(
                    lax.dot_general(score_grad, joint_ref[0:e, keys], TN, preferred_element_type=jnp.float32)
                )
            joint_ref[s:e, lanes] = (jnp.where(first, found[0], found[1]) * scale).astype(jnp.bfloat16)
        joint_ref[:, keys] = (key_sum[...] * scale).astype(jnp.bfloat16)
        joint_ref[:, values] = value_sum[...].astype(jnp.bfloat16)

        events = {
            0: [(0, 1)],
            1: [(0, 2)],
            2: [(0, 3), (1, 1)],
            3: [(0, 4), (1, 2)],
            4: [(0, 5), (1, 3), (2, 1)],
            5: [(0, 6), (1, 4), (2, 2)],
        }
        for k, steps_of in events.items():
            @pl.when(p == k)
            def _(k=k, steps_of=steps_of):
                if k == 1:
                    for sign in (1, -1):
                        share_step(sign, 2)
                if k == 5:
                    for sign in (1, -1):
                        share_step(sign, 1)
                for c, stage in steps_of:
                    sum_step(c, stage)
        for c in range(1, 4):
            @pl.when(p == 2 * c - 1)
            def _(c=c):
                if c >= 2:
                    sum_sent(c - 2)
                for k in range(3):
                    at = pl.ds(k * width + (c - 1) * 256, 256)
                    own_ref[c % 2, :, k * 256 : (k + 1) * 256] = jnp.dot(
                        flipped_ref[...], joint_ref[:, at], preferred_element_type=jnp.float32
                    ).astype(jnp.bfloat16)
                sum_step(c, 0)

        return 0

    lax.fori_loop(0, pairs, attend, 0)

    rounds = [beside_core, beside_x, beside_y]
    rounds += [((plane + 1 - 2 * lax.rem(plane, 2)) * slabs + here, core), (lax.rem(plane + 2, planes) * slabs + here, core)]

    def tally(k):
        return remote(("tally", k), tally_ref.at[2 * k], tally_ref.at[2 * k + 1], rounds[k])

    def tally_step(k):
        tally(k).wait_recv()
        total = tally_ref[2 * k] + tally_ref[2 * k + 1]
        if k + 1 < len(rounds):
            tally_ref[2 * k + 2] = total
            tally(k + 1).start()
        else:
            vector_ref[...] = total

    def finish_step(i, _):
        at = chunk_of(i)
        back = lax.dot_general(joint_ref[at, :], projection_ref[...], NT, preferred_element_type=jnp.float32)
        _, normal, spread_by = row_norm(tokens_ref[at, :].astype(jnp.float32), gains_ref[...], gains_ref[...])
        scaled = back * gains_ref[...]
        inner = (
            scaled
            - jnp.mean(scaled, axis=1, keepdims=True)
            - normal * jnp.mean(scaled * normal, axis=1, keepdims=True)
        )
        token_ref[at, :] += inner * spread_by
        vector_ref[0:1, :] += jnp.sum(back * normal, axis=0, keepdims=True)
        vector_ref[1:2, :] += jnp.sum(back, axis=0, keepdims=True)
        return 0

    def add_made(at, value):
        residual_ref[at, :] += gate_col[at, 0:1] * value

    def end_made(at, value):
        layer_ref[at, :] = (residual_ref[at, :] + gate_col[at, 0:1] * value).astype(jnp.bfloat16)

    def gather_made(source, act):
        copy = fetch(2, source, b_ref)
        copy.start()
        copy.wait()
        unsort(b_ref, act)

    lax.fori_loop(0, steps // 2, finish_step, 0)
    for c, stage in ((0, 7), (1, 5), (2, 3), (3, 1)):
        sum_step(c, stage)
    lax.fori_loop(steps // 2, steps, finish_step, 0)
    tally_ref[0] = vector_ref[...]
    tally(0).start()
    for c, stage in ((0, 8), (1, 6), (2, 4), (3, 2)):
        sum_step(c, stage)
    gather_made(made_all.at[0], add_made)
    for c, stage in ((1, 7), (2, 5), (3, 3)):
        sum_step(c, stage)
    tally_step(0)
    for piece in range(2):
        to_core(1, 0, piece).wait_recv()
    gather_made(core_land.at[1, 0], add_made)
    for c, stage in ((1, 8), (2, 6), (3, 4)):
        sum_step(c, stage)
    tally_step(1)
    for piece in range(2):
        to_y(1, piece).wait_recv()
    gather_made(y_land.at[1], end_made)
    for c, stage in ((2, 7), (3, 5)):
        sum_step(c, stage)
    tally_step(2)
    share_end()
    for c, stage in ((2, 8), (3, 6)):
        sum_step(c, stage)
    tally_step(3)
    sum_step(3, 7)
    tally_step(4)
    sum_step(3, 8)

    for which in range(2):
        for piece in range(2):
            for second in range(2):
                to_core(which, second, piece).wait_send()
    for piece in range(2):
        to_y(1, piece).wait_send()
    for k in range(3):
        dot_copy(k).wait_send()
    for sign, r in ways:
        @pl.when(target(sign, r)[1])
        def _(sign=sign, r=r):
            share_x(sign, r).wait_send()
    for sign in (1, -1):
        @pl.when(target(sign, 1)[1])
        def _(sign=sign):
            share_z(sign, 1).wait_send()
    for c in (2, 3):
        sum_sent(c)
    for c in range(4):
        for d in range(1, planes):
            sum_copy(c, "zz", d).wait_send()
        for stage in ("yy", "xx", "cc"):
            sum_copy(c, stage).wait_send()
    for k in range(len(rounds)):
        tally(k).wait_send()
    assert len(ids) <= send_sem.shape[0]


def rear_stage(
    tokens, gains, projection, mixing, factors, biases, centroids, route, lengths, cotangent,
    flipped, joint, mixed, logs, residual, place, loads, dots, back, made, near, far, planes, slabs, total_tokens,
):
    count, width = tokens.shape
    rows = back.shape[1]
    half = width // 2
    bf16, f32 = jnp.bfloat16, jnp.float32
    shape = jax.ShapeDtypeStruct
    anywhere = pl.BlockSpec(memory_space=pl.ANY)
    local = pl.BlockSpec(memory_space=pltpu.VMEM)
    dma = pltpu.SemaphoreType.DMA
    packed = near.shape[1:]
    outs = [
        (shape((count, width), bf16), local),
        (shape((count, width), f32), local),
        (shape((16, width), f32), local),
        (shape((width, half), f32), local),
        (shape((half, width), f32), local),
        (shape((4, width, width), bf16), anywhere),
        (shape((2, 2, rows, width), bf16), anywhere),
        (shape((2, rows, width), bf16), anywhere),
        (shape((planes,) + packed, bf16), anywhere),
        (shape((2, planes - 1) + packed, bf16), anywhere),
    ]
    row = lambda v: v.reshape(1, -1)
    copies = 120
    return pl.pallas_call(
        partial(rear_kernel, planes, slabs, total_tokens),
        out_shape=[o[0] for o in outs],
        in_specs=[pl.BlockSpec(memory_space=pltpu.SMEM)]
        + [local] * 10
        + [anywhere]
        + [local] * 2
        + [anywhere]
        + [local] * 3
        + [anywhere] * 4,
        out_specs=[o[1] for o in outs],
        scratch_shapes=[
            pltpu.VMEM((count, 3 * width), bf16),
            pltpu.VMEM((count, width), f32),
            pltpu.VMEM((count, count), f32),
            pltpu.VMEM((count, width), bf16),
            pltpu.VMEM((rows, width), bf16),
            pltpu.VMEM((rows, width), bf16),
            pltpu.VMEM((count, 8), f32),
            pltpu.VMEM((count, 128), f32),
            pltpu.VMEM((3, 8, rows), f32),
            pltpu.VMEM((2,) + packed, bf16),
            pltpu.VMEM((2,) + packed, bf16),
            pltpu.VMEM((2, width, width), bf16),
            pltpu.VMEM((4, width // 2, width), bf16),
            pltpu.VMEM((4, width // 4, width), bf16),
            pltpu.VMEM((4, width // 8, width), bf16),
            pltpu.VMEM((4, planes - 1, width // 16, half), bf16),
            pltpu.VMEM((4, width // 16, half), bf16),
            pltpu.VMEM((10, 16, width), f32),
            pltpu.VMEM((2, count, 128), f32),
            dma((copies,)),
            dma((copies,)),
            dma((8,)),
        ],
        compiler_params=pltpu.CompilerParams(
            collective_id=1, has_side_effects=True, vmem_limit_bytes=VMEM_LIMIT
        ),
    )(
        lengths[0],
        tokens,
        row(gains),
        projection,
        mixing,
        row(factors),
        row(biases),
        jnp.pad(centroids, ((0, -centroids.shape[0] % 8), (0, 0))),
        route,
        cotangent,
        flipped,
        joint,
        mixed,
        logs,
        residual,
        place,
        loads,
        dots,
        back,
        made,
        near,
        far,
    )


TILE = 256
ALIGN = 16


def aligned_rows(count, experts):
    return -(-(count + experts * (ALIGN - 1)) // ALIGN) * ALIGN


def gelu_pair(values):
    bell = jnp.exp2(values * values * (-0.5 * HALF_LOG))
    near = 1.0 / (1.0 + (0.3275911 * 0.7071067811865476) * jnp.abs(values))
    series = 1.061405429 * 0.5 * near - 1.453152027 * 0.5
    series = series * near + 1.421413741 * 0.5
    series = series * near - 0.284496736 * 0.5
    series = series * near + 0.254829592 * 0.5
    tail = series * near * bell
    below = jnp.where(values >= 0.0, 1.0 - tail, tail)
    return values * below, below + values * bell * 0.3989422804014327


def expert_kernel_body(
    experts,
    sources,
    rows,
    limit,
    width,
    hidden,
    meta_ref,
    *refs,
):
    sent_own, sent_others, cot_own, cot_others, gate_own, gate_others = refs[:6]
    up_near, up_far, down_near, down_far = refs[6:10]
    refs = refs[10:]
    sent_refs = [sent_own] + [sent_others.at[s] for s in range(sources - 1)]
    cot_refs = [cot_own] + [cot_others.at[s] for s in range(sources - 1)]
    gate_refs = [gate_own] + [gate_others.at[s] for s in range(sources - 1)]
    back_all, made_all, dots_all, near_out, far_out = refs[:5]
    back_outs = [back_all.at[s] for s in range(sources)]
    made_outs = [made_all.at[s] for s in range(sources)]
    dot_outs = [dots_all.at[s] for s in range(sources)]
    (x_ref, c_ref, g_ref, column_ref, up_ref, down_ref, gu_ref, gd_ref, pack_ref, zero_ref) = refs[5:15]
    weight_sem, row_sem, out_sem, grad_sem, zero_sem = refs[15:]
    half = hidden // 2
    own = meta_ref[0]

    def size_of(s, e):
        return meta_ref[1 + s * experts + e]

    source_at, joined_at, tiles = {}, {}, []
    first = []
    base = 0
    for s in range(sources):
        at = 0
        for e in range(experts):
            source_at[s, e] = at
            at = at + size_of(s, e)
        source_at[s, experts] = at
    for e in range(experts):
        first.append(base)
        at = base
        for s in range(sources):
            joined_at[s, e] = at
            at = at + size_of(s, e)
        number = (at - base + (TILE - 1)) // TILE
        tiles.append(number)
        base = base + number * TILE

    bits = [1 << b for b in range(limit.bit_length()) if ALIGN <= (1 << b)]

    def pieces(s, e):
        size = size_of(s, e)
        for i, piece in enumerate(bits):
            yield i, piece, (size & piece) != 0, size & (piece - 1)

    def move_in(s, e, act):
        for i, piece, taken, offset in pieces(s, e):
            @pl.when(taken)
            def _(i=i, piece=piece, offset=offset):
                src = pl.ds(pl.multiple_of(source_at[s, e] + offset, ALIGN), piece)
                dst = pl.ds(pl.multiple_of(joined_at[s, e] + offset, ALIGN), piece)
                k = s * experts + e
                act(pltpu.make_async_copy(sent_refs[s].at[src], x_ref.at[dst], row_sem.at[0, k, i]))
                act(pltpu.make_async_copy(cot_refs[s].at[src], c_ref.at[dst], row_sem.at[1, k, i]))

    def move_out(s, e, act):
        for i, piece, taken, offset in pieces(s, e):
            @pl.when(taken)
            def _(i=i, piece=piece, offset=offset):
                src = pl.ds(pl.multiple_of(source_at[s, e] + offset, ALIGN), piece)
                dst = pl.ds(pl.multiple_of(joined_at[s, e] + offset, ALIGN), piece)
                k = s * experts + e
                act(pltpu.make_async_copy(x_ref.at[dst], made_outs[s].at[src], out_sem.at[0, k, i]))
                act(pltpu.make_async_copy(c_ref.at[dst], back_outs[s].at[src], out_sem.at[1, k, i]))

    def move_weights(e, act):
        slot = e - own + experts - 1
        for j, (ups, downs) in enumerate(((up_near, down_near), (up_far, down_far))):
            part = pl.ds(j * half, half)
            act(pltpu.make_async_copy(ups.at[slot], up_ref.at[e, :, part], weight_sem.at[e, j, 0]))
            act(pltpu.make_async_copy(downs.at[slot], down_ref.at[e, part], weight_sem.at[e, j, 1]))

    zero_ref[...] = jnp.zeros_like(zero_ref)
    for e in range(experts):
        @pl.when(tiles[e] > 0)
        def _(e=e):
            last = pl.ds(pl.multiple_of(first[e] + (tiles[e] - 1) * TILE, TILE), TILE)
            x_ref[last, :] = jnp.zeros((TILE, width), jnp.bfloat16)
            c_ref[last, :] = jnp.zeros((TILE, width), jnp.bfloat16)
            g_ref[last, :] = jnp.zeros((TILE, 128), jnp.float32)

    for e in range(experts):
        move_weights(e, lambda copy: copy.start())
        for s in range(sources):
            move_in(s, e, lambda copy: copy.start())

    tail_chunks = rows // ALIGN

    def tail(s, act):
        def one(i, _):
            @pl.when(i * ALIGN >= source_at[s, experts])
            def _():
                dst = pl.ds(pl.multiple_of(i * ALIGN, ALIGN), ALIGN)
                act(pltpu.make_async_copy(zero_ref, made_outs[s].at[dst], zero_sem.at[0, s, i]))
                act(pltpu.make_async_copy(zero_ref, back_outs[s].at[dst], zero_sem.at[1, s, i]))
            return 0
        lax.fori_loop(tail_chunks - 5, tail_chunks, one, 0)

    for s in range(sources):
        tail(s, lambda copy: copy.start())

    for s in range(sources):
        column_ref[...] = jnp.broadcast_to(
            jnp.transpose(jnp.broadcast_to(gate_refs[s][0:1, :], (128, rows)))[:, 0:128], (rows, 128)
        )
        for e in range(experts):
            def one(i, _, s=s, e=e):
                src = pl.ds(pl.multiple_of(source_at[s, e] + i * ALIGN, ALIGN), ALIGN)
                dst = pl.ds(pl.multiple_of(joined_at[s, e] + i * ALIGN, ALIGN), ALIGN)
                g_ref[dst, :] = column_ref[src, :]
                return 0
            lax.fori_loop(0, size_of(s, e) // ALIGN, one, 0)

    for e in range(experts):
        move_weights(e, lambda copy: copy.wait())
        for s in range(sources):
            move_in(s, e, lambda copy: copy.wait())
        gu_ref[...] = jnp.zeros_like(gu_ref)
        gd_ref[...] = jnp.zeros_like(gd_ref)

        def tile(t, _, e=e):
            at = pl.ds(pl.multiple_of(first[e] + t * TILE, TILE), TILE)
            x, c, gate = x_ref[at, :], c_ref[at, :], g_ref[at, 0:1]
            before = jnp.dot(x, up_ref[e], preferred_element_type=jnp.float32)
            active, slope = gelu_pair(before)
            through = lax.dot_general(c, down_ref[e], NT, preferred_element_type=jnp.float32)
            grad = (through * (slope * gate)).astype(jnp.bfloat16)
            gated = (active * gate).astype(jnp.bfloat16)
            made = jnp.dot(active.astype(jnp.bfloat16), down_ref[e], preferred_element_type=jnp.float32)
            g_ref[at, :] = jnp.broadcast_to(
                jnp.sum(made * c.astype(jnp.float32), axis=1, keepdims=True), (TILE, 128)
            )
            gd_ref[...] += lax.dot_general(gated, c, TN, preferred_element_type=jnp.float32)
            gu_ref[...] += lax.dot_general(x, grad, TN, preferred_element_type=jnp.float32)
            back = lax.dot_general(grad, up_ref[e], NT, preferred_element_type=jnp.float32)
            x_ref[at, :] = made.astype(jnp.bfloat16)
            c_ref[at, :] = back.astype(jnp.bfloat16)
            return 0

        lax.fori_loop(0, tiles[e], tile, 0)
        for s in range(sources):
            move_out(s, e, lambda copy: copy.start())

        slot = e % 2
        grads = lambda e, slot: [
            pltpu.make_async_copy(pack_ref.at[slot, j], ref.at[e], grad_sem.at[slot, j])
            for j, ref in enumerate((near_out, far_out))
        ]
        if e >= 2:
            for copy in grads(e - 2, slot):
                copy.wait()
        for j in range(2):
            pack_ref[slot, j, 0:width, :] = gu_ref[:, j * half : (j + 1) * half].astype(jnp.bfloat16)
            for part in range(2):
                pack_ref[slot, j, width + part * half : width + (part + 1) * half, :] = gd_ref[
                    j * half : (j + 1) * half, part * half : (part + 1) * half
                ].astype(jnp.bfloat16)
        for copy in grads(e, slot):
            copy.start()

    for s in range(sources):
        for e in range(experts):
            def one(i, _, s=s, e=e):
                src = pl.ds(pl.multiple_of(source_at[s, e] + i * ALIGN, ALIGN), ALIGN)
                dst = pl.ds(pl.multiple_of(joined_at[s, e] + i * ALIGN, ALIGN), ALIGN)
                column_ref[src, :] = g_ref[dst, :]
                return 0
            lax.fori_loop(0, size_of(s, e) // ALIGN, one, 0)
        dot_outs[s][...] = jnp.transpose(column_ref[...])[0:8, :]

    for e in range(experts):
        for s in range(sources):
            move_out(s, e, lambda copy: copy.wait())
    for s in range(sources):
        tail(s, lambda copy: copy.wait())
    for e in range(max(0, experts - 2), experts):
        for copy in grads(e, e % 2):
            copy.wait()


def expert_stage(meta, sent, cot, gates, weights, experts, limit):
    rows, width = sent[0].shape
    sources = 1 + sent[1].shape[0]
    half = weights[0].shape[2]
    hidden = 2 * half
    joined = -(-(sources * rows + experts * (TILE - 1)) // TILE) * TILE
    limit = -(-limit // ALIGN) * ALIGN
    pieces = limit.bit_length() - ALIGN.bit_length() + 1
    anywhere = pl.BlockSpec(memory_space=pl.ANY)
    local = pl.BlockSpec(memory_space=pltpu.VMEM)
    slots = 2 * experts - 1
    dma = pltpu.SemaphoreType.DMA
    packed = (width + hidden, half)
    return pl.pallas_call(
        partial(expert_kernel_body, experts, sources, rows, limit, width, hidden),
        out_shape=(
            jax.ShapeDtypeStruct((sources, rows, width), jnp.bfloat16),
            jax.ShapeDtypeStruct((sources, rows, width), jnp.bfloat16),
            jax.ShapeDtypeStruct((sources, 8, rows), jnp.float32),
            jax.ShapeDtypeStruct((experts,) + packed, jnp.bfloat16),
            jax.ShapeDtypeStruct((experts,) + packed, jnp.bfloat16),
        ),
        in_specs=[pl.BlockSpec(memory_space=pltpu.SMEM)]
        + [anywhere] * 4
        + [local] * 2
        + [anywhere] * 4,
        out_specs=(anywhere, anywhere, local, anywhere, anywhere),
        scratch_shapes=[
            pltpu.VMEM((joined, width), jnp.bfloat16),
            pltpu.VMEM((joined, width), jnp.bfloat16),
            pltpu.VMEM((joined, 128), jnp.float32),
            pltpu.VMEM((rows, 128), jnp.float32),
            pltpu.VMEM((experts, width, hidden), jnp.bfloat16),
            pltpu.VMEM((experts, hidden, width), jnp.bfloat16),
            pltpu.VMEM((width, hidden), jnp.float32),
            pltpu.VMEM((hidden, width), jnp.float32),
            pltpu.VMEM((2, 2) + packed, jnp.bfloat16),
            pltpu.VMEM((ALIGN, width), jnp.bfloat16),
            dma((experts, 2, 2)),
            dma((2, sources * experts, pieces)),
            dma((2, sources * experts, pieces)),
            dma((2, 2)),
            dma((2, sources, rows // ALIGN)),
        ],
        compiler_params=pltpu.CompilerParams(vmem_limit_bytes=VMEM_LIMIT),
        cost_estimate=pl.CostEstimate(
            flops=12 * sources * rows * width * hidden, bytes_accessed=100_000_000, transcendentals=sources * rows * hidden
        ),
    )(meta, *sent, *cot, *gates, *weights)


def per_device(
    tokens,
    gains,
    shifts,
    projection,
    mixing,
    factors,
    biases,
    centroids,
    expanding,
    contracting,
    routes,
    lengths,
    cotangent,
):
    count, width = tokens.shape
    experts = centroids.shape[0]
    groups = lax.axis_size("expert")
    slabs = groups // experts
    limit = 2 * count // experts
    total_tokens = count * groups * lax.axis_size("tensor")

    flipped, joint, mixed, logs, residual, place, loads, sent_own, cot_own, gate_own, sent_others, cot_others, gate_others, *weights = front_stage(
        tokens, gains, shifts, projection, mixing, factors, biases, centroids, expanding, contracting, routes, lengths, cotangent, experts, slabs
    )
    sizes = jnp.concatenate((gate_own[1:2, :experts], gate_others[:, 1, :experts]), axis=0)
    meta = jnp.concatenate(
        [lax.div(lax.axis_index("expert"), slabs)[None], sizes.reshape(-1).astype(jnp.int32)]
    )
    back, made, dots, near, far = expert_stage(
        meta, (sent_own, sent_others), (cot_own, cot_others), (gate_own, gate_others), weights, experts, limit
    )
    layer_output, token_grad, vectors, up_grad, down_grad, shared, *_ = rear_stage(
        tokens, gains, projection, mixing, factors, biases, centroids, routes, lengths, cotangent,
        flipped, joint, mixed, logs, residual, place, loads, dots, back, made, near, far, experts, slabs, total_tokens,
    )
    mixing_grad = shared[0].astype(jnp.float32)
    projection_grad = (
        shared[1:].reshape(3, width, 3, width // 3).transpose(1, 2, 0, 3).reshape(width, 3 * width).astype(jnp.float32)
    )
    return (
        layer_output,
        vectors[4, 0],
        token_grad,
        vectors[0],
        vectors[1],
        projection_grad,
        mixing_grad,
        vectors[2],
        vectors[3],
        vectors[8 : 8 + experts],
        up_grad[None],
        down_grad[None],
    )


def solution(mesh):
    placed = (
        P(("expert", "tensor"), None),
        P(),
        P(),
        P(),
        P(),
        P(),
        P(),
        P(),
        P("expert", None, "tensor"),
        P("expert", "tensor", None),
        P(("expert", "tensor"), None),
        P(("expert", "tensor"), None),
        P(("expert", "tensor"), None),
    )
    near = mesh.shape["expert"] == 16 and mesh.shape["tensor"] == 2
    return jax.shard_map(
        per_device if near else moving_tokens,
        mesh=mesh,
        in_specs=placed,
        out_specs=(
            P(("expert", "tensor"), None),
            P(),
            P(("expert", "tensor"), None),
            P(),
            P(),
            P(),
            P(),
            P(),
            P(),
            P(),
            P("expert", None, "tensor"),
            P("expert", "tensor", None),
        ),
        check_vma=False,
    )
```

```python
from functools import partial

import jax
import jax.numpy as jnp
from jax import lax
from jax.experimental import pallas as pl
from jax.experimental.pallas import tpu as pltpu
from jax.sharding import PartitionSpec as P

HEADS = 12


highest = lax.Precision.HIGHEST
epsilon = 1e-05


def running(values):
    places = jnp.arange(values.shape[0])
    return jnp.sum(jnp.where(places[:, None] >= places[None, :], values[None, :], 0), axis=1)


def earlier(picks):
    places = jnp.arange(picks.shape[0])
    before = (places[:, None] > places[None, :]).astype(jnp.bfloat16)
    return jnp.dot(
        before, picks.astype(jnp.bfloat16), preferred_element_type=jnp.float32
    ).astype(jnp.int32)


def norm_parts(values, gain, shift):
    centered = values - jnp.mean(values, axis=1, keepdims=True)
    scale = lax.rsqrt(jnp.mean(centered * centered, axis=1, keepdims=True) + epsilon)
    normal = centered * scale
    return (normal * gain + shift, normal, scale)


def norm_back(upstream, normal, scale, gain):
    scaled = upstream * gain
    inner = (
        scaled
        - jnp.mean(scaled, axis=1, keepdims=True)
        - normal * jnp.mean(scaled * normal, axis=1, keepdims=True)
    )
    return (inner * scale, jnp.sum(upstream * normal, axis=0), jnp.sum(upstream, axis=0))


def gelu_slope(values):
    return (
        0.5 * (1.0 + lax.erf(values * 0.7071067811865476))
        + values * jnp.exp(-0.5 * values * values) * 0.3989422804014327
    )


def expert_forward(gathered, upward, downward):
    before = jnp.dot(gathered, upward, preferred_element_type=jnp.float32)
    active = jax.nn.gelu(before, approximate=False).astype(jnp.bfloat16)
    return jnp.dot(active, downward, preferred_element_type=jnp.float32)


def expert_backward(gathered, incoming, upward, downward):
    before = jnp.dot(gathered, upward, preferred_element_type=jnp.float32)
    active = jax.nn.gelu(before, approximate=False).astype(jnp.bfloat16)
    down_grad = jnp.einsum("rf,rd->fd", active, incoming, preferred_element_type=jnp.float32)
    through = jnp.einsum("rd,fd->rf", incoming, downward, preferred_element_type=jnp.float32)
    hidden_grad = (through * gelu_slope(before)).astype(jnp.bfloat16)
    up_grad = jnp.einsum("rd,rf->df", gathered, hidden_grad, preferred_element_type=jnp.float32)
    return (up_grad, down_grad, hidden_grad)


def head_forward(allowed, item):
    query, keys, values = item
    factor = query.shape[1] ** (-0.5)
    scores = jnp.einsum("qd,kd->qk", query, keys, preferred_element_type=jnp.float32) * factor
    scores = jnp.where(allowed, scores, -1000000000.0)
    peak = jnp.max(scores, axis=1, keepdims=True)
    weights = jnp.exp(scores - peak)
    total = jnp.sum(weights, axis=1, keepdims=True)
    mixed = jnp.dot(
        (weights / total).astype(jnp.bfloat16), values, preferred_element_type=jnp.float32
    )
    return (mixed.astype(jnp.bfloat16), (peak + jnp.log(total))[:, 0])


def head_backward(allowed, item):
    query, keys, values, upstream, log_total = item
    factor = query.shape[1] ** (-0.5)
    scores = jnp.einsum("qd,kd->qk", query, keys, preferred_element_type=jnp.float32) * factor
    scores = jnp.where(allowed, scores, -1000000000.0)
    probs = jnp.exp(scores - log_total[:, None])
    value_grad = jnp.einsum(
        "qk,qd->kd", probs.astype(jnp.bfloat16), upstream, preferred_element_type=jnp.float32
    )
    prob_grad = jnp.einsum("qd,kd->qk", upstream, values, preferred_element_type=jnp.float32)
    inner = jnp.sum(prob_grad * probs, axis=1, keepdims=True)
    score_grad = (probs * (prob_grad - inner)).astype(jnp.bfloat16)
    query_grad = (
        jnp.einsum("qk,kd->qd", score_grad, keys, preferred_element_type=jnp.float32) * factor
    )
    key_grad = (
        jnp.einsum("qk,qd->kd", score_grad, query, preferred_element_type=jnp.float32) * factor
    )
    return (query_grad, key_grad, value_grad)


def moving_tokens(
    tokens,
    gains,
    shifts,
    projection,
    mixing,
    factors,
    biases,
    centroids,
    expanding,
    contracting,
    routes,
    lengths,
    cotangent,
):
    count, width = tokens.shape
    experts = centroids.shape[0]
    groups = lax.axis_size("expert")
    slab_count = groups // experts
    capacity = max(2, 2 * count // experts)
    total_tokens = count * groups * lax.axis_size("tensor")
    average = total_tokens / experts
    route = routes[:, 0]
    picks = route[:, None] == jnp.arange(experts, dtype=jnp.int32)[None, :]
    picks_int = picks.astype(jnp.int32)
    picks_float = picks.astype(jnp.float32)
    loads = lax.psum(jnp.sum(picks_float, axis=0), ("expert", "tensor"))
    spread = (loads - average) / average
    token_spread = jnp.sum(jnp.where(picks, spread[None, :], 0.0), axis=1)
    ranks = jnp.sum(earlier(picks) * picks_int, axis=1)
    slots = route * capacity + ranks
    places = jnp.arange(count, dtype=jnp.int32)
    documents = jnp.sum(
        (places[:, None] >= running(lengths[0])[None, :]).astype(jnp.int32), axis=1
    )
    allowed = (places[:, None] >= places[None, :]) & (documents[:, None] == documents[None, :])
    inputs = tokens.astype(jnp.float32)
    entry, entry_normal, entry_scale = norm_parts(inputs, gains, shifts)
    entry = entry.astype(jnp.bfloat16)
    joint = jnp.dot(entry, projection, preferred_element_type=jnp.float32).astype(jnp.bfloat16)
    heads = joint.reshape(count, 3, HEADS, width // HEADS).transpose(1, 2, 0, 3)
    mixed, log_total = lax.map(partial(head_forward, allowed), (heads[0], heads[1], heads[2]))
    mixed_rows = mixed.transpose(1, 0, 2).reshape(count, width)
    residual = inputs + jnp.dot(mixed_rows, mixing, preferred_element_type=jnp.float32)
    normed, mixer_normal, mixer_scale = norm_parts(residual, factors, biases)
    chosen = jnp.dot(picks.astype(jnp.bfloat16), centroids, preferred_element_type=jnp.float32)
    gates = jax.nn.sigmoid(jnp.sum(normed * chosen, axis=1))
    outgoing = (
        jnp.zeros((experts * capacity, width), jnp.bfloat16)
        .at[slots]
        .set(normed.astype(jnp.bfloat16))
    )
    copies = jnp.broadcast_to(
        outgoing.reshape(experts, 1, capacity, width), (experts, slab_count, capacity, width)
    ).reshape(groups, capacity, width)
    arrived = lax.all_to_all(copies, "expert", split_axis=0, concat_axis=0, tiled=True)
    sources = groups * capacity
    own_rows = arrived.reshape(sources, width)
    gathered = lax.all_gather(own_rows, "tensor", axis=0, tiled=True)
    produced = lax.psum_scatter(
        expert_forward(gathered, expanding[0], contracting[0]).astype(jnp.bfloat16),
        "tensor",
        scatter_dimension=0,
        tiled=True,
    )
    returned = lax.all_to_all(
        produced.reshape(arrived.shape), "expert", split_axis=0, concat_axis=0, tiled=True
    )
    combined = jnp.sum(
        returned.reshape(experts, slab_count, capacity, width).astype(jnp.float32), axis=1
    ).reshape(experts * capacity, width)
    picked = combined[slots]
    layer_output = (residual + gates[:, None] * picked).astype(jnp.bfloat16)
    balance_part = jnp.sum(token_spread * gates) / total_tokens
    upstream = cotangent.astype(jnp.float32)
    gate_grad = jnp.sum(upstream * picked, axis=1)
    logit_grad = (gate_grad + token_spread / total_tokens) * gates * (1.0 - gates)
    scaled_rows = (gates[:, None] * upstream).astype(jnp.bfloat16)
    grad_slots = jnp.zeros((experts * capacity, width), jnp.bfloat16).at[slots].set(scaled_rows)
    grad_copies = jnp.broadcast_to(
        grad_slots.reshape(experts, 1, capacity, width), (experts, slab_count, capacity, width)
    ).reshape(groups, capacity, width)
    incoming = lax.all_to_all(
        grad_copies, "expert", split_axis=0, concat_axis=0, tiled=True
    ).reshape(sources, width)
    incoming_pair = lax.all_gather(incoming, "tensor", axis=0, tiled=True)
    up_share, down_share, hidden_grad = expert_backward(
        gathered, incoming_pair, expanding[0], contracting[0]
    )
    back_rows = lax.psum_scatter(
        jnp.einsum(
            "rf,df->rd", hidden_grad, expanding[0], preferred_element_type=jnp.float32
        ).astype(jnp.bfloat16),
        "tensor",
        scatter_dimension=0,
        tiled=True,
    )
    back = lax.all_to_all(
        back_rows.reshape(arrived.shape), "expert", split_axis=0, concat_axis=0, tiled=True
    )
    back_sum = jnp.sum(
        back.reshape(experts, slab_count, capacity, width).astype(jnp.float32), axis=1
    ).reshape(experts * capacity, width)
    normed_grad = back_sum[slots] + logit_grad[:, None] * chosen
    centroid_grad = jnp.einsum(
        "te,td->ed", picks_float, logit_grad[:, None] * normed, precision=highest
    )
    mixer_back, factor_grad, bias_grad = norm_back(normed_grad, mixer_normal, mixer_scale, factors)
    residual_grad = upstream + mixer_back
    branch_grad = residual_grad.astype(jnp.bfloat16)
    mixing_grad = jnp.einsum(
        "td,te->de", mixed_rows, branch_grad, preferred_element_type=jnp.float32
    )
    mixed_grad = jnp.einsum(
        "te,de->td", branch_grad, mixing, preferred_element_type=jnp.float32
    ).astype(jnp.bfloat16)
    head_grads = mixed_grad.reshape(count, HEADS, width // HEADS).transpose(1, 0, 2)
    query_grad, key_grad, value_grad = lax.map(
        partial(head_backward, allowed), (heads[0], heads[1], heads[2], head_grads, log_total)
    )
    joint_grad = (
        jnp.stack((query_grad, key_grad, value_grad))
        .transpose(2, 0, 1, 3)
        .reshape(count, 3 * width)
        .astype(jnp.bfloat16)
    )
    projection_grad = jnp.einsum("td,te->de", entry, joint_grad, preferred_element_type=jnp.float32)
    entry_back = jnp.einsum("te,de->td", joint_grad, projection, preferred_element_type=jnp.float32)
    entry_input, gain_grad, shift_grad = norm_back(entry_back, entry_normal, entry_scale, gains)
    token_grad = residual_grad + entry_input
    summed = lax.psum(
        (
            gain_grad,
            shift_grad,
            projection_grad,
            mixing_grad,
            factor_grad,
            bias_grad,
            centroid_grad,
            balance_part,
        ),
        ("expert", "tensor"),
    )
    return (
        layer_output,
        summed[7],
        token_grad,
        summed[0],
        summed[1],
        summed[2],
        summed[3],
        summed[4],
        summed[5],
        summed[6],
        up_share[None],
        down_share[None],
    )


HALF_LOG = 1.4426950408889634
LN2 = 0.6931471805599453
NT = (((1,), (1,)), ((), ()))
TN = (((0,), (0,)), ((), ()))
VMEM_LIMIT = 60 * 1024 * 1024


def query_blocks(count):
    step = 256 if count > 256 else count
    return [(i, min(i + step, count)) for i in range(0, count, step)]


def document_starts(lengths_ref, places):
    starts = jnp.zeros_like(places)
    end = 0
    for d in range(lengths_ref.shape[0]):
        end = end + lengths_ref[d]
        starts = jnp.where(places >= end, end, starts)
    return starts


MESH = pl.DeviceIdType.MESH


def neighbours(slabs):
    me, core = lax.axis_index("expert"), lax.axis_index("tensor")
    plane = lax.div(me, slabs)
    x = lax.rem(me, 2)
    y = lax.rem(lax.div(me, 2), 2)
    return me, core, plane, (me + 1 - 2 * x, core), (me + 2 - 4 * y, core), (me, 1 - core)


def greet(partners):
    barrier = pltpu.get_barrier_semaphore()
    number = 0
    for device, there in partners:
        @pl.when(there)
        def _(device=device):
            pl.semaphore_signal(barrier, inc=1, device_id=device, device_id_type=MESH)
        number = number + there.astype(jnp.int32)
    pl.semaphore_wait(barrier, number)


def score_bias(bias_ref, lengths_ref, count):
    places = lax.broadcasted_iota(jnp.int32, (1, count), 1)
    starts = document_starts(lengths_ref, places)
    for s, e in query_blocks(count):
        row = lax.broadcasted_iota(jnp.int32, (e - s, count), 0) + s
        seen = (row <= places) & (row >= starts)
        bias_ref[s:e, :] = jnp.where(seen, 0.0, -1e9)


def row_norm(values, gain, shift):
    centered = values - jnp.mean(values, axis=1, keepdims=True)
    scale = lax.rsqrt(jnp.mean(centered * centered, axis=1, keepdims=True) + epsilon)
    normal = centered * scale
    return normal * gain + shift, normal, scale


def chosen_rows(route, centroids_ref, experts):
    chosen = jnp.zeros((route.shape[0], centroids_ref.shape[1]), jnp.float32)
    for e in range(experts):
        chosen = jnp.where(route == e, centroids_ref[e : e + 1, :].astype(jnp.float32), chosen)
    return chosen


def front_kernel(
    planes,
    slabs,
    lengths_ref,
    tokens_ref,
    gains_ref,
    shifts_ref,
    projection_ref,
    mixing_ref,
    factors_ref,
    biases_ref,
    centroids_ref,
    route_row_ref,
    route_ref,
    cot_ref,
    up_ref,
    down_ref,
    flipped_ref,
    joint_ref,
    mixed_ref,
    logs_ref,
    residual_ref,
    place_ref,
    loads_ref,
    sent_own,
    cot_own,
    gate_own,
    sent_others,
    cot_others,
    gate_others,
    up_near,
    up_far,
    down_near,
    down_far,
    bias_ref,
    order_ref,
    normed_ref,
    entry_ref,
    tally_ref,
    send_sem,
    recv_sem,
    local_sem,
):
    count, width = tokens_ref.shape
    experts = planes
    rows = sent_own.shape[0]
    half_rows = rows // 2
    pairs = width // 128
    factor = (width // HEADS) ** (-0.5) * HALF_LOG
    middle = planes - 1
    me, core, plane, beside_x, beside_y, beside_core = neighbours(slabs)
    hop_two = lax.rem(plane + 2, planes)
    hop_one = plane + 1 - 2 * lax.rem(plane, 2)
    here = lax.rem(me, slabs)
    always = plane >= 0
    greet(
        [
            (beside_x, always),
            (beside_y, always),
            (beside_core, always),
            ((hop_two * slabs + here, core), always),
            ((me + slabs, core), plane < planes - 1),
            ((me - slabs, core), plane > 0),
        ]
    )

    def remote(i, src, dst, device):
        return pltpu.make_async_remote_copy(
            src_ref=src, dst_ref=dst, send_sem=send_sem.at[i], recv_sem=recv_sem.at[i], device_id=device, device_id_type=MESH
        )

    owns, nears, fars = (up_ref, down_ref), (up_near, down_near), (up_far, down_far)
    stride = 2 * (planes - 1) + 2 * planes - 1

    def hop(kind, sign, r):
        src = owns[kind].at[0] if r == 1 else nears[kind].at[middle - sign * (r - 1)]
        i = kind * stride + (r - 1) * 2 + (sign > 0)
        return remote(i, src, nears[kind].at[middle - sign * r], (me + sign * slabs, core))

    def hop_sent(sign, r):
        ahead = plane if sign > 0 else planes - 1 - plane
        return (ahead >= r - 1) & (ahead < planes - 1)

    def hop_came(sign, r):
        ahead = plane if sign > 0 else planes - 1 - plane
        return ahead >= r

    def aside(kind, slot):
        src = owns[kind].at[0] if slot == middle else nears[kind].at[slot]
        i = kind * stride + 2 * (planes - 1) + slot
        return remote(i, src, fars[kind].at[slot], beside_x)

    def held(slot):
        at = plane + slot - middle
        return (at >= 0) & (at < planes)

    def own_weights(kind):
        return pltpu.make_async_copy(owns[kind].at[0], nears[kind].at[middle], local_sem.at[kind])

    for kind in range(2):
        for sign in (1, -1):
            @pl.when(hop_sent(sign, 1))
            def _(kind=kind, sign=sign):
                hop(kind, sign, 1).start()
        aside(kind, middle).start()
        own_weights(kind).start()

    def forward_weights(kind, r):
        for sign in (1, -1):
            slot = middle - sign * r

            @pl.when(hop_came(sign, r))
            def _(sign=sign, slot=slot):
                hop(kind, sign, r).wait_recv()
                aside(kind, slot).start()

            if r < planes - 1:
                @pl.when(hop_sent(sign, r + 1))
                def _(sign=sign):
                    hop(kind, sign, r + 1).start()

    base = 2 * stride

    def row_copy(which, part, piece):
        own, others = ((cot_own, cot_others), (sent_own, sent_others))[which]
        at = pl.ds(piece * half_rows, half_rows)
        i = base + which * 6 + part * 2 + piece
        if part == 0:
            return remote(i, own.at[at], others.at[1, at], beside_y)
        if part == 1:
            return remote(i, own.at[at], others.at[0, at], beside_core)
        return remote(i, others.at[1, at], others.at[2, at], beside_core)

    def gate_copy(part):
        i = base + 12 + part
        if part == 0:
            return remote(i, gate_own, gate_others.at[1], beside_y)
        if part == 1:
            return remote(i, gate_own, gate_others.at[0], beside_core)
        return remote(i, gate_others.at[1], gate_others.at[2], beside_core)

    rounds = [beside_core, beside_x, beside_y, (hop_one * slabs + here, core), (hop_two * slabs + here, core)]

    def tally(k):
        return remote(base + 15 + k, tally_ref.at[2 * k], tally_ref.at[2 * k + 1], rounds[k])

    def tally_step(k):
        tally(k).wait_recv()
        total = tally_ref[2 * k] + tally_ref[2 * k + 1]
        if k + 1 < len(rounds):
            tally_ref[2 * k + 2] = total
            tally(k + 1).start()
        else:
            loads_ref[...] = total

    number = lax.broadcasted_iota(jnp.int32, (8, count), 0)
    picks = jnp.where(number == route_row_ref[...], 1.0, 0.0)
    chunk = 128
    for s in range(0, count, chunk):
        row = lax.broadcasted_iota(jnp.int32, (chunk, count), 0) + s
        column = lax.broadcasted_iota(jnp.int32, (chunk, count), 1)
        order_ref[s : s + chunk, :] = jnp.where(row < column, 1.0, 0.0).astype(jnp.bfloat16)
    ranks = jnp.dot(picks.astype(jnp.bfloat16), order_ref[0:count, :], preferred_element_type=jnp.float32)
    counts = jnp.sum(picks, axis=1, keepdims=True)
    padded = jnp.ceil(counts * (1.0 / ALIGN)) * ALIGN
    place = jnp.zeros((1, count), jnp.float32)
    start = jnp.zeros((1, 1), jnp.float32)
    for e in range(experts):
        place = place + picks[e : e + 1, :] * (ranks[e : e + 1, :] + start)
        start = start + padded[e : e + 1, :]
    place_ref[...] = jnp.broadcast_to(place, (8, count))
    tally_ref[0] = jnp.broadcast_to(counts, (8, 128))
    tally(0).start()
    for s in range(0, rows, 64):
        row = lax.broadcasted_iota(jnp.int32, (64, count), 0) + s
        order_ref[s : s + 64, :] = jnp.where(row.astype(jnp.float32) == place, 1.0, 0.0).astype(jnp.bfloat16)

    def sort_rows(source_ref, to_ref, which):
        for piece in range(2):
            at = slice(piece * half_rows, (piece + 1) * half_rows)
            to_ref[at, :] = jnp.dot(
                order_ref[at, :], source_ref[...], preferred_element_type=jnp.float32
            ).astype(jnp.bfloat16)
            row_copy(which, 0, piece).start()
            row_copy(which, 1, piece).start()

    sort_rows(cot_ref, cot_own, 0)

    def project(i, _):
        at = pl.ds(pl.multiple_of(i * 192, 192), 192)
        entry, _, _ = row_norm(tokens_ref[at, :].astype(jnp.float32), gains_ref[...], shifts_ref[...])
        entry = entry.astype(jnp.bfloat16)
        entry_ref[at, :] = entry
        joint_ref[at, :] = jnp.dot(entry, projection_ref[...], preferred_element_type=jnp.float32).astype(jnp.bfloat16)
        return 0

    lax.fori_loop(0, count // 192, project, 0)
    score_bias(bias_ref, lengths_ref, count)
    forward_weights(0, 1)
    tally_step(0)

    first = lax.broadcasted_iota(jnp.int32, (1, 128), 1) < 64

    def attend(p, _):
        lanes = pl.ds(pl.multiple_of(p * 128, 128), 128)
        keys = pl.ds(pl.multiple_of(width + p * 128, 128), 128)
        values = pl.ds(pl.multiple_of(2 * width + p * 128, 128), 128)
        for s, e in query_blocks(count):
            outs = []
            for half in range(2):
                q = jnp.where(first == (half == 0), joint_ref[s:e, lanes], jnp.bfloat16(0))
                scores = lax.dot_general(joint_ref[0:e, keys], q, NT, preferred_element_type=jnp.float32)
                scores = scores * factor + bias_ref[0:e, s:e]
                peak = jnp.max(scores, axis=0, keepdims=True)
                weights = jnp.exp2(scores - peak)
                total = jnp.sum(weights, axis=0, keepdims=True)
                probs = (weights * (1.0 / total)).astype(jnp.bfloat16)
                outs.append(
                    lax.dot_general(probs, joint_ref[0:e, values], TN, preferred_element_type=jnp.float32)
                )
                logs_ref[p, half : half + 1, s:e] = peak + jnp.log2(total)
            mixed_ref[s:e, lanes] = jnp.where(first, outs[0], outs[1]).astype(jnp.bfloat16)

        @pl.when(p == 2)
        def _():
            forward_weights(1, 1)
            tally_step(1)

        @pl.when(p == 4)
        def _():
            forward_weights(0, 2)
            tally_step(2)

        return 0

    lax.fori_loop(0, pairs, attend, 0)

    lane = lax.broadcasted_iota(jnp.int32, (1, 128), 1)

    def mix(i, _):
        at = pl.ds(pl.multiple_of(i * 192, 192), 192)
        residual = tokens_ref[at, :].astype(jnp.float32) + jnp.dot(
            mixed_ref[at, :], mixing_ref[...], preferred_element_type=jnp.float32
        )
        residual_ref[at, :] = residual
        normed, _, _ = row_norm(residual, factors_ref[...], biases_ref[...])
        chosen = chosen_rows(route_ref[at, :], centroids_ref, experts)
        gate = 1.0 / (1.0 + jnp.exp(-jnp.sum(normed * chosen, axis=1, keepdims=True)))
        high = gate.astype(jnp.bfloat16).astype(jnp.float32)
        mid = (gate - high).astype(jnp.bfloat16).astype(jnp.float32)
        low = gate - high - mid
        parts = jnp.where(lane == 0, high, jnp.where(lane == 1, mid, jnp.where(lane == 2, low, 0.0)))
        normed_ref[at, 0:width] = normed.astype(jnp.bfloat16)
        normed_ref[at, width : width + 128] = parts.astype(jnp.bfloat16)
        return 0

    lax.fori_loop(0, count // 192, mix, 0)
    for piece in range(2):
        at = slice(piece * half_rows, (piece + 1) * half_rows)
        moved = jnp.dot(order_ref[at, :], normed_ref[...], preferred_element_type=jnp.float32)
        sent_own[at, :] = moved[:, 0:width].astype(jnp.bfloat16)
        row_copy(1, 0, piece).start()
        row_copy(1, 1, piece).start()
        bias_ref[at, 0:128] = jnp.broadcast_to(
            jnp.sum(moved[:, width : width + 128], axis=1, keepdims=True), (half_rows, 128)
        )
    forward_weights(1, 2)
    tally_step(3)
    for piece in range(2):
        row_copy(0, 0, piece).wait_recv()
        row_copy(0, 2, piece).start()
    gates = jnp.transpose(bias_ref[0:rows, 0:128])
    gate_own[0:1, :] = gates[0:1, :]
    gate_own[1:2, :] = jnp.zeros((1, rows), jnp.float32)
    for e in range(8):
        gate_own[1:2, e : e + 1] = padded[e : e + 1, :]
    gate_copy(0).start()
    gate_copy(1).start()
    for s in range(0, count, 384):
        flipped_ref[:, s : s + 384] = jnp.transpose(entry_ref[s : s + 384, :])

    for kind in range(2):
        forward_weights(kind, 3)
    gate_copy(0).wait_recv()
    gate_copy(2).start()
    tally_step(4)
    for piece in range(2):
        row_copy(1, 0, piece).wait_recv()
        row_copy(1, 2, piece).start()

    for which in range(2):
        for part in range(3):
            for piece in range(2):
                copy = row_copy(which, part, piece)
                copy.wait_send()
                if part:
                    copy.wait_recv()
    for part in range(3):
        gate_copy(part).wait_send()
        if part:
            gate_copy(part).wait_recv()
    for k in range(len(rounds)):
        tally(k).wait_send()
    for kind in range(2):
        own_weights(kind).wait()
        for r in range(1, planes):
            for sign in (1, -1):
                @pl.when(hop_sent(sign, r))
                def _(kind=kind, sign=sign, r=r):
                    hop(kind, sign, r).wait_send()
        for slot in range(2 * planes - 1):
            @pl.when(held(slot))
            def _(kind=kind, slot=slot):
                aside(kind, slot).wait()


def front_stage(
    tokens, gains, shifts, projection, mixing, factors, biases, centroids, expanding, contracting, route, lengths, cotangent, planes, slabs
):
    count, width = tokens.shape
    rows = aligned_rows(count, planes)
    pairs = width // 128
    slots = 2 * planes - 1
    bf16, f32 = jnp.bfloat16, jnp.float32
    shape = jax.ShapeDtypeStruct
    anywhere = pl.BlockSpec(memory_space=pl.ANY)
    local = pl.BlockSpec(memory_space=pltpu.VMEM)
    dma = pltpu.SemaphoreType.DMA
    copies = 2 * (2 * (planes - 1) + slots) + 12 + 3 + 5
    outs = [
        (shape((width, count), bf16), local),
        (shape((count, 3 * width), bf16), local),
        (shape((count, width), bf16), local),
        (shape((pairs, 2, count), f32), local),
        (shape((count, width), f32), local),
        (shape((8, count), f32), local),
        (shape((8, 128), f32), local),
        (shape((rows, width), bf16), local),
        (shape((rows, width), bf16), local),
        (shape((8, rows), f32), local),
        (shape((3, rows, width), bf16), anywhere),
        (shape((3, rows, width), bf16), anywhere),
        (shape((3, 8, rows), f32), anywhere),
        (shape((slots,) + expanding.shape[1:], bf16), anywhere),
        (shape((slots,) + expanding.shape[1:], bf16), anywhere),
        (shape((slots,) + contracting.shape[1:], bf16), anywhere),
        (shape((slots,) + contracting.shape[1:], bf16), anywhere),
    ]
    row = lambda v: v.reshape(1, -1)
    return pl.pallas_call(
        partial(front_kernel, planes, slabs),
        out_shape=[o[0] for o in outs],
        in_specs=[pl.BlockSpec(memory_space=pltpu.SMEM)] + [local] * 11 + [anywhere] * 2,
        out_specs=[o[1] for o in outs],
        scratch_shapes=[
            pltpu.VMEM((rows, count), f32),
            pltpu.VMEM((rows, count), bf16),
            pltpu.VMEM((count, width + 128), bf16),
            pltpu.VMEM((count, width), bf16),
            pltpu.VMEM((10, 8, 128), f32),
            dma((copies,)),
            dma((copies,)),
            dma((2,)),
        ],
        compiler_params=pltpu.CompilerParams(
            collective_id=0, has_side_effects=True, vmem_limit_bytes=VMEM_LIMIT
        ),
    )(
        lengths[0],
        tokens,
        row(gains),
        row(shifts),
        projection,
        mixing,
        row(factors),
        row(biases),
        jnp.pad(centroids, ((0, -centroids.shape[0] % 8), (0, 0))),
        row(route),
        route,
        cotangent,
        expanding,
        contracting,
    )


STEP = 192


def rear_kernel(
    planes,
    slabs,
    total_tokens,
    lengths_ref,
    tokens_ref,
    gains_ref,
    projection_ref,
    mixing_ref,
    factors_ref,
    biases_ref,
    centroids_ref,
    route_ref,
    cot_ref,
    flipped_ref,
    joint_in,
    mixed_ref,
    logs_ref,
    residual_in,
    place_ref,
    loads_ref,
    dots_ref,
    back_all,
    made_all,
    near_all,
    far_all,
    layer_ref,
    token_ref,
    vector_ref,
    up_out,
    down_out,
    shared_out,
    core_land,
    y_land,
    x_land,
    z_land,
    joint_ref,
    residual_ref,
    bias_ref,
    upstream_ref,
    a_ref,
    b_ref,
    place_col,
    gate_col,
    dot_land,
    part_ref,
    stage_ref,
    own_ref,
    own_core,
    own_first,
    own_second,
    own_z,
    piece_ref,
    tally_ref,
    key_sums,
    send_sem,
    recv_sem,
    local_sem,
):
    count, width = tokens_ref.shape
    experts = planes
    rows = a_ref.shape[0]
    half_rows = rows // 2
    pairs = width // 128
    half = width // 2
    scale = (width // HEADS) ** (-0.5)
    factor = scale * HALF_LOG
    average = total_tokens / experts
    me, core, plane, beside_x, beside_y, beside_core = neighbours(slabs)
    x = lax.rem(me, 2)
    y = lax.rem(lax.div(me, 2), 2)
    here = lax.rem(me, slabs)
    diagonal = (beside_y[0], 1 - core)
    always = plane >= 0
    others = [(lax.rem(plane + d, planes) * slabs + here, core) for d in range(1, planes)]
    greet([(d, always) for d in [beside_x, beside_y, beside_core, diagonal] + others])
    ids = {}

    def remote(key, src, dst, device):
        i = ids.setdefault(key, len(ids))
        return pltpu.make_async_remote_copy(
            src_ref=src, dst_ref=dst, send_sem=send_sem.at[i], recv_sem=recv_sem.at[i], device_id=device, device_id_type=MESH
        )

    def fetch(i, src, dst):
        return pltpu.make_async_copy(src, dst, local_sem.at[i])

    loads = [fetch(0, joint_in, joint_ref), fetch(1, residual_in, residual_ref)]
    for copy in loads:
        copy.start()

    alls = (back_all, made_all)

    def to_core(which, second, piece):
        at = pl.ds(piece * half_rows, half_rows)
        return remote(
            ("core", which, second, piece), alls[which].at[1 + 2 * second, at], core_land.at[which, second, at], beside_core
        )

    def to_y(which, piece):
        size = half_rows // (1 + which)
        at = pl.ds(piece * size, size)
        return remote(("y", which, piece), a_ref.at[at], y_land.at[which, at], beside_y)

    def dot_copy(k):
        return remote(("dot", k), dots_ref.at[1 + k], dot_land.at[k], (beside_core, beside_y, diagonal)[k])

    for which in range(2):
        for second in (1, 0):
            for piece in range(2):
                to_core(which, second, piece).start()
        if which == 0:
            for k in range(3):
                dot_copy(k).start()

    def target(sign, r):
        e = plane + sign * r
        return jnp.clip(e, 0, planes - 1), (e >= 0) & (e < planes)

    def share_x(sign, r):
        e, _ = target(sign, r)
        return remote(("x", sign, r), far_all.at[e], x_land.at[e], beside_x)

    def share_z(sign, r):
        return remote(
            ("z", sign, r),
            stage_ref.at[0 if sign > 0 else 1],
            z_land.at[0 if sign > 0 else 1, r - 1],
            (jnp.clip(me + sign * slabs, 0, planes * slabs - 1), core),
        )

    ways = [(s, r) for r in range(planes - 1, 0, -1) for s in (1, -1)] + [(1, 0)]
    def start_shares(distance):
        for sign, r in ways:
            if r == distance:
                @pl.when(target(sign, r)[1])
                def _(sign=sign, r=r):
                    share_x(sign, r).start()

    for distance in range(planes - 1, 1, -1):
        start_shares(distance)

    def add_pieces(into, sources, size, step):
        def one(i, _):
            at = pl.ds(pl.multiple_of(i * step, step), step)
            total = sources[0][at, :].astype(jnp.float32)
            for s in sources[1:]:
                total = total + s[at, :].astype(jnp.float32)
            into[at, :] = total.astype(into.dtype)
            return 0
        lax.fori_loop(0, size // step, one, 0)

    def share_step(sign, r):
        e, valid = target(sign, r)
        lane = 0 if sign > 0 else 1

        @pl.when(valid)
        def _():
            first = fetch(2, near_all.at[e], part_ref.at[0])
            first.start()
            share_x(sign, r).wait_recv()
            second = fetch(3, x_land.at[e], part_ref.at[1])
            second.start()
            if r < planes - 1:
                @pl.when(target(sign, r + 1)[1])
                def _():
                    share_z(sign, r + 1).wait_send()
            first.wait()
            second.wait()
            add_pieces(stage_ref.at[lane], [part_ref.at[0], part_ref.at[1]], part_ref.shape[1], 96)
            if r < planes - 1:
                @pl.when((plane - sign >= 0) & (plane - sign < planes))
                def _():
                    share_z(sign, r + 1).wait_recv()
                    third = fetch(2, z_land.at[lane, r], part_ref.at[0])
                    third.start()
                    third.wait()
                    add_pieces(stage_ref.at[lane], [stage_ref.at[lane], part_ref.at[0]], part_ref.shape[1], 96)
            share_z(sign, r).start()

    def share_end():
        share_x(1, 0).wait_recv()
        copies = [fetch(2, near_all.at[plane], part_ref.at[0]), fetch(3, x_land.at[plane], part_ref.at[1])]
        for copy in copies:
            copy.start()
        for copy in copies:
            copy.wait()

        def put(sources, more):
            def rows_of(i, _):
                at = pl.ds(pl.multiple_of(i * 96, 96), 96)
                total = sources[0][at, :].astype(jnp.float32)
                if len(sources) > 1:
                    total = total + sources[1][at, :].astype(jnp.float32)
                up_out[at, :] = up_out[at, :] + total if more else total
                return 0
            lax.fori_loop(0, width // 96, rows_of, 0)

            def columns_of(i, _):
                at = pl.ds(pl.multiple_of(i * 96, 96), 96)
                for part in range(2):
                    source_at = pl.ds(pl.multiple_of(width + part * half + i * 96, 32), 96)
                    total = sources[0][source_at, :].astype(jnp.float32)
                    if len(sources) > 1:
                        total = total + sources[1][source_at, :].astype(jnp.float32)
                    to = slice(part * half, (part + 1) * half)
                    down_out[at, to] = down_out[at, to] + total if more else total
                return 0
            lax.fori_loop(0, half // 96, columns_of, 0)

        put([part_ref.at[0], part_ref.at[1]], False)
        for sign in (1, -1):
            lane = 0 if sign > 0 else 1

            @pl.when((plane - sign >= 0) & (plane - sign < planes))
            def _(sign=sign, lane=lane):
                share_z(sign, 1).wait_recv()
                third = fetch(2, z_land.at[lane, 0], part_ref.at[0])
                third.start()
                third.wait()
                put([part_ref.at[0]], True)

    q1, q2, q3, q4 = width // 2, width // 4, width // 8, width // 16
    base1 = core * q1
    base2 = base1 + y * q2
    base3 = base2 + x * q3

    def spot(start, size):
        return pl.ds(pl.multiple_of(start, 16), size)

    def corner(p):
        return lax.div(p, 2) * q4, pl.multiple_of(lax.rem(p, 2) * half, 128)

    def sum_copy(c, stage, d=0):
        own = own_ref.at[c % 3]
        if stage == "core":
            return remote((c, stage), own.at[spot((1 - core) * q1, q1)], own_core.at[c], beside_core)
        if stage == "first":
            return remote((c, stage), own.at[spot(base1 + (1 - y) * q2, q2)], own_first.at[c], beside_y)
        if stage == "second":
            return remote((c, stage), own.at[spot(base2 + (1 - x) * q3, q3)], own_second.at[c], beside_x)
        if stage == "z":
            r, k = corner(lax.rem(plane + d, planes))
            return remote(
                (c, stage, d), own.at[spot(base3 + r, q4), pl.ds(k, half)], own_z.at[c, d - 1], others[d - 1]
            )
        out = shared_out.at[c]
        if stage == "zz":
            r, k = corner(plane)
            return remote(
                (c, stage, d), piece_ref.at[c], out.at[spot(base3 + r, q4), pl.ds(k, half)], others[d - 1]
            )
        if stage == "second back":
            at = spot(base3, q3)
            return remote((c, stage), out.at[at], out.at[at], beside_x)
        if stage == "first back":
            at = spot(base2, q2)
            return remote((c, stage), out.at[at], out.at[at], beside_y)
        at = spot(base1, q1)
        return remote((c, stage), out.at[at], out.at[at], beside_core)

    def add_rows(c, start, size, came, step):
        def one(i, _):
            at = pl.ds(pl.multiple_of(i * step, step), step)
            mine = spot(start + i * step, step)
            own_ref[c % 3, mine, :] = (
                own_ref[c % 3, mine, :].astype(jnp.float32) + came[c, at, :].astype(jnp.float32)
            ).astype(jnp.bfloat16)
            return 0
        lax.fori_loop(0, size // step, one, 0)

    def keep_piece(c):
        r, k = corner(plane)
        return fetch(4 + c, piece_ref.at[c], shared_out.at[c, spot(base3 + r, q4), pl.ds(k, half)])

    def sum_step(c, stage):
        if stage == 0:
            sum_copy(c, "core").start()
        elif stage == 1:
            sum_copy(c, "core").wait_recv()
            add_rows(c, base1, q1, own_core, 48)
            sum_copy(c, "first").start()
        elif stage == 2:
            sum_copy(c, "first").wait_recv()
            add_rows(c, base2, q2, own_first, 48)
            sum_copy(c, "second").start()
        elif stage == 3:
            sum_copy(c, "second").wait_recv()
            add_rows(c, base3, q3, own_second, 48)
            for d in range(1, planes):
                sum_copy(c, "z", d).start()
        elif stage == 4:
            r, k = corner(plane)
            total = own_ref[c % 3, spot(base3 + r, q4), pl.ds(k, half)].astype(jnp.float32)
            for d in range(1, planes):
                sum_copy(c, "z", d).wait_recv()
                total = total + own_z[c, d - 1].astype(jnp.float32)
            piece_ref[c] = total.astype(jnp.bfloat16)
            keep_piece(c).start()
            for d in range(1, planes):
                sum_copy(c, "zz", d).start()
        elif stage == 5:
            keep_piece(c).wait()
            for d in range(1, planes):
                sum_copy(c, "zz", d).wait_recv()
            sum_copy(c, "second back").start()
        elif stage == 6:
            sum_copy(c, "second back").wait_recv()
            sum_copy(c, "first back").start()
        elif stage == 7:
            sum_copy(c, "first back").wait_recv()
            sum_copy(c, "cc").start()
        else:
            sum_copy(c, "cc").wait_recv()

    def sum_sent(c):
        for stage in ("core", "first", "second"):
            sum_copy(c, stage).wait_send()
        for d in range(1, planes):
            sum_copy(c, "z", d).wait_send()

    def sum_for_y(which):
        for piece in range(2):
            at = pl.ds(piece * half_rows, half_rows)
            first = fetch(2, alls[which].at[2, at], a_ref.at[at])
            first.start()
            to_core(which, 1, piece).wait_recv()
            second = fetch(3, core_land.at[which, 1, at], b_ref.at[at])
            second.start()
            first.wait()
            second.wait()
            add_pieces(a_ref.at[at], [a_ref.at[at], b_ref.at[at]], half_rows, 32)
            if which == 0:
                to_y(which, piece).start()

    sum_for_y(0)
    place_col[...] = jnp.transpose(place_ref[...])
    score_bias(bias_ref, lengths_ref, count)
    for copy in loads:
        copy.wait()
    vector_ref[...] = jnp.zeros_like(vector_ref)
    number = lax.broadcasted_iota(jnp.int32, (1, rows), 1).astype(jnp.float32)

    def order_of(at):
        return jnp.where(place_col[at, 0:1] == number, 1.0, 0.0)

    def chunk_of(i):
        return pl.ds(pl.multiple_of(i * STEP, STEP), STEP)

    steps = count // STEP

    def unsort(buffer, act):
        def one(i, _):
            at = chunk_of(i)
            act(at, jnp.dot(order_of(at).astype(jnp.bfloat16), buffer[...], preferred_element_type=jnp.float32))
            return 0
        lax.fori_loop(0, steps, one, 0)

    def set_token(at, value):
        token_ref[at, :] = value

    def add_token(at, value):
        token_ref[at, :] += value

    own_back = fetch(2, back_all.at[0], b_ref)
    own_back.start()
    own_back.wait()
    unsort(b_ref, set_token)
    for piece in range(2):
        to_core(0, 0, piece).wait_recv()
    core_back = fetch(2, core_land.at[0, 0], b_ref)
    core_back.start()
    core_back.wait()
    unsort(b_ref, add_token)
    for sign in (1, -1):
        share_step(sign, planes - 1)
    start_shares(1)
    for piece in range(2):
        to_y(0, piece).wait_recv()
    y_back = fetch(2, y_land.at[0], b_ref)
    y_back.start()
    y_back.wait()
    unsort(b_ref, add_token)
    for k in range(3):
        dot_copy(k).wait_recv()
    dots = dots_ref[0] + dot_land[0] + dot_land[1] + dot_land[2]
    dots = dots[0:1, :]

    def norm_step(i, _):
        at = chunk_of(i)
        normed, normal, spread_by = row_norm(residual_ref[at, :], factors_ref[...], biases_ref[...])
        route = route_ref[at, :]
        chosen = chosen_rows(route, centroids_ref, experts)
        gate = 1.0 / (1.0 + jnp.exp(-jnp.sum(normed * chosen, axis=1, keepdims=True)))
        gate_col[at, :] = jnp.broadcast_to(gate, (STEP, 128))
        gate_grad = jnp.sum(order_of(at) * dots, axis=1, keepdims=True)
        spread = jnp.zeros((STEP, 1), jnp.float32)
        for e in range(experts):
            spread = jnp.where(route == e, (loads_ref[e : e + 1, 0:1] - average) * (1.0 / average), spread)
        logit = (gate_grad + spread * (1.0 / total_tokens)) * gate * (1.0 - gate)
        above = token_ref[at, :] + logit * chosen
        pull = logit * normed
        vector_ref[2:3, :] += jnp.sum(above * normal, axis=0, keepdims=True)
        vector_ref[3:4, :] += jnp.sum(above, axis=0, keepdims=True)
        for e in range(experts):
            vector_ref[8 + e : 9 + e, :] += jnp.sum(jnp.where(route == e, pull, 0.0), axis=0, keepdims=True)
        vector_ref[4:5, :] += jnp.broadcast_to(
            jnp.sum(spread * gate, axis=0, keepdims=True) * (1.0 / total_tokens), (1, width)
        )
        scaled = above * factors_ref[...]
        inner = (
            scaled
            - jnp.mean(scaled, axis=1, keepdims=True)
            - normal * jnp.mean(scaled * normal, axis=1, keepdims=True)
        )
        grad = cot_ref[at, :].astype(jnp.float32) + inner * spread_by
        token_ref[at, :] = grad
        branch = grad.astype(jnp.bfloat16)
        layer_ref[at, :] = branch
        upstream_ref[at, :] = lax.dot_general(
            branch, mixing_ref[...], NT, preferred_element_type=jnp.float32
        ).astype(jnp.bfloat16)
        return 0

    lax.fori_loop(0, steps, norm_step, 0)
    own_ref[0] = lax.dot_general(
        mixed_ref[...], layer_ref[...], TN, preferred_element_type=jnp.float32
    ).astype(jnp.bfloat16)
    sum_step(0, 0)
    for piece in range(2):
        to_y(0, piece).wait_send()
    sum_for_y(1)
    for piece in range(2):
        to_y(1, piece).start()
    for sign in (1, -1):
        share_step(sign, planes - 2)

    first = lax.broadcasted_iota(jnp.int32, (1, 128), 1) < 64

    def attend(p, _):
        lanes = pl.ds(pl.multiple_of(p * 128, 128), 128)
        keys = pl.ds(pl.multiple_of(width + p * 128, 128), 128)
        values = pl.ds(pl.multiple_of(2 * width + p * 128, 128), 128)
        key_sum, value_sum = key_sums.at[0], key_sums.at[1]
        key_sum[...] = jnp.zeros_like(key_sum)
        value_sum[...] = jnp.zeros_like(value_sum)
        for s, e in query_blocks(count):
            both = jnp.transpose(
                upstream_ref[s:e, lanes].astype(jnp.float32) * mixed_ref[s:e, lanes].astype(jnp.float32)
            )
            found = []
            for h in range(2):
                mine = first == (h == 0)
                inner = jnp.sum(both[64 * h : 64 * h + 64, :], axis=0, keepdims=True)
                q = jnp.where(mine, joint_ref[s:e, lanes], jnp.bfloat16(0))
                u = jnp.where(mine, upstream_ref[s:e, lanes], jnp.bfloat16(0))
                scores = lax.dot_general(joint_ref[0:e, keys], q, NT, preferred_element_type=jnp.float32)
                probs = jnp.exp2(scores * factor + bias_ref[0:e, s:e] - logs_ref[p, h : h + 1, s:e])
                prob_grad = lax.dot_general(joint_ref[0:e, values], u, NT, preferred_element_type=jnp.float32)
                score_grad = (probs * (prob_grad - inner)).astype(jnp.bfloat16)
                value_sum[0:e, :] += jnp.dot(probs.astype(jnp.bfloat16), u, preferred_element_type=jnp.float32)
                key_sum[0:e, :] += jnp.dot(score_grad, q, preferred_element_type=jnp.float32)
                found.append(
                    lax.dot_general(score_grad, joint_ref[0:e, keys], TN, preferred_element_type=jnp.float32)
                )
            joint_ref[s:e, lanes] = (jnp.where(first, found[0], found[1]) * scale).astype(jnp.bfloat16)
        joint_ref[:, keys] = (key_sum[...] * scale).astype(jnp.bfloat16)
        joint_ref[:, values] = value_sum[...].astype(jnp.bfloat16)

        events = {
            0: [(0, 1)],
            2: [(0, 2), (1, 1)],
            3: [(0, 3)],
            4: [(0, 4), (1, 2), (2, 1)],
            5: [(0, 5), (1, 3)],
        }
        for k, steps_of in events.items():
            @pl.when(p == k)
            def _(k=k, steps_of=steps_of):
                for c, stage in steps_of:
                    sum_step(c, stage)
                if k == 2:
                    start_shares(0)
                if k in (2, 4):
                    to_y(1, 1 + k // 2).start()
                if k == 4:
                    for sign in (1, -1):
                        share_step(sign, 1)
        for c in range(1, 4):
            @pl.when(p == 2 * c - 1)
            def _(c=c):
                if c == 3:
                    sum_sent(0)
                for k in range(3):
                    at = pl.ds(k * width + (c - 1) * 256, 256)
                    own_ref[c % 3, :, k * 256 : (k + 1) * 256] = jnp.dot(
                        flipped_ref[...], joint_ref[:, at], preferred_element_type=jnp.float32
                    ).astype(jnp.bfloat16)
                sum_step(c, 0)

        return 0

    lax.fori_loop(0, pairs, attend, 0)

    rounds = [beside_core, beside_x, beside_y]
    rounds += [((plane + 1 - 2 * lax.rem(plane, 2)) * slabs + here, core), (lax.rem(plane + 2, planes) * slabs + here, core)]

    def tally(k):
        return remote(("tally", k), tally_ref.at[2 * k], tally_ref.at[2 * k + 1], rounds[k])

    def tally_step(k):
        tally(k).wait_recv()
        total = tally_ref[2 * k] + tally_ref[2 * k + 1]
        if k + 1 < len(rounds):
            tally_ref[2 * k + 2] = total
            tally(k + 1).start()
        else:
            vector_ref[...] = total

    def finish_step(i, _):
        at = chunk_of(i)
        back = lax.dot_general(joint_ref[at, :], projection_ref[...], NT, preferred_element_type=jnp.float32)
        _, normal, spread_by = row_norm(tokens_ref[at, :].astype(jnp.float32), gains_ref[...], gains_ref[...])
        scaled = back * gains_ref[...]
        inner = (
            scaled
            - jnp.mean(scaled, axis=1, keepdims=True)
            - normal * jnp.mean(scaled * normal, axis=1, keepdims=True)
        )
        token_ref[at, :] += inner * spread_by
        vector_ref[0:1, :] += jnp.sum(back * normal, axis=0, keepdims=True)
        vector_ref[1:2, :] += jnp.sum(back, axis=0, keepdims=True)
        return 0

    def end_made(at, value):
        layer_ref[at, :] = (residual_ref[at, :] + gate_col[at, 0:1] * value).astype(jnp.bfloat16)

    def load(source, into):
        copy = fetch(2, source, into)
        copy.start()
        copy.wait()

    lax.fori_loop(0, steps // 2, finish_step, 0)
    for c, stage in ((0, 6), (1, 4), (2, 2), (3, 1)):
        sum_step(c, stage)
    lax.fori_loop(steps // 2, steps, finish_step, 0)
    tally_ref[0] = vector_ref[...]
    tally(0).start()
    for c, stage in ((0, 7), (1, 5), (2, 3), (3, 2)):
        sum_step(c, stage)
    for piece in range(4):
        to_y(1, piece).wait_send()
    load(made_all.at[0], a_ref)
    for piece in range(2):
        to_core(1, 0, piece).wait_recv()
    load(core_land.at[1, 0], b_ref)
    add_pieces(a_ref, [a_ref, b_ref], rows, 32)
    tally_step(0)
    for c, stage in ((0, 8), (1, 6), (2, 4), (3, 3)):
        sum_step(c, stage)
    for piece in range(4):
        to_y(1, piece).wait_recv()
    load(y_land.at[1], b_ref)
    add_pieces(a_ref, [a_ref, b_ref], rows, 32)
    tally_step(1)
    for c, stage in ((1, 7), (2, 5), (3, 4)):
        sum_step(c, stage)
    unsort(a_ref, end_made)
    tally_step(2)
    for c, stage in ((1, 8), (2, 6), (3, 5)):
        sum_step(c, stage)
    share_end()
    tally_step(3)
    for c, stage in ((2, 7), (3, 6)):
        sum_step(c, stage)
    tally_step(4)
    for c, stage in ((2, 8), (3, 7), (3, 8)):
        sum_step(c, stage)

    for which in range(2):
        for piece in range(2):
            for second in range(2):
                to_core(which, second, piece).wait_send()
    for k in range(3):
        dot_copy(k).wait_send()
    for sign, r in ways:
        @pl.when(target(sign, r)[1])
        def _(sign=sign, r=r):
            share_x(sign, r).wait_send()
    for sign in (1, -1):
        @pl.when(target(sign, 1)[1])
        def _(sign=sign):
            share_z(sign, 1).wait_send()
    for c in (1, 2, 3):
        sum_sent(c)
    for c in range(4):
        for d in range(1, planes):
            sum_copy(c, "zz", d).wait_send()
        for stage in ("second back", "first back", "cc"):
            sum_copy(c, stage).wait_send()
    for k in range(len(rounds)):
        tally(k).wait_send()
    assert len(ids) <= send_sem.shape[0]


def rear_stage(
    tokens, gains, projection, mixing, factors, biases, centroids, route, lengths, cotangent,
    flipped, joint, mixed, logs, residual, place, loads, dots, back, made, near, far, planes, slabs, total_tokens,
):
    count, width = tokens.shape
    rows = back.shape[1]
    half = width // 2
    bf16, f32 = jnp.bfloat16, jnp.float32
    shape = jax.ShapeDtypeStruct
    anywhere = pl.BlockSpec(memory_space=pl.ANY)
    local = pl.BlockSpec(memory_space=pltpu.VMEM)
    dma = pltpu.SemaphoreType.DMA
    packed = near.shape[1:]
    outs = [
        (shape((count, width), bf16), local),
        (shape((count, width), f32), local),
        (shape((16, width), f32), local),
        (shape((width, half), f32), local),
        (shape((half, width), f32), local),
        (shape((4, width, width), bf16), anywhere),
        (shape((2, 2, rows, width), bf16), anywhere),
        (shape((2, rows, width), bf16), anywhere),
        (shape((planes,) + packed, bf16), anywhere),
        (shape((2, planes - 1) + packed, bf16), anywhere),
    ]
    row = lambda v: v.reshape(1, -1)
    copies = 120
    return pl.pallas_call(
        partial(rear_kernel, planes, slabs, total_tokens),
        out_shape=[o[0] for o in outs],
        in_specs=[pl.BlockSpec(memory_space=pltpu.SMEM)]
        + [local] * 10
        + [anywhere]
        + [local] * 2
        + [anywhere]
        + [local] * 3
        + [anywhere] * 4,
        out_specs=[o[1] for o in outs],
        scratch_shapes=[
            pltpu.VMEM((count, 3 * width), bf16),
            pltpu.VMEM((count, width), f32),
            pltpu.VMEM((count, count), f32),
            pltpu.VMEM((count, width), bf16),
            pltpu.VMEM((rows, width), bf16),
            pltpu.VMEM((rows, width), bf16),
            pltpu.VMEM((count, 8), f32),
            pltpu.VMEM((count, 128), f32),
            pltpu.VMEM((3, 8, rows), f32),
            pltpu.VMEM((2,) + packed, bf16),
            pltpu.VMEM((2,) + packed, bf16),
            pltpu.VMEM((3, width, width), bf16),
            pltpu.VMEM((4, width // 2, width), bf16),
            pltpu.VMEM((4, width // 4, width), bf16),
            pltpu.VMEM((4, width // 8, width), bf16),
            pltpu.VMEM((4, planes - 1, width // 16, half), bf16),
            pltpu.VMEM((4, width // 16, half), bf16),
            pltpu.VMEM((10, 16, width), f32),
            pltpu.VMEM((2, count, 128), f32),
            dma((copies,)),
            dma((copies,)),
            dma((8,)),
        ],
        compiler_params=pltpu.CompilerParams(
            collective_id=1, has_side_effects=True, vmem_limit_bytes=VMEM_LIMIT
        ),
    )(
        lengths[0],
        tokens,
        row(gains),
        projection,
        mixing,
        row(factors),
        row(biases),
        jnp.pad(centroids, ((0, -centroids.shape[0] % 8), (0, 0))),
        route,
        cotangent,
        flipped,
        joint,
        mixed,
        logs,
        residual,
        place,
        loads,
        dots,
        back,
        made,
        near,
        far,
    )


TILE = 256
ALIGN = 16


def aligned_rows(count, experts):
    return -(-(count + experts * (ALIGN - 1)) // ALIGN) * ALIGN


def gelu_pair(values):
    bell = jnp.exp2(values * values * (-0.5 * HALF_LOG))
    near = 1.0 / (1.0 + (0.3275911 * 0.7071067811865476) * jnp.abs(values))
    series = 1.061405429 * 0.5 * near - 1.453152027 * 0.5
    series = series * near + 1.421413741 * 0.5
    series = series * near - 0.284496736 * 0.5
    series = series * near + 0.254829592 * 0.5
    tail = series * near * bell
    below = jnp.where(values >= 0.0, 1.0 - tail, tail)
    return values * below, below + values * bell * 0.3989422804014327


def expert_kernel_body(
    experts,
    sources,
    rows,
    limit,
    width,
    hidden,
    meta_ref,
    *refs,
):
    sent_own, sent_others, cot_own, cot_others, gate_own, gate_others = refs[:6]
    up_near, up_far, down_near, down_far = refs[6:10]
    refs = refs[10:]
    sent_refs = [sent_own] + [sent_others.at[s] for s in range(sources - 1)]
    cot_refs = [cot_own] + [cot_others.at[s] for s in range(sources - 1)]
    gate_refs = [gate_own] + [gate_others.at[s] for s in range(sources - 1)]
    back_all, made_all, dots_all, near_out, far_out = refs[:5]
    back_outs = [back_all.at[s] for s in range(sources)]
    made_outs = [made_all.at[s] for s in range(sources)]
    dot_outs = [dots_all.at[s] for s in range(sources)]
    (x_ref, c_ref, g_ref, column_ref, up_ref, down_ref, gu_ref, gd_ref, pack_ref, zero_ref) = refs[5:15]
    weight_sem, row_sem, out_sem, grad_sem, zero_sem = refs[15:]
    half = hidden // 2
    own = meta_ref[0]

    def size_of(s, e):
        return meta_ref[1 + s * experts + e]

    source_at, joined_at, tiles = {}, {}, []
    first = []
    base = 0
    for s in range(sources):
        at = 0
        for e in range(experts):
            source_at[s, e] = at
            at = at + size_of(s, e)
        source_at[s, experts] = at
    for e in range(experts):
        first.append(base)
        at = base
        for s in range(sources):
            joined_at[s, e] = at
            at = at + size_of(s, e)
        number = (at - base + (TILE - 1)) // TILE
        tiles.append(number)
        base = base + number * TILE

    bits = [1 << b for b in range(limit.bit_length()) if ALIGN <= (1 << b)]

    def pieces(s, e):
        size = size_of(s, e)
        for i, piece in enumerate(bits):
            yield i, piece, (size & piece) != 0, size & (piece - 1)

    def move_in(s, e, act):
        for i, piece, taken, offset in pieces(s, e):
            @pl.when(taken)
            def _(i=i, piece=piece, offset=offset):
                src = pl.ds(pl.multiple_of(source_at[s, e] + offset, ALIGN), piece)
                dst = pl.ds(pl.multiple_of(joined_at[s, e] + offset, ALIGN), piece)
                k = s * experts + e
                act(pltpu.make_async_copy(sent_refs[s].at[src], x_ref.at[dst], row_sem.at[0, k, i]))
                act(pltpu.make_async_copy(cot_refs[s].at[src], c_ref.at[dst], row_sem.at[1, k, i]))

    def move_out(s, e, act):
        for i, piece, taken, offset in pieces(s, e):
            @pl.when(taken)
            def _(i=i, piece=piece, offset=offset):
                src = pl.ds(pl.multiple_of(source_at[s, e] + offset, ALIGN), piece)
                dst = pl.ds(pl.multiple_of(joined_at[s, e] + offset, ALIGN), piece)
                k = s * experts + e
                act(pltpu.make_async_copy(x_ref.at[dst], made_outs[s].at[src], out_sem.at[0, k, i]))
                act(pltpu.make_async_copy(c_ref.at[dst], back_outs[s].at[src], out_sem.at[1, k, i]))

    def move_weights(e, act):
        slot = e - own + experts - 1
        for j, (ups, downs) in enumerate(((up_near, down_near), (up_far, down_far))):
            part = pl.ds(j * half, half)
            act(pltpu.make_async_copy(ups.at[slot], up_ref.at[e, :, part], weight_sem.at[e, j, 0]))
            act(pltpu.make_async_copy(downs.at[slot], down_ref.at[e, part], weight_sem.at[e, j, 1]))

    zero_ref[...] = jnp.zeros_like(zero_ref)
    for e in range(experts):
        @pl.when(tiles[e] > 0)
        def _(e=e):
            last = pl.ds(pl.multiple_of(first[e] + (tiles[e] - 1) * TILE, TILE), TILE)
            x_ref[last, :] = jnp.zeros((TILE, width), jnp.bfloat16)
            c_ref[last, :] = jnp.zeros((TILE, width), jnp.bfloat16)
            g_ref[last, :] = jnp.zeros((TILE, 128), jnp.float32)

    for e in range(experts):
        move_weights(e, lambda copy: copy.start())
        for s in range(sources):
            move_in(s, e, lambda copy: copy.start())

    tail_chunks = rows // ALIGN

    def tail(s, act):
        def one(i, _):
            @pl.when(i * ALIGN >= source_at[s, experts])
            def _():
                dst = pl.ds(pl.multiple_of(i * ALIGN, ALIGN), ALIGN)
                act(pltpu.make_async_copy(zero_ref, made_outs[s].at[dst], zero_sem.at[0, s, i]))
                act(pltpu.make_async_copy(zero_ref, back_outs[s].at[dst], zero_sem.at[1, s, i]))
            return 0
        lax.fori_loop(tail_chunks - 5, tail_chunks, one, 0)

    for s in range(sources):
        tail(s, lambda copy: copy.start())

    for s in range(sources):
        column_ref[...] = jnp.broadcast_to(
            jnp.transpose(jnp.broadcast_to(gate_refs[s][0:1, :], (128, rows)))[:, 0:128], (rows, 128)
        )
        for e in range(experts):
            def one(i, _, s=s, e=e):
                src = pl.ds(pl.multiple_of(source_at[s, e] + i * ALIGN, ALIGN), ALIGN)
                dst = pl.ds(pl.multiple_of(joined_at[s, e] + i * ALIGN, ALIGN), ALIGN)
                g_ref[dst, :] = column_ref[src, :]
                return 0
            lax.fori_loop(0, size_of(s, e) // ALIGN, one, 0)

    for e in range(experts):
        move_weights(e, lambda copy: copy.wait())
        for s in range(sources):
            move_in(s, e, lambda copy: copy.wait())
        gu_ref[...] = jnp.zeros_like(gu_ref)
        gd_ref[...] = jnp.zeros_like(gd_ref)

        def tile(t, _, e=e):
            at = pl.ds(pl.multiple_of(first[e] + t * TILE, TILE), TILE)
            x, c, gate = x_ref[at, :], c_ref[at, :], g_ref[at, 0:1]
            before = jnp.dot(x, up_ref[e], preferred_element_type=jnp.float32)
            active, slope = gelu_pair(before)
            through = lax.dot_general(c, down_ref[e], NT, preferred_element_type=jnp.float32)
            grad = (through * (slope * gate)).astype(jnp.bfloat16)
            gated = (active * gate).astype(jnp.bfloat16)
            made = jnp.dot(active.astype(jnp.bfloat16), down_ref[e], preferred_element_type=jnp.float32)
            g_ref[at, :] = jnp.broadcast_to(
                jnp.sum(made * c.astype(jnp.float32), axis=1, keepdims=True), (TILE, 128)
            )
            gd_ref[...] += lax.dot_general(gated, c, TN, preferred_element_type=jnp.float32)
            gu_ref[...] += lax.dot_general(x, grad, TN, preferred_element_type=jnp.float32)
            back = lax.dot_general(grad, up_ref[e], NT, preferred_element_type=jnp.float32)
            x_ref[at, :] = made.astype(jnp.bfloat16)
            c_ref[at, :] = back.astype(jnp.bfloat16)
            return 0

        lax.fori_loop(0, tiles[e], tile, 0)
        for s in range(sources):
            move_out(s, e, lambda copy: copy.start())

        slot = e % 2
        grads = lambda e, slot: [
            pltpu.make_async_copy(pack_ref.at[slot, j], ref.at[e], grad_sem.at[slot, j])
            for j, ref in enumerate((near_out, far_out))
        ]
        if e >= 2:
            for copy in grads(e - 2, slot):
                copy.wait()
        for j in range(2):
            pack_ref[slot, j, 0:width, :] = gu_ref[:, j * half : (j + 1) * half].astype(jnp.bfloat16)
            for part in range(2):
                pack_ref[slot, j, width + part * half : width + (part + 1) * half, :] = gd_ref[
                    j * half : (j + 1) * half, part * half : (part + 1) * half
                ].astype(jnp.bfloat16)
        for copy in grads(e, slot):
            copy.start()

    for s in range(sources):
        for e in range(experts):
            def one(i, _, s=s, e=e):
                src = pl.ds(pl.multiple_of(source_at[s, e] + i * ALIGN, ALIGN), ALIGN)
                dst = pl.ds(pl.multiple_of(joined_at[s, e] + i * ALIGN, ALIGN), ALIGN)
                column_ref[src, :] = g_ref[dst, :]
                return 0
            lax.fori_loop(0, size_of(s, e) // ALIGN, one, 0)
        dot_outs[s][...] = jnp.transpose(column_ref[...])[0:8, :]

    for e in range(experts):
        for s in range(sources):
            move_out(s, e, lambda copy: copy.wait())
    for s in range(sources):
        tail(s, lambda copy: copy.wait())
    for e in range(max(0, experts - 2), experts):
        for copy in grads(e, e % 2):
            copy.wait()


def expert_stage(meta, sent, cot, gates, weights, experts, limit):
    rows, width = sent[0].shape
    sources = 1 + sent[1].shape[0]
    half = weights[0].shape[2]
    hidden = 2 * half
    joined = -(-(sources * rows + experts * (TILE - 1)) // TILE) * TILE
    limit = -(-limit // ALIGN) * ALIGN
    pieces = limit.bit_length() - ALIGN.bit_length() + 1
    anywhere = pl.BlockSpec(memory_space=pl.ANY)
    local = pl.BlockSpec(memory_space=pltpu.VMEM)
    slots = 2 * experts - 1
    dma = pltpu.SemaphoreType.DMA
    packed = (width + hidden, half)
    return pl.pallas_call(
        partial(expert_kernel_body, experts, sources, rows, limit, width, hidden),
        out_shape=(
            jax.ShapeDtypeStruct((sources, rows, width), jnp.bfloat16),
            jax.ShapeDtypeStruct((sources, rows, width), jnp.bfloat16),
            jax.ShapeDtypeStruct((sources, 8, rows), jnp.float32),
            jax.ShapeDtypeStruct((experts,) + packed, jnp.bfloat16),
            jax.ShapeDtypeStruct((experts,) + packed, jnp.bfloat16),
        ),
        in_specs=[pl.BlockSpec(memory_space=pltpu.SMEM)]
        + [anywhere] * 4
        + [local] * 2
        + [anywhere] * 4,
        out_specs=(anywhere, anywhere, local, anywhere, anywhere),
        scratch_shapes=[
            pltpu.VMEM((joined, width), jnp.bfloat16),
            pltpu.VMEM((joined, width), jnp.bfloat16),
            pltpu.VMEM((joined, 128), jnp.float32),
            pltpu.VMEM((rows, 128), jnp.float32),
            pltpu.VMEM((experts, width, hidden), jnp.bfloat16),
            pltpu.VMEM((experts, hidden, width), jnp.bfloat16),
            pltpu.VMEM((width, hidden), jnp.float32),
            pltpu.VMEM((hidden, width), jnp.float32),
            pltpu.VMEM((2, 2) + packed, jnp.bfloat16),
            pltpu.VMEM((ALIGN, width), jnp.bfloat16),
            dma((experts, 2, 2)),
            dma((2, sources * experts, pieces)),
            dma((2, sources * experts, pieces)),
            dma((2, 2)),
            dma((2, sources, rows // ALIGN)),
        ],
        compiler_params=pltpu.CompilerParams(vmem_limit_bytes=VMEM_LIMIT),
        cost_estimate=pl.CostEstimate(
            flops=12 * sources * rows * width * hidden, bytes_accessed=100_000_000, transcendentals=sources * rows * hidden
        ),
    )(meta, *sent, *cot, *gates, *weights)


def arrange(shared):
    width = shared.shape[1]
    third = width // 3

    def kernel(shared_ref, mixing_ref, projection_ref):
        @pl.when(pl.program_id(0) == 0)
        def _():
            mixing_ref[...] = shared_ref[0].astype(jnp.float32)

        @pl.when(pl.program_id(0) > 0)
        def _():
            projection_ref[...] = shared_ref[0].astype(jnp.float32)

    return pl.pallas_call(
        kernel,
        out_shape=(
            jax.ShapeDtypeStruct((width, width), jnp.float32),
            jax.ShapeDtypeStruct((width, 3 * width), jnp.float32),
        ),
        grid=(4, 3),
        in_specs=[pl.BlockSpec((1, width, third), lambda c, k: (c, 0, k))],
        out_specs=(
            pl.BlockSpec((width, third), lambda c, k: (0, jnp.where(c == 0, k, 2))),
            pl.BlockSpec((width, third), lambda c, k: (0, jnp.where(c == 0, 0, 3 * k + c - 1))),
        ),
        compiler_params=pltpu.CompilerParams(vmem_limit_bytes=VMEM_LIMIT),
    )(shared)


def per_device(
    tokens,
    gains,
    shifts,
    projection,
    mixing,
    factors,
    biases,
    centroids,
    expanding,
    contracting,
    routes,
    lengths,
    cotangent,
):
    count, width = tokens.shape
    experts = centroids.shape[0]
    groups = lax.axis_size("expert")
    slabs = groups // experts
    limit = 2 * count // experts
    total_tokens = count * groups * lax.axis_size("tensor")

    flipped, joint, mixed, logs, residual, place, loads, sent_own, cot_own, gate_own, sent_others, cot_others, gate_others, *weights = front_stage(
        tokens, gains, shifts, projection, mixing, factors, biases, centroids, expanding, contracting, routes, lengths, cotangent, experts, slabs
    )
    sizes = jnp.concatenate((gate_own[1:2, :experts], gate_others[:, 1, :experts]), axis=0)
    meta = jnp.concatenate(
        [lax.div(lax.axis_index("expert"), slabs)[None], sizes.reshape(-1).astype(jnp.int32)]
    )
    back, made, dots, near, far = expert_stage(
        meta, (sent_own, sent_others), (cot_own, cot_others), (gate_own, gate_others), weights, experts, limit
    )
    layer_output, token_grad, vectors, up_grad, down_grad, shared, *_ = rear_stage(
        tokens, gains, projection, mixing, factors, biases, centroids, routes, lengths, cotangent,
        flipped, joint, mixed, logs, residual, place, loads, dots, back, made, near, far, experts, slabs, total_tokens,
    )
    mixing_grad, projection_grad = arrange(shared)
    return (
        layer_output,
        vectors[4, 0],
        token_grad,
        vectors[0],
        vectors[1],
        projection_grad,
        mixing_grad,
        vectors[2],
        vectors[3],
        vectors[8 : 8 + experts],
        up_grad[None],
        down_grad[None],
    )


def solution(mesh):
    placed = (
        P(("expert", "tensor"), None),
        P(),
        P(),
        P(),
        P(),
        P(),
        P(),
        P(),
        P("expert", None, "tensor"),
        P("expert", "tensor", None),
        P(("expert", "tensor"), None),
        P(("expert", "tensor"), None),
        P(("expert", "tensor"), None),
    )
    near = mesh.shape["expert"] == 16 and mesh.shape["tensor"] == 2
    return jax.shard_map(
        per_device if near else moving_tokens,
        mesh=mesh,
        in_specs=placed,
        out_specs=(
            P(("expert", "tensor"), None),
            P(),
            P(("expert", "tensor"), None),
            P(),
            P(),
            P(),
            P(),
            P(),
            P(),
            P(),
            P("expert", None, "tensor"),
            P("expert", "tensor", None),
        ),
        check_vma=False,
    )
```

```python
from functools import partial

import jax
import jax.numpy as jnp
from jax import lax
from jax.experimental import pallas as pl
from jax.experimental.pallas import tpu as pltpu
from jax.sharding import PartitionSpec as P

HEADS = 12


highest = lax.Precision.HIGHEST
epsilon = 1e-05


def running(values):
    places = jnp.arange(values.shape[0])
    return jnp.sum(jnp.where(places[:, None] >= places[None, :], values[None, :], 0), axis=1)


def earlier(picks):
    places = jnp.arange(picks.shape[0])
    before = (places[:, None] > places[None, :]).astype(jnp.bfloat16)
    return jnp.dot(
        before, picks.astype(jnp.bfloat16), preferred_element_type=jnp.float32
    ).astype(jnp.int32)


def norm_parts(values, gain, shift):
    centered = values - jnp.mean(values, axis=1, keepdims=True)
    scale = lax.rsqrt(jnp.mean(centered * centered, axis=1, keepdims=True) + epsilon)
    normal = centered * scale
    return (normal * gain + shift, normal, scale)


def norm_back(upstream, normal, scale, gain):
    scaled = upstream * gain
    inner = (
        scaled
        - jnp.mean(scaled, axis=1, keepdims=True)
        - normal * jnp.mean(scaled * normal, axis=1, keepdims=True)
    )
    return (inner * scale, jnp.sum(upstream * normal, axis=0), jnp.sum(upstream, axis=0))


def gelu_slope(values):
    return (
        0.5 * (1.0 + lax.erf(values * 0.7071067811865476))
        + values * jnp.exp(-0.5 * values * values) * 0.3989422804014327
    )


def expert_forward(gathered, upward, downward):
    before = jnp.dot(gathered, upward, preferred_element_type=jnp.float32)
    active = jax.nn.gelu(before, approximate=False).astype(jnp.bfloat16)
    return jnp.dot(active, downward, preferred_element_type=jnp.float32)


def expert_backward(gathered, incoming, upward, downward):
    before = jnp.dot(gathered, upward, preferred_element_type=jnp.float32)
    active = jax.nn.gelu(before, approximate=False).astype(jnp.bfloat16)
    down_grad = jnp.einsum("rf,rd->fd", active, incoming, preferred_element_type=jnp.float32)
    through = jnp.einsum("rd,fd->rf", incoming, downward, preferred_element_type=jnp.float32)
    hidden_grad = (through * gelu_slope(before)).astype(jnp.bfloat16)
    up_grad = jnp.einsum("rd,rf->df", gathered, hidden_grad, preferred_element_type=jnp.float32)
    return (up_grad, down_grad, hidden_grad)


def head_forward(allowed, item):
    query, keys, values = item
    factor = query.shape[1] ** (-0.5)
    scores = jnp.einsum("qd,kd->qk", query, keys, preferred_element_type=jnp.float32) * factor
    scores = jnp.where(allowed, scores, -1000000000.0)
    peak = jnp.max(scores, axis=1, keepdims=True)
    weights = jnp.exp(scores - peak)
    total = jnp.sum(weights, axis=1, keepdims=True)
    mixed = jnp.dot(
        (weights / total).astype(jnp.bfloat16), values, preferred_element_type=jnp.float32
    )
    return (mixed.astype(jnp.bfloat16), (peak + jnp.log(total))[:, 0])


def head_backward(allowed, item):
    query, keys, values, upstream, log_total = item
    factor = query.shape[1] ** (-0.5)
    scores = jnp.einsum("qd,kd->qk", query, keys, preferred_element_type=jnp.float32) * factor
    scores = jnp.where(allowed, scores, -1000000000.0)
    probs = jnp.exp(scores - log_total[:, None])
    value_grad = jnp.einsum(
        "qk,qd->kd", probs.astype(jnp.bfloat16), upstream, preferred_element_type=jnp.float32
    )
    prob_grad = jnp.einsum("qd,kd->qk", upstream, values, preferred_element_type=jnp.float32)
    inner = jnp.sum(prob_grad * probs, axis=1, keepdims=True)
    score_grad = (probs * (prob_grad - inner)).astype(jnp.bfloat16)
    query_grad = (
        jnp.einsum("qk,kd->qd", score_grad, keys, preferred_element_type=jnp.float32) * factor
    )
    key_grad = (
        jnp.einsum("qk,qd->kd", score_grad, query, preferred_element_type=jnp.float32) * factor
    )
    return (query_grad, key_grad, value_grad)


def moving_tokens(
    tokens,
    gains,
    shifts,
    projection,
    mixing,
    factors,
    biases,
    centroids,
    expanding,
    contracting,
    routes,
    lengths,
    cotangent,
):
    count, width = tokens.shape
    experts = centroids.shape[0]
    groups = lax.axis_size("expert")
    slab_count = groups // experts
    capacity = max(2, 2 * count // experts)
    total_tokens = count * groups * lax.axis_size("tensor")
    average = total_tokens / experts
    route = routes[:, 0]
    picks = route[:, None] == jnp.arange(experts, dtype=jnp.int32)[None, :]
    picks_int = picks.astype(jnp.int32)
    picks_float = picks.astype(jnp.float32)
    loads = lax.psum(jnp.sum(picks_float, axis=0), ("expert", "tensor"))
    spread = (loads - average) / average
    token_spread = jnp.sum(jnp.where(picks, spread[None, :], 0.0), axis=1)
    ranks = jnp.sum(earlier(picks) * picks_int, axis=1)
    slots = route * capacity + ranks
    places = jnp.arange(count, dtype=jnp.int32)
    documents = jnp.sum(
        (places[:, None] >= running(lengths[0])[None, :]).astype(jnp.int32), axis=1
    )
    allowed = (places[:, None] >= places[None, :]) & (documents[:, None] == documents[None, :])
    inputs = tokens.astype(jnp.float32)
    entry, entry_normal, entry_scale = norm_parts(inputs, gains, shifts)
    entry = entry.astype(jnp.bfloat16)
    joint = jnp.dot(entry, projection, preferred_element_type=jnp.float32).astype(jnp.bfloat16)
    heads = joint.reshape(count, 3, HEADS, width // HEADS).transpose(1, 2, 0, 3)
    mixed, log_total = lax.map(partial(head_forward, allowed), (heads[0], heads[1], heads[2]))
    mixed_rows = mixed.transpose(1, 0, 2).reshape(count, width)
    residual = inputs + jnp.dot(mixed_rows, mixing, preferred_element_type=jnp.float32)
    normed, mixer_normal, mixer_scale = norm_parts(residual, factors, biases)
    chosen = jnp.dot(picks.astype(jnp.bfloat16), centroids, preferred_element_type=jnp.float32)
    gates = jax.nn.sigmoid(jnp.sum(normed * chosen, axis=1))
    outgoing = (
        jnp.zeros((experts * capacity, width), jnp.bfloat16)
        .at[slots]
        .set(normed.astype(jnp.bfloat16))
    )
    copies = jnp.broadcast_to(
        outgoing.reshape(experts, 1, capacity, width), (experts, slab_count, capacity, width)
    ).reshape(groups, capacity, width)
    arrived = lax.all_to_all(copies, "expert", split_axis=0, concat_axis=0, tiled=True)
    sources = groups * capacity
    own_rows = arrived.reshape(sources, width)
    gathered = lax.all_gather(own_rows, "tensor", axis=0, tiled=True)
    produced = lax.psum_scatter(
        expert_forward(gathered, expanding[0], contracting[0]).astype(jnp.bfloat16),
        "tensor",
        scatter_dimension=0,
        tiled=True,
    )
    returned = lax.all_to_all(
        produced.reshape(arrived.shape), "expert", split_axis=0, concat_axis=0, tiled=True
    )
    combined = jnp.sum(
        returned.reshape(experts, slab_count, capacity, width).astype(jnp.float32), axis=1
    ).reshape(experts * capacity, width)
    picked = combined[slots]
    layer_output = (residual + gates[:, None] * picked).astype(jnp.bfloat16)
    balance_part = jnp.sum(token_spread * gates) / total_tokens
    upstream = cotangent.astype(jnp.float32)
    gate_grad = jnp.sum(upstream * picked, axis=1)
    logit_grad = (gate_grad + token_spread / total_tokens) * gates * (1.0 - gates)
    scaled_rows = (gates[:, None] * upstream).astype(jnp.bfloat16)
    grad_slots = jnp.zeros((experts * capacity, width), jnp.bfloat16).at[slots].set(scaled_rows)
    grad_copies = jnp.broadcast_to(
        grad_slots.reshape(experts, 1, capacity, width), (experts, slab_count, capacity, width)
    ).reshape(groups, capacity, width)
    incoming = lax.all_to_all(
        grad_copies, "expert", split_axis=0, concat_axis=0, tiled=True
    ).reshape(sources, width)
    incoming_pair = lax.all_gather(incoming, "tensor", axis=0, tiled=True)
    up_share, down_share, hidden_grad = expert_backward(
        gathered, incoming_pair, expanding[0], contracting[0]
    )
    back_rows = lax.psum_scatter(
        jnp.einsum(
            "rf,df->rd", hidden_grad, expanding[0], preferred_element_type=jnp.float32
        ).astype(jnp.bfloat16),
        "tensor",
        scatter_dimension=0,
        tiled=True,
    )
    back = lax.all_to_all(
        back_rows.reshape(arrived.shape), "expert", split_axis=0, concat_axis=0, tiled=True
    )
    back_sum = jnp.sum(
        back.reshape(experts, slab_count, capacity, width).astype(jnp.float32), axis=1
    ).reshape(experts * capacity, width)
    normed_grad = back_sum[slots] + logit_grad[:, None] * chosen
    centroid_grad = jnp.einsum(
        "te,td->ed", picks_float, logit_grad[:, None] * normed, precision=highest
    )
    mixer_back, factor_grad, bias_grad = norm_back(normed_grad, mixer_normal, mixer_scale, factors)
    residual_grad = upstream + mixer_back
    branch_grad = residual_grad.astype(jnp.bfloat16)
    mixing_grad = jnp.einsum(
        "td,te->de", mixed_rows, branch_grad, preferred_element_type=jnp.float32
    )
    mixed_grad = jnp.einsum(
        "te,de->td", branch_grad, mixing, preferred_element_type=jnp.float32
    ).astype(jnp.bfloat16)
    head_grads = mixed_grad.reshape(count, HEADS, width // HEADS).transpose(1, 0, 2)
    query_grad, key_grad, value_grad = lax.map(
        partial(head_backward, allowed), (heads[0], heads[1], heads[2], head_grads, log_total)
    )
    joint_grad = (
        jnp.stack((query_grad, key_grad, value_grad))
        .transpose(2, 0, 1, 3)
        .reshape(count, 3 * width)
        .astype(jnp.bfloat16)
    )
    projection_grad = jnp.einsum("td,te->de", entry, joint_grad, preferred_element_type=jnp.float32)
    entry_back = jnp.einsum("te,de->td", joint_grad, projection, preferred_element_type=jnp.float32)
    entry_input, gain_grad, shift_grad = norm_back(entry_back, entry_normal, entry_scale, gains)
    token_grad = residual_grad + entry_input
    summed = lax.psum(
        (
            gain_grad,
            shift_grad,
            projection_grad,
            mixing_grad,
            factor_grad,
            bias_grad,
            centroid_grad,
            balance_part,
        ),
        ("expert", "tensor"),
    )
    return (
        layer_output,
        summed[7],
        token_grad,
        summed[0],
        summed[1],
        summed[2],
        summed[3],
        summed[4],
        summed[5],
        summed[6],
        up_share[None],
        down_share[None],
    )


HALF_LOG = 1.4426950408889634
LN2 = 0.6931471805599453
NT = (((1,), (1,)), ((), ()))
TN = (((0,), (0,)), ((), ()))
VMEM_LIMIT = 60 * 1024 * 1024


def query_blocks(count):
    step = 256 if count > 256 else count
    return [(i, min(i + step, count)) for i in range(0, count, step)]


def document_starts(lengths_ref, places):
    starts = jnp.zeros_like(places)
    end = 0
    for d in range(lengths_ref.shape[0]):
        end = end + lengths_ref[d]
        starts = jnp.where(places >= end, end, starts)
    return starts


MESH = pl.DeviceIdType.MESH


def neighbours(slabs):
    me, core = lax.axis_index("expert"), lax.axis_index("tensor")
    plane = lax.div(me, slabs)
    x = lax.rem(me, 2)
    y = lax.rem(lax.div(me, 2), 2)
    return me, core, plane, (me + 1 - 2 * x, core), (me + 2 - 4 * y, core), (me, 1 - core)


def greet(partners):
    barrier = pltpu.get_barrier_semaphore()
    number = 0
    for device, there in partners:
        @pl.when(there)
        def _(device=device):
            pl.semaphore_signal(barrier, inc=1, device_id=device, device_id_type=MESH)
        number = number + there.astype(jnp.int32)
    pl.semaphore_wait(barrier, number)


def score_bias(bias_ref, lengths_ref, count):
    places = lax.broadcasted_iota(jnp.int32, (1, count), 1)
    starts = document_starts(lengths_ref, places)
    for s, e in query_blocks(count):
        row = lax.broadcasted_iota(jnp.int32, (e - s, count), 0) + s
        seen = (row <= places) & (row >= starts)
        bias_ref[s:e, :] = jnp.where(seen, 0.0, -1e9)


def row_norm(values, gain, shift):
    centered = values - jnp.mean(values, axis=1, keepdims=True)
    scale = lax.rsqrt(jnp.mean(centered * centered, axis=1, keepdims=True) + epsilon)
    normal = centered * scale
    return normal * gain + shift, normal, scale


def chosen_rows(route, centroids_ref, experts):
    chosen = jnp.zeros((route.shape[0], centroids_ref.shape[1]), jnp.float32)
    for e in range(experts):
        chosen = jnp.where(route == e, centroids_ref[e : e + 1, :].astype(jnp.float32), chosen)
    return chosen


def front_kernel(
    planes,
    slabs,
    lengths_ref,
    tokens_ref,
    norms_ref,
    projection_ref,
    mixing_ref,
    centroids_ref,
    route_row_ref,
    route_ref,
    cot_ref,
    up_ref,
    down_ref,
    flipped_ref,
    joint_ref,
    mixed_ref,
    logs_ref,
    residual_ref,
    place_ref,
    loads_ref,
    sent_all,
    cot_all,
    gate_all,
    up_near,
    up_far,
    down_near,
    down_far,
    bias_ref,
    order_ref,
    normed_ref,
    entry_ref,
    sent_own,
    cot_own,
    gate_own,
    tally_ref,
    send_sem,
    recv_sem,
    local_sem,
):
    count, width = tokens_ref.shape
    experts = planes
    rows = sent_own.shape[0]
    half_rows = rows // 2
    pairs = width // 128
    factor = (width // HEADS) ** (-0.5) * HALF_LOG
    middle = planes - 1
    me, core, plane, beside_x, beside_y, beside_core = neighbours(slabs)
    hop_two = lax.rem(plane + 2, planes)
    hop_one = plane + 1 - 2 * lax.rem(plane, 2)
    here = lax.rem(me, slabs)
    always = plane >= 0
    greet(
        [
            (beside_x, always),
            (beside_y, always),
            (beside_core, always),
            ((hop_two * slabs + here, core), always),
            ((me + slabs, core), plane < planes - 1),
            ((me - slabs, core), plane > 0),
        ]
    )

    def remote(i, src, dst, device):
        return pltpu.make_async_remote_copy(
            src_ref=src, dst_ref=dst, send_sem=send_sem.at[i], recv_sem=recv_sem.at[i], device_id=device, device_id_type=MESH
        )

    owns, nears, fars = (up_ref, down_ref), (up_near, down_near), (up_far, down_far)
    stride = 2 * (planes - 1) + 2 * planes - 1

    def hop(kind, sign, r):
        src = owns[kind].at[0] if r == 1 else nears[kind].at[middle - sign * (r - 1)]
        i = kind * stride + (r - 1) * 2 + (sign > 0)
        return remote(i, src, nears[kind].at[middle - sign * r], (me + sign * slabs, core))

    def hop_sent(sign, r):
        ahead = plane if sign > 0 else planes - 1 - plane
        return (ahead >= r - 1) & (ahead < planes - 1)

    def hop_came(sign, r):
        ahead = plane if sign > 0 else planes - 1 - plane
        return ahead >= r

    def aside(kind, slot):
        src = owns[kind].at[0] if slot == middle else nears[kind].at[slot]
        i = kind * stride + 2 * (planes - 1) + slot
        return remote(i, src, fars[kind].at[slot], beside_x)

    def held(slot):
        at = plane + slot - middle
        return (at >= 0) & (at < planes)

    def own_weights(kind):
        return pltpu.make_async_copy(owns[kind].at[0], nears[kind].at[middle], local_sem.at[kind])

    for kind in range(2):
        for sign in (1, -1):
            @pl.when(hop_sent(sign, 1))
            def _(kind=kind, sign=sign):
                hop(kind, sign, 1).start()
        aside(kind, middle).start()
        own_weights(kind).start()

    def forward_weights(kind, r):
        for sign in (1, -1):
            slot = middle - sign * r

            @pl.when(hop_came(sign, r))
            def _(sign=sign, slot=slot):
                hop(kind, sign, r).wait_recv()
                aside(kind, slot).start()

            if r < planes - 1:
                @pl.when(hop_sent(sign, r + 1))
                def _(sign=sign):
                    hop(kind, sign, r + 1).start()

    base = 2 * stride

    def row_copy(which, part, piece):
        own, everyone = ((cot_own, cot_all), (sent_own, sent_all))[which]
        at = pl.ds(piece * half_rows, half_rows)
        i = base + which * 6 + part * 2 + piece
        if part == 0:
            return remote(i, own.at[at], everyone.at[2, at], beside_y)
        if part == 1:
            return remote(i, own.at[at], everyone.at[1, at], beside_core)
        return remote(i, everyone.at[2, at], everyone.at[3, at], beside_core)

    def gate_copy(part):
        i = base + 12 + part
        if part == 0:
            return remote(i, gate_own, gate_all.at[2], beside_y)
        if part == 1:
            return remote(i, gate_own, gate_all.at[1], beside_core)
        return remote(i, gate_all.at[2], gate_all.at[3], beside_core)

    def own_rows(which):
        source, everyone = ((cot_own, cot_all), (sent_own, sent_all), (gate_own, gate_all))[which]
        return pltpu.make_async_copy(source, everyone.at[0], local_sem.at[2 + which])

    rounds = [beside_core, beside_x, beside_y, (hop_one * slabs + here, core), (hop_two * slabs + here, core)]

    def tally(k):
        return remote(base + 15 + k, tally_ref.at[2 * k], tally_ref.at[2 * k + 1], rounds[k])

    def tally_step(k):
        tally(k).wait_recv()
        total = tally_ref[2 * k] + tally_ref[2 * k + 1]
        if k + 1 < len(rounds):
            tally_ref[2 * k + 2] = total
            tally(k + 1).start()
        else:
            loads_ref[...] = total

    number = lax.broadcasted_iota(jnp.int32, (8, count), 0)
    picks = jnp.where(number == route_row_ref[...], 1.0, 0.0)
    chunk = 128
    for s in range(0, count, chunk):
        row = lax.broadcasted_iota(jnp.int32, (chunk, count), 0) + s
        column = lax.broadcasted_iota(jnp.int32, (chunk, count), 1)
        order_ref[s : s + chunk, :] = jnp.where(row < column, 1.0, 0.0).astype(jnp.bfloat16)
    ranks = jnp.dot(picks.astype(jnp.bfloat16), order_ref[0:count, :], preferred_element_type=jnp.float32)
    counts = jnp.sum(picks, axis=1, keepdims=True)
    padded = jnp.ceil(counts * (1.0 / ALIGN)) * ALIGN
    place = jnp.zeros((1, count), jnp.float32)
    start = jnp.zeros((1, 1), jnp.float32)
    for e in range(experts):
        place = place + picks[e : e + 1, :] * (ranks[e : e + 1, :] + start)
        start = start + padded[e : e + 1, :]
    place_ref[...] = jnp.broadcast_to(place, (8, count))
    tally_ref[0] = jnp.broadcast_to(counts, (8, 128))
    tally(0).start()
    for s in range(0, rows, 64):
        row = lax.broadcasted_iota(jnp.int32, (64, count), 0) + s
        order_ref[s : s + 64, :] = jnp.where(row.astype(jnp.float32) == place, 1.0, 0.0).astype(jnp.bfloat16)

    def sort_rows(source_ref, to_ref, which):
        for piece in range(2):
            at = slice(piece * half_rows, (piece + 1) * half_rows)
            to_ref[at, :] = jnp.dot(
                order_ref[at, :], source_ref[...], preferred_element_type=jnp.float32
            ).astype(jnp.bfloat16)
            row_copy(which, 0, piece).start()
            row_copy(which, 1, piece).start()

    sort_rows(cot_ref, cot_own, 0)
    own_rows(0).start()

    def project(i, _):
        at = pl.ds(pl.multiple_of(i * 192, 192), 192)
        entry, _, _ = row_norm(tokens_ref[at, :].astype(jnp.float32), norms_ref[0:1, :], norms_ref[1:2, :])
        entry = entry.astype(jnp.bfloat16)
        entry_ref[at, :] = entry
        joint_ref[at, :] = jnp.dot(entry, projection_ref[...], preferred_element_type=jnp.float32).astype(jnp.bfloat16)
        return 0

    lax.fori_loop(0, count // 192, project, 0)
    score_bias(bias_ref, lengths_ref, count)
    forward_weights(0, 1)
    tally_step(0)

    first = lax.broadcasted_iota(jnp.int32, (1, 128), 1) < 64

    def attend(p, _):
        lanes = pl.ds(pl.multiple_of(p * 128, 128), 128)
        keys = pl.ds(pl.multiple_of(width + p * 128, 128), 128)
        values = pl.ds(pl.multiple_of(2 * width + p * 128, 128), 128)
        for s, e in query_blocks(count):
            outs = []
            for half in range(2):
                q = jnp.where(first == (half == 0), joint_ref[s:e, lanes], jnp.bfloat16(0))
                scores = lax.dot_general(joint_ref[0:e, keys], q, NT, preferred_element_type=jnp.float32)
                scores = scores * factor + bias_ref[0:e, s:e]
                peak = jnp.max(scores, axis=0, keepdims=True)
                weights = jnp.exp2(scores - peak)
                total = jnp.sum(weights, axis=0, keepdims=True)
                probs = (weights * (1.0 / total)).astype(jnp.bfloat16)
                outs.append(
                    lax.dot_general(probs, joint_ref[0:e, values], TN, preferred_element_type=jnp.float32)
                )
                logs_ref[p, half : half + 1, s:e] = peak + jnp.log2(total)
            mixed_ref[s:e, lanes] = jnp.where(first, outs[0], outs[1]).astype(jnp.bfloat16)

        @pl.when(p == 2)
        def _():
            forward_weights(1, 1)
            tally_step(1)

        @pl.when(p == 4)
        def _():
            forward_weights(0, 2)
            tally_step(2)

        return 0

    lax.fori_loop(0, pairs, attend, 0)

    lane = lax.broadcasted_iota(jnp.int32, (1, 128), 1)

    def mix(i, _):
        at = pl.ds(pl.multiple_of(i * 192, 192), 192)
        residual = tokens_ref[at, :].astype(jnp.float32) + jnp.dot(
            mixed_ref[at, :], mixing_ref[...], preferred_element_type=jnp.float32
        )
        residual_ref[at, :] = residual
        normed, _, _ = row_norm(residual, norms_ref[2:3, :], norms_ref[3:4, :])
        chosen = chosen_rows(route_ref[at, :], centroids_ref, experts)
        gate = 1.0 / (1.0 + jnp.exp(-jnp.sum(normed * chosen, axis=1, keepdims=True)))
        high = gate.astype(jnp.bfloat16).astype(jnp.float32)
        mid = (gate - high).astype(jnp.bfloat16).astype(jnp.float32)
        low = gate - high - mid
        parts = jnp.where(lane == 0, high, jnp.where(lane == 1, mid, jnp.where(lane == 2, low, 0.0)))
        normed_ref[at, 0:width] = normed.astype(jnp.bfloat16)
        normed_ref[at, width : width + 128] = parts.astype(jnp.bfloat16)
        return 0

    lax.fori_loop(0, count // 192, mix, 0)
    for piece in range(2):
        at = slice(piece * half_rows, (piece + 1) * half_rows)
        moved = jnp.dot(order_ref[at, :], normed_ref[...], preferred_element_type=jnp.float32)
        sent_own[at, :] = moved[:, 0:width].astype(jnp.bfloat16)
        row_copy(1, 0, piece).start()
        row_copy(1, 1, piece).start()
        bias_ref[at, 0:128] = jnp.broadcast_to(
            jnp.sum(moved[:, width : width + 128], axis=1, keepdims=True), (half_rows, 128)
        )
    forward_weights(1, 2)
    tally_step(3)
    for piece in range(2):
        row_copy(0, 0, piece).wait_recv()
        row_copy(0, 2, piece).start()
    gates = jnp.transpose(bias_ref[0:rows, 0:128])
    gate_own[0:1, :] = gates[0:1, :]
    gate_own[1:2, :] = jnp.zeros((1, rows), jnp.float32)
    for e in range(8):
        gate_own[1:2, e : e + 1] = padded[e : e + 1, :]
    gate_copy(0).start()
    gate_copy(1).start()
    own_rows(1).start()
    own_rows(2).start()
    for s in range(0, count, 384):
        flipped_ref[:, s : s + 384] = jnp.transpose(entry_ref[s : s + 384, :])

    for kind in range(2):
        forward_weights(kind, 3)
    gate_copy(0).wait_recv()
    gate_copy(2).start()
    tally_step(4)
    for piece in range(2):
        row_copy(1, 0, piece).wait_recv()
        row_copy(1, 2, piece).start()

    for which in range(2):
        for part in range(3):
            for piece in range(2):
                copy = row_copy(which, part, piece)
                copy.wait_send()
                if part:
                    copy.wait_recv()
    for part in range(3):
        gate_copy(part).wait_send()
        if part:
            gate_copy(part).wait_recv()
    for k in range(len(rounds)):
        tally(k).wait_send()
    for which in range(3):
        own_rows(which).wait()
    for kind in range(2):
        own_weights(kind).wait()
        for r in range(1, planes):
            for sign in (1, -1):
                @pl.when(hop_sent(sign, r))
                def _(kind=kind, sign=sign, r=r):
                    hop(kind, sign, r).wait_send()
        for slot in range(2 * planes - 1):
            @pl.when(held(slot))
            def _(kind=kind, slot=slot):
                aside(kind, slot).wait()


def front_stage(
    tokens, norms, projection, mixing, centroids, expanding, contracting, route, lengths, cotangent, planes, slabs
):
    count, width = tokens.shape
    rows = aligned_rows(count, planes)
    pairs = width // 128
    slots = 2 * planes - 1
    bf16, f32 = jnp.bfloat16, jnp.float32
    shape = jax.ShapeDtypeStruct
    anywhere = pl.BlockSpec(memory_space=pl.ANY)
    local = pl.BlockSpec(memory_space=pltpu.VMEM)
    dma = pltpu.SemaphoreType.DMA
    copies = 2 * (2 * (planes - 1) + slots) + 12 + 3 + 5
    outs = [
        (shape((width, count), bf16), local),
        (shape((count, 3 * width), bf16), local),
        (shape((count, width), bf16), local),
        (shape((pairs, 2, count), f32), local),
        (shape((count, width), f32), local),
        (shape((8, count), f32), local),
        (shape((8, 128), f32), local),
        (shape((4, rows, width), bf16), anywhere),
        (shape((4, rows, width), bf16), anywhere),
        (shape((4, 8, rows), f32), anywhere),
        (shape((slots,) + expanding.shape[1:], bf16), anywhere),
        (shape((slots,) + expanding.shape[1:], bf16), anywhere),
        (shape((slots,) + contracting.shape[1:], bf16), anywhere),
        (shape((slots,) + contracting.shape[1:], bf16), anywhere),
    ]
    return pl.pallas_call(
        partial(front_kernel, planes, slabs),
        out_shape=[o[0] for o in outs],
        in_specs=[pl.BlockSpec(memory_space=pltpu.SMEM)] + [local] * 8 + [anywhere] * 2,
        out_specs=[o[1] for o in outs],
        scratch_shapes=[
            pltpu.VMEM((rows, count), f32),
            pltpu.VMEM((rows, count), bf16),
            pltpu.VMEM((count, width + 128), bf16),
            pltpu.VMEM((count, width), bf16),
            pltpu.VMEM((rows, width), bf16),
            pltpu.VMEM((rows, width), bf16),
            pltpu.VMEM((8, rows), f32),
            pltpu.VMEM((10, 8, 128), f32),
            dma((copies,)),
            dma((copies,)),
            dma((5,)),
        ],
        compiler_params=pltpu.CompilerParams(
            collective_id=0, has_side_effects=True, vmem_limit_bytes=VMEM_LIMIT
        ),
    )(
        lengths[0],
        tokens,
        norms,
        projection,
        mixing,
        centroids,
        route.reshape(1, -1),
        route,
        cotangent,
        expanding,
        contracting,
    )


STEP = 192


def rear_kernel(
    planes,
    slabs,
    total_tokens,
    lengths_ref,
    tokens_ref,
    norms_ref,
    projection_ref,
    mixing_ref,
    centroids_ref,
    route_ref,
    cot_ref,
    flipped_ref,
    joint_in,
    mixed_ref,
    logs_ref,
    residual_in,
    place_ref,
    loads_ref,
    dots_ref,
    back_all,
    made_all,
    near_all,
    far_all,
    layer_ref,
    token_ref,
    vector_ref,
    up_out,
    down_out,
    shared_out,
    core_land,
    y_land,
    x_land,
    z_land,
    joint_ref,
    residual_ref,
    bias_ref,
    upstream_ref,
    a_ref,
    b_ref,
    place_col,
    gate_col,
    dot_land,
    part_ref,
    stage_ref,
    own_ref,
    own_core,
    own_first,
    own_second,
    own_z,
    piece_ref,
    tally_ref,
    key_sums,
    send_sem,
    recv_sem,
    local_sem,
):
    count, width = tokens_ref.shape
    experts = planes
    rows = a_ref.shape[0]
    half_rows = rows // 2
    pairs = width // 128
    half = width // 2
    scale = (width // HEADS) ** (-0.5)
    factor = scale * HALF_LOG
    average = total_tokens / experts
    me, core, plane, beside_x, beside_y, beside_core = neighbours(slabs)
    x = lax.rem(me, 2)
    y = lax.rem(lax.div(me, 2), 2)
    here = lax.rem(me, slabs)
    diagonal = (beside_y[0], 1 - core)
    always = plane >= 0
    others = [(lax.rem(plane + d, planes) * slabs + here, core) for d in range(1, planes)]
    greet([(d, always) for d in [beside_x, beside_y, beside_core, diagonal] + others])
    ids = {}

    def remote(key, src, dst, device):
        i = ids.setdefault(key, len(ids))
        return pltpu.make_async_remote_copy(
            src_ref=src, dst_ref=dst, send_sem=send_sem.at[i], recv_sem=recv_sem.at[i], device_id=device, device_id_type=MESH
        )

    def fetch(i, src, dst):
        return pltpu.make_async_copy(src, dst, local_sem.at[i])

    loads = [fetch(0, joint_in, joint_ref), fetch(1, residual_in, residual_ref)]
    for copy in loads:
        copy.start()

    alls = (back_all, made_all)

    def to_core(which, second, piece):
        at = pl.ds(piece * half_rows, half_rows)
        return remote(
            ("core", which, second, piece), alls[which].at[1 + 2 * second, at], core_land.at[which, second, at], beside_core
        )

    def to_y(which, piece):
        size = half_rows // (1 + which)
        at = pl.ds(piece * size, size)
        return remote(("y", which, piece), a_ref.at[at], y_land.at[which, at], beside_y)

    def dot_copy(k):
        return remote(("dot", k), dots_ref.at[1 + k], dot_land.at[k], (beside_core, beside_y, diagonal)[k])

    for which in range(2):
        for second in (1, 0):
            for piece in range(2):
                to_core(which, second, piece).start()
        if which == 0:
            for k in range(3):
                dot_copy(k).start()

    def target(sign, r):
        e = plane + sign * r
        return jnp.clip(e, 0, planes - 1), (e >= 0) & (e < planes)

    def share_x(sign, r):
        e, _ = target(sign, r)
        return remote(("x", sign, r), far_all.at[e], x_land.at[e], beside_x)

    def share_z(sign, r):
        return remote(
            ("z", sign, r),
            stage_ref.at[0 if sign > 0 else 1],
            z_land.at[0 if sign > 0 else 1, r - 1],
            (jnp.clip(me + sign * slabs, 0, planes * slabs - 1), core),
        )

    ways = [(s, r) for r in range(planes - 1, 0, -1) for s in (1, -1)] + [(1, 0)]
    def start_shares(distance):
        for sign, r in ways:
            if r == distance:
                @pl.when(target(sign, r)[1])
                def _(sign=sign, r=r):
                    share_x(sign, r).start()

    for distance in range(planes - 1, 1, -1):
        start_shares(distance)

    def add_pieces(into, sources, size, step):
        def one(i, _):
            at = pl.ds(pl.multiple_of(i * step, step), step)
            total = sources[0][at, :].astype(jnp.float32)
            for s in sources[1:]:
                total = total + s[at, :].astype(jnp.float32)
            into[at, :] = total.astype(into.dtype)
            return 0
        lax.fori_loop(0, size // step, one, 0)

    def share_step(sign, r):
        e, valid = target(sign, r)
        lane = 0 if sign > 0 else 1

        @pl.when(valid)
        def _():
            first = fetch(2, near_all.at[e], part_ref.at[0])
            first.start()
            share_x(sign, r).wait_recv()
            second = fetch(3, x_land.at[e], part_ref.at[1])
            second.start()
            if r < planes - 1:
                @pl.when(target(sign, r + 1)[1])
                def _():
                    share_z(sign, r + 1).wait_send()
            first.wait()
            second.wait()
            add_pieces(stage_ref.at[lane], [part_ref.at[0], part_ref.at[1]], part_ref.shape[1], 96)
            if r < planes - 1:
                @pl.when((plane - sign >= 0) & (plane - sign < planes))
                def _():
                    share_z(sign, r + 1).wait_recv()
                    third = fetch(2, z_land.at[lane, r], part_ref.at[0])
                    third.start()
                    third.wait()
                    add_pieces(stage_ref.at[lane], [stage_ref.at[lane], part_ref.at[0]], part_ref.shape[1], 96)
            share_z(sign, r).start()

    def share_end():
        share_x(1, 0).wait_recv()
        copies = [fetch(2, near_all.at[plane], part_ref.at[0]), fetch(3, x_land.at[plane], part_ref.at[1])]
        for copy in copies:
            copy.start()
        for copy in copies:
            copy.wait()

        def put(sources, more):
            def rows_of(i, _):
                at = pl.ds(pl.multiple_of(i * 96, 96), 96)
                total = sources[0][at, :].astype(jnp.float32)
                if len(sources) > 1:
                    total = total + sources[1][at, :].astype(jnp.float32)
                up_out[at, :] = up_out[at, :] + total if more else total
                return 0
            lax.fori_loop(0, width // 96, rows_of, 0)

            def columns_of(i, _):
                at = pl.ds(pl.multiple_of(i * 96, 96), 96)
                for part in range(2):
                    source_at = pl.ds(pl.multiple_of(width + part * half + i * 96, 32), 96)
                    total = sources[0][source_at, :].astype(jnp.float32)
                    if len(sources) > 1:
                        total = total + sources[1][source_at, :].astype(jnp.float32)
                    to = slice(part * half, (part + 1) * half)
                    down_out[at, to] = down_out[at, to] + total if more else total
                return 0
            lax.fori_loop(0, half // 96, columns_of, 0)

        put([part_ref.at[0], part_ref.at[1]], False)
        for sign in (1, -1):
            lane = 0 if sign > 0 else 1

            @pl.when((plane - sign >= 0) & (plane - sign < planes))
            def _(sign=sign, lane=lane):
                share_z(sign, 1).wait_recv()
                third = fetch(2, z_land.at[lane, 0], part_ref.at[0])
                third.start()
                third.wait()
                put([part_ref.at[0]], True)

    q1, q2, q3, q4 = width // 2, width // 4, width // 8, width // 16
    base1 = core * q1
    base2 = base1 + y * q2
    base3 = base2 + x * q3

    def spot(start, size):
        return pl.ds(pl.multiple_of(start, 16), size)

    def corner(p):
        return lax.div(p, 2) * q4, pl.multiple_of(lax.rem(p, 2) * half, 128)

    def sum_copy(c, stage, d=0):
        own = own_ref.at[c % 3]
        if stage == "core":
            return remote((c, stage), own.at[spot((1 - core) * q1, q1)], own_core.at[c], beside_core)
        if stage == "first":
            return remote((c, stage), own.at[spot(base1 + (1 - y) * q2, q2)], own_first.at[c], beside_y)
        if stage == "second":
            return remote((c, stage), own.at[spot(base2 + (1 - x) * q3, q3)], own_second.at[c], beside_x)
        if stage == "z":
            r, k = corner(lax.rem(plane + d, planes))
            return remote(
                (c, stage, d), own.at[spot(base3 + r, q4), pl.ds(k, half)], own_z.at[c, d - 1], others[d - 1]
            )
        out = shared_out.at[c]
        if stage == "zz":
            r, k = corner(plane)
            return remote(
                (c, stage, d), piece_ref.at[c], out.at[spot(base3 + r, q4), pl.ds(k, half)], others[d - 1]
            )
        if stage == "second back":
            at = spot(base3, q3)
            return remote((c, stage), out.at[at], out.at[at], beside_x)
        if stage == "first back":
            at = spot(base2, q2)
            return remote((c, stage), out.at[at], out.at[at], beside_y)
        at = spot(base1, q1)
        return remote((c, stage), out.at[at], out.at[at], beside_core)

    def add_rows(c, start, size, came, step):
        def one(i, _):
            at = pl.ds(pl.multiple_of(i * step, step), step)
            mine = spot(start + i * step, step)
            own_ref[c % 3, mine, :] = (
                own_ref[c % 3, mine, :].astype(jnp.float32) + came[c, at, :].astype(jnp.float32)
            ).astype(jnp.bfloat16)
            return 0
        lax.fori_loop(0, size // step, one, 0)

    def keep_piece(c):
        r, k = corner(plane)
        return fetch(4 + c, piece_ref.at[c], shared_out.at[c, spot(base3 + r, q4), pl.ds(k, half)])

    def sum_step(c, stage):
        if stage == 0:
            sum_copy(c, "core").start()
        elif stage == 1:
            sum_copy(c, "core").wait_recv()
            add_rows(c, base1, q1, own_core, 48)
            sum_copy(c, "first").start()
        elif stage == 2:
            sum_copy(c, "first").wait_recv()
            add_rows(c, base2, q2, own_first, 48)
            sum_copy(c, "second").start()
        elif stage == 3:
            sum_copy(c, "second").wait_recv()
            add_rows(c, base3, q3, own_second, 48)
            for d in range(1, planes):
                sum_copy(c, "z", d).start()
        elif stage == 4:
            r, k = corner(plane)
            total = own_ref[c % 3, spot(base3 + r, q4), pl.ds(k, half)].astype(jnp.float32)
            for d in range(1, planes):
                sum_copy(c, "z", d).wait_recv()
                total = total + own_z[c, d - 1].astype(jnp.float32)
            piece_ref[c] = total.astype(jnp.bfloat16)
            keep_piece(c).start()
            for d in range(1, planes):
                sum_copy(c, "zz", d).start()
        elif stage == 5:
            keep_piece(c).wait()
            for d in range(1, planes):
                sum_copy(c, "zz", d).wait_recv()
            sum_copy(c, "second back").start()
        elif stage == 6:
            sum_copy(c, "second back").wait_recv()
            sum_copy(c, "first back").start()
        elif stage == 7:
            sum_copy(c, "first back").wait_recv()
            sum_copy(c, "cc").start()
        else:
            sum_copy(c, "cc").wait_recv()

    def sum_sent(c):
        for stage in ("core", "first", "second"):
            sum_copy(c, stage).wait_send()
        for d in range(1, planes):
            sum_copy(c, "z", d).wait_send()

    def sum_for_y(which):
        for piece in range(2):
            at = pl.ds(piece * half_rows, half_rows)
            first = fetch(2, alls[which].at[2, at], a_ref.at[at])
            first.start()
            to_core(which, 1, piece).wait_recv()
            second = fetch(3, core_land.at[which, 1, at], b_ref.at[at])
            second.start()
            first.wait()
            second.wait()
            add_pieces(a_ref.at[at], [a_ref.at[at], b_ref.at[at]], half_rows, 32)
            if which == 0:
                to_y(which, piece).start()

    sum_for_y(0)
    place_col[...] = jnp.transpose(place_ref[...])
    score_bias(bias_ref, lengths_ref, count)
    for copy in loads:
        copy.wait()
    vector_ref[...] = jnp.zeros_like(vector_ref)
    number = lax.broadcasted_iota(jnp.int32, (1, rows), 1).astype(jnp.float32)

    def order_of(at):
        return jnp.where(place_col[at, 0:1] == number, 1.0, 0.0)

    def chunk_of(i):
        return pl.ds(pl.multiple_of(i * STEP, STEP), STEP)

    steps = count // STEP

    def unsort(buffer, act):
        def one(i, _):
            at = chunk_of(i)
            act(at, jnp.dot(order_of(at).astype(jnp.bfloat16), buffer[...], preferred_element_type=jnp.float32))
            return 0
        lax.fori_loop(0, steps, one, 0)

    def set_token(at, value):
        token_ref[at, :] = value

    def add_token(at, value):
        token_ref[at, :] += value

    own_back = fetch(2, back_all.at[0], b_ref)
    own_back.start()
    own_back.wait()
    unsort(b_ref, set_token)
    for piece in range(2):
        to_core(0, 0, piece).wait_recv()
    core_back = fetch(2, core_land.at[0, 0], b_ref)
    core_back.start()
    core_back.wait()
    unsort(b_ref, add_token)
    for sign in (1, -1):
        share_step(sign, planes - 1)
    start_shares(1)
    for piece in range(2):
        to_y(0, piece).wait_recv()
    y_back = fetch(2, y_land.at[0], b_ref)
    y_back.start()
    y_back.wait()
    unsort(b_ref, add_token)
    for k in range(3):
        dot_copy(k).wait_recv()
    dots = dots_ref[0] + dot_land[0] + dot_land[1] + dot_land[2]
    dots = dots[0:1, :]

    def norm_step(i, _):
        at = chunk_of(i)
        normed, normal, spread_by = row_norm(residual_ref[at, :], norms_ref[2:3, :], norms_ref[3:4, :])
        route = route_ref[at, :]
        chosen = chosen_rows(route, centroids_ref, experts)
        gate = 1.0 / (1.0 + jnp.exp(-jnp.sum(normed * chosen, axis=1, keepdims=True)))
        gate_col[at, :] = jnp.broadcast_to(gate, (STEP, 128))
        gate_grad = jnp.sum(order_of(at) * dots, axis=1, keepdims=True)
        spread = jnp.zeros((STEP, 1), jnp.float32)
        for e in range(experts):
            spread = jnp.where(route == e, (loads_ref[e : e + 1, 0:1] - average) * (1.0 / average), spread)
        logit = (gate_grad + spread * (1.0 / total_tokens)) * gate * (1.0 - gate)
        above = token_ref[at, :] + logit * chosen
        pull = logit * normed
        vector_ref[2:3, :] += jnp.sum(above * normal, axis=0, keepdims=True)
        vector_ref[3:4, :] += jnp.sum(above, axis=0, keepdims=True)
        for e in range(experts):
            vector_ref[8 + e : 9 + e, :] += jnp.sum(jnp.where(route == e, pull, 0.0), axis=0, keepdims=True)
        vector_ref[4:5, :] += jnp.broadcast_to(
            jnp.sum(spread * gate, axis=0, keepdims=True) * (1.0 / total_tokens), (1, width)
        )
        scaled = above * norms_ref[2:3, :]
        inner = (
            scaled
            - jnp.mean(scaled, axis=1, keepdims=True)
            - normal * jnp.mean(scaled * normal, axis=1, keepdims=True)
        )
        grad = cot_ref[at, :].astype(jnp.float32) + inner * spread_by
        token_ref[at, :] = grad
        branch = grad.astype(jnp.bfloat16)
        layer_ref[at, :] = branch
        upstream_ref[at, :] = lax.dot_general(
            branch, mixing_ref[...], NT, preferred_element_type=jnp.float32
        ).astype(jnp.bfloat16)
        return 0

    lax.fori_loop(0, steps, norm_step, 0)
    own_ref[0] = lax.dot_general(
        mixed_ref[...], layer_ref[...], TN, preferred_element_type=jnp.float32
    ).astype(jnp.bfloat16)
    sum_step(0, 0)
    for piece in range(2):
        to_y(0, piece).wait_send()
    sum_for_y(1)
    for piece in range(2):
        to_y(1, piece).start()
    for sign in (1, -1):
        share_step(sign, planes - 2)

    first = lax.broadcasted_iota(jnp.int32, (1, 128), 1) < 64

    def attend(p, _):
        lanes = pl.ds(pl.multiple_of(p * 128, 128), 128)
        keys = pl.ds(pl.multiple_of(width + p * 128, 128), 128)
        values = pl.ds(pl.multiple_of(2 * width + p * 128, 128), 128)
        key_sum, value_sum = key_sums.at[0], key_sums.at[1]
        key_sum[...] = jnp.zeros_like(key_sum)
        value_sum[...] = jnp.zeros_like(value_sum)
        for s, e in query_blocks(count):
            both = jnp.transpose(
                upstream_ref[s:e, lanes].astype(jnp.float32) * mixed_ref[s:e, lanes].astype(jnp.float32)
            )
            found = []
            for h in range(2):
                mine = first == (h == 0)
                inner = jnp.sum(both[64 * h : 64 * h + 64, :], axis=0, keepdims=True)
                q = jnp.where(mine, joint_ref[s:e, lanes], jnp.bfloat16(0))
                u = jnp.where(mine, upstream_ref[s:e, lanes], jnp.bfloat16(0))
                scores = lax.dot_general(joint_ref[0:e, keys], q, NT, preferred_element_type=jnp.float32)
                probs = jnp.exp2(scores * factor + bias_ref[0:e, s:e] - logs_ref[p, h : h + 1, s:e])
                prob_grad = lax.dot_general(joint_ref[0:e, values], u, NT, preferred_element_type=jnp.float32)
                score_grad = (probs * (prob_grad - inner)).astype(jnp.bfloat16)
                value_sum[0:e, :] += jnp.dot(probs.astype(jnp.bfloat16), u, preferred_element_type=jnp.float32)
                key_sum[0:e, :] += jnp.dot(score_grad, q, preferred_element_type=jnp.float32)
                found.append(
                    lax.dot_general(score_grad, joint_ref[0:e, keys], TN, preferred_element_type=jnp.float32)
                )
            joint_ref[s:e, lanes] = (jnp.where(first, found[0], found[1]) * scale).astype(jnp.bfloat16)
        joint_ref[:, keys] = (key_sum[...] * scale).astype(jnp.bfloat16)
        joint_ref[:, values] = value_sum[...].astype(jnp.bfloat16)

        events = {
            0: [(0, 1)],
            2: [(0, 2), (1, 1)],
            3: [(0, 3)],
            4: [(0, 4), (1, 2), (2, 1)],
            5: [(0, 5), (1, 3)],
        }
        for k, steps_of in events.items():
            @pl.when(p == k)
            def _(k=k, steps_of=steps_of):
                for c, stage in steps_of:
                    sum_step(c, stage)
                if k == 2:
                    start_shares(0)
                if k in (2, 4):
                    to_y(1, 1 + k // 2).start()
                if k == 4:
                    for sign in (1, -1):
                        share_step(sign, 1)
        for c in range(1, 4):
            @pl.when(p == 2 * c - 1)
            def _(c=c):
                if c == 3:
                    sum_sent(0)
                for k in range(3):
                    at = pl.ds(k * width + (c - 1) * 256, 256)
                    own_ref[c % 3, :, k * 256 : (k + 1) * 256] = jnp.dot(
                        flipped_ref[...], joint_ref[:, at], preferred_element_type=jnp.float32
                    ).astype(jnp.bfloat16)
                sum_step(c, 0)

        return 0

    lax.fori_loop(0, pairs, attend, 0)

    rounds = [beside_core, beside_x, beside_y]
    rounds += [((plane + 1 - 2 * lax.rem(plane, 2)) * slabs + here, core), (lax.rem(plane + 2, planes) * slabs + here, core)]

    def tally(k):
        return remote(("tally", k), tally_ref.at[2 * k], tally_ref.at[2 * k + 1], rounds[k])

    def tally_step(k):
        tally(k).wait_recv()
        total = tally_ref[2 * k] + tally_ref[2 * k + 1]
        if k + 1 < len(rounds):
            tally_ref[2 * k + 2] = total
            tally(k + 1).start()
        else:
            vector_ref[...] = total

    def finish_step(i, _):
        at = chunk_of(i)
        back = lax.dot_general(joint_ref[at, :], projection_ref[...], NT, preferred_element_type=jnp.float32)
        _, normal, spread_by = row_norm(tokens_ref[at, :].astype(jnp.float32), norms_ref[0:1, :], norms_ref[1:2, :])
        scaled = back * norms_ref[0:1, :]
        inner = (
            scaled
            - jnp.mean(scaled, axis=1, keepdims=True)
            - normal * jnp.mean(scaled * normal, axis=1, keepdims=True)
        )
        token_ref[at, :] += inner * spread_by
        vector_ref[0:1, :] += jnp.sum(back * normal, axis=0, keepdims=True)
        vector_ref[1:2, :] += jnp.sum(back, axis=0, keepdims=True)
        return 0

    def end_made(at, value):
        layer_ref[at, :] = (residual_ref[at, :] + gate_col[at, 0:1] * value).astype(jnp.bfloat16)

    def load(source, into):
        copy = fetch(2, source, into)
        copy.start()
        copy.wait()

    lax.fori_loop(0, steps // 2, finish_step, 0)
    for c, stage in ((0, 6), (1, 4), (2, 2), (3, 1)):
        sum_step(c, stage)
    lax.fori_loop(steps // 2, steps, finish_step, 0)
    tally_ref[0] = vector_ref[...]
    tally(0).start()
    for c, stage in ((0, 7), (1, 5), (2, 3), (3, 2)):
        sum_step(c, stage)
    for piece in range(4):
        to_y(1, piece).wait_send()
    load(made_all.at[0], a_ref)
    for piece in range(2):
        to_core(1, 0, piece).wait_recv()
    load(core_land.at[1, 0], b_ref)
    add_pieces(a_ref, [a_ref, b_ref], rows, 32)
    tally_step(0)
    for c, stage in ((0, 8), (1, 6), (2, 4), (3, 3)):
        sum_step(c, stage)
    for piece in range(4):
        to_y(1, piece).wait_recv()
    load(y_land.at[1], b_ref)
    add_pieces(a_ref, [a_ref, b_ref], rows, 32)
    tally_step(1)
    for c, stage in ((1, 7), (2, 5), (3, 4)):
        sum_step(c, stage)
    unsort(a_ref, end_made)
    tally_step(2)
    for c, stage in ((1, 8), (2, 6), (3, 5)):
        sum_step(c, stage)
    share_end()
    tally_step(3)
    for c, stage in ((2, 7), (3, 6)):
        sum_step(c, stage)
    tally_step(4)
    for c, stage in ((2, 8), (3, 7), (3, 8)):
        sum_step(c, stage)

    for which in range(2):
        for piece in range(2):
            for second in range(2):
                to_core(which, second, piece).wait_send()
    for k in range(3):
        dot_copy(k).wait_send()
    for sign, r in ways:
        @pl.when(target(sign, r)[1])
        def _(sign=sign, r=r):
            share_x(sign, r).wait_send()
    for sign in (1, -1):
        @pl.when(target(sign, 1)[1])
        def _(sign=sign):
            share_z(sign, 1).wait_send()
    for c in (1, 2, 3):
        sum_sent(c)
    for c in range(4):
        for d in range(1, planes):
            sum_copy(c, "zz", d).wait_send()
        for stage in ("second back", "first back", "cc"):
            sum_copy(c, stage).wait_send()
    for k in range(len(rounds)):
        tally(k).wait_send()
    assert len(ids) <= send_sem.shape[0]


def rear_stage(
    tokens, norms, projection, mixing, centroids, route, lengths, cotangent,
    flipped, joint, mixed, logs, residual, place, loads, dots, back, made, near, far, planes, slabs, total_tokens,
):
    count, width = tokens.shape
    rows = back.shape[1]
    half = width // 2
    bf16, f32 = jnp.bfloat16, jnp.float32
    shape = jax.ShapeDtypeStruct
    anywhere = pl.BlockSpec(memory_space=pl.ANY)
    local = pl.BlockSpec(memory_space=pltpu.VMEM)
    dma = pltpu.SemaphoreType.DMA
    packed = near.shape[1:]
    outs = [
        (shape((count, width), bf16), local),
        (shape((count, width), f32), local),
        (shape((16, width), f32), local),
        (shape((width, half), f32), local),
        (shape((half, width), f32), local),
        (shape((4, width, width), bf16), anywhere),
        (shape((2, 2, rows, width), bf16), anywhere),
        (shape((2, rows, width), bf16), anywhere),
        (shape((planes,) + packed, bf16), anywhere),
        (shape((2, planes - 1) + packed, bf16), anywhere),
    ]
    copies = 120
    return pl.pallas_call(
        partial(rear_kernel, planes, slabs, total_tokens),
        out_shape=[o[0] for o in outs],
        in_specs=[pl.BlockSpec(memory_space=pltpu.SMEM)]
        + [local] * 8
        + [anywhere]
        + [local] * 2
        + [anywhere]
        + [local] * 3
        + [anywhere] * 4,
        out_specs=[o[1] for o in outs],
        scratch_shapes=[
            pltpu.VMEM((count, 3 * width), bf16),
            pltpu.VMEM((count, width), f32),
            pltpu.VMEM((count, count), f32),
            pltpu.VMEM((count, width), bf16),
            pltpu.VMEM((rows, width), bf16),
            pltpu.VMEM((rows, width), bf16),
            pltpu.VMEM((count, 8), f32),
            pltpu.VMEM((count, 128), f32),
            pltpu.VMEM((3, 8, rows), f32),
            pltpu.VMEM((2,) + packed, bf16),
            pltpu.VMEM((2,) + packed, bf16),
            pltpu.VMEM((3, width, width), bf16),
            pltpu.VMEM((4, width // 2, width), bf16),
            pltpu.VMEM((4, width // 4, width), bf16),
            pltpu.VMEM((4, width // 8, width), bf16),
            pltpu.VMEM((4, planes - 1, width // 16, half), bf16),
            pltpu.VMEM((4, width // 16, half), bf16),
            pltpu.VMEM((10, 16, width), f32),
            pltpu.VMEM((2, count, 128), f32),
            dma((copies,)),
            dma((copies,)),
            dma((8,)),
        ],
        compiler_params=pltpu.CompilerParams(
            collective_id=1, has_side_effects=True, vmem_limit_bytes=VMEM_LIMIT
        ),
    )(
        lengths[0],
        tokens,
        norms,
        projection,
        mixing,
        centroids,
        route,
        cotangent,
        flipped,
        joint,
        mixed,
        logs,
        residual,
        place,
        loads,
        dots,
        back,
        made,
        near,
        far,
    )


TILE = 256
ALIGN = 16


def aligned_rows(count, experts):
    return -(-(count + experts * (ALIGN - 1)) // ALIGN) * ALIGN


def gelu_pair(values):
    bell = jnp.exp2(values * values * (-0.5 * HALF_LOG))
    near = 1.0 / (1.0 + (0.3275911 * 0.7071067811865476) * jnp.abs(values))
    series = 1.061405429 * 0.5 * near - 1.453152027 * 0.5
    series = series * near + 1.421413741 * 0.5
    series = series * near - 0.284496736 * 0.5
    series = series * near + 0.254829592 * 0.5
    tail = series * near * bell
    below = jnp.where(values >= 0.0, 1.0 - tail, tail)
    return values * below, below + values * bell * 0.3989422804014327


def expert_kernel_body(
    experts,
    sources,
    limit,
    meta_ref,
    sent_all,
    cot_all,
    gate_all,
    up_near,
    up_far,
    down_near,
    down_far,
    back_all,
    made_all,
    dots_all,
    near_out,
    far_out,
    table,
    x_ref,
    c_ref,
    g_ref,
    column_ref,
    up_ref,
    down_ref,
    gu_ref,
    gd_ref,
    pack_ref,
    zero_ref,
    weight_sem,
    in_sem,
    out_sem,
    grad_sem,
    zero_sem,
):
    rows, width = sent_all.shape[1:]
    half = up_near.shape[2]
    own = meta_ref[0]
    spots = sources * experts

    base = 0
    ends = [0] * sources
    for e in range(experts):
        at = base
        for s in range(sources):
            size = meta_ref[1 + s * experts + e]
            table[0, e * sources + s] = size
            table[1, e * sources + s] = ends[s]
            table[2, e * sources + s] = at
            ends[s] = ends[s] + size
            at = at + size
        number = (at - base + (TILE - 1)) // TILE
        table[3, e] = base
        table[4, e] = number
        base = base + number * TILE
    for s in range(sources):
        table[5, s] = ends[s]

    bits = [1 << b for b in range(limit.bit_length()) if ALIGN <= (1 << b)]

    def move(k, act, outward):
        s, e = lax.rem(k, sources), lax.div(k, sources)
        size = table[0, k]
        for piece in bits:
            @pl.when((size & piece) != 0)
            def _(piece=piece):
                offset = size & (piece - 1)
                src = pl.ds(pl.multiple_of(table[1, k] + offset, ALIGN), piece)
                dst = pl.ds(pl.multiple_of(table[2, k] + offset, ALIGN), piece)
                if outward:
                    act(pltpu.make_async_copy(x_ref.at[dst], made_all.at[s, src], out_sem.at[0]))
                    act(pltpu.make_async_copy(c_ref.at[dst], back_all.at[s, src], out_sem.at[1]))
                else:
                    act(pltpu.make_async_copy(sent_all.at[s, src], x_ref.at[dst], in_sem.at[e, 0]))
                    act(pltpu.make_async_copy(cot_all.at[s, src], c_ref.at[dst], in_sem.at[e, 1]))

    def each(low, high, act):
        def one(i, _):
            act(i)
            return 0
        lax.fori_loop(low, high, one, 0)

    def begin(copy):
        copy.start()

    def end(copy):
        copy.wait()

    def move_weights(e, act):
        slot = e - own + experts - 1
        for j, (ups, downs) in enumerate(((up_near, down_near), (up_far, down_far))):
            part = pl.ds(j * half, half)
            act(pltpu.make_async_copy(ups.at[slot], up_ref.at[e, :, part], weight_sem.at[e, j, 0]))
            act(pltpu.make_async_copy(downs.at[slot], down_ref.at[e, part], weight_sem.at[e, j, 1]))

    zero_ref[...] = jnp.zeros_like(zero_ref)

    def bring(e):
        @pl.when(table[4, e] > 0)
        def _():
            last = pl.ds(pl.multiple_of(table[3, e] + (table[4, e] - 1) * TILE, TILE), TILE)
            x_ref[last, :] = jnp.zeros((TILE, width), jnp.bfloat16)
            c_ref[last, :] = jnp.zeros((TILE, width), jnp.bfloat16)
            g_ref[last, :] = jnp.zeros((TILE, 128), jnp.float32)

        move_weights(e, begin)
        each(e * sources, (e + 1) * sources, lambda k: move(k, begin, False))

    each(0, experts, bring)

    chunks = experts + 1

    def tail(k, act):
        s, i = lax.div(k, chunks), lax.rem(k, chunks) + rows // ALIGN - chunks

        @pl.when(i * ALIGN >= table[5, s])
        def _():
            dst = pl.ds(pl.multiple_of(i * ALIGN, ALIGN), ALIGN)
            act(pltpu.make_async_copy(zero_ref, made_all.at[s, dst], zero_sem.at[0]))
            act(pltpu.make_async_copy(zero_ref, back_all.at[s, dst], zero_sem.at[1]))

    each(0, sources * chunks, lambda k: tail(k, begin))

    def shift(s, outward):
        def segment(e):
            k = e * sources + s

            def one(i):
                src = pl.ds(pl.multiple_of(table[1, k] + i * ALIGN, ALIGN), ALIGN)
                dst = pl.ds(pl.multiple_of(table[2, k] + i * ALIGN, ALIGN), ALIGN)
                if outward:
                    column_ref[src, :] = g_ref[dst, :]
                else:
                    g_ref[dst, :] = column_ref[src, :]

            each(0, table[0, k] // ALIGN, one)

        each(0, experts, segment)

    def gates_in(s):
        column_ref[...] = jnp.transpose(jnp.broadcast_to(gate_all[s, 0:1, :], (128, rows)))
        shift(s, False)

    each(0, sources, gates_in)

    def grads(e):
        slot = lax.rem(e, 2)
        return [
            pltpu.make_async_copy(pack_ref.at[slot, j], ref.at[e], grad_sem.at[slot, j])
            for j, ref in enumerate((near_out, far_out))
        ]

    def work(e):
        move_weights(e, end)
        each(e * sources, (e + 1) * sources, lambda k: move(k, end, False))
        gu_ref[...] = jnp.zeros_like(gu_ref)
        gd_ref[...] = jnp.zeros_like(gd_ref)

        def tile(t):
            at = pl.ds(pl.multiple_of(table[3, e] + t * TILE, TILE), TILE)
            x, c, gate = x_ref[at, :], c_ref[at, :], g_ref[at, 0:1]
            before = jnp.dot(x, up_ref[e], preferred_element_type=jnp.float32)
            active, slope = gelu_pair(before)
            through = lax.dot_general(c, down_ref[e], NT, preferred_element_type=jnp.float32)
            grad = (through * (slope * gate)).astype(jnp.bfloat16)
            gated = (active * gate).astype(jnp.bfloat16)
            made = jnp.dot(active.astype(jnp.bfloat16), down_ref[e], preferred_element_type=jnp.float32)
            g_ref[at, :] = jnp.broadcast_to(
                jnp.sum(made * c.astype(jnp.float32), axis=1, keepdims=True), (TILE, 128)
            )
            gd_ref[...] += lax.dot_general(gated, c, TN, preferred_element_type=jnp.float32)
            gu_ref[...] += lax.dot_general(x, grad, TN, preferred_element_type=jnp.float32)
            back = lax.dot_general(grad, up_ref[e], NT, preferred_element_type=jnp.float32)
            x_ref[at, :] = made.astype(jnp.bfloat16)
            c_ref[at, :] = back.astype(jnp.bfloat16)

        each(0, table[4, e], tile)
        each(e * sources, (e + 1) * sources, lambda k: move(k, begin, True))

        @pl.when(e >= 2)
        def _():
            for copy in grads(e - 2):
                copy.wait()

        slot = lax.rem(e, 2)
        for j in range(2):
            pack_ref[slot, j, 0:width, :] = gu_ref[:, j * half : (j + 1) * half].astype(jnp.bfloat16)
            for part in range(2):
                pack_ref[slot, j, width + part * half : width + (part + 1) * half, :] = gd_ref[
                    j * half : (j + 1) * half, part * half : (part + 1) * half
                ].astype(jnp.bfloat16)
        for copy in grads(e):
            copy.start()

    each(0, experts, work)

    def sums_out(s):
        shift(s, True)
        dots_all[s] = jnp.transpose(column_ref[...])[0:8, :]

    each(0, sources, sums_out)
    each(0, spots, lambda k: move(k, end, True))
    each(0, sources * chunks, lambda k: tail(k, end))
    for e in range(max(0, experts - 2), experts):
        for copy in grads(e):
            copy.wait()


def expert_stage(meta, sent, cot, gates, weights, experts, limit):
    sources, rows, width = sent.shape
    half = weights[0].shape[2]
    hidden = 2 * half
    joined = -(-(sources * rows + experts * (TILE - 1)) // TILE) * TILE
    limit = -(-limit // ALIGN) * ALIGN
    anywhere = pl.BlockSpec(memory_space=pl.ANY)
    local = pl.BlockSpec(memory_space=pltpu.VMEM)
    dma = pltpu.SemaphoreType.DMA
    packed = (width + hidden, half)
    return pl.pallas_call(
        partial(expert_kernel_body, experts, sources, limit),
        out_shape=(
            jax.ShapeDtypeStruct((sources, rows, width), jnp.bfloat16),
            jax.ShapeDtypeStruct((sources, rows, width), jnp.bfloat16),
            jax.ShapeDtypeStruct((sources, 8, rows), jnp.float32),
            jax.ShapeDtypeStruct((experts,) + packed, jnp.bfloat16),
            jax.ShapeDtypeStruct((experts,) + packed, jnp.bfloat16),
        ),
        in_specs=[pl.BlockSpec(memory_space=pltpu.SMEM)] + [anywhere] * 2 + [local] + [anywhere] * 4,
        out_specs=(anywhere, anywhere, local, anywhere, anywhere),
        scratch_shapes=[
            pltpu.SMEM((6, sources * experts), jnp.int32),
            pltpu.VMEM((joined, width), jnp.bfloat16),
            pltpu.VMEM((joined, width), jnp.bfloat16),
            pltpu.VMEM((joined, 128), jnp.float32),
            pltpu.VMEM((rows, 128), jnp.float32),
            pltpu.VMEM((experts, width, hidden), jnp.bfloat16),
            pltpu.VMEM((experts, hidden, width), jnp.bfloat16),
            pltpu.VMEM((width, hidden), jnp.float32),
            pltpu.VMEM((hidden, width), jnp.float32),
            pltpu.VMEM((2, 2) + packed, jnp.bfloat16),
            pltpu.VMEM((ALIGN, width), jnp.bfloat16),
            dma((experts, 2, 2)),
            dma((experts, 2)),
            dma((2,)),
            dma((2, 2)),
            dma((2,)),
        ],
        compiler_params=pltpu.CompilerParams(vmem_limit_bytes=VMEM_LIMIT),
        cost_estimate=pl.CostEstimate(
            flops=12 * sources * rows * width * hidden, bytes_accessed=100_000_000, transcendentals=sources * rows * hidden
        ),
    )(meta, sent, cot, gates, *weights)


def arrange(shared, layer, token, vectors, up, down, experts):
    count, width = layer.shape
    third, half = width // 3, width // 2
    steps = 6

    def kernel(shared_ref, layer_ref, token_ref, vectors_ref, up_ref, down_ref, *outs):
        mixing_out, projection_out, layer_out, token_out, up_out, down_out, *vector_outs, centroids_out, balance_out = outs
        mixing_out[...] = shared_ref[0].astype(jnp.float32)
        for k in range(3):
            for c in range(3):
                at = k * width + c * third
                projection_out[:, at : at + third] = shared_ref[1 + c, :, k * third : (k + 1) * third].astype(jnp.float32)
        layer_out[...] = layer_ref[...]
        token_out[...] = token_ref[...]
        up_out[0] = up_ref[...]
        down_out[0] = down_ref[...]
        for i, out in enumerate(vector_outs):
            out[...] = vectors_ref[i]
        centroids_out[...] = vectors_ref[8 : 8 + experts, :]
        balance_out[...] = vectors_ref[4:5, 0:128]

    f32 = jnp.float32
    shape = jax.ShapeDtypeStruct
    rows = lambda n, m: pl.BlockSpec((n // steps, m), lambda i: (i, 0))
    slab = lambda n, m: pl.BlockSpec((1, n // steps, m), lambda i: (0, i, 0))
    whole = lambda *dims: pl.BlockSpec(dims, lambda i: (0,) * len(dims))
    return pl.pallas_call(
        kernel,
        out_shape=[
            shape((width, width), f32),
            shape((width, 3 * width), f32),
            shape((count, width), jnp.bfloat16),
            shape((count, width), f32),
            shape((1, width, half), f32),
            shape((1, half, width), f32),
        ]
        + [shape((width,), f32)] * 4
        + [shape((experts, width), f32), shape((1, 128), f32)],
        grid=(steps,),
        in_specs=[
            pl.BlockSpec((4, width // steps, width), lambda i: (0, i, 0)),
            rows(count, width),
            rows(count, width),
            whole(16, width),
            rows(width, half),
            rows(half, width),
        ],
        out_specs=[
            rows(width, width),
            rows(width, 3 * width),
            rows(count, width),
            rows(count, width),
            slab(width, half),
            slab(half, width),
        ]
        + [whole(width)] * 4
        + [whole(experts, width), whole(1, 128)],
        compiler_params=pltpu.CompilerParams(vmem_limit_bytes=VMEM_LIMIT),
    )(shared, layer, token, vectors, up, down)


def per_device(
    tokens,
    gains,
    shifts,
    projection,
    mixing,
    factors,
    biases,
    centroids,
    expanding,
    contracting,
    routes,
    lengths,
    cotangent,
):
    count, width = tokens.shape
    experts = centroids.shape[0]
    groups = lax.axis_size("expert")
    slabs = groups // experts
    limit = 2 * count // experts
    total_tokens = count * groups * lax.axis_size("tensor")

    norms = jnp.stack((gains, shifts, factors, biases))
    flipped, joint, mixed, logs, residual, place, loads, sent, cot, gates, *weights = front_stage(
        tokens, norms, projection, mixing, centroids, expanding, contracting, routes, lengths, cotangent, experts, slabs
    )
    meta = jnp.concatenate(
        [lax.div(lax.axis_index("expert"), slabs)[None], gates[:, 1, :experts].reshape(-1).astype(jnp.int32)]
    )
    back, made, dots, near, far = expert_stage(meta, sent, cot, gates, weights, experts, limit)
    layer, token, vectors, up, down, shared, *_ = rear_stage(
        tokens, norms, projection, mixing, centroids, routes, lengths, cotangent,
        flipped, joint, mixed, logs, residual, place, loads, dots, back, made, near, far, experts, slabs, total_tokens,
    )
    (
        mixing_grad, projection_grad, layer_output, token_grad, up_grad, down_grad,
        gain_grad, shift_grad, factor_grad, bias_grad, centroid_grad, balance,
    ) = arrange(shared, layer, token, vectors, up, down, experts)
    return (
        layer_output,
        balance[0, 0],
        token_grad,
        gain_grad,
        shift_grad,
        projection_grad,
        mixing_grad,
        factor_grad,
        bias_grad,
        centroid_grad,
        up_grad,
        down_grad,
    )


def solution(mesh):
    placed = (
        P(("expert", "tensor"), None),
        P(),
        P(),
        P(),
        P(),
        P(),
        P(),
        P(),
        P("expert", None, "tensor"),
        P("expert", "tensor", None),
        P(("expert", "tensor"), None),
        P(("expert", "tensor"), None),
        P(("expert", "tensor"), None),
    )
    near = mesh.shape["expert"] == 16 and mesh.shape["tensor"] == 2
    return jax.shard_map(
        per_device if near else moving_tokens,
        mesh=mesh,
        in_specs=placed,
        out_specs=(
            P(("expert", "tensor"), None),
            P(),
            P(("expert", "tensor"), None),
            P(),
            P(),
            P(),
            P(),
            P(),
            P(),
            P(),
            P("expert", None, "tensor"),
            P("expert", "tensor", None),
        ),
        check_vma=False,
    )
```

```python
from functools import partial

import jax
import jax.numpy as jnp
from jax import lax
from jax.experimental import pallas as pl
from jax.experimental.pallas import tpu as pltpu
from jax.sharding import PartitionSpec as P

HEADS = 12


highest = lax.Precision.HIGHEST
epsilon = 1e-05


def running(values):
    places = jnp.arange(values.shape[0])
    return jnp.sum(jnp.where(places[:, None] >= places[None, :], values[None, :], 0), axis=1)


def earlier(picks):
    places = jnp.arange(picks.shape[0])
    before = (places[:, None] > places[None, :]).astype(jnp.bfloat16)
    return jnp.dot(
        before, picks.astype(jnp.bfloat16), preferred_element_type=jnp.float32
    ).astype(jnp.int32)


def norm_parts(values, gain, shift):
    centered = values - jnp.mean(values, axis=1, keepdims=True)
    scale = lax.rsqrt(jnp.mean(centered * centered, axis=1, keepdims=True) + epsilon)
    normal = centered * scale
    return (normal * gain + shift, normal, scale)


def norm_back(upstream, normal, scale, gain):
    scaled = upstream * gain
    inner = (
        scaled
        - jnp.mean(scaled, axis=1, keepdims=True)
        - normal * jnp.mean(scaled * normal, axis=1, keepdims=True)
    )
    return (inner * scale, jnp.sum(upstream * normal, axis=0), jnp.sum(upstream, axis=0))


def gelu_slope(values):
    return (
        0.5 * (1.0 + lax.erf(values * 0.7071067811865476))
        + values * jnp.exp(-0.5 * values * values) * 0.3989422804014327
    )


def expert_forward(gathered, upward, downward):
    before = jnp.dot(gathered, upward, preferred_element_type=jnp.float32)
    active = jax.nn.gelu(before, approximate=False).astype(jnp.bfloat16)
    return jnp.dot(active, downward, preferred_element_type=jnp.float32)


def expert_backward(gathered, incoming, upward, downward):
    before = jnp.dot(gathered, upward, preferred_element_type=jnp.float32)
    active = jax.nn.gelu(before, approximate=False).astype(jnp.bfloat16)
    down_grad = jnp.einsum("rf,rd->fd", active, incoming, preferred_element_type=jnp.float32)
    through = jnp.einsum("rd,fd->rf", incoming, downward, preferred_element_type=jnp.float32)
    hidden_grad = (through * gelu_slope(before)).astype(jnp.bfloat16)
    up_grad = jnp.einsum("rd,rf->df", gathered, hidden_grad, preferred_element_type=jnp.float32)
    return (up_grad, down_grad, hidden_grad)


def head_forward(allowed, item):
    query, keys, values = item
    factor = query.shape[1] ** (-0.5)
    scores = jnp.einsum("qd,kd->qk", query, keys, preferred_element_type=jnp.float32) * factor
    scores = jnp.where(allowed, scores, -1000000000.0)
    peak = jnp.max(scores, axis=1, keepdims=True)
    weights = jnp.exp(scores - peak)
    total = jnp.sum(weights, axis=1, keepdims=True)
    mixed = jnp.dot(
        (weights / total).astype(jnp.bfloat16), values, preferred_element_type=jnp.float32
    )
    return (mixed.astype(jnp.bfloat16), (peak + jnp.log(total))[:, 0])


def head_backward(allowed, item):
    query, keys, values, upstream, log_total = item
    factor = query.shape[1] ** (-0.5)
    scores = jnp.einsum("qd,kd->qk", query, keys, preferred_element_type=jnp.float32) * factor
    scores = jnp.where(allowed, scores, -1000000000.0)
    probs = jnp.exp(scores - log_total[:, None])
    value_grad = jnp.einsum(
        "qk,qd->kd", probs.astype(jnp.bfloat16), upstream, preferred_element_type=jnp.float32
    )
    prob_grad = jnp.einsum("qd,kd->qk", upstream, values, preferred_element_type=jnp.float32)
    inner = jnp.sum(prob_grad * probs, axis=1, keepdims=True)
    score_grad = (probs * (prob_grad - inner)).astype(jnp.bfloat16)
    query_grad = (
        jnp.einsum("qk,kd->qd", score_grad, keys, preferred_element_type=jnp.float32) * factor
    )
    key_grad = (
        jnp.einsum("qk,qd->kd", score_grad, query, preferred_element_type=jnp.float32) * factor
    )
    return (query_grad, key_grad, value_grad)


def moving_tokens(
    tokens,
    gains,
    shifts,
    projection,
    mixing,
    factors,
    biases,
    centroids,
    expanding,
    contracting,
    routes,
    lengths,
    cotangent,
):
    count, width = tokens.shape
    experts = centroids.shape[0]
    groups = lax.axis_size("expert")
    slab_count = groups // experts
    capacity = max(2, 2 * count // experts)
    total_tokens = count * groups * lax.axis_size("tensor")
    average = total_tokens / experts
    route = routes[:, 0]
    picks = route[:, None] == jnp.arange(experts, dtype=jnp.int32)[None, :]
    picks_int = picks.astype(jnp.int32)
    picks_float = picks.astype(jnp.float32)
    loads = lax.psum(jnp.sum(picks_float, axis=0), ("expert", "tensor"))
    spread = (loads - average) / average
    token_spread = jnp.sum(jnp.where(picks, spread[None, :], 0.0), axis=1)
    ranks = jnp.sum(earlier(picks) * picks_int, axis=1)
    slots = route * capacity + ranks
    places = jnp.arange(count, dtype=jnp.int32)
    documents = jnp.sum(
        (places[:, None] >= running(lengths[0])[None, :]).astype(jnp.int32), axis=1
    )
    allowed = (places[:, None] >= places[None, :]) & (documents[:, None] == documents[None, :])
    inputs = tokens.astype(jnp.float32)
    entry, entry_normal, entry_scale = norm_parts(inputs, gains, shifts)
    entry = entry.astype(jnp.bfloat16)
    joint = jnp.dot(entry, projection, preferred_element_type=jnp.float32).astype(jnp.bfloat16)
    heads = joint.reshape(count, 3, HEADS, width // HEADS).transpose(1, 2, 0, 3)
    mixed, log_total = lax.map(partial(head_forward, allowed), (heads[0], heads[1], heads[2]))
    mixed_rows = mixed.transpose(1, 0, 2).reshape(count, width)
    residual = inputs + jnp.dot(mixed_rows, mixing, preferred_element_type=jnp.float32)
    normed, mixer_normal, mixer_scale = norm_parts(residual, factors, biases)
    chosen = jnp.dot(picks.astype(jnp.bfloat16), centroids, preferred_element_type=jnp.float32)
    gates = jax.nn.sigmoid(jnp.sum(normed * chosen, axis=1))
    outgoing = (
        jnp.zeros((experts * capacity, width), jnp.bfloat16)
        .at[slots]
        .set(normed.astype(jnp.bfloat16))
    )
    copies = jnp.broadcast_to(
        outgoing.reshape(experts, 1, capacity, width), (experts, slab_count, capacity, width)
    ).reshape(groups, capacity, width)
    arrived = lax.all_to_all(copies, "expert", split_axis=0, concat_axis=0, tiled=True)
    sources = groups * capacity
    own_rows = arrived.reshape(sources, width)
    gathered = lax.all_gather(own_rows, "tensor", axis=0, tiled=True)
    produced = lax.psum_scatter(
        expert_forward(gathered, expanding[0], contracting[0]).astype(jnp.bfloat16),
        "tensor",
        scatter_dimension=0,
        tiled=True,
    )
    returned = lax.all_to_all(
        produced.reshape(arrived.shape), "expert", split_axis=0, concat_axis=0, tiled=True
    )
    combined = jnp.sum(
        returned.reshape(experts, slab_count, capacity, width).astype(jnp.float32), axis=1
    ).reshape(experts * capacity, width)
    picked = combined[slots]
    layer_output = (residual + gates[:, None] * picked).astype(jnp.bfloat16)
    balance_part = jnp.sum(token_spread * gates) / total_tokens
    upstream = cotangent.astype(jnp.float32)
    gate_grad = jnp.sum(upstream * picked, axis=1)
    logit_grad = (gate_grad + token_spread / total_tokens) * gates * (1.0 - gates)
    scaled_rows = (gates[:, None] * upstream).astype(jnp.bfloat16)
    grad_slots = jnp.zeros((experts * capacity, width), jnp.bfloat16).at[slots].set(scaled_rows)
    grad_copies = jnp.broadcast_to(
        grad_slots.reshape(experts, 1, capacity, width), (experts, slab_count, capacity, width)
    ).reshape(groups, capacity, width)
    incoming = lax.all_to_all(
        grad_copies, "expert", split_axis=0, concat_axis=0, tiled=True
    ).reshape(sources, width)
    incoming_pair = lax.all_gather(incoming, "tensor", axis=0, tiled=True)
    up_share, down_share, hidden_grad = expert_backward(
        gathered, incoming_pair, expanding[0], contracting[0]
    )
    back_rows = lax.psum_scatter(
        jnp.einsum(
            "rf,df->rd", hidden_grad, expanding[0], preferred_element_type=jnp.float32
        ).astype(jnp.bfloat16),
        "tensor",
        scatter_dimension=0,
        tiled=True,
    )
    back = lax.all_to_all(
        back_rows.reshape(arrived.shape), "expert", split_axis=0, concat_axis=0, tiled=True
    )
    back_sum = jnp.sum(
        back.reshape(experts, slab_count, capacity, width).astype(jnp.float32), axis=1
    ).reshape(experts * capacity, width)
    normed_grad = back_sum[slots] + logit_grad[:, None] * chosen
    centroid_grad = jnp.einsum(
        "te,td->ed", picks_float, logit_grad[:, None] * normed, precision=highest
    )
    mixer_back, factor_grad, bias_grad = norm_back(normed_grad, mixer_normal, mixer_scale, factors)
    residual_grad = upstream + mixer_back
    branch_grad = residual_grad.astype(jnp.bfloat16)
    mixing_grad = jnp.einsum(
        "td,te->de", mixed_rows, branch_grad, preferred_element_type=jnp.float32
    )
    mixed_grad = jnp.einsum(
        "te,de->td", branch_grad, mixing, preferred_element_type=jnp.float32
    ).astype(jnp.bfloat16)
    head_grads = mixed_grad.reshape(count, HEADS, width // HEADS).transpose(1, 0, 2)
    query_grad, key_grad, value_grad = lax.map(
        partial(head_backward, allowed), (heads[0], heads[1], heads[2], head_grads, log_total)
    )
    joint_grad = (
        jnp.stack((query_grad, key_grad, value_grad))
        .transpose(2, 0, 1, 3)
        .reshape(count, 3 * width)
        .astype(jnp.bfloat16)
    )
    projection_grad = jnp.einsum("td,te->de", entry, joint_grad, preferred_element_type=jnp.float32)
    entry_back = jnp.einsum("te,de->td", joint_grad, projection, preferred_element_type=jnp.float32)
    entry_input, gain_grad, shift_grad = norm_back(entry_back, entry_normal, entry_scale, gains)
    token_grad = residual_grad + entry_input
    summed = lax.psum(
        (
            gain_grad,
            shift_grad,
            projection_grad,
            mixing_grad,
            factor_grad,
            bias_grad,
            centroid_grad,
            balance_part,
        ),
        ("expert", "tensor"),
    )
    return (
        layer_output,
        summed[7],
        token_grad,
        summed[0],
        summed[1],
        summed[2],
        summed[3],
        summed[4],
        summed[5],
        summed[6],
        up_share[None],
        down_share[None],
    )


HALF_LOG = 1.4426950408889634
LN2 = 0.6931471805599453
NT = (((1,), (1,)), ((), ()))
TN = (((0,), (0,)), ((), ()))
VMEM_LIMIT = 60 * 1024 * 1024


def query_blocks(count):
    step = 256 if count > 256 else count
    return [(i, min(i + step, count)) for i in range(0, count, step)]


def document_starts(lengths_ref, places):
    starts = jnp.zeros_like(places)
    end = 0
    for d in range(lengths_ref.shape[0]):
        end = end + lengths_ref[d]
        starts = jnp.where(places >= end, end, starts)
    return starts


MESH = pl.DeviceIdType.MESH


def neighbours(slabs):
    me, core = lax.axis_index("expert"), lax.axis_index("tensor")
    plane = lax.div(me, slabs)
    x = lax.rem(me, 2)
    y = lax.rem(lax.div(me, 2), 2)
    return me, core, plane, (me + 1 - 2 * x, core), (me + 2 - 4 * y, core), (me, 1 - core)


def greet(partners):
    barrier = pltpu.get_barrier_semaphore()
    number = 0
    for device, there in partners:
        @pl.when(there)
        def _(device=device):
            pl.semaphore_signal(barrier, inc=1, device_id=device, device_id_type=MESH)
        number = number + there.astype(jnp.int32)
    pl.semaphore_wait(barrier, number)


def score_bias(bias_ref, lengths_ref, count):
    places = lax.broadcasted_iota(jnp.int32, (1, count), 1)
    starts = document_starts(lengths_ref, places)
    for s, e in query_blocks(count):
        row = lax.broadcasted_iota(jnp.int32, (e - s, count), 0) + s
        seen = (row <= places) & (row >= starts)
        bias_ref[s:e, :] = jnp.where(seen, 0.0, -1e9)


def row_norm(values, gain, shift):
    centered = values - jnp.mean(values, axis=1, keepdims=True)
    scale = lax.rsqrt(jnp.mean(centered * centered, axis=1, keepdims=True) + epsilon)
    normal = centered * scale
    return normal * gain + shift, normal, scale


def chosen_rows(route, centroids_ref, experts):
    chosen = jnp.zeros((route.shape[0], centroids_ref.shape[1]), jnp.float32)
    for e in range(experts):
        chosen = jnp.where(route == e, centroids_ref[e : e + 1, :].astype(jnp.float32), chosen)
    return chosen


def front_kernel(
    planes,
    slabs,
    lengths_ref,
    tokens_ref,
    norms_ref,
    projection_ref,
    mixing_ref,
    centroids_ref,
    route_row_ref,
    route_ref,
    cot_ref,
    up_ref,
    down_ref,
    flipped_ref,
    joint_ref,
    mixed_ref,
    logs_ref,
    residual_ref,
    place_ref,
    loads_ref,
    sent_all,
    cot_all,
    gate_all,
    up_near,
    up_far,
    down_near,
    down_far,
    bias_ref,
    order_ref,
    normed_ref,
    entry_ref,
    sent_own,
    cot_own,
    gate_own,
    tally_ref,
    send_sem,
    recv_sem,
    local_sem,
):
    count, width = tokens_ref.shape
    experts = planes
    rows = sent_own.shape[0]
    half_rows = rows // 2
    pairs = width // 128
    factor = (width // HEADS) ** (-0.5) * HALF_LOG
    middle = planes - 1
    me, core, plane, beside_x, beside_y, beside_core = neighbours(slabs)
    hop_two = lax.rem(plane + 2, planes)
    hop_one = plane + 1 - 2 * lax.rem(plane, 2)
    here = lax.rem(me, slabs)
    always = plane >= 0
    greet(
        [
            (beside_x, always),
            (beside_y, always),
            (beside_core, always),
            ((hop_two * slabs + here, core), always),
            ((me + slabs, core), plane < planes - 1),
            ((me - slabs, core), plane > 0),
        ]
    )

    def remote(i, src, dst, device):
        return pltpu.make_async_remote_copy(
            src_ref=src, dst_ref=dst, send_sem=send_sem.at[i], recv_sem=recv_sem.at[i], device_id=device, device_id_type=MESH
        )

    owns, nears, fars = (up_ref, down_ref), (up_near, down_near), (up_far, down_far)
    stride = 2 * (planes - 1) + 2 * planes - 1

    def hop(kind, sign, r):
        src = owns[kind].at[0] if r == 1 else nears[kind].at[middle - sign * (r - 1)]
        i = kind * stride + (r - 1) * 2 + (sign > 0)
        return remote(i, src, nears[kind].at[middle - sign * r], (me + sign * slabs, core))

    def hop_sent(sign, r):
        ahead = plane if sign > 0 else planes - 1 - plane
        return (ahead >= r - 1) & (ahead < planes - 1)

    def hop_came(sign, r):
        ahead = plane if sign > 0 else planes - 1 - plane
        return ahead >= r

    def aside(kind, slot):
        src = owns[kind].at[0] if slot == middle else nears[kind].at[slot]
        i = kind * stride + 2 * (planes - 1) + slot
        return remote(i, src, fars[kind].at[slot], beside_x)

    def held(slot):
        at = plane + slot - middle
        return (at >= 0) & (at < planes)

    def handed(kind, sign):
        i = copies_end + kind
        return remote(i, fars[kind].at[middle], fars[kind].at[middle - sign], (me + sign * slabs, core))

    def aside_there(slot):
        if slot == middle - 1:
            return held(slot) & (plane != 1)
        if slot == middle + 1:
            return held(slot) & (plane != planes - 2)
        return held(slot)

    def own_weights(kind):
        return pltpu.make_async_copy(owns[kind].at[0], nears[kind].at[middle], local_sem.at[kind])

    for kind in range(2):
        for sign in (1, -1):
            @pl.when(hop_sent(sign, 1))
            def _(kind=kind, sign=sign):
                hop(kind, sign, 1).start()
        aside(kind, middle).start()
        own_weights(kind).start()

    def forward_weights(kind, r):
        for sign in (1, -1):
            slot = middle - sign * r

            @pl.when(hop_came(sign, r))
            def _(sign=sign):
                hop(kind, sign, r).wait_recv()

            @pl.when(aside_there(slot))
            def _(slot=slot):
                aside(kind, slot).start()

            if r < planes - 1:
                @pl.when(hop_sent(sign, r + 1))
                def _(sign=sign):
                    hop(kind, sign, r + 1).start()

    base = 2 * stride
    copies_end = base + 20

    def hand_on(kind):
        aside(kind, middle).wait_recv()
        for sign in (1, -1):
            @pl.when(plane == (0 if sign > 0 else planes - 1))
            def _(sign=sign):
                handed(kind, sign).start()

    def row_copy(which, part, piece):
        own, everyone = ((cot_own, cot_all), (sent_own, sent_all))[which]
        at = pl.ds(piece * half_rows, half_rows)
        i = base + which * 6 + part * 2 + piece
        if part == 0:
            return remote(i, own.at[at], everyone.at[2, at], beside_y)
        if part == 1:
            return remote(i, own.at[at], everyone.at[1, at], beside_core)
        return remote(i, everyone.at[2, at], everyone.at[3, at], beside_core)

    def gate_copy(part):
        i = base + 12 + part
        if part == 0:
            return remote(i, gate_own, gate_all.at[2], beside_y)
        if part == 1:
            return remote(i, gate_own, gate_all.at[1], beside_core)
        return remote(i, gate_all.at[2], gate_all.at[3], beside_core)

    def own_rows(which):
        source, everyone = ((cot_own, cot_all), (sent_own, sent_all), (gate_own, gate_all))[which]
        return pltpu.make_async_copy(source, everyone.at[0], local_sem.at[2 + which])

    rounds = [beside_core, beside_x, beside_y, (hop_one * slabs + here, core), (hop_two * slabs + here, core)]

    def tally(k):
        return remote(base + 15 + k, tally_ref.at[2 * k], tally_ref.at[2 * k + 1], rounds[k])

    def tally_step(k):
        tally(k).wait_recv()
        total = tally_ref[2 * k] + tally_ref[2 * k + 1]
        if k + 1 < len(rounds):
            tally_ref[2 * k + 2] = total
            tally(k + 1).start()
        else:
            loads_ref[...] = total

    number = lax.broadcasted_iota(jnp.int32, (8, count), 0)
    picks = jnp.where(number == route_row_ref[...], 1.0, 0.0)
    chunk = 128
    for s in range(0, count, chunk):
        row = lax.broadcasted_iota(jnp.int32, (chunk, count), 0) + s
        column = lax.broadcasted_iota(jnp.int32, (chunk, count), 1)
        order_ref[s : s + chunk, :] = jnp.where(row < column, 1.0, 0.0).astype(jnp.bfloat16)
    ranks = jnp.dot(picks.astype(jnp.bfloat16), order_ref[0:count, :], preferred_element_type=jnp.float32)
    counts = jnp.sum(picks, axis=1, keepdims=True)
    padded = jnp.ceil(counts * (1.0 / ALIGN)) * ALIGN
    place = jnp.zeros((1, count), jnp.float32)
    start = jnp.zeros((1, 1), jnp.float32)
    for e in range(experts):
        place = place + picks[e : e + 1, :] * (ranks[e : e + 1, :] + start)
        start = start + padded[e : e + 1, :]
    place_ref[...] = jnp.broadcast_to(place, (8, count))
    tally_ref[0] = jnp.broadcast_to(counts, (8, 128))
    tally(0).start()
    for s in range(0, rows, 64):
        row = lax.broadcasted_iota(jnp.int32, (64, count), 0) + s
        order_ref[s : s + 64, :] = jnp.where(row.astype(jnp.float32) == place, 1.0, 0.0).astype(jnp.bfloat16)

    def sort_rows(source_ref, to_ref, which):
        for piece in range(2):
            at = slice(piece * half_rows, (piece + 1) * half_rows)
            to_ref[at, :] = jnp.dot(
                order_ref[at, :], source_ref[...], preferred_element_type=jnp.float32
            ).astype(jnp.bfloat16)
            row_copy(which, 0, piece).start()
            row_copy(which, 1, piece).start()

    sort_rows(cot_ref, cot_own, 0)
    own_rows(0).start()

    def project(i, _):
        at = pl.ds(pl.multiple_of(i * 192, 192), 192)
        entry, _, _ = row_norm(tokens_ref[at, :].astype(jnp.float32), norms_ref[0:1, :], norms_ref[1:2, :])
        entry = entry.astype(jnp.bfloat16)
        entry_ref[at, :] = entry
        joint_ref[at, :] = jnp.dot(entry, projection_ref[...], preferred_element_type=jnp.float32).astype(jnp.bfloat16)
        return 0

    lax.fori_loop(0, count // 192, project, 0)
    score_bias(bias_ref, lengths_ref, count)
    forward_weights(0, 1)
    tally_step(0)

    first = lax.broadcasted_iota(jnp.int32, (1, 128), 1) < 64

    def attend(p, _):
        lanes = pl.ds(pl.multiple_of(p * 128, 128), 128)
        keys = pl.ds(pl.multiple_of(width + p * 128, 128), 128)
        values = pl.ds(pl.multiple_of(2 * width + p * 128, 128), 128)
        for s, e in query_blocks(count):
            outs = []
            for half in range(2):
                q = jnp.where(first == (half == 0), joint_ref[s:e, lanes], jnp.bfloat16(0))
                scores = lax.dot_general(joint_ref[0:e, keys], q, NT, preferred_element_type=jnp.float32)
                scores = scores * factor + bias_ref[0:e, s:e]
                peak = jnp.max(scores, axis=0, keepdims=True)
                weights = jnp.exp2(scores - peak)
                total = jnp.sum(weights, axis=0, keepdims=True)
                probs = (weights * (1.0 / total)).astype(jnp.bfloat16)
                outs.append(
                    lax.dot_general(probs, joint_ref[0:e, values], TN, preferred_element_type=jnp.float32)
                )
                logs_ref[p, half : half + 1, s:e] = peak + jnp.log2(total)
            mixed_ref[s:e, lanes] = jnp.where(first, outs[0], outs[1]).astype(jnp.bfloat16)

        @pl.when(p == 2)
        def _():
            forward_weights(1, 1)
            hand_on(0)
            tally_step(1)

        @pl.when(p == 4)
        def _():
            hand_on(1)
            forward_weights(0, 2)
            tally_step(2)

        return 0

    lax.fori_loop(0, pairs, attend, 0)

    lane = lax.broadcasted_iota(jnp.int32, (1, 128), 1)

    def mix(i, _):
        at = pl.ds(pl.multiple_of(i * 192, 192), 192)
        residual = tokens_ref[at, :].astype(jnp.float32) + jnp.dot(
            mixed_ref[at, :], mixing_ref[...], preferred_element_type=jnp.float32
        )
        residual_ref[at, :] = residual
        normed, _, _ = row_norm(residual, norms_ref[2:3, :], norms_ref[3:4, :])
        chosen = chosen_rows(route_ref[at, :], centroids_ref, experts)
        gate = 1.0 / (1.0 + jnp.exp(-jnp.sum(normed * chosen, axis=1, keepdims=True)))
        high = gate.astype(jnp.bfloat16).astype(jnp.float32)
        mid = (gate - high).astype(jnp.bfloat16).astype(jnp.float32)
        low = gate - high - mid
        parts = jnp.where(lane == 0, high, jnp.where(lane == 1, mid, jnp.where(lane == 2, low, 0.0)))
        normed_ref[at, 0:width] = normed.astype(jnp.bfloat16)
        normed_ref[at, width : width + 128] = parts.astype(jnp.bfloat16)
        return 0

    lax.fori_loop(0, count // 192, mix, 0)
    for piece in range(2):
        at = slice(piece * half_rows, (piece + 1) * half_rows)
        moved = jnp.dot(order_ref[at, :], normed_ref[...], preferred_element_type=jnp.float32)
        sent_own[at, :] = moved[:, 0:width].astype(jnp.bfloat16)
        row_copy(1, 0, piece).start()
        row_copy(1, 1, piece).start()
        bias_ref[at, 0:128] = jnp.broadcast_to(
            jnp.sum(moved[:, width : width + 128], axis=1, keepdims=True), (half_rows, 128)
        )
    forward_weights(1, 2)
    tally_step(3)
    for piece in range(2):
        row_copy(0, 0, piece).wait_recv()
        row_copy(0, 2, piece).start()
    gates = jnp.transpose(bias_ref[0:rows, 0:128])
    gate_own[0:1, :] = gates[0:1, :]
    gate_own[1:2, :] = jnp.zeros((1, rows), jnp.float32)
    for e in range(8):
        gate_own[1:2, e : e + 1] = padded[e : e + 1, :]
    gate_copy(0).start()
    gate_copy(1).start()
    own_rows(1).start()
    own_rows(2).start()
    for s in range(0, count, 384):
        flipped_ref[:, s : s + 384] = jnp.transpose(entry_ref[s : s + 384, :])

    for kind in range(2):
        forward_weights(kind, 3)
    gate_copy(0).wait_recv()
    gate_copy(2).start()
    tally_step(4)
    for piece in range(2):
        row_copy(1, 0, piece).wait_recv()
        row_copy(1, 2, piece).start()

    for which in range(2):
        for part in range(3):
            for piece in range(2):
                copy = row_copy(which, part, piece)
                copy.wait_send()
                if part:
                    copy.wait_recv()
    for part in range(3):
        gate_copy(part).wait_send()
        if part:
            gate_copy(part).wait_recv()
    for k in range(len(rounds)):
        tally(k).wait_send()
    for which in range(3):
        own_rows(which).wait()
    for kind in range(2):
        own_weights(kind).wait()
        for r in range(1, planes):
            for sign in (1, -1):
                @pl.when(hop_sent(sign, r))
                def _(kind=kind, sign=sign, r=r):
                    hop(kind, sign, r).wait_send()
        for slot in range(2 * planes - 1):
            if slot == middle:
                aside(kind, slot).wait_send()
                continue

            @pl.when(aside_there(slot))
            def _(kind=kind, slot=slot):
                aside(kind, slot).wait()
        for sign in (1, -1):
            @pl.when(plane == (0 if sign > 0 else planes - 1))
            def _(kind=kind, sign=sign):
                handed(kind, sign).wait_send()

            @pl.when(plane == (1 if sign > 0 else planes - 2))
            def _(kind=kind, sign=sign):
                handed(kind, sign).wait_recv()


def front_stage(
    tokens, norms, projection, mixing, centroids, expanding, contracting, route, lengths, cotangent, planes, slabs
):
    count, width = tokens.shape
    rows = aligned_rows(count, planes)
    pairs = width // 128
    slots = 2 * planes - 1
    bf16, f32 = jnp.bfloat16, jnp.float32
    shape = jax.ShapeDtypeStruct
    anywhere = pl.BlockSpec(memory_space=pl.ANY)
    local = pl.BlockSpec(memory_space=pltpu.VMEM)
    dma = pltpu.SemaphoreType.DMA
    copies = 2 * (2 * (planes - 1) + slots) + 12 + 3 + 5 + 2
    outs = [
        (shape((width, count), bf16), local),
        (shape((count, 3 * width), bf16), local),
        (shape((count, width), bf16), local),
        (shape((pairs, 2, count), f32), local),
        (shape((count, width), f32), local),
        (shape((8, count), f32), local),
        (shape((8, 128), f32), local),
        (shape((4, rows, width), bf16), anywhere),
        (shape((4, rows, width), bf16), anywhere),
        (shape((4, 8, rows), f32), anywhere),
        (shape((slots,) + expanding.shape[1:], bf16), anywhere),
        (shape((slots,) + expanding.shape[1:], bf16), anywhere),
        (shape((slots,) + contracting.shape[1:], bf16), anywhere),
        (shape((slots,) + contracting.shape[1:], bf16), anywhere),
    ]
    return pl.pallas_call(
        partial(front_kernel, planes, slabs),
        out_shape=[o[0] for o in outs],
        in_specs=[pl.BlockSpec(memory_space=pltpu.SMEM)] + [local] * 8 + [anywhere] * 2,
        out_specs=[o[1] for o in outs],
        scratch_shapes=[
            pltpu.VMEM((rows, count), f32),
            pltpu.VMEM((rows, count), bf16),
            pltpu.VMEM((count, width + 128), bf16),
            pltpu.VMEM((count, width), bf16),
            pltpu.VMEM((rows, width), bf16),
            pltpu.VMEM((rows, width), bf16),
            pltpu.VMEM((8, rows), f32),
            pltpu.VMEM((10, 8, 128), f32),
            dma((copies,)),
            dma((copies,)),
            dma((5,)),
        ],
        compiler_params=pltpu.CompilerParams(
            collective_id=0, has_side_effects=True, vmem_limit_bytes=VMEM_LIMIT
        ),
    )(
        lengths[0],
        tokens,
        norms,
        projection,
        mixing,
        centroids,
        route.reshape(1, -1),
        route,
        cotangent,
        expanding,
        contracting,
    )


STEP = 192


def rear_kernel(
    planes,
    slabs,
    total_tokens,
    lengths_ref,
    tokens_ref,
    norms_ref,
    projection_ref,
    mixing_ref,
    centroids_ref,
    route_ref,
    cot_ref,
    flipped_ref,
    joint_in,
    mixed_ref,
    logs_ref,
    residual_in,
    place_ref,
    loads_ref,
    dots_ref,
    back_all,
    made_all,
    near_all,
    far_all,
    layer_ref,
    token_ref,
    vector_ref,
    up_out,
    down_out,
    shared_out,
    core_land,
    y_land,
    x_land,
    z_land,
    joint_ref,
    residual_ref,
    bias_ref,
    upstream_ref,
    a_ref,
    b_ref,
    made_ref,
    place_col,
    gate_col,
    dot_land,
    part_ref,
    stage_ref,
    own_ref,
    own_core,
    own_first,
    own_second,
    own_z,
    piece_ref,
    tally_ref,
    key_sums,
    send_sem,
    recv_sem,
    local_sem,
):
    count, width = tokens_ref.shape
    experts = planes
    rows = a_ref.shape[0]
    half_rows = rows // 2
    pairs = width // 128
    half = width // 2
    scale = (width // HEADS) ** (-0.5)
    factor = scale * HALF_LOG
    average = total_tokens / experts
    me, core, plane, beside_x, beside_y, beside_core = neighbours(slabs)
    x = lax.rem(me, 2)
    y = lax.rem(lax.div(me, 2), 2)
    here = lax.rem(me, slabs)
    diagonal = (beside_y[0], 1 - core)
    always = plane >= 0
    others = [(lax.rem(plane + d, planes) * slabs + here, core) for d in range(1, planes)]
    greet([(d, always) for d in [beside_x, beside_y, beside_core, diagonal] + others])
    ids = {}

    def remote(key, src, dst, device):
        i = ids.setdefault(key, len(ids))
        return pltpu.make_async_remote_copy(
            src_ref=src, dst_ref=dst, send_sem=send_sem.at[i], recv_sem=recv_sem.at[i], device_id=device, device_id_type=MESH
        )

    def fetch(i, src, dst):
        return pltpu.make_async_copy(src, dst, local_sem.at[i])

    loads = [fetch(0, joint_in, joint_ref), fetch(1, residual_in, residual_ref)]
    for copy in loads:
        copy.start()

    alls = (back_all, made_all)

    def to_core(which, second, piece):
        at = pl.ds(piece * half_rows, half_rows)
        return remote(
            ("core", which, second, piece), alls[which].at[1 + 2 * second, at], core_land.at[which, second, at], beside_core
        )

    def to_y(which, piece):
        at = pl.ds(piece * half_rows, half_rows)
        return remote(("y", which, piece), (a_ref, made_ref)[which].at[at], y_land.at[which, at], beside_y)

    def dot_copy(k):
        return remote(("dot", k), dots_ref.at[1 + k], dot_land.at[k], (beside_core, beside_y, diagonal)[k])

    for which in range(2):
        for second in (1, 0):
            for piece in range(2):
                to_core(which, second, piece).start()
        if which == 0:
            for k in range(3):
                dot_copy(k).start()

    def target(sign, r):
        e = plane + sign * r
        return jnp.clip(e, 0, planes - 1), (e >= 0) & (e < planes)

    def share_x(sign, r):
        e, _ = target(sign, r)
        return remote(("x", sign, r), far_all.at[e], x_land.at[e], beside_x)

    def share_z(sign, r):
        return remote(
            ("z", sign, r),
            stage_ref.at[0 if sign > 0 else 1],
            z_land.at[0 if sign > 0 else 1, r - 1],
            (jnp.clip(me + sign * slabs, 0, planes * slabs - 1), core),
        )

    ways = [(s, r) for r in range(planes - 1, 0, -1) for s in (1, -1)] + [(1, 0)]
    def start_shares(distance):
        for sign, r in ways:
            if r == distance:
                @pl.when(target(sign, r)[1])
                def _(sign=sign, r=r):
                    share_x(sign, r).start()

    for distance in range(planes - 1, 1, -1):
        start_shares(distance)

    def add_pieces(into, sources, size, step):
        def one(i, _):
            at = pl.ds(pl.multiple_of(i * step, step), step)
            total = sources[0][at, :].astype(jnp.float32)
            for s in sources[1:]:
                total = total + s[at, :].astype(jnp.float32)
            into[at, :] = total.astype(into.dtype)
            return 0
        lax.fori_loop(0, size // step, one, 0)

    def share_step(sign, r):
        e, valid = target(sign, r)
        lane = 0 if sign > 0 else 1

        @pl.when(valid)
        def _():
            first = fetch(2, near_all.at[e], part_ref.at[0])
            first.start()
            share_x(sign, r).wait_recv()
            second = fetch(3, x_land.at[e], part_ref.at[1])
            second.start()
            if r < planes - 1:
                @pl.when(target(sign, r + 1)[1])
                def _():
                    share_z(sign, r + 1).wait_send()
            first.wait()
            second.wait()
            add_pieces(stage_ref.at[lane], [part_ref.at[0], part_ref.at[1]], part_ref.shape[1], 96)
            if r < planes - 1:
                @pl.when((plane - sign >= 0) & (plane - sign < planes))
                def _():
                    share_z(sign, r + 1).wait_recv()
                    third = fetch(2, z_land.at[lane, r], part_ref.at[0])
                    third.start()
                    third.wait()
                    add_pieces(stage_ref.at[lane], [stage_ref.at[lane], part_ref.at[0]], part_ref.shape[1], 96)
            share_z(sign, r).start()

    def share_end():
        share_x(1, 0).wait_recv()
        copies = [fetch(2, near_all.at[plane], part_ref.at[0]), fetch(3, x_land.at[plane], part_ref.at[1])]
        for copy in copies:
            copy.start()
        for copy in copies:
            copy.wait()

        def put(sources, more):
            def rows_of(i, _):
                at = pl.ds(pl.multiple_of(i * 96, 96), 96)
                total = sources[0][at, :].astype(jnp.float32)
                if len(sources) > 1:
                    total = total + sources[1][at, :].astype(jnp.float32)
                up_out[at, :] = up_out[at, :] + total if more else total
                return 0
            lax.fori_loop(0, width // 96, rows_of, 0)

            def columns_of(i, _):
                at = pl.ds(pl.multiple_of(i * 96, 96), 96)
                for part in range(2):
                    source_at = pl.ds(pl.multiple_of(width + part * half + i * 96, 32), 96)
                    total = sources[0][source_at, :].astype(jnp.float32)
                    if len(sources) > 1:
                        total = total + sources[1][source_at, :].astype(jnp.float32)
                    to = slice(part * half, (part + 1) * half)
                    down_out[at, to] = down_out[at, to] + total if more else total
                return 0
            lax.fori_loop(0, half // 96, columns_of, 0)

        put([part_ref.at[0], part_ref.at[1]], False)
        for sign in (1, -1):
            lane = 0 if sign > 0 else 1

            @pl.when((plane - sign >= 0) & (plane - sign < planes))
            def _(sign=sign, lane=lane):
                share_z(sign, 1).wait_recv()
                third = fetch(2, z_land.at[lane, 0], part_ref.at[0])
                third.start()
                third.wait()
                put([part_ref.at[0]], True)

    q1, q2, q3, q4 = width // 2, width // 4, width // 8, width // 16
    base1 = core * q1
    base2 = base1 + y * q2
    base3 = base2 + x * q3

    def spot(start, size):
        return pl.ds(pl.multiple_of(start, 16), size)

    def corner(p):
        return lax.div(p, 2) * q4, pl.multiple_of(lax.rem(p, 2) * half, 128)

    def sum_copy(c, stage, d=0):
        own = own_ref.at[c]
        if stage == "core":
            return remote((c, stage), own.at[spot((1 - core) * q1, q1)], own_core.at[c], beside_core)
        if stage == "first":
            return remote((c, stage), own.at[spot(base1 + (1 - y) * q2, q2)], own_first.at[c], beside_y)
        if stage == "second":
            return remote((c, stage), own.at[spot(base2 + (1 - x) * q3, q3)], own_second.at[c], beside_x)
        if stage == "z":
            r, k = corner(lax.rem(plane + d, planes))
            return remote(
                (c, stage, d), own.at[spot(base3 + r, q4), pl.ds(k, half)], own_z.at[c, d - 1], others[d - 1]
            )
        out = shared_out.at[c]
        if stage == "zz":
            r, k = corner(plane)
            return remote(
                (c, stage, d), piece_ref.at[c], out.at[spot(base3 + r, q4), pl.ds(k, half)], others[d - 1]
            )
        if stage == "second back":
            at = spot(base3, q3)
            return remote((c, stage), out.at[at], out.at[at], beside_x)
        if stage == "first back":
            at = spot(base2, q2)
            return remote((c, stage), out.at[at], out.at[at], beside_y)
        at = spot(base1, q1)
        return remote((c, stage), out.at[at], out.at[at], beside_core)

    def add_rows(c, start, size, came, step):
        def one(i, _):
            at = pl.ds(pl.multiple_of(i * step, step), step)
            mine = spot(start + i * step, step)
            own_ref[c, mine, :] = (
                own_ref[c, mine, :].astype(jnp.float32) + came[c, at, :].astype(jnp.float32)
            ).astype(jnp.bfloat16)
            return 0
        lax.fori_loop(0, size // step, one, 0)

    def keep_piece(c):
        r, k = corner(plane)
        return fetch(4 + c, piece_ref.at[c], shared_out.at[c, spot(base3 + r, q4), pl.ds(k, half)])

    def sum_step(c, stage):
        if stage == 0:
            sum_copy(c, "core").start()
        elif stage == 1:
            sum_copy(c, "core").wait_recv()
            add_rows(c, base1, q1, own_core, 48)
            sum_copy(c, "first").start()
        elif stage == 2:
            sum_copy(c, "first").wait_recv()
            add_rows(c, base2, q2, own_first, 48)
            sum_copy(c, "second").start()
        elif stage == 3:
            sum_copy(c, "second").wait_recv()
            add_rows(c, base3, q3, own_second, 48)
            for d in range(1, planes):
                sum_copy(c, "z", d).start()
        elif stage == 4:
            r, k = corner(plane)
            total = own_ref[c, spot(base3 + r, q4), pl.ds(k, half)].astype(jnp.float32)
            for d in range(1, planes):
                sum_copy(c, "z", d).wait_recv()
                total = total + own_z[c, d - 1].astype(jnp.float32)
            piece_ref[c] = total.astype(jnp.bfloat16)
            keep_piece(c).start()
            for d in range(1, planes):
                sum_copy(c, "zz", d).start()
        elif stage == 5:
            keep_piece(c).wait()
            for d in range(1, planes):
                sum_copy(c, "zz", d).wait_recv()
            sum_copy(c, "second back").start()
        elif stage == 6:
            sum_copy(c, "second back").wait_recv()
            sum_copy(c, "first back").start()
        elif stage == 7:
            sum_copy(c, "first back").wait_recv()
            sum_copy(c, "cc").start()
        else:
            sum_copy(c, "cc").wait_recv()

    def sum_sent(c):
        for stage in ("core", "first", "second"):
            sum_copy(c, stage).wait_send()
        for d in range(1, planes):
            sum_copy(c, "z", d).wait_send()

    def sum_for_y(which):
        into = (a_ref, made_ref)[which]
        for piece in range(2):
            at = pl.ds(piece * half_rows, half_rows)
            first = fetch(2, alls[which].at[2, at], into.at[at])
            first.start()
            to_core(which, 1, piece).wait_recv()
            second = fetch(3, core_land.at[which, 1, at], b_ref.at[at])
            second.start()
            first.wait()
            second.wait()
            add_pieces(into.at[at], [into.at[at], b_ref.at[at]], half_rows, 32)
            to_y(which, piece).start()

    sum_for_y(0)
    sum_for_y(1)
    place_col[...] = jnp.transpose(place_ref[...])
    score_bias(bias_ref, lengths_ref, count)
    for copy in loads:
        copy.wait()
    vector_ref[...] = jnp.zeros_like(vector_ref)
    number = lax.broadcasted_iota(jnp.int32, (1, rows), 1).astype(jnp.float32)

    def order_of(at):
        return jnp.where(place_col[at, 0:1] == number, 1.0, 0.0)

    def chunk_of(i):
        return pl.ds(pl.multiple_of(i * STEP, STEP), STEP)

    steps = count // STEP

    def unsort(buffer, act):
        def one(i, _):
            at = chunk_of(i)
            act(at, jnp.dot(order_of(at).astype(jnp.bfloat16), buffer[...], preferred_element_type=jnp.float32))
            return 0
        lax.fori_loop(0, steps, one, 0)

    def set_token(at, value):
        token_ref[at, :] = value

    def add_token(at, value):
        token_ref[at, :] += value

    own_back = fetch(2, back_all.at[0], b_ref)
    own_back.start()
    own_back.wait()
    unsort(b_ref, set_token)
    for piece in range(2):
        to_core(0, 0, piece).wait_recv()
    core_back = fetch(2, core_land.at[0, 0], b_ref)
    core_back.start()
    core_back.wait()
    unsort(b_ref, add_token)
    for sign in (1, -1):
        share_step(sign, planes - 1)
    start_shares(1)
    for piece in range(2):
        to_y(0, piece).wait_recv()
    y_back = fetch(2, y_land.at[0], b_ref)
    y_back.start()
    y_back.wait()
    unsort(b_ref, add_token)
    for sign in (1, -1):
        share_step(sign, planes - 2)
    for k in range(3):
        dot_copy(k).wait_recv()
    dots = dots_ref[0] + dot_land[0] + dot_land[1] + dot_land[2]
    dots = dots[0:1, :]

    def norm_step(i, _):
        at = chunk_of(i)
        normed, normal, spread_by = row_norm(residual_ref[at, :], norms_ref[2:3, :], norms_ref[3:4, :])
        route = route_ref[at, :]
        chosen = chosen_rows(route, centroids_ref, experts)
        gate = 1.0 / (1.0 + jnp.exp(-jnp.sum(normed * chosen, axis=1, keepdims=True)))
        gate_col[at, :] = jnp.broadcast_to(gate, (STEP, 128))
        gate_grad = jnp.sum(order_of(at) * dots, axis=1, keepdims=True)
        spread = jnp.zeros((STEP, 1), jnp.float32)
        for e in range(experts):
            spread = jnp.where(route == e, (loads_ref[e : e + 1, 0:1] - average) * (1.0 / average), spread)
        logit = (gate_grad + spread * (1.0 / total_tokens)) * gate * (1.0 - gate)
        above = token_ref[at, :] + logit * chosen
        pull = logit * normed
        vector_ref[2:3, :] += jnp.sum(above * normal, axis=0, keepdims=True)
        vector_ref[3:4, :] += jnp.sum(above, axis=0, keepdims=True)
        for e in range(experts):
            vector_ref[8 + e : 9 + e, :] += jnp.sum(jnp.where(route == e, pull, 0.0), axis=0, keepdims=True)
        vector_ref[4:5, :] += jnp.broadcast_to(
            jnp.sum(spread * gate, axis=0, keepdims=True) * (1.0 / total_tokens), (1, width)
        )
        scaled = above * norms_ref[2:3, :]
        inner = (
            scaled
            - jnp.mean(scaled, axis=1, keepdims=True)
            - normal * jnp.mean(scaled * normal, axis=1, keepdims=True)
        )
        grad = cot_ref[at, :].astype(jnp.float32) + inner * spread_by
        token_ref[at, :] = grad
        branch = grad.astype(jnp.bfloat16)
        layer_ref[at, :] = branch
        upstream_ref[at, :] = lax.dot_general(
            branch, mixing_ref[...], NT, preferred_element_type=jnp.float32
        ).astype(jnp.bfloat16)
        return 0

    lax.fori_loop(0, steps, norm_step, 0)
    own_ref[0] = lax.dot_general(
        mixed_ref[...], layer_ref[...], TN, preferred_element_type=jnp.float32
    ).astype(jnp.bfloat16)
    sum_step(0, 0)

    first = lax.broadcasted_iota(jnp.int32, (1, 128), 1) < 64

    def attend(p, _):
        lanes = pl.ds(pl.multiple_of(p * 128, 128), 128)
        keys = pl.ds(pl.multiple_of(width + p * 128, 128), 128)
        values = pl.ds(pl.multiple_of(2 * width + p * 128, 128), 128)
        key_sum, value_sum = key_sums.at[0], key_sums.at[1]
        key_sum[...] = jnp.zeros_like(key_sum)
        value_sum[...] = jnp.zeros_like(value_sum)
        for s, e in query_blocks(count):
            both = jnp.transpose(
                upstream_ref[s:e, lanes].astype(jnp.float32) * mixed_ref[s:e, lanes].astype(jnp.float32)
            )
            found = []
            for h in range(2):
                mine = first == (h == 0)
                inner = jnp.sum(both[64 * h : 64 * h + 64, :], axis=0, keepdims=True)
                q = jnp.where(mine, joint_ref[s:e, lanes], jnp.bfloat16(0))
                u = jnp.where(mine, upstream_ref[s:e, lanes], jnp.bfloat16(0))
                scores = lax.dot_general(joint_ref[0:e, keys], q, NT, preferred_element_type=jnp.float32)
                probs = jnp.exp2(scores * factor + bias_ref[0:e, s:e] - logs_ref[p, h : h + 1, s:e])
                prob_grad = lax.dot_general(joint_ref[0:e, values], u, NT, preferred_element_type=jnp.float32)
                score_grad = (probs * (prob_grad - inner)).astype(jnp.bfloat16)
                value_sum[0:e, :] += jnp.dot(probs.astype(jnp.bfloat16), u, preferred_element_type=jnp.float32)
                key_sum[0:e, :] += jnp.dot(score_grad, q, preferred_element_type=jnp.float32)
                found.append(
                    lax.dot_general(score_grad, joint_ref[0:e, keys], TN, preferred_element_type=jnp.float32)
                )
            joint_ref[s:e, lanes] = (jnp.where(first, found[0], found[1]) * scale).astype(jnp.bfloat16)
        joint_ref[:, keys] = (key_sum[...] * scale).astype(jnp.bfloat16)
        joint_ref[:, values] = value_sum[...].astype(jnp.bfloat16)

        events = {
            0: [],
            1: [(0, 1)],
            2: [(1, 1)],
            3: [(0, 2)],
            4: [(1, 2), (2, 1)],
        }
        for k, steps_of in events.items():
            @pl.when(p == k)
            def _(k=k, steps_of=steps_of):
                for c, stage in steps_of:
                    sum_step(c, stage)
                if k == 0:
                    start_shares(0)
                if k == 2:
                    for sign in (1, -1):
                        share_step(sign, 1)
        for c in range(1, 4):
            @pl.when(p == 2 * c - 1)
            def _(c=c):
                for k in range(3):
                    at = pl.ds(k * width + (c - 1) * 256, 256)
                    own_ref[c, :, k * 256 : (k + 1) * 256] = jnp.dot(
                        flipped_ref[...], joint_ref[:, at], preferred_element_type=jnp.float32
                    ).astype(jnp.bfloat16)
                sum_step(c, 0)

        return 0

    lax.fori_loop(0, pairs, attend, 0)

    rounds = [beside_core, beside_x, beside_y]
    rounds += [((plane + 1 - 2 * lax.rem(plane, 2)) * slabs + here, core), (lax.rem(plane + 2, planes) * slabs + here, core)]

    def tally(k):
        return remote(("tally", k), tally_ref.at[2 * k], tally_ref.at[2 * k + 1], rounds[k])

    def tally_step(k):
        tally(k).wait_recv()
        total = tally_ref[2 * k] + tally_ref[2 * k + 1]
        if k + 1 < len(rounds):
            tally_ref[2 * k + 2] = total
            tally(k + 1).start()
        else:
            vector_ref[...] = total

    def finish_step(i, _):
        at = chunk_of(i)
        back = lax.dot_general(joint_ref[at, :], projection_ref[...], NT, preferred_element_type=jnp.float32)
        _, normal, spread_by = row_norm(tokens_ref[at, :].astype(jnp.float32), norms_ref[0:1, :], norms_ref[1:2, :])
        scaled = back * norms_ref[0:1, :]
        inner = (
            scaled
            - jnp.mean(scaled, axis=1, keepdims=True)
            - normal * jnp.mean(scaled * normal, axis=1, keepdims=True)
        )
        token_ref[at, :] += inner * spread_by
        vector_ref[0:1, :] += jnp.sum(back * normal, axis=0, keepdims=True)
        vector_ref[1:2, :] += jnp.sum(back, axis=0, keepdims=True)
        return 0

    def end_made(at, value):
        layer_ref[at, :] = (residual_ref[at, :] + gate_col[at, 0:1] * value).astype(jnp.bfloat16)

    def load(source, into):
        copy = fetch(2, source, into)
        copy.start()
        copy.wait()

    def sum_steps(*which):
        for c, stage in which:
            sum_step(c, stage)

    lax.fori_loop(0, steps // 2, finish_step, 0)
    sum_steps((3, 1), (0, 3), (1, 3), (2, 2))
    lax.fori_loop(steps // 2, steps, finish_step, 0)
    tally_ref[0] = vector_ref[...]
    tally(0).start()
    sum_steps((0, 4), (1, 4), (2, 3))
    for piece in range(2):
        to_y(0, piece).wait_send()
    load(made_all.at[0], a_ref)
    for piece in range(2):
        to_core(1, 0, piece).wait_recv()
    load(core_land.at[1, 0], b_ref)
    add_pieces(a_ref, [a_ref, b_ref], rows, 32)
    sum_steps((3, 2), (0, 5), (1, 5), (2, 4))
    tally_step(0)
    for piece in range(2):
        to_y(1, piece).wait_recv()
    load(y_land.at[1], b_ref)
    add_pieces(a_ref, [a_ref, b_ref], rows, 32)
    sum_steps((3, 3), (0, 6), (1, 6), (2, 5))
    tally_step(1)
    unsort(a_ref, end_made)
    sum_steps((3, 4), (2, 6))
    tally_step(2)
    share_end()
    sum_steps((3, 5), (0, 7), (1, 7))
    tally_step(3)
    sum_steps((3, 6), (2, 7))
    tally_step(4)
    sum_steps((0, 8), (1, 8), (2, 8), (3, 7), (3, 8))

    for which in range(2):
        for piece in range(2):
            for second in range(2):
                to_core(which, second, piece).wait_send()
    for piece in range(2):
        to_y(1, piece).wait_send()
    for k in range(3):
        dot_copy(k).wait_send()
    for sign, r in ways:
        @pl.when(target(sign, r)[1])
        def _(sign=sign, r=r):
            share_x(sign, r).wait_send()
    for sign in (1, -1):
        @pl.when(target(sign, 1)[1])
        def _(sign=sign):
            share_z(sign, 1).wait_send()
    for c in range(4):
        sum_sent(c)
    for c in range(4):
        for d in range(1, planes):
            sum_copy(c, "zz", d).wait_send()
        for stage in ("second back", "first back", "cc"):
            sum_copy(c, stage).wait_send()
    for k in range(len(rounds)):
        tally(k).wait_send()
    assert len(ids) <= send_sem.shape[0]


def rear_stage(
    tokens, norms, projection, mixing, centroids, route, lengths, cotangent,
    flipped, joint, mixed, logs, residual, place, loads, dots, back, made, near, far, planes, slabs, total_tokens,
):
    count, width = tokens.shape
    rows = back.shape[1]
    half = width // 2
    bf16, f32 = jnp.bfloat16, jnp.float32
    shape = jax.ShapeDtypeStruct
    anywhere = pl.BlockSpec(memory_space=pl.ANY)
    local = pl.BlockSpec(memory_space=pltpu.VMEM)
    dma = pltpu.SemaphoreType.DMA
    packed = near.shape[1:]
    outs = [
        (shape((count, width), bf16), local),
        (shape((count, width), f32), local),
        (shape((16, width), f32), local),
        (shape((width, half), f32), local),
        (shape((half, width), f32), local),
        (shape((4, width, width), bf16), anywhere),
        (shape((2, 2, rows, width), bf16), anywhere),
        (shape((2, rows, width), bf16), anywhere),
        (shape((planes,) + packed, bf16), anywhere),
        (shape((2, planes - 1) + packed, bf16), anywhere),
    ]
    copies = 120
    return pl.pallas_call(
        partial(rear_kernel, planes, slabs, total_tokens),
        out_shape=[o[0] for o in outs],
        in_specs=[pl.BlockSpec(memory_space=pltpu.SMEM)]
        + [local] * 8
        + [anywhere]
        + [local] * 2
        + [anywhere]
        + [local] * 3
        + [anywhere] * 4,
        out_specs=[o[1] for o in outs],
        scratch_shapes=[
            pltpu.VMEM((count, 3 * width), bf16),
            pltpu.VMEM((count, width), f32),
            pltpu.VMEM((count, count), f32),
            pltpu.VMEM((count, width), bf16),
            pltpu.VMEM((rows, width), bf16),
            pltpu.VMEM((rows, width), bf16),
            pltpu.VMEM((rows, width), bf16),
            pltpu.VMEM((count, 8), f32),
            pltpu.VMEM((count, 128), f32),
            pltpu.VMEM((3, 8, rows), f32),
            pltpu.VMEM((2,) + packed, bf16),
            pltpu.VMEM((2,) + packed, bf16),
            pltpu.VMEM((4, width, width), bf16),
            pltpu.VMEM((4, width // 2, width), bf16),
            pltpu.VMEM((4, width // 4, width), bf16),
            pltpu.VMEM((4, width // 8, width), bf16),
            pltpu.VMEM((4, planes - 1, width // 16, half), bf16),
            pltpu.VMEM((4, width // 16, half), bf16),
            pltpu.VMEM((10, 16, width), f32),
            pltpu.VMEM((2, count, 128), f32),
            dma((copies,)),
            dma((copies,)),
            dma((8,)),
        ],
        compiler_params=pltpu.CompilerParams(
            collective_id=1, has_side_effects=True, vmem_limit_bytes=VMEM_LIMIT
        ),
    )(
        lengths[0],
        tokens,
        norms,
        projection,
        mixing,
        centroids,
        route,
        cotangent,
        flipped,
        joint,
        mixed,
        logs,
        residual,
        place,
        loads,
        dots,
        back,
        made,
        near,
        far,
    )


TILE = 256
ALIGN = 16


def aligned_rows(count, experts):
    return -(-(count + experts * (ALIGN - 1)) // ALIGN) * ALIGN


def gelu_pair(values):
    bell = jnp.exp2(values * values * (-0.5 * HALF_LOG))
    near = 1.0 / (1.0 + (0.3275911 * 0.7071067811865476) * jnp.abs(values))
    series = 1.061405429 * 0.5 * near - 1.453152027 * 0.5
    series = series * near + 1.421413741 * 0.5
    series = series * near - 0.284496736 * 0.5
    series = series * near + 0.254829592 * 0.5
    tail = series * near * bell
    below = jnp.where(values >= 0.0, 1.0 - tail, tail)
    return values * below, below + values * bell * 0.3989422804014327


def expert_kernel_body(
    experts,
    sources,
    limit,
    meta_ref,
    sent_all,
    cot_all,
    gate_all,
    up_near,
    up_far,
    down_near,
    down_far,
    back_all,
    made_all,
    dots_all,
    near_out,
    far_out,
    table,
    x_ref,
    c_ref,
    g_ref,
    column_ref,
    up_ref,
    down_ref,
    gu_ref,
    gd_ref,
    pack_ref,
    zero_ref,
    weight_sem,
    in_sem,
    out_sem,
    grad_sem,
    zero_sem,
):
    rows, width = sent_all.shape[1:]
    half = up_near.shape[2]
    own = meta_ref[0]
    spots = sources * experts

    base = 0
    ends = [0] * sources
    for e in range(experts):
        at = base
        for s in range(sources):
            size = meta_ref[1 + s * experts + e]
            table[0, e * sources + s] = size
            table[1, e * sources + s] = ends[s]
            table[2, e * sources + s] = at
            ends[s] = ends[s] + size
            at = at + size
        number = (at - base + (TILE - 1)) // TILE
        table[3, e] = base
        table[4, e] = number
        base = base + number * TILE
    for s in range(sources):
        table[5, s] = ends[s]

    bits = [1 << b for b in range(limit.bit_length()) if ALIGN <= (1 << b)]

    def move(k, act, outward):
        s, e = lax.rem(k, sources), lax.div(k, sources)
        size = table[0, k]
        for piece in bits:
            @pl.when((size & piece) != 0)
            def _(piece=piece):
                offset = size & (piece - 1)
                src = pl.ds(pl.multiple_of(table[1, k] + offset, ALIGN), piece)
                dst = pl.ds(pl.multiple_of(table[2, k] + offset, ALIGN), piece)
                if outward:
                    act(pltpu.make_async_copy(x_ref.at[dst], made_all.at[s, src], out_sem.at[0]))
                    act(pltpu.make_async_copy(c_ref.at[dst], back_all.at[s, src], out_sem.at[1]))
                else:
                    act(pltpu.make_async_copy(sent_all.at[s, src], x_ref.at[dst], in_sem.at[e, 0]))
                    act(pltpu.make_async_copy(cot_all.at[s, src], c_ref.at[dst], in_sem.at[e, 1]))

    def each(low, high, act):
        def one(i, _):
            act(i)
            return 0
        lax.fori_loop(low, high, one, 0)

    def begin(copy):
        copy.start()

    def end(copy):
        copy.wait()

    def move_weights(e, act):
        slot = e - own + experts - 1
        for j, (ups, downs) in enumerate(((up_near, down_near), (up_far, down_far))):
            part = pl.ds(j * half, half)
            act(pltpu.make_async_copy(ups.at[slot], up_ref.at[e, :, part], weight_sem.at[e, j, 0]))
            act(pltpu.make_async_copy(downs.at[slot], down_ref.at[e, part], weight_sem.at[e, j, 1]))

    zero_ref[...] = jnp.zeros_like(zero_ref)

    def bring(e):
        @pl.when(table[4, e] > 0)
        def _():
            last = pl.ds(pl.multiple_of(table[3, e] + (table[4, e] - 1) * TILE, TILE), TILE)
            x_ref[last, :] = jnp.zeros((TILE, width), jnp.bfloat16)
            c_ref[last, :] = jnp.zeros((TILE, width), jnp.bfloat16)
            g_ref[last, :] = jnp.zeros((TILE, 128), jnp.float32)

        move_weights(e, begin)
        each(e * sources, (e + 1) * sources, lambda k: move(k, begin, False))

    each(0, experts, bring)

    chunks = experts + 1

    def tail(k, act):
        s, i = lax.div(k, chunks), lax.rem(k, chunks) + rows // ALIGN - chunks

        @pl.when(i * ALIGN >= table[5, s])
        def _():
            dst = pl.ds(pl.multiple_of(i * ALIGN, ALIGN), ALIGN)
            act(pltpu.make_async_copy(zero_ref, made_all.at[s, dst], zero_sem.at[0]))
            act(pltpu.make_async_copy(zero_ref, back_all.at[s, dst], zero_sem.at[1]))

    each(0, sources * chunks, lambda k: tail(k, begin))

    def shift(s, outward):
        def segment(e):
            k = e * sources + s

            def one(i):
                src = pl.ds(pl.multiple_of(table[1, k] + i * ALIGN, ALIGN), ALIGN)
                dst = pl.ds(pl.multiple_of(table[2, k] + i * ALIGN, ALIGN), ALIGN)
                if outward:
                    column_ref[src, :] = g_ref[dst, :]
                else:
                    g_ref[dst, :] = column_ref[src, :]

            each(0, table[0, k] // ALIGN, one)

        each(0, experts, segment)

    def gates_in(s):
        column_ref[...] = jnp.transpose(jnp.broadcast_to(gate_all[s, 0:1, :], (128, rows)))
        shift(s, False)

    each(0, sources, gates_in)

    def grads(e):
        slot = lax.rem(e, 2)
        return [
            pltpu.make_async_copy(pack_ref.at[slot, j], ref.at[e], grad_sem.at[slot, j])
            for j, ref in enumerate((near_out, far_out))
        ]

    def work(e):
        move_weights(e, end)
        each(e * sources, (e + 1) * sources, lambda k: move(k, end, False))
        gu_ref[...] = jnp.zeros_like(gu_ref)
        gd_ref[...] = jnp.zeros_like(gd_ref)

        def tile(t):
            at = pl.ds(pl.multiple_of(table[3, e] + t * TILE, TILE), TILE)
            x, c, gate = x_ref[at, :], c_ref[at, :], g_ref[at, 0:1]
            before = jnp.dot(x, up_ref[e], preferred_element_type=jnp.float32)
            active, slope = gelu_pair(before)
            through = lax.dot_general(c, down_ref[e], NT, preferred_element_type=jnp.float32)
            grad = (through * (slope * gate)).astype(jnp.bfloat16)
            gated = (active * gate).astype(jnp.bfloat16)
            made = jnp.dot(active.astype(jnp.bfloat16), down_ref[e], preferred_element_type=jnp.float32)
            g_ref[at, :] = jnp.broadcast_to(
                jnp.sum(made * c.astype(jnp.float32), axis=1, keepdims=True), (TILE, 128)
            )
            gd_ref[...] += lax.dot_general(gated, c, TN, preferred_element_type=jnp.float32)
            gu_ref[...] += lax.dot_general(x, grad, TN, preferred_element_type=jnp.float32)
            back = lax.dot_general(grad, up_ref[e], NT, preferred_element_type=jnp.float32)
            x_ref[at, :] = made.astype(jnp.bfloat16)
            c_ref[at, :] = back.astype(jnp.bfloat16)

        each(0, table[4, e], tile)
        each(e * sources, (e + 1) * sources, lambda k: move(k, begin, True))

        @pl.when(e >= 2)
        def _():
            for copy in grads(e - 2):
                copy.wait()

        slot = lax.rem(e, 2)
        for j in range(2):
            pack_ref[slot, j, 0:width, :] = gu_ref[:, j * half : (j + 1) * half].astype(jnp.bfloat16)
            for part in range(2):
                pack_ref[slot, j, width + part * half : width + (part + 1) * half, :] = gd_ref[
                    j * half : (j + 1) * half, part * half : (part + 1) * half
                ].astype(jnp.bfloat16)
        for copy in grads(e):
            copy.start()

    each(0, experts, work)

    def sums_out(s):
        shift(s, True)
        dots_all[s] = jnp.transpose(column_ref[...])[0:8, :]

    each(0, sources, sums_out)
    each(0, spots, lambda k: move(k, end, True))
    each(0, sources * chunks, lambda k: tail(k, end))
    for e in range(max(0, experts - 2), experts):
        for copy in grads(e):
            copy.wait()


def expert_stage(meta, sent, cot, gates, weights, experts, limit):
    sources, rows, width = sent.shape
    half = weights[0].shape[2]
    hidden = 2 * half
    joined = -(-(sources * rows + experts * (TILE - 1)) // TILE) * TILE
    limit = -(-limit // ALIGN) * ALIGN
    anywhere = pl.BlockSpec(memory_space=pl.ANY)
    local = pl.BlockSpec(memory_space=pltpu.VMEM)
    dma = pltpu.SemaphoreType.DMA
    packed = (width + hidden, half)
    return pl.pallas_call(
        partial(expert_kernel_body, experts, sources, limit),
        out_shape=(
            jax.ShapeDtypeStruct((sources, rows, width), jnp.bfloat16),
            jax.ShapeDtypeStruct((sources, rows, width), jnp.bfloat16),
            jax.ShapeDtypeStruct((sources, 8, rows), jnp.float32),
            jax.ShapeDtypeStruct((experts,) + packed, jnp.bfloat16),
            jax.ShapeDtypeStruct((experts,) + packed, jnp.bfloat16),
        ),
        in_specs=[pl.BlockSpec(memory_space=pltpu.SMEM)] + [anywhere] * 2 + [local] + [anywhere] * 4,
        out_specs=(anywhere, anywhere, local, anywhere, anywhere),
        scratch_shapes=[
            pltpu.SMEM((6, sources * experts), jnp.int32),
            pltpu.VMEM((joined, width), jnp.bfloat16),
            pltpu.VMEM((joined, width), jnp.bfloat16),
            pltpu.VMEM((joined, 128), jnp.float32),
            pltpu.VMEM((rows, 128), jnp.float32),
            pltpu.VMEM((experts, width, hidden), jnp.bfloat16),
            pltpu.VMEM((experts, hidden, width), jnp.bfloat16),
            pltpu.VMEM((width, hidden), jnp.float32),
            pltpu.VMEM((hidden, width), jnp.float32),
            pltpu.VMEM((2, 2) + packed, jnp.bfloat16),
            pltpu.VMEM((ALIGN, width), jnp.bfloat16),
            dma((experts, 2, 2)),
            dma((experts, 2)),
            dma((2,)),
            dma((2, 2)),
            dma((2,)),
        ],
        compiler_params=pltpu.CompilerParams(vmem_limit_bytes=VMEM_LIMIT),
        cost_estimate=pl.CostEstimate(
            flops=12 * sources * rows * width * hidden, bytes_accessed=100_000_000, transcendentals=sources * rows * hidden
        ),
    )(meta, sent, cot, gates, *weights)


def arrange(shared, layer, token, vectors, up, down, experts):
    count, width = layer.shape
    third, half = width // 3, width // 2
    steps = 6

    def kernel(shared_ref, layer_ref, token_ref, vectors_ref, up_ref, down_ref, *outs):
        mixing_out, projection_out, layer_out, token_out, up_out, down_out, *vector_outs, centroids_out, balance_out = outs
        mixing_out[...] = shared_ref[0].astype(jnp.float32)
        for k in range(3):
            for c in range(3):
                at = k * width + c * third
                projection_out[:, at : at + third] = shared_ref[1 + c, :, k * third : (k + 1) * third].astype(jnp.float32)
        layer_out[...] = layer_ref[...]
        token_out[...] = token_ref[...]
        up_out[0] = up_ref[...]
        down_out[0] = down_ref[...]
        for i, out in enumerate(vector_outs):
            out[...] = vectors_ref[i]
        centroids_out[...] = vectors_ref[8 : 8 + experts, :]
        balance_out[...] = vectors_ref[4:5, 0:128]

    f32 = jnp.float32
    shape = jax.ShapeDtypeStruct
    rows = lambda n, m: pl.BlockSpec((n // steps, m), lambda i: (i, 0))
    slab = lambda n, m: pl.BlockSpec((1, n // steps, m), lambda i: (0, i, 0))
    whole = lambda *dims: pl.BlockSpec(dims, lambda i: (0,) * len(dims))
    return pl.pallas_call(
        kernel,
        out_shape=[
            shape((width, width), f32),
            shape((width, 3 * width), f32),
            shape((count, width), jnp.bfloat16),
            shape((count, width), f32),
            shape((1, width, half), f32),
            shape((1, half, width), f32),
        ]
        + [shape((width,), f32)] * 4
        + [shape((experts, width), f32), shape((1, 128), f32)],
        grid=(steps,),
        in_specs=[
            pl.BlockSpec((4, width // steps, width), lambda i: (0, i, 0)),
            rows(count, width),
            rows(count, width),
            whole(16, width),
            rows(width, half),
            rows(half, width),
        ],
        out_specs=[
            rows(width, width),
            rows(width, 3 * width),
            rows(count, width),
            rows(count, width),
            slab(width, half),
            slab(half, width),
        ]
        + [whole(width)] * 4
        + [whole(experts, width), whole(1, 128)],
        compiler_params=pltpu.CompilerParams(vmem_limit_bytes=VMEM_LIMIT),
    )(shared, layer, token, vectors, up, down)


def per_device(
    tokens,
    gains,
    shifts,
    projection,
    mixing,
    factors,
    biases,
    centroids,
    expanding,
    contracting,
    routes,
    lengths,
    cotangent,
):
    count, width = tokens.shape
    experts = centroids.shape[0]
    groups = lax.axis_size("expert")
    slabs = groups // experts
    limit = 2 * count // experts
    total_tokens = count * groups * lax.axis_size("tensor")

    norms = jnp.stack((gains, shifts, factors, biases))
    flipped, joint, mixed, logs, residual, place, loads, sent, cot, gates, *weights = front_stage(
        tokens, norms, projection, mixing, centroids, expanding, contracting, routes, lengths, cotangent, experts, slabs
    )
    meta = jnp.concatenate(
        [lax.div(lax.axis_index("expert"), slabs)[None], gates[:, 1, :experts].reshape(-1).astype(jnp.int32)]
    )
    back, made, dots, near, far = expert_stage(meta, sent, cot, gates, weights, experts, limit)
    layer, token, vectors, up, down, shared, *_ = rear_stage(
        tokens, norms, projection, mixing, centroids, routes, lengths, cotangent,
        flipped, joint, mixed, logs, residual, place, loads, dots, back, made, near, far, experts, slabs, total_tokens,
    )
    (
        mixing_grad, projection_grad, layer_output, token_grad, up_grad, down_grad,
        gain_grad, shift_grad, factor_grad, bias_grad, centroid_grad, balance,
    ) = arrange(shared, layer, token, vectors, up, down, experts)
    return (
        layer_output,
        balance[0, 0],
        token_grad,
        gain_grad,
        shift_grad,
        projection_grad,
        mixing_grad,
        factor_grad,
        bias_grad,
        centroid_grad,
        up_grad,
        down_grad,
    )


def solution(mesh):
    placed = (
        P(("expert", "tensor"), None),
        P(),
        P(),
        P(),
        P(),
        P(),
        P(),
        P(),
        P("expert", None, "tensor"),
        P("expert", "tensor", None),
        P(("expert", "tensor"), None),
        P(("expert", "tensor"), None),
        P(("expert", "tensor"), None),
    )
    near = mesh.shape["expert"] == 16 and mesh.shape["tensor"] == 2
    return jax.shard_map(
        per_device if near else moving_tokens,
        mesh=mesh,
        in_specs=placed,
        out_specs=(
            P(("expert", "tensor"), None),
            P(),
            P(("expert", "tensor"), None),
            P(),
            P(),
            P(),
            P(),
            P(),
            P(),
            P(),
            P("expert", None, "tensor"),
            P("expert", "tensor", None),
        ),
        check_vma=False,
    )
```

```python
from functools import partial

import jax
import jax.numpy as jnp
from jax import lax
from jax.experimental import pallas as pl
from jax.experimental.pallas import tpu as pltpu
from jax.sharding import PartitionSpec as P

HEADS = 12


highest = lax.Precision.HIGHEST
epsilon = 1e-05


def running(values):
    places = jnp.arange(values.shape[0])
    return jnp.sum(jnp.where(places[:, None] >= places[None, :], values[None, :], 0), axis=1)


def earlier(picks):
    places = jnp.arange(picks.shape[0])
    before = (places[:, None] > places[None, :]).astype(jnp.bfloat16)
    return jnp.dot(
        before, picks.astype(jnp.bfloat16), preferred_element_type=jnp.float32
    ).astype(jnp.int32)


def norm_parts(values, gain, shift):
    centered = values - jnp.mean(values, axis=1, keepdims=True)
    scale = lax.rsqrt(jnp.mean(centered * centered, axis=1, keepdims=True) + epsilon)
    normal = centered * scale
    return (normal * gain + shift, normal, scale)


def norm_back(upstream, normal, scale, gain):
    scaled = upstream * gain
    inner = (
        scaled
        - jnp.mean(scaled, axis=1, keepdims=True)
        - normal * jnp.mean(scaled * normal, axis=1, keepdims=True)
    )
    return (inner * scale, jnp.sum(upstream * normal, axis=0), jnp.sum(upstream, axis=0))


def gelu_slope(values):
    return (
        0.5 * (1.0 + lax.erf(values * 0.7071067811865476))
        + values * jnp.exp(-0.5 * values * values) * 0.3989422804014327
    )


def expert_forward(gathered, upward, downward):
    before = jnp.dot(gathered, upward, preferred_element_type=jnp.float32)
    active = jax.nn.gelu(before, approximate=False).astype(jnp.bfloat16)
    return jnp.dot(active, downward, preferred_element_type=jnp.float32)


def expert_backward(gathered, incoming, upward, downward):
    before = jnp.dot(gathered, upward, preferred_element_type=jnp.float32)
    active = jax.nn.gelu(before, approximate=False).astype(jnp.bfloat16)
    down_grad = jnp.einsum("rf,rd->fd", active, incoming, preferred_element_type=jnp.float32)
    through = jnp.einsum("rd,fd->rf", incoming, downward, preferred_element_type=jnp.float32)
    hidden_grad = (through * gelu_slope(before)).astype(jnp.bfloat16)
    up_grad = jnp.einsum("rd,rf->df", gathered, hidden_grad, preferred_element_type=jnp.float32)
    return (up_grad, down_grad, hidden_grad)


def head_forward(allowed, item):
    query, keys, values = item
    factor = query.shape[1] ** (-0.5)
    scores = jnp.einsum("qd,kd->qk", query, keys, preferred_element_type=jnp.float32) * factor
    scores = jnp.where(allowed, scores, -1000000000.0)
    peak = jnp.max(scores, axis=1, keepdims=True)
    weights = jnp.exp(scores - peak)
    total = jnp.sum(weights, axis=1, keepdims=True)
    mixed = jnp.dot(
        (weights / total).astype(jnp.bfloat16), values, preferred_element_type=jnp.float32
    )
    return (mixed.astype(jnp.bfloat16), (peak + jnp.log(total))[:, 0])


def head_backward(allowed, item):
    query, keys, values, upstream, log_total = item
    factor = query.shape[1] ** (-0.5)
    scores = jnp.einsum("qd,kd->qk", query, keys, preferred_element_type=jnp.float32) * factor
    scores = jnp.where(allowed, scores, -1000000000.0)
    probs = jnp.exp(scores - log_total[:, None])
    value_grad = jnp.einsum(
        "qk,qd->kd", probs.astype(jnp.bfloat16), upstream, preferred_element_type=jnp.float32
    )
    prob_grad = jnp.einsum("qd,kd->qk", upstream, values, preferred_element_type=jnp.float32)
    inner = jnp.sum(prob_grad * probs, axis=1, keepdims=True)
    score_grad = (probs * (prob_grad - inner)).astype(jnp.bfloat16)
    query_grad = (
        jnp.einsum("qk,kd->qd", score_grad, keys, preferred_element_type=jnp.float32) * factor
    )
    key_grad = (
        jnp.einsum("qk,qd->kd", score_grad, query, preferred_element_type=jnp.float32) * factor
    )
    return (query_grad, key_grad, value_grad)


def moving_tokens(
    tokens,
    gains,
    shifts,
    projection,
    mixing,
    factors,
    biases,
    centroids,
    expanding,
    contracting,
    routes,
    lengths,
    cotangent,
):
    count, width = tokens.shape
    experts = centroids.shape[0]
    groups = lax.axis_size("expert")
    slab_count = groups // experts
    capacity = max(2, 2 * count // experts)
    total_tokens = count * groups * lax.axis_size("tensor")
    average = total_tokens / experts
    route = routes[:, 0]
    picks = route[:, None] == jnp.arange(experts, dtype=jnp.int32)[None, :]
    picks_int = picks.astype(jnp.int32)
    picks_float = picks.astype(jnp.float32)
    loads = lax.psum(jnp.sum(picks_float, axis=0), ("expert", "tensor"))
    spread = (loads - average) / average
    token_spread = jnp.sum(jnp.where(picks, spread[None, :], 0.0), axis=1)
    ranks = jnp.sum(earlier(picks) * picks_int, axis=1)
    slots = route * capacity + ranks
    places = jnp.arange(count, dtype=jnp.int32)
    documents = jnp.sum(
        (places[:, None] >= running(lengths[0])[None, :]).astype(jnp.int32), axis=1
    )
    allowed = (places[:, None] >= places[None, :]) & (documents[:, None] == documents[None, :])
    inputs = tokens.astype(jnp.float32)
    entry, entry_normal, entry_scale = norm_parts(inputs, gains, shifts)
    entry = entry.astype(jnp.bfloat16)
    joint = jnp.dot(entry, projection, preferred_element_type=jnp.float32).astype(jnp.bfloat16)
    heads = joint.reshape(count, 3, HEADS, width // HEADS).transpose(1, 2, 0, 3)
    mixed, log_total = lax.map(partial(head_forward, allowed), (heads[0], heads[1], heads[2]))
    mixed_rows = mixed.transpose(1, 0, 2).reshape(count, width)
    residual = inputs + jnp.dot(mixed_rows, mixing, preferred_element_type=jnp.float32)
    normed, mixer_normal, mixer_scale = norm_parts(residual, factors, biases)
    chosen = jnp.dot(picks.astype(jnp.bfloat16), centroids, preferred_element_type=jnp.float32)
    gates = jax.nn.sigmoid(jnp.sum(normed * chosen, axis=1))
    outgoing = (
        jnp.zeros((experts * capacity, width), jnp.bfloat16)
        .at[slots]
        .set(normed.astype(jnp.bfloat16))
    )
    copies = jnp.broadcast_to(
        outgoing.reshape(experts, 1, capacity, width), (experts, slab_count, capacity, width)
    ).reshape(groups, capacity, width)
    arrived = lax.all_to_all(copies, "expert", split_axis=0, concat_axis=0, tiled=True)
    sources = groups * capacity
    own_rows = arrived.reshape(sources, width)
    gathered = lax.all_gather(own_rows, "tensor", axis=0, tiled=True)
    produced = lax.psum_scatter(
        expert_forward(gathered, expanding[0], contracting[0]).astype(jnp.bfloat16),
        "tensor",
        scatter_dimension=0,
        tiled=True,
    )
    returned = lax.all_to_all(
        produced.reshape(arrived.shape), "expert", split_axis=0, concat_axis=0, tiled=True
    )
    combined = jnp.sum(
        returned.reshape(experts, slab_count, capacity, width).astype(jnp.float32), axis=1
    ).reshape(experts * capacity, width)
    picked = combined[slots]
    layer_output = (residual + gates[:, None] * picked).astype(jnp.bfloat16)
    balance_part = jnp.sum(token_spread * gates) / total_tokens
    upstream = cotangent.astype(jnp.float32)
    gate_grad = jnp.sum(upstream * picked, axis=1)
    logit_grad = (gate_grad + token_spread / total_tokens) * gates * (1.0 - gates)
    scaled_rows = (gates[:, None] * upstream).astype(jnp.bfloat16)
    grad_slots = jnp.zeros((experts * capacity, width), jnp.bfloat16).at[slots].set(scaled_rows)
    grad_copies = jnp.broadcast_to(
        grad_slots.reshape(experts, 1, capacity, width), (experts, slab_count, capacity, width)
    ).reshape(groups, capacity, width)
    incoming = lax.all_to_all(
        grad_copies, "expert", split_axis=0, concat_axis=0, tiled=True
    ).reshape(sources, width)
    incoming_pair = lax.all_gather(incoming, "tensor", axis=0, tiled=True)
    up_share, down_share, hidden_grad = expert_backward(
        gathered, incoming_pair, expanding[0], contracting[0]
    )
    back_rows = lax.psum_scatter(
        jnp.einsum(
            "rf,df->rd", hidden_grad, expanding[0], preferred_element_type=jnp.float32
        ).astype(jnp.bfloat16),
        "tensor",
        scatter_dimension=0,
        tiled=True,
    )
    back = lax.all_to_all(
        back_rows.reshape(arrived.shape), "expert", split_axis=0, concat_axis=0, tiled=True
    )
    back_sum = jnp.sum(
        back.reshape(experts, slab_count, capacity, width).astype(jnp.float32), axis=1
    ).reshape(experts * capacity, width)
    normed_grad = back_sum[slots] + logit_grad[:, None] * chosen
    centroid_grad = jnp.einsum(
        "te,td->ed", picks_float, logit_grad[:, None] * normed, precision=highest
    )
    mixer_back, factor_grad, bias_grad = norm_back(normed_grad, mixer_normal, mixer_scale, factors)
    residual_grad = upstream + mixer_back
    branch_grad = residual_grad.astype(jnp.bfloat16)
    mixing_grad = jnp.einsum(
        "td,te->de", mixed_rows, branch_grad, preferred_element_type=jnp.float32
    )
    mixed_grad = jnp.einsum(
        "te,de->td", branch_grad, mixing, preferred_element_type=jnp.float32
    ).astype(jnp.bfloat16)
    head_grads = mixed_grad.reshape(count, HEADS, width // HEADS).transpose(1, 0, 2)
    query_grad, key_grad, value_grad = lax.map(
        partial(head_backward, allowed), (heads[0], heads[1], heads[2], head_grads, log_total)
    )
    joint_grad = (
        jnp.stack((query_grad, key_grad, value_grad))
        .transpose(2, 0, 1, 3)
        .reshape(count, 3 * width)
        .astype(jnp.bfloat16)
    )
    projection_grad = jnp.einsum("td,te->de", entry, joint_grad, preferred_element_type=jnp.float32)
    entry_back = jnp.einsum("te,de->td", joint_grad, projection, preferred_element_type=jnp.float32)
    entry_input, gain_grad, shift_grad = norm_back(entry_back, entry_normal, entry_scale, gains)
    token_grad = residual_grad + entry_input
    summed = lax.psum(
        (
            gain_grad,
            shift_grad,
            projection_grad,
            mixing_grad,
            factor_grad,
            bias_grad,
            centroid_grad,
            balance_part,
        ),
        ("expert", "tensor"),
    )
    return (
        layer_output,
        summed[7],
        token_grad,
        summed[0],
        summed[1],
        summed[2],
        summed[3],
        summed[4],
        summed[5],
        summed[6],
        up_share[None],
        down_share[None],
    )


HALF_LOG = 1.4426950408889634
LN2 = 0.6931471805599453
NT = (((1,), (1,)), ((), ()))
TN = (((0,), (0,)), ((), ()))
VMEM_LIMIT = 60 * 1024 * 1024


def query_blocks(count):
    step = 256 if count > 256 else count
    return [(i, min(i + step, count)) for i in range(0, count, step)]


def document_starts(lengths_ref, places):
    starts = jnp.zeros_like(places)
    end = 0
    for d in range(lengths_ref.shape[0]):
        end = end + lengths_ref[d]
        starts = jnp.where(places >= end, end, starts)
    return starts


MESH = pl.DeviceIdType.MESH


def neighbours(slabs):
    me, core = lax.axis_index("expert"), lax.axis_index("tensor")
    plane = lax.div(me, slabs)
    x = lax.rem(me, 2)
    y = lax.rem(lax.div(me, 2), 2)
    return me, core, plane, (me + 1 - 2 * x, core), (me + 2 - 4 * y, core), (me, 1 - core)


def greet(partners):
    barrier = pltpu.get_barrier_semaphore()
    number = 0
    for device, there in partners:
        @pl.when(there)
        def _(device=device):
            pl.semaphore_signal(barrier, inc=1, device_id=device, device_id_type=MESH)
        number = number + there.astype(jnp.int32)
    pl.semaphore_wait(barrier, number)


def score_bias(bias_ref, lengths_ref, count):
    places = lax.broadcasted_iota(jnp.int32, (1, count), 1)
    starts = document_starts(lengths_ref, places)
    for s, e in query_blocks(count):
        row = lax.broadcasted_iota(jnp.int32, (e - s, count), 0) + s
        seen = (row <= places) & (row >= starts)
        bias_ref[s:e, :] = jnp.where(seen, 0.0, -1e9)


def row_norm(values, gain, shift):
    centered = values - jnp.mean(values, axis=1, keepdims=True)
    scale = lax.rsqrt(jnp.mean(centered * centered, axis=1, keepdims=True) + epsilon)
    normal = centered * scale
    return normal * gain + shift, normal, scale


def chosen_rows(route, centroids_ref, experts):
    chosen = jnp.zeros((route.shape[0], centroids_ref.shape[1]), jnp.float32)
    for e in range(experts):
        chosen = jnp.where(route == e, centroids_ref[e : e + 1, :].astype(jnp.float32), chosen)
    return chosen


def front_kernel(
    planes,
    slabs,
    lengths_ref,
    tokens_in,
    norms_ref,
    projection_in,
    mixing_in,
    centroids_ref,
    route_row_ref,
    route_ref,
    cot_in,
    up_ref,
    down_ref,
    flipped_out,
    joint_out,
    mixed_out,
    logs_ref,
    residual_out,
    place_ref,
    loads_ref,
    sent_all,
    cot_all,
    gate_all,
    up_near,
    up_far,
    down_near,
    down_far,
    bias_ref,
    order_ref,
    normed_ref,
    entry_ref,
    sent_own,
    cot_own,
    gate_own,
    tally_ref,
    tokens_ref,
    projection_ref,
    mixing_ref,
    cot_ref,
    flipped_ref,
    joint_ref,
    mixed_ref,
    residual_ref,
    send_sem,
    recv_sem,
    local_sem,
):
    count, width = tokens_ref.shape
    experts = planes
    pairs_in = ((cot_in, cot_ref), (tokens_in, tokens_ref), (projection_in, projection_ref), (mixing_in, mixing_ref))
    brought = [pltpu.make_async_copy(a, b, local_sem.at[5 + i]) for i, (a, b) in enumerate(pairs_in)]
    pairs_out = ((joint_ref, joint_out), (mixed_ref, mixed_out), (residual_ref, residual_out), (flipped_ref, flipped_out))
    taken = [pltpu.make_async_copy(a, b, local_sem.at[9 + i]) for i, (a, b) in enumerate(pairs_out)]
    for copy in brought:
        copy.start()
    rows = sent_own.shape[0]
    half_rows = rows // 2
    pairs = width // 128
    factor = (width // HEADS) ** (-0.5) * HALF_LOG
    middle = planes - 1
    me, core, plane, beside_x, beside_y, beside_core = neighbours(slabs)
    hop_two = lax.rem(plane + 2, planes)
    hop_one = plane + 1 - 2 * lax.rem(plane, 2)
    here = lax.rem(me, slabs)
    always = plane >= 0
    greet(
        [
            (beside_x, always),
            (beside_y, always),
            (beside_core, always),
            ((hop_two * slabs + here, core), always),
            ((me + slabs, core), plane < planes - 1),
            ((me - slabs, core), plane > 0),
        ]
    )

    def remote(i, src, dst, device):
        return pltpu.make_async_remote_copy(
            src_ref=src, dst_ref=dst, send_sem=send_sem.at[i], recv_sem=recv_sem.at[i], device_id=device, device_id_type=MESH
        )

    owns, nears, fars = (up_ref, down_ref), (up_near, down_near), (up_far, down_far)
    stride = 2 * (planes - 1) + 2 * planes - 1

    def hop(kind, sign, r):
        src = owns[kind].at[0] if r == 1 else nears[kind].at[middle - sign * (r - 1)]
        i = kind * stride + (r - 1) * 2 + (sign > 0)
        return remote(i, src, nears[kind].at[middle - sign * r], (me + sign * slabs, core))

    def hop_sent(sign, r):
        ahead = plane if sign > 0 else planes - 1 - plane
        return (ahead >= r - 1) & (ahead < planes - 1)

    def hop_came(sign, r):
        ahead = plane if sign > 0 else planes - 1 - plane
        return ahead >= r

    def aside(kind, slot):
        src = owns[kind].at[0] if slot == middle else nears[kind].at[slot]
        i = kind * stride + 2 * (planes - 1) + slot
        return remote(i, src, fars[kind].at[slot], beside_x)

    def held(slot):
        at = plane + slot - middle
        return (at >= 0) & (at < planes)

    def handed(kind, sign):
        i = copies_end + kind
        return remote(i, fars[kind].at[middle], fars[kind].at[middle - sign], (me + sign * slabs, core))

    def aside_there(slot):
        if slot == middle - 1:
            return held(slot) & (plane != 1)
        if slot == middle + 1:
            return held(slot) & (plane != planes - 2)
        return held(slot)

    def own_weights(kind):
        return pltpu.make_async_copy(owns[kind].at[0], nears[kind].at[middle], local_sem.at[kind])

    for kind in range(2):
        for sign in (1, -1):
            @pl.when(hop_sent(sign, 1))
            def _(kind=kind, sign=sign):
                hop(kind, sign, 1).start()
        aside(kind, middle).start()
        own_weights(kind).start()

    def forward_weights(kind, r):
        for sign in (1, -1):
            slot = middle - sign * r

            @pl.when(hop_came(sign, r))
            def _(sign=sign):
                hop(kind, sign, r).wait_recv()

            @pl.when(aside_there(slot))
            def _(slot=slot):
                aside(kind, slot).start()

            if r < planes - 1:
                @pl.when(hop_sent(sign, r + 1))
                def _(sign=sign):
                    hop(kind, sign, r + 1).start()

    base = 2 * stride
    copies_end = base + 20

    def hand_on(kind):
        aside(kind, middle).wait_recv()
        for sign in (1, -1):
            @pl.when(plane == (0 if sign > 0 else planes - 1))
            def _(sign=sign):
                handed(kind, sign).start()

    def row_copy(which, part, piece):
        own, everyone = ((cot_own, cot_all), (sent_own, sent_all))[which]
        at = pl.ds(piece * half_rows, half_rows)
        i = base + which * 6 + part * 2 + piece
        if part == 0:
            return remote(i, own.at[at], everyone.at[2, at], beside_y)
        if part == 1:
            return remote(i, own.at[at], everyone.at[1, at], beside_core)
        return remote(i, everyone.at[2, at], everyone.at[3, at], beside_core)

    def gate_copy(part):
        i = base + 12 + part
        if part == 0:
            return remote(i, gate_own, gate_all.at[2], beside_y)
        if part == 1:
            return remote(i, gate_own, gate_all.at[1], beside_core)
        return remote(i, gate_all.at[2], gate_all.at[3], beside_core)

    def own_rows(which):
        source, everyone = ((cot_own, cot_all), (sent_own, sent_all), (gate_own, gate_all))[which]
        return pltpu.make_async_copy(source, everyone.at[0], local_sem.at[2 + which])

    rounds = [beside_core, beside_x, beside_y, (hop_one * slabs + here, core), (hop_two * slabs + here, core)]

    def tally(k):
        return remote(base + 15 + k, tally_ref.at[2 * k], tally_ref.at[2 * k + 1], rounds[k])

    def tally_step(k):
        tally(k).wait_recv()
        total = tally_ref[2 * k] + tally_ref[2 * k + 1]
        if k + 1 < len(rounds):
            tally_ref[2 * k + 2] = total
            tally(k + 1).start()
        else:
            loads_ref[...] = total

    number = lax.broadcasted_iota(jnp.int32, (8, count), 0)
    picks = jnp.where(number == route_row_ref[...], 1.0, 0.0)
    chunk = 128
    for s in range(0, count, chunk):
        row = lax.broadcasted_iota(jnp.int32, (chunk, count), 0) + s
        column = lax.broadcasted_iota(jnp.int32, (chunk, count), 1)
        order_ref[s : s + chunk, :] = jnp.where(row < column, 1.0, 0.0).astype(jnp.bfloat16)
    ranks = jnp.dot(picks.astype(jnp.bfloat16), order_ref[0:count, :], preferred_element_type=jnp.float32)
    counts = jnp.sum(picks, axis=1, keepdims=True)
    padded = jnp.ceil(counts * (1.0 / ALIGN)) * ALIGN
    place = jnp.zeros((1, count), jnp.float32)
    start = jnp.zeros((1, 1), jnp.float32)
    for e in range(experts):
        place = place + picks[e : e + 1, :] * (ranks[e : e + 1, :] + start)
        start = start + padded[e : e + 1, :]
    place_ref[...] = jnp.broadcast_to(place, (8, count))
    tally_ref[0] = jnp.broadcast_to(counts, (8, 128))
    tally(0).start()
    for s in range(0, rows, 64):
        row = lax.broadcasted_iota(jnp.int32, (64, count), 0) + s
        order_ref[s : s + 64, :] = jnp.where(row.astype(jnp.float32) == place, 1.0, 0.0).astype(jnp.bfloat16)

    def sort_rows(source_ref, to_ref, which):
        for piece in range(2):
            at = slice(piece * half_rows, (piece + 1) * half_rows)
            to_ref[at, :] = jnp.dot(
                order_ref[at, :], source_ref[...], preferred_element_type=jnp.float32
            ).astype(jnp.bfloat16)
            row_copy(which, 0, piece).start()
            row_copy(which, 1, piece).start()

    brought[0].wait()
    sort_rows(cot_ref, cot_own, 0)
    own_rows(0).start()

    def project(i, _):
        at = pl.ds(pl.multiple_of(i * 192, 192), 192)
        entry, _, _ = row_norm(tokens_ref[at, :].astype(jnp.float32), norms_ref[0:1, :], norms_ref[1:2, :])
        entry = entry.astype(jnp.bfloat16)
        entry_ref[at, :] = entry
        joint_ref[at, :] = jnp.dot(entry, projection_ref[...], preferred_element_type=jnp.float32).astype(jnp.bfloat16)
        return 0

    for copy in brought[1:]:
        copy.wait()
    lax.fori_loop(0, count // 192, project, 0)
    taken[0].start()
    score_bias(bias_ref, lengths_ref, count)
    forward_weights(0, 1)
    tally_step(0)

    first = lax.broadcasted_iota(jnp.int32, (1, 128), 1) < 64

    def attend(p, _):
        lanes = pl.ds(pl.multiple_of(p * 128, 128), 128)
        keys = pl.ds(pl.multiple_of(width + p * 128, 128), 128)
        values = pl.ds(pl.multiple_of(2 * width + p * 128, 128), 128)
        for s, e in query_blocks(count):
            outs = []
            for half in range(2):
                q = jnp.where(first == (half == 0), joint_ref[s:e, lanes], jnp.bfloat16(0))
                scores = lax.dot_general(joint_ref[0:e, keys], q, NT, preferred_element_type=jnp.float32)
                scores = scores * factor + bias_ref[0:e, s:e]
                peak = jnp.max(scores, axis=0, keepdims=True)
                weights = jnp.exp2(scores - peak)
                total = jnp.sum(weights, axis=0, keepdims=True)
                probs = (weights * (1.0 / total)).astype(jnp.bfloat16)
                outs.append(
                    lax.dot_general(probs, joint_ref[0:e, values], TN, preferred_element_type=jnp.float32)
                )
                logs_ref[p, half : half + 1, s:e] = peak + jnp.log2(total)
            mixed_ref[s:e, lanes] = jnp.where(first, outs[0], outs[1]).astype(jnp.bfloat16)

        @pl.when(p == 2)
        def _():
            forward_weights(1, 1)
            hand_on(0)
            tally_step(1)

        @pl.when(p == 4)
        def _():
            hand_on(1)
            forward_weights(0, 2)
            tally_step(2)

        return 0

    lax.fori_loop(0, pairs, attend, 0)
    taken[1].start()

    lane = lax.broadcasted_iota(jnp.int32, (1, 128), 1)

    def mix(i, _):
        at = pl.ds(pl.multiple_of(i * 192, 192), 192)
        residual = tokens_ref[at, :].astype(jnp.float32) + jnp.dot(
            mixed_ref[at, :], mixing_ref[...], preferred_element_type=jnp.float32
        )
        residual_ref[at, :] = residual
        normed, _, _ = row_norm(residual, norms_ref[2:3, :], norms_ref[3:4, :])
        chosen = chosen_rows(route_ref[at, :], centroids_ref, experts)
        gate = 1.0 / (1.0 + jnp.exp(-jnp.sum(normed * chosen, axis=1, keepdims=True)))
        high = gate.astype(jnp.bfloat16).astype(jnp.float32)
        mid = (gate - high).astype(jnp.bfloat16).astype(jnp.float32)
        low = gate - high - mid
        parts = jnp.where(lane == 0, high, jnp.where(lane == 1, mid, jnp.where(lane == 2, low, 0.0)))
        normed_ref[at, 0:width] = normed.astype(jnp.bfloat16)
        normed_ref[at, width : width + 128] = parts.astype(jnp.bfloat16)
        return 0

    lax.fori_loop(0, count // 192, mix, 0)
    taken[2].start()
    for piece in range(2):
        at = slice(piece * half_rows, (piece + 1) * half_rows)
        moved = jnp.dot(order_ref[at, :], normed_ref[...], preferred_element_type=jnp.float32)
        sent_own[at, :] = moved[:, 0:width].astype(jnp.bfloat16)
        row_copy(1, 0, piece).start()
        row_copy(1, 1, piece).start()
        bias_ref[at, 0:128] = jnp.broadcast_to(
            jnp.sum(moved[:, width : width + 128], axis=1, keepdims=True), (half_rows, 128)
        )
    forward_weights(1, 2)
    tally_step(3)
    for piece in range(2):
        row_copy(0, 0, piece).wait_recv()
        row_copy(0, 2, piece).start()
    gates = jnp.transpose(bias_ref[0:rows, 0:128])
    gate_own[0:1, :] = gates[0:1, :]
    gate_own[1:2, :] = jnp.zeros((1, rows), jnp.float32)
    for e in range(8):
        gate_own[1:2, e : e + 1] = padded[e : e + 1, :]
    gate_copy(0).start()
    gate_copy(1).start()
    own_rows(1).start()
    own_rows(2).start()
    for s in range(0, count, 384):
        flipped_ref[:, s : s + 384] = jnp.transpose(entry_ref[s : s + 384, :])
    taken[3].start()

    for kind in range(2):
        forward_weights(kind, 3)
    gate_copy(0).wait_recv()
    gate_copy(2).start()
    tally_step(4)
    for piece in range(2):
        row_copy(1, 0, piece).wait_recv()
        row_copy(1, 2, piece).start()

    for which in range(2):
        for part in range(3):
            for piece in range(2):
                copy = row_copy(which, part, piece)
                copy.wait_send()
                if part:
                    copy.wait_recv()
    for part in range(3):
        gate_copy(part).wait_send()
        if part:
            gate_copy(part).wait_recv()
    for k in range(len(rounds)):
        tally(k).wait_send()
    for copy in taken:
        copy.wait()
    for which in range(3):
        own_rows(which).wait()
    for kind in range(2):
        own_weights(kind).wait()
        for r in range(1, planes):
            for sign in (1, -1):
                @pl.when(hop_sent(sign, r))
                def _(kind=kind, sign=sign, r=r):
                    hop(kind, sign, r).wait_send()
        for slot in range(2 * planes - 1):
            if slot == middle:
                aside(kind, slot).wait_send()
                continue

            @pl.when(aside_there(slot))
            def _(kind=kind, slot=slot):
                aside(kind, slot).wait()
        for sign in (1, -1):
            @pl.when(plane == (0 if sign > 0 else planes - 1))
            def _(kind=kind, sign=sign):
                handed(kind, sign).wait_send()

            @pl.when(plane == (1 if sign > 0 else planes - 2))
            def _(kind=kind, sign=sign):
                handed(kind, sign).wait_recv()


def front_stage(
    tokens, norms, projection, mixing, centroids, expanding, contracting, route, lengths, cotangent, planes, slabs
):
    count, width = tokens.shape
    rows = aligned_rows(count, planes)
    pairs = width // 128
    slots = 2 * planes - 1
    bf16, f32 = jnp.bfloat16, jnp.float32
    shape = jax.ShapeDtypeStruct
    anywhere = pl.BlockSpec(memory_space=pl.ANY)
    local = pl.BlockSpec(memory_space=pltpu.VMEM)
    dma = pltpu.SemaphoreType.DMA
    copies = 2 * (2 * (planes - 1) + slots) + 12 + 3 + 5 + 2
    outs = [
        (shape((width, count), bf16), anywhere),
        (shape((count, 3 * width), bf16), anywhere),
        (shape((count, width), bf16), anywhere),
        (shape((pairs, 2, count), f32), local),
        (shape((count, width), f32), anywhere),
        (shape((8, count), f32), local),
        (shape((8, 128), f32), local),
        (shape((4, rows, width), bf16), anywhere),
        (shape((4, rows, width), bf16), anywhere),
        (shape((4, 8, rows), f32), anywhere),
        (shape((slots,) + expanding.shape[1:], bf16), anywhere),
        (shape((slots,) + expanding.shape[1:], bf16), anywhere),
        (shape((slots,) + contracting.shape[1:], bf16), anywhere),
        (shape((slots,) + contracting.shape[1:], bf16), anywhere),
    ]
    return pl.pallas_call(
        partial(front_kernel, planes, slabs),
        out_shape=[o[0] for o in outs],
        in_specs=[pl.BlockSpec(memory_space=pltpu.SMEM)] + [anywhere, local] + [anywhere] * 2 + [local] * 3 + [anywhere] * 3,
        out_specs=[o[1] for o in outs],
        scratch_shapes=[
            pltpu.VMEM((rows, count), f32),
            pltpu.VMEM((rows, count), bf16),
            pltpu.VMEM((count, width + 128), bf16),
            pltpu.VMEM((count, width), bf16),
            pltpu.VMEM((rows, width), bf16),
            pltpu.VMEM((rows, width), bf16),
            pltpu.VMEM((8, rows), f32),
            pltpu.VMEM((10, 8, 128), f32),
            pltpu.VMEM(tokens.shape, bf16),
            pltpu.VMEM(projection.shape, bf16),
            pltpu.VMEM(mixing.shape, bf16),
            pltpu.VMEM(cotangent.shape, bf16),
            pltpu.VMEM((width, count), bf16),
            pltpu.VMEM((count, 3 * width), bf16),
            pltpu.VMEM((count, width), bf16),
            pltpu.VMEM((count, width), f32),
            dma((copies,)),
            dma((copies,)),
            dma((13,)),
        ],
        compiler_params=pltpu.CompilerParams(
            collective_id=0, has_side_effects=True, vmem_limit_bytes=VMEM_LIMIT
        ),
    )(
        lengths[0],
        tokens,
        norms,
        projection,
        mixing,
        centroids,
        route.reshape(1, -1),
        route,
        cotangent,
        expanding,
        contracting,
    )


STEP = 192


def rear_kernel(
    planes,
    slabs,
    total_tokens,
    lengths_ref,
    tokens_in,
    norms_ref,
    projection_in,
    mixing_ref,
    centroids_ref,
    route_ref,
    cot_in,
    flipped_in,
    joint_in,
    mixed_in,
    logs_ref,
    residual_in,
    place_ref,
    loads_ref,
    dots_ref,
    back_all,
    made_all,
    near_all,
    far_all,
    layer_to,
    token_to,
    vector_ref,
    up_to,
    down_to,
    shared_out,
    core_land,
    y_land,
    x_land,
    z_land,
    joint_ref,
    residual_ref,
    bias_ref,
    upstream_ref,
    a_ref,
    b_ref,
    made_ref,
    place_col,
    gate_col,
    dot_land,
    part_ref,
    stage_ref,
    own_ref,
    own_core,
    own_first,
    own_second,
    own_z,
    piece_ref,
    tally_ref,
    key_sums,
    tokens_ref,
    projection_ref,
    cot_ref,
    flipped_ref,
    mixed_ref,
    layer_ref,
    token_ref,
    up_out,
    down_out,
    send_sem,
    recv_sem,
    local_sem,
):
    count, width = tokens_ref.shape
    experts = planes
    rows = a_ref.shape[0]
    half_rows = rows // 2
    pairs = width // 128
    half = width // 2
    scale = (width // HEADS) ** (-0.5)
    factor = scale * HALF_LOG
    average = total_tokens / experts
    me, core, plane, beside_x, beside_y, beside_core = neighbours(slabs)
    x = lax.rem(me, 2)
    y = lax.rem(lax.div(me, 2), 2)
    here = lax.rem(me, slabs)
    diagonal = (beside_y[0], 1 - core)
    always = plane >= 0
    others = [(lax.rem(plane + d, planes) * slabs + here, core) for d in range(1, planes)]
    across_plane = (me + 3 - 2 * x - 4 * y, core)

    def fetch(i, src, dst):
        return pltpu.make_async_copy(src, dst, local_sem.at[i])

    loads = [
        fetch(0, residual_in, residual_ref),
        fetch(1, joint_in, joint_ref),
        fetch(8, cot_in, cot_ref),
        fetch(9, mixed_in, mixed_ref),
        fetch(10, flipped_in, flipped_ref),
        fetch(11, tokens_in, tokens_ref),
        fetch(12, projection_in, projection_ref),
    ]
    results = [
        fetch(13, token_ref, token_to),
        fetch(14, layer_ref, layer_to),
        fetch(15, up_out, up_to),
        fetch(16, down_out, down_to),
    ]
    greet([(d, always) for d in [beside_x, beside_y, beside_core, diagonal, across_plane] + others])
    ids = {}

    def remote(key, src, dst, device):
        i = ids.setdefault(key, len(ids))
        return pltpu.make_async_remote_copy(
            src_ref=src, dst_ref=dst, send_sem=send_sem.at[i], recv_sem=recv_sem.at[i], device_id=device, device_id_type=MESH
        )

    alls = (back_all, made_all)

    def to_core(which, second, piece):
        at = pl.ds(piece * half_rows, half_rows)
        return remote(
            ("core", which, second, piece), alls[which].at[1 + 2 * second, at], core_land.at[which, second, at], beside_core
        )

    def to_y(which, piece):
        at = pl.ds(piece * half_rows, half_rows)
        return remote(("y", which, piece), (a_ref, made_ref)[which].at[at], y_land.at[which, at], beside_y)

    def dot_copy(k):
        return remote(("dot", k), dots_ref.at[1 + k], dot_land.at[k], (beside_core, beside_y, diagonal)[k])

    for which in range(2):
        for second in (1, 0):
            for piece in range(2):
                to_core(which, second, piece).start()
        if which == 0:
            for k in range(3):
                dot_copy(k).start()

    def target(sign, r):
        e = plane + sign * r
        return jnp.clip(e, 0, planes - 1), (e >= 0) & (e < planes)

    def share_x(sign, r):
        e, _ = target(sign, r)
        return remote(("x", sign, r), far_all.at[e], x_land.at[e], beside_x)

    def share_z(sign, r):
        return remote(
            ("z", sign, r),
            stage_ref.at[0 if sign > 0 else 1],
            z_land.at[0 if sign > 0 else 1, r - 1],
            (jnp.clip(me + sign * slabs, 0, planes * slabs - 1), core),
        )

    ways = [(s, r) for r in range(planes - 1, 0, -1) for s in (1, -1)] + [(1, 0)]
    def start_shares(distance):
        for sign, r in ways:
            if r == distance:
                @pl.when(target(sign, r)[1])
                def _(sign=sign, r=r):
                    share_x(sign, r).start()

    for distance in range(planes - 1, 1, -1):
        start_shares(distance)

    def add_pieces(into, sources, size, step):
        def one(i, _):
            at = pl.ds(pl.multiple_of(i * step, step), step)
            total = sources[0][at, :].astype(jnp.float32)
            for s in sources[1:]:
                total = total + s[at, :].astype(jnp.float32)
            into[at, :] = total.astype(into.dtype)
            return 0
        lax.fori_loop(0, size // step, one, 0)

    def share_step(sign, r):
        e, valid = target(sign, r)
        lane = 0 if sign > 0 else 1

        @pl.when(valid)
        def _():
            first = fetch(2, near_all.at[e], part_ref.at[0])
            first.start()
            share_x(sign, r).wait_recv()
            second = fetch(3, x_land.at[e], part_ref.at[1])
            second.start()
            if r < planes - 1:
                @pl.when(target(sign, r + 1)[1])
                def _():
                    share_z(sign, r + 1).wait_send()
            first.wait()
            second.wait()
            add_pieces(stage_ref.at[lane], [part_ref.at[0], part_ref.at[1]], part_ref.shape[1], 96)
            if r < planes - 1:
                @pl.when((plane - sign >= 0) & (plane - sign < planes))
                def _():
                    share_z(sign, r + 1).wait_recv()
                    third = fetch(2, z_land.at[lane, r], part_ref.at[0])
                    third.start()
                    third.wait()
                    add_pieces(stage_ref.at[lane], [stage_ref.at[lane], part_ref.at[0]], part_ref.shape[1], 96)
            share_z(sign, r).start()

    def share_end():
        share_x(1, 0).wait_recv()
        copies = [fetch(2, near_all.at[plane], part_ref.at[0]), fetch(3, x_land.at[plane], part_ref.at[1])]
        for copy in copies:
            copy.start()
        for copy in copies:
            copy.wait()

        def put(sources, more):
            def rows_of(i, _):
                at = pl.ds(pl.multiple_of(i * 96, 96), 96)
                total = sources[0][at, :].astype(jnp.float32)
                if len(sources) > 1:
                    total = total + sources[1][at, :].astype(jnp.float32)
                up_out[at, :] = up_out[at, :] + total if more else total
                return 0
            lax.fori_loop(0, width // 96, rows_of, 0)

            def columns_of(i, _):
                at = pl.ds(pl.multiple_of(i * 96, 96), 96)
                for part in range(2):
                    source_at = pl.ds(pl.multiple_of(width + part * half + i * 96, 32), 96)
                    total = sources[0][source_at, :].astype(jnp.float32)
                    if len(sources) > 1:
                        total = total + sources[1][source_at, :].astype(jnp.float32)
                    to = slice(part * half, (part + 1) * half)
                    down_out[at, to] = down_out[at, to] + total if more else total
                return 0
            lax.fori_loop(0, half // 96, columns_of, 0)

        put([part_ref.at[0], part_ref.at[1]], False)
        for sign in (1, -1):
            lane = 0 if sign > 0 else 1

            @pl.when((plane - sign >= 0) & (plane - sign < planes))
            def _(sign=sign, lane=lane):
                share_z(sign, 1).wait_recv()
                third = fetch(2, z_land.at[lane, 0], part_ref.at[0])
                third.start()
                third.wait()
                put([part_ref.at[0]], True)

    q1, q2, q3, q4 = width // 2, width // 4, width // 8, width // 16
    base1 = core * q1
    base2 = base1 + y * q2
    base3 = base2 + x * q3

    def spot(start, size):
        return pl.ds(pl.multiple_of(start, 16), size)

    def corner(p):
        return lax.div(p, 2) * q4, pl.multiple_of(lax.rem(p, 2) * half, 128)

    def sum_copy(c, stage, d=0):
        own = own_ref.at[c]
        if stage == "core":
            return remote((c, stage), own.at[spot((1 - core) * q1, q1)], own_core.at[c], beside_core)
        if stage == "plane":
            at = base1 + (y if d == 0 else 1 - y) * q2 + (x if d == 1 else 1 - x) * q3
            land = own_second.at[c] if d == 2 else own_first.at[c, pl.ds(d * q3, q3)]
            return remote((c, stage, d), own.at[spot(at, q3)], land, (beside_x, beside_y, across_plane)[d])
        if stage == "first":
            return remote((c, stage), own.at[spot(base1 + (1 - y) * q2, q2)], own_first.at[c], beside_y)
        if stage == "second":
            return remote((c, stage), own.at[spot(base2 + (1 - x) * q3, q3)], own_second.at[c], beside_x)
        if stage == "z":
            r, k = corner(lax.rem(plane + d, planes))
            return remote(
                (c, stage, d), own.at[spot(base3 + r, q4), pl.ds(k, half)], own_z.at[c, d - 1], others[d - 1]
            )
        out = shared_out.at[c]
        if stage == "zz":
            r, k = corner(plane)
            return remote(
                (c, stage, d), piece_ref.at[c], out.at[spot(base3 + r, q4), pl.ds(k, half)], others[d - 1]
            )
        if stage == "plane back":
            at = spot(base3, q3)
            return remote((c, stage, d), out.at[at], out.at[at], (beside_x, beside_y, across_plane)[d])
        if stage == "second back":
            at = spot(base3, q3)
            return remote((c, stage), out.at[at], out.at[at], beside_x)
        if stage == "first back":
            at = spot(base2, q2)
            return remote((c, stage), out.at[at], out.at[at], beside_y)
        at = spot(base1, q1)
        return remote((c, stage), out.at[at], out.at[at], beside_core)

    def add_rows(c, start, size, came, step):
        def one(i, _):
            at = pl.ds(pl.multiple_of(i * step, step), step)
            mine = spot(start + i * step, step)
            own_ref[c, mine, :] = (
                own_ref[c, mine, :].astype(jnp.float32) + came[c, at, :].astype(jnp.float32)
            ).astype(jnp.bfloat16)
            return 0
        lax.fori_loop(0, size // step, one, 0)

    def keep_piece(c):
        r, k = corner(plane)
        return fetch(4 + c, piece_ref.at[c], shared_out.at[c, spot(base3 + r, q4), pl.ds(k, half)])

    def sum_step(c, stage):
        if stage == 0:
            sum_copy(c, "core").start()
        elif stage == 1:
            sum_copy(c, "core").wait_recv()
            add_rows(c, base1, q1, own_core, 48)
            sum_copy(c, "first").start()
        elif stage == 2:
            sum_copy(c, "first").wait_recv()
            add_rows(c, base2, q2, own_first, 48)
            sum_copy(c, "second").start()
        elif stage == 3:
            sum_copy(c, "second").wait_recv()
            add_rows(c, base3, q3, own_second, 48)
            for d in range(1, planes):
                sum_copy(c, "z", d).start()
        elif stage == 4:
            r, k = corner(plane)
            total = own_ref[c, spot(base3 + r, q4), pl.ds(k, half)].astype(jnp.float32)
            for d in range(1, planes):
                sum_copy(c, "z", d).wait_recv()
                total = total + own_z[c, d - 1].astype(jnp.float32)
            piece_ref[c] = total.astype(jnp.bfloat16)
            keep_piece(c).start()
            for d in range(1, planes):
                sum_copy(c, "zz", d).start()
        elif stage == 5:
            keep_piece(c).wait()
            for d in range(1, planes):
                sum_copy(c, "zz", d).wait_recv()
            sum_copy(c, "second back").start()
        elif stage == 6:
            sum_copy(c, "second back").wait_recv()
            sum_copy(c, "first back").start()
        elif stage == 7:
            sum_copy(c, "first back").wait_recv()
            sum_copy(c, "cc").start()
        else:
            sum_copy(c, "cc").wait_recv()

    def last_step(stage):
        c = 3
        if stage == 1:
            sum_copy(c, "core").wait_recv()
            add_rows(c, base1, q1, own_core, 48)
            for d in range(3):
                sum_copy(c, "plane", d).start()
        elif stage == 2:
            for d in range(3):
                sum_copy(c, "plane", d).wait_recv()

            def one(i, _):
                mine = spot(base3 + i * 48, 48)
                total = own_ref[c, mine, :].astype(jnp.float32)
                for d in range(2):
                    total = total + own_first[c, spot(d * q3 + i * 48, 48), :].astype(jnp.float32)
                total = total + own_second[c, spot(i * 48, 48), :].astype(jnp.float32)
                own_ref[c, mine, :] = total.astype(jnp.bfloat16)
                return 0
            lax.fori_loop(0, q3 // 48, one, 0)
            for d in range(1, planes):
                sum_copy(c, "z", d).start()
        elif stage == 3:
            sum_step(c, 4)
        elif stage == 4:
            keep_piece(c).wait()
            for d in range(1, planes):
                sum_copy(c, "zz", d).wait_recv()
            for d in range(3):
                sum_copy(c, "plane back", d).start()
        elif stage == 5:
            for d in range(3):
                sum_copy(c, "plane back", d).wait_recv()
            sum_copy(c, "cc").start()
        else:
            sum_copy(c, "cc").wait_recv()

    def sum_sent(c):
        sum_copy(c, "core").wait_send()
        if c < 3:
            for stage in ("first", "second", "second back", "first back"):
                sum_copy(c, stage).wait_send()
        else:
            for d in range(3):
                sum_copy(c, "plane", d).wait_send()
                sum_copy(c, "plane back", d).wait_send()
        for d in range(1, planes):
            sum_copy(c, "z", d).wait_send()

    def sum_for_y(which):
        into = (a_ref, made_ref)[which]
        for piece in range(2):
            at = pl.ds(piece * half_rows, half_rows)
            first = fetch(2, alls[which].at[2, at], into.at[at])
            first.start()
            to_core(which, 1, piece).wait_recv()
            second = fetch(3, core_land.at[which, 1, at], b_ref.at[at])
            second.start()
            first.wait()
            second.wait()
            add_pieces(into.at[at], [into.at[at], b_ref.at[at]], half_rows, 32)
            to_y(which, piece).start()

    sum_for_y(0)
    for copy in loads:
        copy.start()
    sum_for_y(1)
    place_col[...] = jnp.transpose(place_ref[...])
    score_bias(bias_ref, lengths_ref, count)
    for copy in loads:
        copy.wait()
    vector_ref[...] = jnp.zeros_like(vector_ref)
    number = lax.broadcasted_iota(jnp.int32, (1, rows), 1).astype(jnp.float32)

    def order_of(at):
        return jnp.where(place_col[at, 0:1] == number, 1.0, 0.0)

    def chunk_of(i):
        return pl.ds(pl.multiple_of(i * STEP, STEP), STEP)

    steps = count // STEP

    def unsort(buffer, act):
        def one(i, _):
            at = chunk_of(i)
            act(at, jnp.dot(order_of(at).astype(jnp.bfloat16), buffer[...], preferred_element_type=jnp.float32))
            return 0
        lax.fori_loop(0, steps, one, 0)

    def set_token(at, value):
        token_ref[at, :] = value

    def add_token(at, value):
        token_ref[at, :] += value

    own_back = fetch(2, back_all.at[0], b_ref)
    own_back.start()
    own_back.wait()
    unsort(b_ref, set_token)
    for piece in range(2):
        to_core(0, 0, piece).wait_recv()
    core_back = fetch(2, core_land.at[0, 0], b_ref)
    core_back.start()
    core_back.wait()
    unsort(b_ref, add_token)
    for sign in (1, -1):
        share_step(sign, planes - 1)
    start_shares(1)
    for piece in range(2):
        to_y(0, piece).wait_recv()
    y_back = fetch(2, y_land.at[0], b_ref)
    y_back.start()
    y_back.wait()
    unsort(b_ref, add_token)
    for sign in (1, -1):
        share_step(sign, planes - 2)
    for k in range(3):
        dot_copy(k).wait_recv()
    dots = dots_ref[0] + dot_land[0] + dot_land[1] + dot_land[2]
    dots = dots[0:1, :]

    def norm_step(i, _):
        at = chunk_of(i)
        normed, normal, spread_by = row_norm(residual_ref[at, :], norms_ref[2:3, :], norms_ref[3:4, :])
        route = route_ref[at, :]
        chosen = chosen_rows(route, centroids_ref, experts)
        gate = 1.0 / (1.0 + jnp.exp(-jnp.sum(normed * chosen, axis=1, keepdims=True)))
        gate_col[at, :] = jnp.broadcast_to(gate, (STEP, 128))
        gate_grad = jnp.sum(order_of(at) * dots, axis=1, keepdims=True)
        spread = jnp.zeros((STEP, 1), jnp.float32)
        for e in range(experts):
            spread = jnp.where(route == e, (loads_ref[e : e + 1, 0:1] - average) * (1.0 / average), spread)
        logit = (gate_grad + spread * (1.0 / total_tokens)) * gate * (1.0 - gate)
        above = token_ref[at, :] + logit * chosen
        pull = logit * normed
        vector_ref[2:3, :] += jnp.sum(above * normal, axis=0, keepdims=True)
        vector_ref[3:4, :] += jnp.sum(above, axis=0, keepdims=True)
        for e in range(experts):
            vector_ref[8 + e : 9 + e, :] += jnp.sum(jnp.where(route == e, pull, 0.0), axis=0, keepdims=True)
        vector_ref[4:5, :] += jnp.broadcast_to(
            jnp.sum(spread * gate, axis=0, keepdims=True) * (1.0 / total_tokens), (1, width)
        )
        scaled = above * norms_ref[2:3, :]
        inner = (
            scaled
            - jnp.mean(scaled, axis=1, keepdims=True)
            - normal * jnp.mean(scaled * normal, axis=1, keepdims=True)
        )
        grad = cot_ref[at, :].astype(jnp.float32) + inner * spread_by
        token_ref[at, :] = grad
        branch = grad.astype(jnp.bfloat16)
        layer_ref[at, :] = branch
        upstream_ref[at, :] = lax.dot_general(
            branch, mixing_ref[...], NT, preferred_element_type=jnp.float32
        ).astype(jnp.bfloat16)
        return 0

    lax.fori_loop(0, steps, norm_step, 0)
    own_ref[0] = lax.dot_general(
        mixed_ref[...], layer_ref[...], TN, preferred_element_type=jnp.float32
    ).astype(jnp.bfloat16)
    sum_step(0, 0)

    first = lax.broadcasted_iota(jnp.int32, (1, 128), 1) < 64

    def attend(p, _):
        lanes = pl.ds(pl.multiple_of(p * 128, 128), 128)
        keys = pl.ds(pl.multiple_of(width + p * 128, 128), 128)
        values = pl.ds(pl.multiple_of(2 * width + p * 128, 128), 128)
        key_sum, value_sum = key_sums.at[0], key_sums.at[1]
        key_sum[...] = jnp.zeros_like(key_sum)
        value_sum[...] = jnp.zeros_like(value_sum)
        for s, e in query_blocks(count):
            both = jnp.transpose(
                upstream_ref[s:e, lanes].astype(jnp.float32) * mixed_ref[s:e, lanes].astype(jnp.float32)
            )
            found = []
            for h in range(2):
                mine = first == (h == 0)
                inner = jnp.sum(both[64 * h : 64 * h + 64, :], axis=0, keepdims=True)
                q = jnp.where(mine, joint_ref[s:e, lanes], jnp.bfloat16(0))
                u = jnp.where(mine, upstream_ref[s:e, lanes], jnp.bfloat16(0))
                scores = lax.dot_general(joint_ref[0:e, keys], q, NT, preferred_element_type=jnp.float32)
                probs = jnp.exp2(scores * factor + bias_ref[0:e, s:e] - logs_ref[p, h : h + 1, s:e])
                prob_grad = lax.dot_general(joint_ref[0:e, values], u, NT, preferred_element_type=jnp.float32)
                score_grad = (probs * (prob_grad - inner)).astype(jnp.bfloat16)
                value_sum[0:e, :] += jnp.dot(probs.astype(jnp.bfloat16), u, preferred_element_type=jnp.float32)
                key_sum[0:e, :] += jnp.dot(score_grad, q, preferred_element_type=jnp.float32)
                found.append(
                    lax.dot_general(score_grad, joint_ref[0:e, keys], TN, preferred_element_type=jnp.float32)
                )
            joint_ref[s:e, lanes] = (jnp.where(first, found[0], found[1]) * scale).astype(jnp.bfloat16)
        joint_ref[:, keys] = (key_sum[...] * scale).astype(jnp.bfloat16)
        joint_ref[:, values] = value_sum[...].astype(jnp.bfloat16)

        events = {
            0: [],
            1: [(0, 1)],
            2: [(1, 1)],
            3: [(0, 2)],
            4: [(1, 2), (2, 1)],
        }
        for k, steps_of in events.items():
            @pl.when(p == k)
            def _(k=k, steps_of=steps_of):
                for c, stage in steps_of:
                    sum_step(c, stage)
                if k == 0:
                    start_shares(0)
                if k == 2:
                    for sign in (1, -1):
                        share_step(sign, 1)
        for c in range(1, 4):
            @pl.when(p == 2 * c - 1)
            def _(c=c):
                for k in range(3):
                    at = pl.ds(k * width + (c - 1) * 256, 256)
                    own_ref[c, :, k * 256 : (k + 1) * 256] = jnp.dot(
                        flipped_ref[...], joint_ref[:, at], preferred_element_type=jnp.float32
                    ).astype(jnp.bfloat16)
                sum_step(c, 0)

        return 0

    lax.fori_loop(0, pairs, attend, 0)

    rounds = [beside_core, beside_x, beside_y]
    rounds += [((plane + 1 - 2 * lax.rem(plane, 2)) * slabs + here, core), (lax.rem(plane + 2, planes) * slabs + here, core)]

    def tally(k):
        return remote(("tally", k), tally_ref.at[2 * k], tally_ref.at[2 * k + 1], rounds[k])

    def tally_step(k):
        tally(k).wait_recv()
        total = tally_ref[2 * k] + tally_ref[2 * k + 1]
        if k + 1 < len(rounds):
            tally_ref[2 * k + 2] = total
            tally(k + 1).start()
        else:
            vector_ref[...] = total

    def finish_step(i, _):
        at = chunk_of(i)
        back = lax.dot_general(joint_ref[at, :], projection_ref[...], NT, preferred_element_type=jnp.float32)
        _, normal, spread_by = row_norm(tokens_ref[at, :].astype(jnp.float32), norms_ref[0:1, :], norms_ref[1:2, :])
        scaled = back * norms_ref[0:1, :]
        inner = (
            scaled
            - jnp.mean(scaled, axis=1, keepdims=True)
            - normal * jnp.mean(scaled * normal, axis=1, keepdims=True)
        )
        token_ref[at, :] += inner * spread_by
        vector_ref[0:1, :] += jnp.sum(back * normal, axis=0, keepdims=True)
        vector_ref[1:2, :] += jnp.sum(back, axis=0, keepdims=True)
        return 0

    def end_made(at, value):
        layer_ref[at, :] = (residual_ref[at, :] + gate_col[at, 0:1] * value).astype(jnp.bfloat16)

    def load(source, into):
        copy = fetch(2, source, into)
        copy.start()
        copy.wait()

    def sum_steps(*which):
        for c, stage in which:
            if c == 3:
                last_step(stage)
            else:
                sum_step(c, stage)

    lax.fori_loop(0, steps // 2, finish_step, 0)
    sum_steps((3, 1), (0, 3), (1, 3), (2, 2))
    lax.fori_loop(steps // 2, steps, finish_step, 0)
    results[0].start()
    tally_ref[0] = vector_ref[...]
    tally(0).start()
    sum_steps((0, 4), (1, 4), (2, 3))
    for piece in range(2):
        to_y(0, piece).wait_send()
    load(made_all.at[0], a_ref)
    for piece in range(2):
        to_core(1, 0, piece).wait_recv()
    load(core_land.at[1, 0], b_ref)
    add_pieces(a_ref, [a_ref, b_ref], rows, 32)
    sum_steps((3, 2), (0, 5), (1, 5), (2, 4))
    tally_step(0)
    for piece in range(2):
        to_y(1, piece).wait_recv()
    load(y_land.at[1], b_ref)
    add_pieces(a_ref, [a_ref, b_ref], rows, 32)
    sum_steps((3, 3), (0, 6), (1, 6), (2, 5))
    tally_step(1)
    unsort(a_ref, end_made)
    results[1].start()
    sum_steps((3, 4), (2, 6))
    tally_step(2)
    share_end()
    results[2].start()
    results[3].start()
    sum_steps((3, 5), (0, 7), (1, 7))
    tally_step(3)
    sum_steps((2, 7),)
    tally_step(4)
    sum_steps((0, 8), (1, 8), (3, 6), (2, 8))
    for copy in results:
        copy.wait()

    for which in range(2):
        for piece in range(2):
            for second in range(2):
                to_core(which, second, piece).wait_send()
    for piece in range(2):
        to_y(1, piece).wait_send()
    for k in range(3):
        dot_copy(k).wait_send()
    for sign, r in ways:
        @pl.when(target(sign, r)[1])
        def _(sign=sign, r=r):
            share_x(sign, r).wait_send()
    for sign in (1, -1):
        @pl.when(target(sign, 1)[1])
        def _(sign=sign):
            share_z(sign, 1).wait_send()
    for c in range(4):
        sum_sent(c)
    for c in range(4):
        for d in range(1, planes):
            sum_copy(c, "zz", d).wait_send()
        sum_copy(c, "cc").wait_send()
    for k in range(len(rounds)):
        tally(k).wait_send()
    assert len(ids) <= send_sem.shape[0]


def rear_stage(
    tokens, norms, projection, mixing, centroids, route, lengths, cotangent,
    flipped, joint, mixed, logs, residual, place, loads, dots, back, made, near, far, planes, slabs, total_tokens,
):
    count, width = tokens.shape
    rows = back.shape[1]
    half = width // 2
    bf16, f32 = jnp.bfloat16, jnp.float32
    shape = jax.ShapeDtypeStruct
    anywhere = pl.BlockSpec(memory_space=pl.ANY)
    local = pl.BlockSpec(memory_space=pltpu.VMEM)
    dma = pltpu.SemaphoreType.DMA
    packed = near.shape[1:]
    outs = [
        (shape((count, width), bf16), anywhere),
        (shape((count, width), f32), anywhere),
        (shape((16, width), f32), local),
        (shape((width, half), f32), anywhere),
        (shape((half, width), f32), anywhere),
        (shape((4, width, width), bf16), anywhere),
        (shape((2, 2, rows, width), bf16), anywhere),
        (shape((2, rows, width), bf16), anywhere),
        (shape((planes,) + packed, bf16), anywhere),
        (shape((2, planes - 1) + packed, bf16), anywhere),
    ]
    copies = 120
    return pl.pallas_call(
        partial(rear_kernel, planes, slabs, total_tokens),
        out_shape=[o[0] for o in outs],
        in_specs=[pl.BlockSpec(memory_space=pltpu.SMEM)]
        + [anywhere, local, anywhere]
        + [local] * 3
        + [anywhere] * 4
        + [local, anywhere]
        + [local] * 3
        + [anywhere] * 4,
        out_specs=[o[1] for o in outs],
        scratch_shapes=[
            pltpu.VMEM((count, 3 * width), bf16),
            pltpu.VMEM((count, width), f32),
            pltpu.VMEM((count, count), f32),
            pltpu.VMEM((count, width), bf16),
            pltpu.VMEM((rows, width), bf16),
            pltpu.VMEM((rows, width), bf16),
            pltpu.VMEM((rows, width), bf16),
            pltpu.VMEM((count, 8), f32),
            pltpu.VMEM((count, 128), f32),
            pltpu.VMEM((3, 8, rows), f32),
            pltpu.VMEM((2,) + packed, bf16),
            pltpu.VMEM((2,) + packed, bf16),
            pltpu.VMEM((4, width, width), bf16),
            pltpu.VMEM((4, width // 2, width), bf16),
            pltpu.VMEM((4, width // 4, width), bf16),
            pltpu.VMEM((4, width // 8, width), bf16),
            pltpu.VMEM((4, planes - 1, width // 16, half), bf16),
            pltpu.VMEM((4, width // 16, half), bf16),
            pltpu.VMEM((10, 16, width), f32),
            pltpu.VMEM((2, count, 128), f32),
            pltpu.VMEM(tokens.shape, bf16),
            pltpu.VMEM(projection.shape, bf16),
            pltpu.VMEM(cotangent.shape, bf16),
            pltpu.VMEM(flipped.shape, bf16),
            pltpu.VMEM(mixed.shape, bf16),
            pltpu.VMEM((count, width), bf16),
            pltpu.VMEM((count, width), f32),
            pltpu.VMEM((width, half), f32),
            pltpu.VMEM((half, width), f32),
            dma((copies,)),
            dma((copies,)),
            dma((17,)),
        ],
        compiler_params=pltpu.CompilerParams(
            collective_id=1, has_side_effects=True, vmem_limit_bytes=VMEM_LIMIT
        ),
    )(
        lengths[0],
        tokens,
        norms,
        projection,
        mixing,
        centroids,
        route,
        cotangent,
        flipped,
        joint,
        mixed,
        logs,
        residual,
        place,
        loads,
        dots,
        back,
        made,
        near,
        far,
    )


TILE = 256
ALIGN = 16


def aligned_rows(count, experts):
    return -(-(count + experts * (ALIGN - 1)) // ALIGN) * ALIGN


def gelu_pair(values):
    bell = jnp.exp2(values * values * (-0.5 * HALF_LOG))
    near = 1.0 / (1.0 + (0.3275911 * 0.7071067811865476) * jnp.abs(values))
    series = 1.061405429 * 0.5 * near - 1.453152027 * 0.5
    series = series * near + 1.421413741 * 0.5
    series = series * near - 0.284496736 * 0.5
    series = series * near + 0.254829592 * 0.5
    tail = series * near * bell
    below = jnp.where(values >= 0.0, 1.0 - tail, tail)
    return values * below, below + values * bell * 0.3989422804014327


def expert_kernel_body(
    experts,
    sources,
    limit,
    meta_ref,
    sent_all,
    cot_all,
    gate_all,
    up_near,
    up_far,
    down_near,
    down_far,
    back_all,
    made_all,
    dots_all,
    near_out,
    far_out,
    table,
    x_ref,
    c_ref,
    g_ref,
    column_ref,
    up_ref,
    down_ref,
    gu_ref,
    gd_ref,
    pack_ref,
    zero_ref,
    weight_sem,
    in_sem,
    out_sem,
    grad_sem,
    zero_sem,
):
    rows, width = sent_all.shape[1:]
    half = up_near.shape[2]
    own = meta_ref[0]
    spots = sources * experts

    base = 0
    ends = [0] * sources
    for e in range(experts):
        at = base
        for s in range(sources):
            size = meta_ref[1 + s * experts + e]
            table[0, e * sources + s] = size
            table[1, e * sources + s] = ends[s]
            table[2, e * sources + s] = at
            ends[s] = ends[s] + size
            at = at + size
        number = (at - base + (TILE - 1)) // TILE
        table[3, e] = base
        table[4, e] = number
        base = base + number * TILE
    for s in range(sources):
        table[5, s] = ends[s]

    bits = [1 << b for b in range(limit.bit_length()) if ALIGN <= (1 << b)]

    def move(k, act, outward):
        s, e = lax.rem(k, sources), lax.div(k, sources)
        size = table[0, k]
        for piece in bits:
            @pl.when((size & piece) != 0)
            def _(piece=piece):
                offset = size & (piece - 1)
                src = pl.ds(pl.multiple_of(table[1, k] + offset, ALIGN), piece)
                dst = pl.ds(pl.multiple_of(table[2, k] + offset, ALIGN), piece)
                if outward:
                    act(pltpu.make_async_copy(x_ref.at[dst], made_all.at[s, src], out_sem.at[0]))
                    act(pltpu.make_async_copy(c_ref.at[dst], back_all.at[s, src], out_sem.at[1]))
                else:
                    act(pltpu.make_async_copy(sent_all.at[s, src], x_ref.at[dst], in_sem.at[e, 0]))
                    act(pltpu.make_async_copy(cot_all.at[s, src], c_ref.at[dst], in_sem.at[e, 1]))

    def each(low, high, act):
        def one(i, _):
            act(i)
            return 0
        lax.fori_loop(low, high, one, 0)

    def begin(copy):
        copy.start()

    def end(copy):
        copy.wait()

    def move_weights(e, act):
        slot = e - own + experts - 1
        for j, (ups, downs) in enumerate(((up_near, down_near), (up_far, down_far))):
            part = pl.ds(j * half, half)
            act(pltpu.make_async_copy(ups.at[slot], up_ref.at[e, :, part], weight_sem.at[e, j, 0]))
            act(pltpu.make_async_copy(downs.at[slot], down_ref.at[e, part], weight_sem.at[e, j, 1]))

    zero_ref[...] = jnp.zeros_like(zero_ref)

    def bring(e):
        @pl.when(table[4, e] > 0)
        def _():
            last = pl.ds(pl.multiple_of(table[3, e] + (table[4, e] - 1) * TILE, TILE), TILE)
            x_ref[last, :] = jnp.zeros((TILE, width), jnp.bfloat16)
            c_ref[last, :] = jnp.zeros((TILE, width), jnp.bfloat16)
            g_ref[last, :] = jnp.zeros((TILE, 128), jnp.float32)

        move_weights(e, begin)
        each(e * sources, (e + 1) * sources, lambda k: move(k, begin, False))

    each(0, experts, bring)

    chunks = experts + 1

    def tail(k, act):
        s, i = lax.div(k, chunks), lax.rem(k, chunks) + rows // ALIGN - chunks

        @pl.when(i * ALIGN >= table[5, s])
        def _():
            dst = pl.ds(pl.multiple_of(i * ALIGN, ALIGN), ALIGN)
            act(pltpu.make_async_copy(zero_ref, made_all.at[s, dst], zero_sem.at[0]))
            act(pltpu.make_async_copy(zero_ref, back_all.at[s, dst], zero_sem.at[1]))

    each(0, sources * chunks, lambda k: tail(k, begin))

    def shift(s, outward):
        def segment(e):
            k = e * sources + s

            def one(i):
                src = pl.ds(pl.multiple_of(table[1, k] + i * ALIGN, ALIGN), ALIGN)
                dst = pl.ds(pl.multiple_of(table[2, k] + i * ALIGN, ALIGN), ALIGN)
                if outward:
                    column_ref[src, :] = g_ref[dst, :]
                else:
                    g_ref[dst, :] = column_ref[src, :]

            each(0, table[0, k] // ALIGN, one)

        each(0, experts, segment)

    def gates_in(s):
        column_ref[...] = jnp.transpose(jnp.broadcast_to(gate_all[s, 0:1, :], (128, rows)))
        shift(s, False)

    each(0, sources, gates_in)

    def grads(e):
        slot = lax.rem(e, 2)
        return [
            pltpu.make_async_copy(pack_ref.at[slot, j], ref.at[e], grad_sem.at[slot, j])
            for j, ref in enumerate((near_out, far_out))
        ]

    def work(e):
        move_weights(e, end)
        each(e * sources, (e + 1) * sources, lambda k: move(k, end, False))
        gu_ref[...] = jnp.zeros_like(gu_ref)
        gd_ref[...] = jnp.zeros_like(gd_ref)

        def tile(t):
            at = pl.ds(pl.multiple_of(table[3, e] + t * TILE, TILE), TILE)
            x, c, gate = x_ref[at, :], c_ref[at, :], g_ref[at, 0:1]
            before = jnp.dot(x, up_ref[e], preferred_element_type=jnp.float32)
            active, slope = gelu_pair(before)
            through = lax.dot_general(c, down_ref[e], NT, preferred_element_type=jnp.float32)
            grad = (through * (slope * gate)).astype(jnp.bfloat16)
            gated = (active * gate).astype(jnp.bfloat16)
            made = jnp.dot(active.astype(jnp.bfloat16), down_ref[e], preferred_element_type=jnp.float32)
            g_ref[at, :] = jnp.broadcast_to(
                jnp.sum(made * c.astype(jnp.float32), axis=1, keepdims=True), (TILE, 128)
            )
            gd_ref[...] += lax.dot_general(gated, c, TN, preferred_element_type=jnp.float32)
            gu_ref[...] += lax.dot_general(x, grad, TN, preferred_element_type=jnp.float32)
            back = lax.dot_general(grad, up_ref[e], NT, preferred_element_type=jnp.float32)
            x_ref[at, :] = made.astype(jnp.bfloat16)
            c_ref[at, :] = back.astype(jnp.bfloat16)

        each(0, table[4, e], tile)
        each(e * sources, (e + 1) * sources, lambda k: move(k, begin, True))

        @pl.when(e >= 2)
        def _():
            for copy in grads(e - 2):
                copy.wait()

        slot = lax.rem(e, 2)
        for j in range(2):
            pack_ref[slot, j, 0:width, :] = gu_ref[:, j * half : (j + 1) * half].astype(jnp.bfloat16)
            for part in range(2):
                pack_ref[slot, j, width + part * half : width + (part + 1) * half, :] = gd_ref[
                    j * half : (j + 1) * half, part * half : (part + 1) * half
                ].astype(jnp.bfloat16)
        for copy in grads(e):
            copy.start()

    each(0, experts, work)

    def sums_out(s):
        shift(s, True)
        dots_all[s] = jnp.transpose(column_ref[...])[0:8, :]

    each(0, sources, sums_out)
    each(0, spots, lambda k: move(k, end, True))
    each(0, sources * chunks, lambda k: tail(k, end))
    for e in range(max(0, experts - 2), experts):
        for copy in grads(e):
            copy.wait()


def expert_stage(meta, sent, cot, gates, weights, experts, limit):
    sources, rows, width = sent.shape
    half = weights[0].shape[2]
    hidden = 2 * half
    joined = -(-(sources * rows + experts * (TILE - 1)) // TILE) * TILE
    limit = -(-limit // ALIGN) * ALIGN
    anywhere = pl.BlockSpec(memory_space=pl.ANY)
    local = pl.BlockSpec(memory_space=pltpu.VMEM)
    dma = pltpu.SemaphoreType.DMA
    packed = (width + hidden, half)
    return pl.pallas_call(
        partial(expert_kernel_body, experts, sources, limit),
        out_shape=(
            jax.ShapeDtypeStruct((sources, rows, width), jnp.bfloat16),
            jax.ShapeDtypeStruct((sources, rows, width), jnp.bfloat16),
            jax.ShapeDtypeStruct((sources, 8, rows), jnp.float32),
            jax.ShapeDtypeStruct((experts,) + packed, jnp.bfloat16),
            jax.ShapeDtypeStruct((experts,) + packed, jnp.bfloat16),
        ),
        in_specs=[pl.BlockSpec(memory_space=pltpu.SMEM)] + [anywhere] * 2 + [local] + [anywhere] * 4,
        out_specs=(anywhere, anywhere, local, anywhere, anywhere),
        scratch_shapes=[
            pltpu.SMEM((6, sources * experts), jnp.int32),
            pltpu.VMEM((joined, width), jnp.bfloat16),
            pltpu.VMEM((joined, width), jnp.bfloat16),
            pltpu.VMEM((joined, 128), jnp.float32),
            pltpu.VMEM((rows, 128), jnp.float32),
            pltpu.VMEM((experts, width, hidden), jnp.bfloat16),
            pltpu.VMEM((experts, hidden, width), jnp.bfloat16),
            pltpu.VMEM((width, hidden), jnp.float32),
            pltpu.VMEM((hidden, width), jnp.float32),
            pltpu.VMEM((2, 2) + packed, jnp.bfloat16),
            pltpu.VMEM((ALIGN, width), jnp.bfloat16),
            dma((experts, 2, 2)),
            dma((experts, 2)),
            dma((2,)),
            dma((2, 2)),
            dma((2,)),
        ],
        compiler_params=pltpu.CompilerParams(vmem_limit_bytes=VMEM_LIMIT),
        cost_estimate=pl.CostEstimate(
            flops=12 * sources * rows * width * hidden, bytes_accessed=100_000_000, transcendentals=sources * rows * hidden
        ),
    )(meta, sent, cot, gates, *weights)


def arrange(shared, layer, token, vectors, up, down, experts):
    count, width = layer.shape
    third, half = width // 3, width // 2
    steps = 6

    def kernel(shared_ref, layer_ref, token_ref, vectors_ref, up_ref, down_ref, *outs):
        mixing_out, projection_out, layer_out, token_out, up_out, down_out, *vector_outs, centroids_out, balance_out = outs
        mixing_out[...] = shared_ref[0].astype(jnp.float32)
        for k in range(3):
            for c in range(3):
                at = k * width + c * third
                projection_out[:, at : at + third] = shared_ref[1 + c, :, k * third : (k + 1) * third].astype(jnp.float32)
        layer_out[...] = layer_ref[...]
        token_out[...] = token_ref[...]
        up_out[0] = up_ref[...]
        down_out[0] = down_ref[...]
        for i, out in enumerate(vector_outs):
            out[...] = vectors_ref[i]
        centroids_out[...] = vectors_ref[8 : 8 + experts, :]
        balance_out[...] = vectors_ref[4:5, 0:128]

    f32 = jnp.float32
    shape = jax.ShapeDtypeStruct
    rows = lambda n, m: pl.BlockSpec((n // steps, m), lambda i: (i, 0))
    slab = lambda n, m: pl.BlockSpec((1, n // steps, m), lambda i: (0, i, 0))
    whole = lambda *dims: pl.BlockSpec(dims, lambda i: (0,) * len(dims))
    return pl.pallas_call(
        kernel,
        out_shape=[
            shape((width, width), f32),
            shape((width, 3 * width), f32),
            shape((count, width), jnp.bfloat16),
            shape((count, width), f32),
            shape((1, width, half), f32),
            shape((1, half, width), f32),
        ]
        + [shape((width,), f32)] * 4
        + [shape((experts, width), f32), shape((1, 128), f32)],
        grid=(steps,),
        in_specs=[
            pl.BlockSpec((4, width // steps, width), lambda i: (0, i, 0)),
            rows(count, width),
            rows(count, width),
            whole(16, width),
            rows(width, half),
            rows(half, width),
        ],
        out_specs=[
            rows(width, width),
            rows(width, 3 * width),
            rows(count, width),
            rows(count, width),
            slab(width, half),
            slab(half, width),
        ]
        + [whole(width)] * 4
        + [whole(experts, width), whole(1, 128)],
        compiler_params=pltpu.CompilerParams(vmem_limit_bytes=VMEM_LIMIT),
    )(shared, layer, token, vectors, up, down)


def per_device(
    tokens,
    gains,
    shifts,
    projection,
    mixing,
    factors,
    biases,
    centroids,
    expanding,
    contracting,
    routes,
    lengths,
    cotangent,
):
    count, width = tokens.shape
    experts = centroids.shape[0]
    groups = lax.axis_size("expert")
    slabs = groups // experts
    limit = 2 * count // experts
    total_tokens = count * groups * lax.axis_size("tensor")

    norms = jnp.stack((gains, shifts, factors, biases))
    flipped, joint, mixed, logs, residual, place, loads, sent, cot, gates, *weights = front_stage(
        tokens, norms, projection, mixing, centroids, expanding, contracting, routes, lengths, cotangent, experts, slabs
    )
    meta = jnp.concatenate(
        [lax.div(lax.axis_index("expert"), slabs)[None], gates[:, 1, :experts].reshape(-1).astype(jnp.int32)]
    )
    back, made, dots, near, far = expert_stage(meta, sent, cot, gates, weights, experts, limit)
    layer, token, vectors, up, down, shared, *_ = rear_stage(
        tokens, norms, projection, mixing, centroids, routes, lengths, cotangent,
        flipped, joint, mixed, logs, residual, place, loads, dots, back, made, near, far, experts, slabs, total_tokens,
    )
    (
        mixing_grad, projection_grad, layer_output, token_grad, up_grad, down_grad,
        gain_grad, shift_grad, factor_grad, bias_grad, centroid_grad, balance,
    ) = arrange(shared, layer, token, vectors, up, down, experts)
    return (
        layer_output,
        balance[0, 0],
        token_grad,
        gain_grad,
        shift_grad,
        projection_grad,
        mixing_grad,
        factor_grad,
        bias_grad,
        centroid_grad,
        up_grad,
        down_grad,
    )


def solution(mesh):
    placed = (
        P(("expert", "tensor"), None),
        P(),
        P(),
        P(),
        P(),
        P(),
        P(),
        P(),
        P("expert", None, "tensor"),
        P("expert", "tensor", None),
        P(("expert", "tensor"), None),
        P(("expert", "tensor"), None),
        P(("expert", "tensor"), None),
    )
    near = mesh.shape["expert"] == 16 and mesh.shape["tensor"] == 2
    return jax.shard_map(
        per_device if near else moving_tokens,
        mesh=mesh,
        in_specs=placed,
        out_specs=(
            P(("expert", "tensor"), None),
            P(),
            P(("expert", "tensor"), None),
            P(),
            P(),
            P(),
            P(),
            P(),
            P(),
            P(),
            P("expert", None, "tensor"),
            P("expert", "tensor", None),
        ),
        check_vma=False,
    )
```

```python
from functools import partial

import jax
import jax.numpy as jnp
from jax import lax
from jax.experimental import pallas as pl
from jax.experimental.pallas import tpu as pltpu
from jax.sharding import PartitionSpec as P

HEADS = 12


highest = lax.Precision.HIGHEST
epsilon = 1e-05


def running(values):
    places = jnp.arange(values.shape[0])
    return jnp.sum(jnp.where(places[:, None] >= places[None, :], values[None, :], 0), axis=1)


def earlier(picks):
    places = jnp.arange(picks.shape[0])
    before = (places[:, None] > places[None, :]).astype(jnp.bfloat16)
    return jnp.dot(
        before, picks.astype(jnp.bfloat16), preferred_element_type=jnp.float32
    ).astype(jnp.int32)


def norm_parts(values, gain, shift):
    centered = values - jnp.mean(values, axis=1, keepdims=True)
    scale = lax.rsqrt(jnp.mean(centered * centered, axis=1, keepdims=True) + epsilon)
    normal = centered * scale
    return (normal * gain + shift, normal, scale)


def norm_back(upstream, normal, scale, gain):
    scaled = upstream * gain
    inner = (
        scaled
        - jnp.mean(scaled, axis=1, keepdims=True)
        - normal * jnp.mean(scaled * normal, axis=1, keepdims=True)
    )
    return (inner * scale, jnp.sum(upstream * normal, axis=0), jnp.sum(upstream, axis=0))


def gelu_slope(values):
    return (
        0.5 * (1.0 + lax.erf(values * 0.7071067811865476))
        + values * jnp.exp(-0.5 * values * values) * 0.3989422804014327
    )


def expert_forward(gathered, upward, downward):
    before = jnp.dot(gathered, upward, preferred_element_type=jnp.float32)
    active = jax.nn.gelu(before, approximate=False).astype(jnp.bfloat16)
    return jnp.dot(active, downward, preferred_element_type=jnp.float32)


def expert_backward(gathered, incoming, upward, downward):
    before = jnp.dot(gathered, upward, preferred_element_type=jnp.float32)
    active = jax.nn.gelu(before, approximate=False).astype(jnp.bfloat16)
    down_grad = jnp.einsum("rf,rd->fd", active, incoming, preferred_element_type=jnp.float32)
    through = jnp.einsum("rd,fd->rf", incoming, downward, preferred_element_type=jnp.float32)
    hidden_grad = (through * gelu_slope(before)).astype(jnp.bfloat16)
    up_grad = jnp.einsum("rd,rf->df", gathered, hidden_grad, preferred_element_type=jnp.float32)
    return (up_grad, down_grad, hidden_grad)


def head_forward(allowed, item):
    query, keys, values = item
    factor = query.shape[1] ** (-0.5)
    scores = jnp.einsum("qd,kd->qk", query, keys, preferred_element_type=jnp.float32) * factor
    scores = jnp.where(allowed, scores, -1000000000.0)
    peak = jnp.max(scores, axis=1, keepdims=True)
    weights = jnp.exp(scores - peak)
    total = jnp.sum(weights, axis=1, keepdims=True)
    mixed = jnp.dot(
        (weights / total).astype(jnp.bfloat16), values, preferred_element_type=jnp.float32
    )
    return (mixed.astype(jnp.bfloat16), (peak + jnp.log(total))[:, 0])


def head_backward(allowed, item):
    query, keys, values, upstream, log_total = item
    factor = query.shape[1] ** (-0.5)
    scores = jnp.einsum("qd,kd->qk", query, keys, preferred_element_type=jnp.float32) * factor
    scores = jnp.where(allowed, scores, -1000000000.0)
    probs = jnp.exp(scores - log_total[:, None])
    value_grad = jnp.einsum(
        "qk,qd->kd", probs.astype(jnp.bfloat16), upstream, preferred_element_type=jnp.float32
    )
    prob_grad = jnp.einsum("qd,kd->qk", upstream, values, preferred_element_type=jnp.float32)
    inner = jnp.sum(prob_grad * probs, axis=1, keepdims=True)
    score_grad = (probs * (prob_grad - inner)).astype(jnp.bfloat16)
    query_grad = (
        jnp.einsum("qk,kd->qd", score_grad, keys, preferred_element_type=jnp.float32) * factor
    )
    key_grad = (
        jnp.einsum("qk,qd->kd", score_grad, query, preferred_element_type=jnp.float32) * factor
    )
    return (query_grad, key_grad, value_grad)


def moving_tokens(
    tokens,
    gains,
    shifts,
    projection,
    mixing,
    factors,
    biases,
    centroids,
    expanding,
    contracting,
    routes,
    lengths,
    cotangent,
):
    count, width = tokens.shape
    experts = centroids.shape[0]
    groups = lax.axis_size("expert")
    slab_count = groups // experts
    capacity = max(2, 2 * count // experts)
    total_tokens = count * groups * lax.axis_size("tensor")
    average = total_tokens / experts
    route = routes[:, 0]
    picks = route[:, None] == jnp.arange(experts, dtype=jnp.int32)[None, :]
    picks_int = picks.astype(jnp.int32)
    picks_float = picks.astype(jnp.float32)
    loads = lax.psum(jnp.sum(picks_float, axis=0), ("expert", "tensor"))
    spread = (loads - average) / average
    token_spread = jnp.sum(jnp.where(picks, spread[None, :], 0.0), axis=1)
    ranks = jnp.sum(earlier(picks) * picks_int, axis=1)
    slots = route * capacity + ranks
    places = jnp.arange(count, dtype=jnp.int32)
    documents = jnp.sum(
        (places[:, None] >= running(lengths[0])[None, :]).astype(jnp.int32), axis=1
    )
    allowed = (places[:, None] >= places[None, :]) & (documents[:, None] == documents[None, :])
    inputs = tokens.astype(jnp.float32)
    entry, entry_normal, entry_scale = norm_parts(inputs, gains, shifts)
    entry = entry.astype(jnp.bfloat16)
    joint = jnp.dot(entry, projection, preferred_element_type=jnp.float32).astype(jnp.bfloat16)
    heads = joint.reshape(count, 3, HEADS, width // HEADS).transpose(1, 2, 0, 3)
    mixed, log_total = lax.map(partial(head_forward, allowed), (heads[0], heads[1], heads[2]))
    mixed_rows = mixed.transpose(1, 0, 2).reshape(count, width)
    residual = inputs + jnp.dot(mixed_rows, mixing, preferred_element_type=jnp.float32)
    normed, mixer_normal, mixer_scale = norm_parts(residual, factors, biases)
    chosen = jnp.dot(picks.astype(jnp.bfloat16), centroids, preferred_element_type=jnp.float32)
    gates = jax.nn.sigmoid(jnp.sum(normed * chosen, axis=1))
    outgoing = (
        jnp.zeros((experts * capacity, width), jnp.bfloat16)
        .at[slots]
        .set(normed.astype(jnp.bfloat16))
    )
    copies = jnp.broadcast_to(
        outgoing.reshape(experts, 1, capacity, width), (experts, slab_count, capacity, width)
    ).reshape(groups, capacity, width)
    arrived = lax.all_to_all(copies, "expert", split_axis=0, concat_axis=0, tiled=True)
    sources = groups * capacity
    own_rows = arrived.reshape(sources, width)
    gathered = lax.all_gather(own_rows, "tensor", axis=0, tiled=True)
    produced = lax.psum_scatter(
        expert_forward(gathered, expanding[0], contracting[0]).astype(jnp.bfloat16),
        "tensor",
        scatter_dimension=0,
        tiled=True,
    )
    returned = lax.all_to_all(
        produced.reshape(arrived.shape), "expert", split_axis=0, concat_axis=0, tiled=True
    )
    combined = jnp.sum(
        returned.reshape(experts, slab_count, capacity, width).astype(jnp.float32), axis=1
    ).reshape(experts * capacity, width)
    picked = combined[slots]
    layer_output = (residual + gates[:, None] * picked).astype(jnp.bfloat16)
    balance_part = jnp.sum(token_spread * gates) / total_tokens
    upstream = cotangent.astype(jnp.float32)
    gate_grad = jnp.sum(upstream * picked, axis=1)
    logit_grad = (gate_grad + token_spread / total_tokens) * gates * (1.0 - gates)
    scaled_rows = (gates[:, None] * upstream).astype(jnp.bfloat16)
    grad_slots = jnp.zeros((experts * capacity, width), jnp.bfloat16).at[slots].set(scaled_rows)
    grad_copies = jnp.broadcast_to(
        grad_slots.reshape(experts, 1, capacity, width), (experts, slab_count, capacity, width)
    ).reshape(groups, capacity, width)
    incoming = lax.all_to_all(
        grad_copies, "expert", split_axis=0, concat_axis=0, tiled=True
    ).reshape(sources, width)
    incoming_pair = lax.all_gather(incoming, "tensor", axis=0, tiled=True)
    up_share, down_share, hidden_grad = expert_backward(
        gathered, incoming_pair, expanding[0], contracting[0]
    )
    back_rows = lax.psum_scatter(
        jnp.einsum(
            "rf,df->rd", hidden_grad, expanding[0], preferred_element_type=jnp.float32
        ).astype(jnp.bfloat16),
        "tensor",
        scatter_dimension=0,
        tiled=True,
    )
    back = lax.all_to_all(
        back_rows.reshape(arrived.shape), "expert", split_axis=0, concat_axis=0, tiled=True
    )
    back_sum = jnp.sum(
        back.reshape(experts, slab_count, capacity, width).astype(jnp.float32), axis=1
    ).reshape(experts * capacity, width)
    normed_grad = back_sum[slots] + logit_grad[:, None] * chosen
    centroid_grad = jnp.einsum(
        "te,td->ed", picks_float, logit_grad[:, None] * normed, precision=highest
    )
    mixer_back, factor_grad, bias_grad = norm_back(normed_grad, mixer_normal, mixer_scale, factors)
    residual_grad = upstream + mixer_back
    branch_grad = residual_grad.astype(jnp.bfloat16)
    mixing_grad = jnp.einsum(
        "td,te->de", mixed_rows, branch_grad, preferred_element_type=jnp.float32
    )
    mixed_grad = jnp.einsum(
        "te,de->td", branch_grad, mixing, preferred_element_type=jnp.float32
    ).astype(jnp.bfloat16)
    head_grads = mixed_grad.reshape(count, HEADS, width // HEADS).transpose(1, 0, 2)
    query_grad, key_grad, value_grad = lax.map(
        partial(head_backward, allowed), (heads[0], heads[1], heads[2], head_grads, log_total)
    )
    joint_grad = (
        jnp.stack((query_grad, key_grad, value_grad))
        .transpose(2, 0, 1, 3)
        .reshape(count, 3 * width)
        .astype(jnp.bfloat16)
    )
    projection_grad = jnp.einsum("td,te->de", entry, joint_grad, preferred_element_type=jnp.float32)
    entry_back = jnp.einsum("te,de->td", joint_grad, projection, preferred_element_type=jnp.float32)
    entry_input, gain_grad, shift_grad = norm_back(entry_back, entry_normal, entry_scale, gains)
    token_grad = residual_grad + entry_input
    summed = lax.psum(
        (
            gain_grad,
            shift_grad,
            projection_grad,
            mixing_grad,
            factor_grad,
            bias_grad,
            centroid_grad,
            balance_part,
        ),
        ("expert", "tensor"),
    )
    return (
        layer_output,
        summed[7],
        token_grad,
        summed[0],
        summed[1],
        summed[2],
        summed[3],
        summed[4],
        summed[5],
        summed[6],
        up_share[None],
        down_share[None],
    )


HALF_LOG = 1.4426950408889634
LN2 = 0.6931471805599453
NT = (((1,), (1,)), ((), ()))
TN = (((0,), (0,)), ((), ()))
VMEM_LIMIT = 60 * 1024 * 1024


def query_blocks(count):
    step = 256 if count > 256 else count
    return [(i, min(i + step, count)) for i in range(0, count, step)]


def document_starts(lengths_ref, places):
    starts = jnp.zeros_like(places)
    end = 0
    for d in range(lengths_ref.shape[0]):
        end = end + lengths_ref[d]
        starts = jnp.where(places >= end, end, starts)
    return starts


MESH = pl.DeviceIdType.MESH


def neighbours(slabs):
    me, core = lax.axis_index("expert"), lax.axis_index("tensor")
    plane = lax.div(me, slabs)
    x = lax.rem(me, 2)
    y = lax.rem(lax.div(me, 2), 2)
    return me, core, plane, (me + 1 - 2 * x, core), (me + 2 - 4 * y, core), (me, 1 - core)


def greet(partners):
    barrier = pltpu.get_barrier_semaphore()
    number = 0
    for device, there in partners:
        @pl.when(there)
        def _(device=device):
            pl.semaphore_signal(barrier, inc=1, device_id=device, device_id_type=MESH)
        number = number + there.astype(jnp.int32)
    pl.semaphore_wait(barrier, number)


def score_bias(bias_ref, lengths_ref, count):
    places = lax.broadcasted_iota(jnp.int32, (1, count), 1)
    starts = document_starts(lengths_ref, places)
    for s, e in query_blocks(count):
        row = lax.broadcasted_iota(jnp.int32, (e - s, count), 0) + s
        seen = (row <= places) & (row >= starts)
        bias_ref[s:e, :] = jnp.where(seen, 0.0, -1e9)


def row_norm(values, gain, shift):
    centered = values - jnp.mean(values, axis=1, keepdims=True)
    scale = lax.rsqrt(jnp.mean(centered * centered, axis=1, keepdims=True) + epsilon)
    normal = centered * scale
    return normal * gain + shift, normal, scale


def chosen_rows(route, centroids_ref, experts):
    chosen = jnp.zeros((route.shape[0], centroids_ref.shape[1]), jnp.float32)
    for e in range(experts):
        chosen = jnp.where(route == e, centroids_ref[e : e + 1, :].astype(jnp.float32), chosen)
    return chosen


def front_kernel(
    planes,
    slabs,
    lengths_ref,
    tokens_in,
    norms_ref,
    projection_in,
    mixing_in,
    centroids_ref,
    route_row_ref,
    route_ref,
    cot_in,
    up_ref,
    down_ref,
    flipped_out,
    joint_out,
    mixed_out,
    logs_ref,
    residual_out,
    place_ref,
    loads_ref,
    sent_all,
    cot_all,
    gate_all,
    up_near,
    up_far,
    down_near,
    down_far,
    bias_ref,
    order_ref,
    normed_ref,
    entry_ref,
    sent_own,
    cot_own,
    gate_own,
    tally_ref,
    tokens_ref,
    projection_ref,
    mixing_ref,
    cot_ref,
    flipped_ref,
    joint_ref,
    mixed_ref,
    residual_ref,
    send_sem,
    recv_sem,
    local_sem,
):
    count, width = tokens_ref.shape
    experts = planes
    pairs_in = ((cot_in, cot_ref), (tokens_in, tokens_ref), (projection_in, projection_ref), (mixing_in, mixing_ref))
    brought = [pltpu.make_async_copy(a, b, local_sem.at[5 + i]) for i, (a, b) in enumerate(pairs_in)]
    pairs_out = ((joint_ref, joint_out), (mixed_ref, mixed_out), (residual_ref, residual_out), (flipped_ref, flipped_out))
    taken = [pltpu.make_async_copy(a, b, local_sem.at[9 + i]) for i, (a, b) in enumerate(pairs_out)]
    for copy in brought:
        copy.start()
    rows = sent_own.shape[0]
    half_rows = rows // 2
    pairs = width // 128
    factor = (width // HEADS) ** (-0.5) * HALF_LOG
    middle = planes - 1
    me, core, plane, beside_x, beside_y, beside_core = neighbours(slabs)
    hop_two = lax.rem(plane + 2, planes)
    hop_one = plane + 1 - 2 * lax.rem(plane, 2)
    here = lax.rem(me, slabs)
    always = plane >= 0
    greet(
        [
            (beside_x, always),
            (beside_y, always),
            (beside_core, always),
            ((hop_two * slabs + here, core), always),
            ((me + slabs, core), plane < planes - 1),
            ((me - slabs, core), plane > 0),
        ]
    )

    def remote(i, src, dst, device):
        return pltpu.make_async_remote_copy(
            src_ref=src, dst_ref=dst, send_sem=send_sem.at[i], recv_sem=recv_sem.at[i], device_id=device, device_id_type=MESH
        )

    owns, nears, fars = (up_ref, down_ref), (up_near, down_near), (up_far, down_far)
    stride = 2 * (planes - 1) + 2 * planes - 1

    def hop(kind, sign, r):
        src = owns[kind].at[0] if r == 1 else nears[kind].at[middle - sign * (r - 1)]
        i = kind * stride + (r - 1) * 2 + (sign > 0)
        return remote(i, src, nears[kind].at[middle - sign * r], (me + sign * slabs, core))

    def hop_sent(sign, r):
        ahead = plane if sign > 0 else planes - 1 - plane
        return (ahead >= r - 1) & (ahead < planes - 1)

    def hop_came(sign, r):
        ahead = plane if sign > 0 else planes - 1 - plane
        return ahead >= r

    def aside(kind, slot):
        src = owns[kind].at[0] if slot == middle else nears[kind].at[slot]
        i = kind * stride + 2 * (planes - 1) + slot
        return remote(i, src, fars[kind].at[slot], beside_x)

    def held(slot):
        at = plane + slot - middle
        return (at >= 0) & (at < planes)

    def handed(kind, sign):
        i = copies_end + kind
        return remote(i, fars[kind].at[middle], fars[kind].at[middle - sign], (me + sign * slabs, core))

    def aside_there(slot):
        if slot == middle - 1:
            return held(slot) & (plane != 1)
        if slot == middle + 1:
            return held(slot) & (plane != planes - 2)
        return held(slot)

    def own_weights(kind):
        return pltpu.make_async_copy(owns[kind].at[0], nears[kind].at[middle], local_sem.at[kind])

    for kind in range(2):
        for sign in (1, -1):
            @pl.when(hop_sent(sign, 1))
            def _(kind=kind, sign=sign):
                hop(kind, sign, 1).start()
        aside(kind, middle).start()
        own_weights(kind).start()

    def forward_weights(kind, r):
        for sign in (1, -1):
            slot = middle - sign * r

            @pl.when(hop_came(sign, r))
            def _(sign=sign):
                hop(kind, sign, r).wait_recv()

            @pl.when(aside_there(slot))
            def _(slot=slot):
                aside(kind, slot).start()

            if r < planes - 1:
                @pl.when(hop_sent(sign, r + 1))
                def _(sign=sign):
                    hop(kind, sign, r + 1).start()

    base = 2 * stride
    copies_end = base + 20

    def hand_on(kind):
        aside(kind, middle).wait_recv()
        for sign in (1, -1):
            @pl.when(plane == (0 if sign > 0 else planes - 1))
            def _(sign=sign):
                handed(kind, sign).start()

    def row_copy(which, part, piece):
        own, everyone = ((cot_own, cot_all), (sent_own, sent_all))[which]
        at = pl.ds(piece * half_rows, half_rows)
        i = base + which * 6 + part * 2 + piece
        if part == 0:
            return remote(i, own.at[at], everyone.at[2, at], beside_y)
        if part == 1:
            return remote(i, own.at[at], everyone.at[1, at], beside_core)
        return remote(i, everyone.at[2, at], everyone.at[3, at], beside_core)

    def gate_copy(part):
        i = base + 12 + part
        if part == 0:
            return remote(i, gate_own, gate_all.at[2], beside_y)
        if part == 1:
            return remote(i, gate_own, gate_all.at[1], beside_core)
        return remote(i, gate_all.at[2], gate_all.at[3], beside_core)

    def own_rows(which):
        source, everyone = ((cot_own, cot_all), (sent_own, sent_all), (gate_own, gate_all))[which]
        return pltpu.make_async_copy(source, everyone.at[0], local_sem.at[2 + which])

    rounds = [beside_core, beside_x, beside_y, (hop_one * slabs + here, core), (hop_two * slabs + here, core)]

    def tally(k):
        return remote(base + 15 + k, tally_ref.at[2 * k], tally_ref.at[2 * k + 1], rounds[k])

    def tally_step(k):
        tally(k).wait_recv()
        total = tally_ref[2 * k] + tally_ref[2 * k + 1]
        if k + 1 < len(rounds):
            tally_ref[2 * k + 2] = total
            tally(k + 1).start()
        else:
            loads_ref[...] = total

    number = lax.broadcasted_iota(jnp.int32, (8, count), 0)
    picks = jnp.where(number == route_row_ref[...], 1.0, 0.0)
    chunk = 128
    for s in range(0, count, chunk):
        row = lax.broadcasted_iota(jnp.int32, (chunk, count), 0) + s
        column = lax.broadcasted_iota(jnp.int32, (chunk, count), 1)
        order_ref[s : s + chunk, :] = jnp.where(row < column, 1.0, 0.0).astype(jnp.bfloat16)
    ranks = jnp.dot(picks.astype(jnp.bfloat16), order_ref[0:count, :], preferred_element_type=jnp.float32)
    counts = jnp.sum(picks, axis=1, keepdims=True)
    padded = jnp.ceil(counts * (1.0 / ALIGN)) * ALIGN
    place = jnp.zeros((1, count), jnp.float32)
    start = jnp.zeros((1, 1), jnp.float32)
    for e in range(experts):
        place = place + picks[e : e + 1, :] * (ranks[e : e + 1, :] + start)
        start = start + padded[e : e + 1, :]
    place_ref[...] = jnp.broadcast_to(place, (8, count))
    tally_ref[0] = jnp.broadcast_to(counts, (8, 128))
    tally(0).start()
    for s in range(0, rows, 64):
        row = lax.broadcasted_iota(jnp.int32, (64, count), 0) + s
        order_ref[s : s + 64, :] = jnp.where(row.astype(jnp.float32) == place, 1.0, 0.0).astype(jnp.bfloat16)

    def sort_rows(source_ref, to_ref, which):
        for piece in range(2):
            at = slice(piece * half_rows, (piece + 1) * half_rows)
            to_ref[at, :] = jnp.dot(
                order_ref[at, :], source_ref[...], preferred_element_type=jnp.float32
            ).astype(jnp.bfloat16)
            row_copy(which, 0, piece).start()
            row_copy(which, 1, piece).start()

    brought[0].wait()
    sort_rows(cot_ref, cot_own, 0)
    own_rows(0).start()

    def project(i, _):
        at = pl.ds(pl.multiple_of(i * 192, 192), 192)
        entry, _, _ = row_norm(tokens_ref[at, :].astype(jnp.float32), norms_ref[0:1, :], norms_ref[1:2, :])
        entry = entry.astype(jnp.bfloat16)
        entry_ref[at, :] = entry
        joint_ref[at, :] = jnp.dot(entry, projection_ref[...], preferred_element_type=jnp.float32).astype(jnp.bfloat16)
        return 0

    for copy in brought[1:]:
        copy.wait()
    lax.fori_loop(0, count // 192, project, 0)
    taken[0].start()
    score_bias(bias_ref, lengths_ref, count)
    forward_weights(0, 1)
    tally_step(0)

    first = lax.broadcasted_iota(jnp.int32, (1, 128), 1) < 64

    def attend(p, _):
        lanes = pl.ds(pl.multiple_of(p * 128, 128), 128)
        keys = pl.ds(pl.multiple_of(width + p * 128, 128), 128)
        values = pl.ds(pl.multiple_of(2 * width + p * 128, 128), 128)
        for s, e in query_blocks(count):
            outs = []
            for half in range(2):
                q = jnp.where(first == (half == 0), joint_ref[s:e, lanes], jnp.bfloat16(0))
                scores = lax.dot_general(joint_ref[0:e, keys], q, NT, preferred_element_type=jnp.float32)
                scores = scores * factor + bias_ref[0:e, s:e]
                peak = jnp.max(scores, axis=0, keepdims=True)
                weights = jnp.exp2(scores - peak)
                total = jnp.sum(weights, axis=0, keepdims=True)
                probs = (weights * (1.0 / total)).astype(jnp.bfloat16)
                outs.append(
                    lax.dot_general(probs, joint_ref[0:e, values], TN, preferred_element_type=jnp.float32)
                )
                logs_ref[p, half : half + 1, s:e] = peak + jnp.log2(total)
            mixed_ref[s:e, lanes] = jnp.where(first, outs[0], outs[1]).astype(jnp.bfloat16)

        @pl.when(p == 2)
        def _():
            forward_weights(1, 1)
            hand_on(0)
            tally_step(1)

        @pl.when(p == 4)
        def _():
            hand_on(1)
            forward_weights(0, 2)
            tally_step(2)

        return 0

    lax.fori_loop(0, pairs, attend, 0)
    taken[1].start()

    lane = lax.broadcasted_iota(jnp.int32, (1, 128), 1)

    def mix(i, _):
        at = pl.ds(pl.multiple_of(i * 192, 192), 192)
        residual = tokens_ref[at, :].astype(jnp.float32) + jnp.dot(
            mixed_ref[at, :], mixing_ref[...], preferred_element_type=jnp.float32
        )
        residual_ref[at, :] = residual
        normed, _, _ = row_norm(residual, norms_ref[2:3, :], norms_ref[3:4, :])
        chosen = chosen_rows(route_ref[at, :], centroids_ref, experts)
        gate = 1.0 / (1.0 + jnp.exp(-jnp.sum(normed * chosen, axis=1, keepdims=True)))
        high = gate.astype(jnp.bfloat16).astype(jnp.float32)
        mid = (gate - high).astype(jnp.bfloat16).astype(jnp.float32)
        low = gate - high - mid
        parts = jnp.where(lane == 0, high, jnp.where(lane == 1, mid, jnp.where(lane == 2, low, 0.0)))
        normed_ref[at, 0:width] = normed.astype(jnp.bfloat16)
        normed_ref[at, width : width + 128] = parts.astype(jnp.bfloat16)
        return 0

    lax.fori_loop(0, count // 192, mix, 0)
    taken[2].start()
    for piece in range(2):
        at = slice(piece * half_rows, (piece + 1) * half_rows)
        moved = jnp.dot(order_ref[at, :], normed_ref[...], preferred_element_type=jnp.float32)
        sent_own[at, :] = moved[:, 0:width].astype(jnp.bfloat16)
        row_copy(1, 0, piece).start()
        row_copy(1, 1, piece).start()
        bias_ref[at, 0:128] = jnp.broadcast_to(
            jnp.sum(moved[:, width : width + 128], axis=1, keepdims=True), (half_rows, 128)
        )
    forward_weights(1, 2)
    tally_step(3)
    for piece in range(2):
        row_copy(0, 0, piece).wait_recv()
        row_copy(0, 2, piece).start()
    gates = jnp.transpose(bias_ref[0:rows, 0:128])
    gate_own[0:1, :] = gates[0:1, :]
    gate_own[1:2, :] = jnp.zeros((1, rows), jnp.float32)
    for e in range(8):
        gate_own[1:2, e : e + 1] = padded[e : e + 1, :]
    gate_copy(0).start()
    gate_copy(1).start()
    own_rows(1).start()
    own_rows(2).start()
    for s in range(0, count, 384):
        flipped_ref[:, s : s + 384] = jnp.transpose(entry_ref[s : s + 384, :])
    taken[3].start()

    for kind in range(2):
        forward_weights(kind, 3)
    gate_copy(0).wait_recv()
    gate_copy(2).start()
    tally_step(4)
    for piece in range(2):
        row_copy(1, 0, piece).wait_recv()
        row_copy(1, 2, piece).start()

    for which in range(2):
        for part in range(3):
            for piece in range(2):
                copy = row_copy(which, part, piece)
                copy.wait_send()
                if part:
                    copy.wait_recv()
    for part in range(3):
        gate_copy(part).wait_send()
        if part:
            gate_copy(part).wait_recv()
    for k in range(len(rounds)):
        tally(k).wait_send()
    for copy in taken:
        copy.wait()
    for which in range(3):
        own_rows(which).wait()
    for kind in range(2):
        own_weights(kind).wait()
        for r in range(1, planes):
            for sign in (1, -1):
                @pl.when(hop_sent(sign, r))
                def _(kind=kind, sign=sign, r=r):
                    hop(kind, sign, r).wait_send()
        for slot in range(2 * planes - 1):
            if slot == middle:
                aside(kind, slot).wait_send()
                continue

            @pl.when(aside_there(slot))
            def _(kind=kind, slot=slot):
                aside(kind, slot).wait()
        for sign in (1, -1):
            @pl.when(plane == (0 if sign > 0 else planes - 1))
            def _(kind=kind, sign=sign):
                handed(kind, sign).wait_send()

            @pl.when(plane == (1 if sign > 0 else planes - 2))
            def _(kind=kind, sign=sign):
                handed(kind, sign).wait_recv()


def front_stage(
    tokens, norms, projection, mixing, centroids, expanding, contracting, route, lengths, cotangent, planes, slabs
):
    count, width = tokens.shape
    rows = aligned_rows(count, planes)
    pairs = width // 128
    slots = 2 * planes - 1
    bf16, f32 = jnp.bfloat16, jnp.float32
    shape = jax.ShapeDtypeStruct
    anywhere = pl.BlockSpec(memory_space=pl.ANY)
    local = pl.BlockSpec(memory_space=pltpu.VMEM)
    dma = pltpu.SemaphoreType.DMA
    copies = 2 * (2 * (planes - 1) + slots) + 12 + 3 + 5 + 2
    outs = [
        (shape((width, count), bf16), anywhere),
        (shape((count, 3 * width), bf16), anywhere),
        (shape((count, width), bf16), anywhere),
        (shape((pairs, 2, count), f32), local),
        (shape((count, width), f32), anywhere),
        (shape((8, count), f32), local),
        (shape((8, 128), f32), local),
        (shape((4, rows, width), bf16), anywhere),
        (shape((4, rows, width), bf16), anywhere),
        (shape((4, 8, rows), f32), anywhere),
        (shape((slots,) + expanding.shape[1:], bf16), anywhere),
        (shape((slots,) + expanding.shape[1:], bf16), anywhere),
        (shape((slots,) + contracting.shape[1:], bf16), anywhere),
        (shape((slots,) + contracting.shape[1:], bf16), anywhere),
    ]
    return pl.pallas_call(
        partial(front_kernel, planes, slabs),
        out_shape=[o[0] for o in outs],
        in_specs=[pl.BlockSpec(memory_space=pltpu.SMEM)] + [anywhere, local] + [anywhere] * 2 + [local] * 3 + [anywhere] * 3,
        out_specs=[o[1] for o in outs],
        scratch_shapes=[
            pltpu.VMEM((rows, count), f32),
            pltpu.VMEM((rows, count), bf16),
            pltpu.VMEM((count, width + 128), bf16),
            pltpu.VMEM((count, width), bf16),
            pltpu.VMEM((rows, width), bf16),
            pltpu.VMEM((rows, width), bf16),
            pltpu.VMEM((8, rows), f32),
            pltpu.VMEM((10, 8, 128), f32),
            pltpu.VMEM(tokens.shape, bf16),
            pltpu.VMEM(projection.shape, bf16),
            pltpu.VMEM(mixing.shape, bf16),
            pltpu.VMEM(cotangent.shape, bf16),
            pltpu.VMEM((width, count), bf16),
            pltpu.VMEM((count, 3 * width), bf16),
            pltpu.VMEM((count, width), bf16),
            pltpu.VMEM((count, width), f32),
            dma((copies,)),
            dma((copies,)),
            dma((13,)),
        ],
        compiler_params=pltpu.CompilerParams(
            collective_id=0, has_side_effects=True, vmem_limit_bytes=VMEM_LIMIT
        ),
    )(
        lengths[0],
        tokens,
        norms,
        projection,
        mixing,
        centroids,
        route.reshape(1, -1),
        route,
        cotangent,
        expanding,
        contracting,
    )


STEP = 192


def rear_kernel(
    planes,
    slabs,
    total_tokens,
    lengths_ref,
    tokens_in,
    norms_ref,
    projection_in,
    mixing_ref,
    centroids_ref,
    route_ref,
    cot_in,
    flipped_in,
    joint_in,
    mixed_in,
    logs_ref,
    residual_in,
    place_ref,
    loads_ref,
    dots_ref,
    back_all,
    made_all,
    near_all,
    far_all,
    layer_to,
    token_to,
    vector_ref,
    up_to,
    down_to,
    shared_out,
    core_land,
    y_land,
    x_land,
    z_land,
    joint_ref,
    residual_ref,
    bias_ref,
    upstream_ref,
    a_ref,
    b_ref,
    made_ref,
    place_col,
    gate_col,
    dot_land,
    part_ref,
    stage_ref,
    own_ref,
    own_core,
    own_first,
    own_second,
    own_z,
    piece_ref,
    tally_ref,
    key_sums,
    tokens_ref,
    projection_ref,
    cot_ref,
    flipped_ref,
    mixed_ref,
    layer_ref,
    token_ref,
    up_out,
    down_out,
    send_sem,
    recv_sem,
    local_sem,
):
    count, width = tokens_ref.shape
    experts = planes
    rows = a_ref.shape[0]
    half_rows = rows // 2
    pairs = width // 128
    half = width // 2
    scale = (width // HEADS) ** (-0.5)
    factor = scale * HALF_LOG
    average = total_tokens / experts
    me, core, plane, beside_x, beside_y, beside_core = neighbours(slabs)
    x = lax.rem(me, 2)
    y = lax.rem(lax.div(me, 2), 2)
    here = lax.rem(me, slabs)
    diagonal = (beside_y[0], 1 - core)
    always = plane >= 0
    others = [(lax.rem(plane + d, planes) * slabs + here, core) for d in range(1, planes)]
    across_plane = (me + 3 - 2 * x - 4 * y, core)

    def fetch(i, src, dst):
        return pltpu.make_async_copy(src, dst, local_sem.at[i])

    loads = [
        fetch(0, residual_in, residual_ref),
        fetch(1, joint_in, joint_ref),
        fetch(8, cot_in, cot_ref),
        fetch(9, mixed_in, mixed_ref),
        fetch(10, flipped_in, flipped_ref),
        fetch(11, tokens_in, tokens_ref),
        fetch(12, projection_in, projection_ref),
    ]
    results = [
        fetch(13, token_ref, token_to),
        fetch(14, layer_ref, layer_to),
        fetch(15, up_out, up_to),
        fetch(16, down_out, down_to),
    ]
    greet([(d, always) for d in [beside_x, beside_y, beside_core, diagonal, across_plane] + others])
    ids = {}

    def remote(key, src, dst, device):
        i = ids.setdefault(key, len(ids))
        return pltpu.make_async_remote_copy(
            src_ref=src, dst_ref=dst, send_sem=send_sem.at[i], recv_sem=recv_sem.at[i], device_id=device, device_id_type=MESH
        )

    alls = (back_all, made_all)

    def to_core(which, second, piece):
        at = pl.ds(piece * half_rows, half_rows)
        return remote(
            ("core", which, second, piece), alls[which].at[1 + 2 * second, at], core_land.at[which, second, at], beside_core
        )

    def to_y(which, piece):
        at = pl.ds(piece * half_rows, half_rows)
        return remote(("y", which, piece), (a_ref, made_ref)[which].at[at], y_land.at[which, at], beside_y)

    def dot_copy(k):
        return remote(("dot", k), dots_ref.at[1 + k], dot_land.at[k], (beside_core, beside_y, diagonal)[k])

    for which in range(2):
        for second in (1, 0):
            for piece in range(2):
                to_core(which, second, piece).start()
        if which == 0:
            for k in range(3):
                dot_copy(k).start()

    def target(sign, r):
        e = plane + sign * r
        return jnp.clip(e, 0, planes - 1), (e >= 0) & (e < planes)

    def share_x(sign, r):
        e, _ = target(sign, r)
        return remote(("x", sign, r), far_all.at[e], x_land.at[e], beside_x)

    def share_z(sign, r):
        return remote(
            ("z", sign, r),
            stage_ref.at[0 if sign > 0 else 1],
            z_land.at[0 if sign > 0 else 1, r - 1],
            (jnp.clip(me + sign * slabs, 0, planes * slabs - 1), core),
        )

    ways = [(s, r) for r in range(planes - 1, 0, -1) for s in (1, -1)] + [(1, 0)]
    def start_shares(distance):
        for sign, r in ways:
            if r == distance:
                @pl.when(target(sign, r)[1])
                def _(sign=sign, r=r):
                    share_x(sign, r).start()

    for distance in range(planes - 1, 1, -1):
        start_shares(distance)

    def add_pieces(into, sources, size, step):
        def one(i, _):
            at = pl.ds(pl.multiple_of(i * step, step), step)
            total = sources[0][at, :].astype(jnp.float32)
            for s in sources[1:]:
                total = total + s[at, :].astype(jnp.float32)
            into[at, :] = total.astype(into.dtype)
            return 0
        lax.fori_loop(0, size // step, one, 0)

    def share_step(sign, r):
        e, valid = target(sign, r)
        lane = 0 if sign > 0 else 1

        @pl.when(valid)
        def _():
            first = fetch(2, near_all.at[e], part_ref.at[0])
            first.start()
            share_x(sign, r).wait_recv()
            second = fetch(3, x_land.at[e], part_ref.at[1])
            second.start()
            if r < planes - 1:
                @pl.when(target(sign, r + 1)[1])
                def _():
                    share_z(sign, r + 1).wait_send()
            first.wait()
            second.wait()
            add_pieces(stage_ref.at[lane], [part_ref.at[0], part_ref.at[1]], part_ref.shape[1], 96)
            if r < planes - 1:
                @pl.when((plane - sign >= 0) & (plane - sign < planes))
                def _():
                    share_z(sign, r + 1).wait_recv()
                    third = fetch(2, z_land.at[lane, r], part_ref.at[0])
                    third.start()
                    third.wait()
                    add_pieces(stage_ref.at[lane], [stage_ref.at[lane], part_ref.at[0]], part_ref.shape[1], 96)
            share_z(sign, r).start()

    def share_end():
        share_x(1, 0).wait_recv()
        copies = [fetch(2, near_all.at[plane], part_ref.at[0]), fetch(3, x_land.at[plane], part_ref.at[1])]
        for copy in copies:
            copy.start()
        for copy in copies:
            copy.wait()

        def put(sources, more):
            def rows_of(i, _):
                at = pl.ds(pl.multiple_of(i * 96, 96), 96)
                total = sources[0][at, :].astype(jnp.float32)
                if len(sources) > 1:
                    total = total + sources[1][at, :].astype(jnp.float32)
                up_out[at, :] = up_out[at, :] + total if more else total
                return 0
            lax.fori_loop(0, width // 96, rows_of, 0)

            def columns_of(i, _):
                at = pl.ds(pl.multiple_of(i * 96, 96), 96)
                for part in range(2):
                    source_at = pl.ds(pl.multiple_of(width + part * half + i * 96, 32), 96)
                    total = sources[0][source_at, :].astype(jnp.float32)
                    if len(sources) > 1:
                        total = total + sources[1][source_at, :].astype(jnp.float32)
                    to = slice(part * half, (part + 1) * half)
                    down_out[at, to] = down_out[at, to] + total if more else total
                return 0
            lax.fori_loop(0, half // 96, columns_of, 0)

        put([part_ref.at[0], part_ref.at[1]], False)
        for sign in (1, -1):
            lane = 0 if sign > 0 else 1

            @pl.when((plane - sign >= 0) & (plane - sign < planes))
            def _(sign=sign, lane=lane):
                share_z(sign, 1).wait_recv()
                third = fetch(2, z_land.at[lane, 0], part_ref.at[0])
                third.start()
                third.wait()
                put([part_ref.at[0]], True)

    q1, q2, q3, q4 = width // 2, width // 4, width // 8, width // 16
    base1 = core * q1
    base2 = base1 + y * q2
    base3 = base2 + x * q3

    def spot(start, size):
        return pl.ds(pl.multiple_of(start, 16), size)

    def corner(p):
        return lax.div(p, 2) * q4, pl.multiple_of(lax.rem(p, 2) * half, 128)

    def sum_copy(c, stage, d=0):
        own = own_ref.at[c]
        if stage == "core":
            return remote((c, stage), own.at[spot((1 - core) * q1, q1)], own_core.at[c], beside_core)
        if stage == "plane":
            at = base1 + (y if d == 0 else 1 - y) * q2 + (x if d == 1 else 1 - x) * q3
            land = own_second.at[c] if d == 2 else own_first.at[c, pl.ds(d * q3, q3)]
            return remote((c, stage, d), own.at[spot(at, q3)], land, (beside_x, beside_y, across_plane)[d])
        if stage == "first":
            return remote((c, stage), own.at[spot(base1 + (1 - y) * q2, q2)], own_first.at[c], beside_y)
        if stage == "second":
            return remote((c, stage), own.at[spot(base2 + (1 - x) * q3, q3)], own_second.at[c], beside_x)
        if stage == "z":
            r, k = corner(lax.rem(plane + d, planes))
            return remote(
                (c, stage, d), own.at[spot(base3 + r, q4), pl.ds(k, half)], own_z.at[c, d - 1], others[d - 1]
            )
        out = shared_out.at[c]
        if stage == "zz":
            r, k = corner(plane)
            return remote(
                (c, stage, d), piece_ref.at[c], out.at[spot(base3 + r, q4), pl.ds(k, half)], others[d - 1]
            )
        if stage == "plane back":
            at = spot(base3, q3)
            return remote((c, stage, d), out.at[at], out.at[at], (beside_x, beside_y, across_plane)[d])
        if stage == "second back":
            at = spot(base3, q3)
            return remote((c, stage), out.at[at], out.at[at], beside_x)
        if stage == "first back":
            at = spot(base2, q2)
            return remote((c, stage), out.at[at], out.at[at], beside_y)
        at = spot(base1, q1)
        return remote((c, stage), out.at[at], out.at[at], beside_core)

    def add_rows(c, start, size, came, step):
        def one(i, _):
            at = pl.ds(pl.multiple_of(i * step, step), step)
            mine = spot(start + i * step, step)
            own_ref[c, mine, :] = (
                own_ref[c, mine, :].astype(jnp.float32) + came[c, at, :].astype(jnp.float32)
            ).astype(jnp.bfloat16)
            return 0
        lax.fori_loop(0, size // step, one, 0)

    def keep_piece(c):
        r, k = corner(plane)
        return fetch(4 + c, piece_ref.at[c], shared_out.at[c, spot(base3 + r, q4), pl.ds(k, half)])

    def sum_step(c, stage):
        if stage == 0:
            sum_copy(c, "core").start()
        elif stage == 1:
            sum_copy(c, "core").wait_recv()
            add_rows(c, base1, q1, own_core, 48)
            sum_copy(c, "first").start()
        elif stage == 2:
            sum_copy(c, "first").wait_recv()
            add_rows(c, base2, q2, own_first, 48)
            sum_copy(c, "second").start()
        elif stage == 3:
            sum_copy(c, "second").wait_recv()
            add_rows(c, base3, q3, own_second, 48)
            for d in range(1, planes):
                sum_copy(c, "z", d).start()
        elif stage == 4:
            r, k = corner(plane)
            total = own_ref[c, spot(base3 + r, q4), pl.ds(k, half)].astype(jnp.float32)
            for d in range(1, planes):
                sum_copy(c, "z", d).wait_recv()
                total = total + own_z[c, d - 1].astype(jnp.float32)
            piece_ref[c] = total.astype(jnp.bfloat16)
            keep_piece(c).start()
            for d in range(1, planes):
                sum_copy(c, "zz", d).start()
        elif stage == 5:
            keep_piece(c).wait()
            for d in range(1, planes):
                sum_copy(c, "zz", d).wait_recv()
            sum_copy(c, "second back").start()
        elif stage == 6:
            sum_copy(c, "second back").wait_recv()
            sum_copy(c, "first back").start()
        elif stage == 7:
            sum_copy(c, "first back").wait_recv()
            sum_copy(c, "cc").start()
        else:
            sum_copy(c, "cc").wait_recv()

    def last_step(c, stage):
        if stage == 1:
            sum_copy(c, "core").wait_recv()
            add_rows(c, base1, q1, own_core, 48)
            for d in range(3):
                sum_copy(c, "plane", d).start()
        elif stage == 2:
            for d in range(3):
                sum_copy(c, "plane", d).wait_recv()

            def one(i, _):
                mine = spot(base3 + i * 48, 48)
                total = own_ref[c, mine, :].astype(jnp.float32)
                for d in range(2):
                    total = total + own_first[c, spot(d * q3 + i * 48, 48), :].astype(jnp.float32)
                total = total + own_second[c, spot(i * 48, 48), :].astype(jnp.float32)
                own_ref[c, mine, :] = total.astype(jnp.bfloat16)
                return 0
            lax.fori_loop(0, q3 // 48, one, 0)
            for d in range(1, planes):
                sum_copy(c, "z", d).start()
        elif stage == 3:
            sum_step(c, 4)
        elif stage == 4:
            keep_piece(c).wait()
            for d in range(1, planes):
                sum_copy(c, "zz", d).wait_recv()
            for d in range(3):
                sum_copy(c, "plane back", d).start()
        elif stage == 5:
            for d in range(3):
                sum_copy(c, "plane back", d).wait_recv()
            sum_copy(c, "cc").start()
        else:
            sum_copy(c, "cc").wait_recv()

    def sum_sent(c):
        sum_copy(c, "core").wait_send()
        if c not in (3,):
            for stage in ("first", "second", "second back", "first back"):
                sum_copy(c, stage).wait_send()
        else:
            for d in range(3):
                sum_copy(c, "plane", d).wait_send()
                sum_copy(c, "plane back", d).wait_send()
        for d in range(1, planes):
            sum_copy(c, "z", d).wait_send()

    def sum_for_y(which):
        into = (a_ref, made_ref)[which]
        for piece in range(2):
            at = pl.ds(piece * half_rows, half_rows)
            first = fetch(2, alls[which].at[2, at], into.at[at])
            first.start()
            to_core(which, 1, piece).wait_recv()
            second = fetch(3, core_land.at[which, 1, at], b_ref.at[at])
            second.start()
            first.wait()
            second.wait()
            add_pieces(into.at[at], [into.at[at], b_ref.at[at]], half_rows, 32)
            to_y(which, piece).start()

    sum_for_y(0)
    for copy in loads:
        copy.start()
    sum_for_y(1)
    place_col[...] = jnp.transpose(place_ref[...])
    score_bias(bias_ref, lengths_ref, count)
    for copy in loads:
        copy.wait()
    vector_ref[...] = jnp.zeros_like(vector_ref)
    number = lax.broadcasted_iota(jnp.int32, (1, rows), 1).astype(jnp.float32)

    def order_of(at):
        return jnp.where(place_col[at, 0:1] == number, 1.0, 0.0)

    def chunk_of(i):
        return pl.ds(pl.multiple_of(i * STEP, STEP), STEP)

    steps = count // STEP

    def unsort(buffer, act):
        def one(i, _):
            at = chunk_of(i)
            act(at, jnp.dot(order_of(at).astype(jnp.bfloat16), buffer[...], preferred_element_type=jnp.float32))
            return 0
        lax.fori_loop(0, steps, one, 0)

    def set_token(at, value):
        token_ref[at, :] = value

    def add_token(at, value):
        token_ref[at, :] += value

    own_back = fetch(2, back_all.at[0], b_ref)
    own_back.start()
    own_back.wait()
    unsort(b_ref, set_token)
    for piece in range(2):
        to_core(0, 0, piece).wait_recv()
    core_back = fetch(2, core_land.at[0, 0], b_ref)
    core_back.start()
    core_back.wait()
    unsort(b_ref, add_token)
    for sign in (1, -1):
        share_step(sign, planes - 1)
    start_shares(1)
    for piece in range(2):
        to_y(0, piece).wait_recv()
    y_back = fetch(2, y_land.at[0], b_ref)
    y_back.start()
    y_back.wait()
    unsort(b_ref, add_token)
    for sign in (1, -1):
        share_step(sign, planes - 2)
    for k in range(3):
        dot_copy(k).wait_recv()
    dots = dots_ref[0] + dot_land[0] + dot_land[1] + dot_land[2]
    dots = dots[0:1, :]

    def norm_step(i, _):
        at = chunk_of(i)
        normed, normal, spread_by = row_norm(residual_ref[at, :], norms_ref[2:3, :], norms_ref[3:4, :])
        route = route_ref[at, :]
        chosen = chosen_rows(route, centroids_ref, experts)
        gate = 1.0 / (1.0 + jnp.exp(-jnp.sum(normed * chosen, axis=1, keepdims=True)))
        gate_col[at, :] = jnp.broadcast_to(gate, (STEP, 128))
        gate_grad = jnp.sum(order_of(at) * dots, axis=1, keepdims=True)
        spread = jnp.zeros((STEP, 1), jnp.float32)
        for e in range(experts):
            spread = jnp.where(route == e, (loads_ref[e : e + 1, 0:1] - average) * (1.0 / average), spread)
        logit = (gate_grad + spread * (1.0 / total_tokens)) * gate * (1.0 - gate)
        above = token_ref[at, :] + logit * chosen
        pull = logit * normed
        vector_ref[2:3, :] += jnp.sum(above * normal, axis=0, keepdims=True)
        vector_ref[3:4, :] += jnp.sum(above, axis=0, keepdims=True)
        for e in range(experts):
            vector_ref[8 + e : 9 + e, :] += jnp.sum(jnp.where(route == e, pull, 0.0), axis=0, keepdims=True)
        vector_ref[4:5, :] += jnp.broadcast_to(
            jnp.sum(spread * gate, axis=0, keepdims=True) * (1.0 / total_tokens), (1, width)
        )
        scaled = above * norms_ref[2:3, :]
        inner = (
            scaled
            - jnp.mean(scaled, axis=1, keepdims=True)
            - normal * jnp.mean(scaled * normal, axis=1, keepdims=True)
        )
        grad = cot_ref[at, :].astype(jnp.float32) + inner * spread_by
        token_ref[at, :] = grad
        branch = grad.astype(jnp.bfloat16)
        layer_ref[at, :] = branch
        upstream_ref[at, :] = lax.dot_general(
            branch, mixing_ref[...], NT, preferred_element_type=jnp.float32
        ).astype(jnp.bfloat16)
        return 0

    lax.fori_loop(0, steps, norm_step, 0)
    own_ref[0] = lax.dot_general(
        mixed_ref[...], layer_ref[...], TN, preferred_element_type=jnp.float32
    ).astype(jnp.bfloat16)
    sum_step(0, 0)

    first = lax.broadcasted_iota(jnp.int32, (1, 128), 1) < 64

    def attend(p, _):
        lanes = pl.ds(pl.multiple_of(p * 128, 128), 128)
        keys = pl.ds(pl.multiple_of(width + p * 128, 128), 128)
        values = pl.ds(pl.multiple_of(2 * width + p * 128, 128), 128)
        key_sum, value_sum = key_sums.at[0], key_sums.at[1]
        key_sum[...] = jnp.zeros_like(key_sum)
        value_sum[...] = jnp.zeros_like(value_sum)
        for s, e in query_blocks(count):
            both = jnp.transpose(
                upstream_ref[s:e, lanes].astype(jnp.float32) * mixed_ref[s:e, lanes].astype(jnp.float32)
            )
            found = []
            for h in range(2):
                mine = first == (h == 0)
                inner = jnp.sum(both[64 * h : 64 * h + 64, :], axis=0, keepdims=True)
                q = jnp.where(mine, joint_ref[s:e, lanes], jnp.bfloat16(0))
                u = jnp.where(mine, upstream_ref[s:e, lanes], jnp.bfloat16(0))
                scores = lax.dot_general(joint_ref[0:e, keys], q, NT, preferred_element_type=jnp.float32)
                probs = jnp.exp2(scores * factor + bias_ref[0:e, s:e] - logs_ref[p, h : h + 1, s:e])
                prob_grad = lax.dot_general(joint_ref[0:e, values], u, NT, preferred_element_type=jnp.float32)
                score_grad = (probs * (prob_grad - inner)).astype(jnp.bfloat16)
                value_sum[0:e, :] += jnp.dot(probs.astype(jnp.bfloat16), u, preferred_element_type=jnp.float32)
                key_sum[0:e, :] += jnp.dot(score_grad, q, preferred_element_type=jnp.float32)
                found.append(
                    lax.dot_general(score_grad, joint_ref[0:e, keys], TN, preferred_element_type=jnp.float32)
                )
            joint_ref[s:e, lanes] = (jnp.where(first, found[0], found[1]) * scale).astype(jnp.bfloat16)
        joint_ref[:, keys] = (key_sum[...] * scale).astype(jnp.bfloat16)
        joint_ref[:, values] = value_sum[...].astype(jnp.bfloat16)

        events = {0: [], 1: [(0, 1)], 2: [(1, 1)], 3: [(0, 2)], 4: [(1, 2), (2, 1)], 5: [(0, 3)]}
        for k, steps_of in events.items():
            @pl.when(p == k)
            def _(k=k, steps_of=steps_of):
                for c, stage in steps_of:
                    (last_step if c in (3,) else sum_step)(c, stage)
                if k == 0:
                    start_shares(0)
                if k == 1:
                    for sign in (1, -1):
                        share_step(sign, 1)
        for c in range(1, 4):
            @pl.when(p == 2 * c - 1)
            def _(c=c):
                for k in range(3):
                    at = pl.ds(k * width + (c - 1) * 256, 256)
                    own_ref[c, :, k * 256 : (k + 1) * 256] = jnp.dot(
                        flipped_ref[...], joint_ref[:, at], preferred_element_type=jnp.float32
                    ).astype(jnp.bfloat16)
                sum_step(c, 0)

        return 0

    lax.fori_loop(0, pairs, attend, 0)

    rounds = [beside_core, beside_x, beside_y]
    rounds += [((plane + 1 - 2 * lax.rem(plane, 2)) * slabs + here, core), (lax.rem(plane + 2, planes) * slabs + here, core)]

    def tally(k):
        return remote(("tally", k), tally_ref.at[2 * k], tally_ref.at[2 * k + 1], rounds[k])

    def tally_step(k):
        tally(k).wait_recv()
        total = tally_ref[2 * k] + tally_ref[2 * k + 1]
        if k + 1 < len(rounds):
            tally_ref[2 * k + 2] = total
            tally(k + 1).start()
        else:
            vector_ref[...] = total

    def finish_step(i, _):
        at = chunk_of(i)
        back = lax.dot_general(joint_ref[at, :], projection_ref[...], NT, preferred_element_type=jnp.float32)
        _, normal, spread_by = row_norm(tokens_ref[at, :].astype(jnp.float32), norms_ref[0:1, :], norms_ref[1:2, :])
        scaled = back * norms_ref[0:1, :]
        inner = (
            scaled
            - jnp.mean(scaled, axis=1, keepdims=True)
            - normal * jnp.mean(scaled * normal, axis=1, keepdims=True)
        )
        token_ref[at, :] += inner * spread_by
        vector_ref[0:1, :] += jnp.sum(back * normal, axis=0, keepdims=True)
        vector_ref[1:2, :] += jnp.sum(back, axis=0, keepdims=True)
        return 0

    def end_made(at, value):
        layer_ref[at, :] = (residual_ref[at, :] + gate_col[at, 0:1] * value).astype(jnp.bfloat16)

    def load(source, into):
        copy = fetch(2, source, into)
        copy.start()
        copy.wait()

    def sum_steps(*which):
        for c, stage in which:
            if c in (3,):
                last_step(c, stage)
            else:
                sum_step(c, stage)

    lax.fori_loop(0, steps // 2, finish_step, 0)
    sum_steps((3, 1), (0, 4), (1, 3), (2, 2))
    lax.fori_loop(steps // 2, steps, finish_step, 0)
    results[0].start()
    tally_ref[0] = vector_ref[...]
    tally(0).start()
    sum_steps((0, 5), (1, 4), (2, 3))
    for piece in range(2):
        to_y(0, piece).wait_send()
    load(made_all.at[0], a_ref)
    for piece in range(2):
        to_core(1, 0, piece).wait_recv()
    load(core_land.at[1, 0], b_ref)
    add_pieces(a_ref, [a_ref, b_ref], rows, 32)
    sum_steps((3, 2), (0, 6), (1, 5), (2, 4))
    tally_step(0)
    for piece in range(2):
        to_y(1, piece).wait_recv()
    load(y_land.at[1], b_ref)
    add_pieces(a_ref, [a_ref, b_ref], rows, 32)
    sum_steps((3, 3), (0, 7), (1, 6), (2, 5))
    tally_step(1)
    unsort(a_ref, end_made)
    results[1].start()
    sum_steps((3, 4), (2, 6))
    tally_step(2)
    share_end()
    results[2].start()
    results[3].start()
    sum_steps((3, 5), (1, 7))
    tally_step(3)
    sum_steps((2, 7),)
    tally_step(4)
    sum_steps((0, 8), (1, 8), (3, 6), (2, 8))
    for copy in results:
        copy.wait()

    for which in range(2):
        for piece in range(2):
            for second in range(2):
                to_core(which, second, piece).wait_send()
    for piece in range(2):
        to_y(1, piece).wait_send()
    for k in range(3):
        dot_copy(k).wait_send()
    for sign, r in ways:
        @pl.when(target(sign, r)[1])
        def _(sign=sign, r=r):
            share_x(sign, r).wait_send()
    for sign in (1, -1):
        @pl.when(target(sign, 1)[1])
        def _(sign=sign):
            share_z(sign, 1).wait_send()
    for c in range(4):
        sum_sent(c)
    for c in range(4):
        for d in range(1, planes):
            sum_copy(c, "zz", d).wait_send()
        sum_copy(c, "cc").wait_send()
    for k in range(len(rounds)):
        tally(k).wait_send()
    assert len(ids) <= send_sem.shape[0]


def rear_stage(
    tokens, norms, projection, mixing, centroids, route, lengths, cotangent,
    flipped, joint, mixed, logs, residual, place, loads, dots, back, made, near, far, planes, slabs, total_tokens,
):
    count, width = tokens.shape
    rows = back.shape[1]
    half = width // 2
    bf16, f32 = jnp.bfloat16, jnp.float32
    shape = jax.ShapeDtypeStruct
    anywhere = pl.BlockSpec(memory_space=pl.ANY)
    local = pl.BlockSpec(memory_space=pltpu.VMEM)
    dma = pltpu.SemaphoreType.DMA
    packed = near.shape[1:]
    outs = [
        (shape((count, width), bf16), anywhere),
        (shape((count, width), f32), anywhere),
        (shape((16, width), f32), local),
        (shape((width, half), f32), anywhere),
        (shape((half, width), f32), anywhere),
        (shape((4, width, width), bf16), anywhere),
        (shape((2, 2, rows, width), bf16), anywhere),
        (shape((2, rows, width), bf16), anywhere),
        (shape((planes,) + packed, bf16), anywhere),
        (shape((2, planes - 1) + packed, bf16), anywhere),
    ]
    copies = 120
    return pl.pallas_call(
        partial(rear_kernel, planes, slabs, total_tokens),
        out_shape=[o[0] for o in outs],
        in_specs=[pl.BlockSpec(memory_space=pltpu.SMEM)]
        + [anywhere, local, anywhere]
        + [local] * 3
        + [anywhere] * 4
        + [local, anywhere]
        + [local] * 3
        + [anywhere] * 4,
        out_specs=[o[1] for o in outs],
        scratch_shapes=[
            pltpu.VMEM((count, 3 * width), bf16),
            pltpu.VMEM((count, width), f32),
            pltpu.VMEM((count, count), f32),
            pltpu.VMEM((count, width), bf16),
            pltpu.VMEM((rows, width), bf16),
            pltpu.VMEM((rows, width), bf16),
            pltpu.VMEM((rows, width), bf16),
            pltpu.VMEM((count, 8), f32),
            pltpu.VMEM((count, 128), f32),
            pltpu.VMEM((3, 8, rows), f32),
            pltpu.VMEM((2,) + packed, bf16),
            pltpu.VMEM((2,) + packed, bf16),
            pltpu.VMEM((4, width, width), bf16),
            pltpu.VMEM((4, width // 2, width), bf16),
            pltpu.VMEM((4, width // 4, width), bf16),
            pltpu.VMEM((4, width // 8, width), bf16),
            pltpu.VMEM((4, planes - 1, width // 16, half), bf16),
            pltpu.VMEM((4, width // 16, half), bf16),
            pltpu.VMEM((10, 16, width), f32),
            pltpu.VMEM((2, count, 128), f32),
            pltpu.VMEM(tokens.shape, bf16),
            pltpu.VMEM(projection.shape, bf16),
            pltpu.VMEM(cotangent.shape, bf16),
            pltpu.VMEM(flipped.shape, bf16),
            pltpu.VMEM(mixed.shape, bf16),
            pltpu.VMEM((count, width), bf16),
            pltpu.VMEM((count, width), f32),
            pltpu.VMEM((width, half), f32),
            pltpu.VMEM((half, width), f32),
            dma((copies,)),
            dma((copies,)),
            dma((17,)),
        ],
        compiler_params=pltpu.CompilerParams(
            collective_id=1, has_side_effects=True, vmem_limit_bytes=VMEM_LIMIT
        ),
    )(
        lengths[0],
        tokens,
        norms,
        projection,
        mixing,
        centroids,
        route,
        cotangent,
        flipped,
        joint,
        mixed,
        logs,
        residual,
        place,
        loads,
        dots,
        back,
        made,
        near,
        far,
    )


TILE = 256
ALIGN = 16


def aligned_rows(count, experts):
    return -(-(count + experts * (ALIGN - 1)) // ALIGN) * ALIGN


def gelu_pair(values):
    bell = jnp.exp2(values * values * (-0.5 * HALF_LOG))
    near = 1.0 / (1.0 + (0.3275911 * 0.7071067811865476) * jnp.abs(values))
    series = 1.061405429 * 0.5 * near - 1.453152027 * 0.5
    series = series * near + 1.421413741 * 0.5
    series = series * near - 0.284496736 * 0.5
    series = series * near + 0.254829592 * 0.5
    tail = series * near * bell
    below = jnp.where(values >= 0.0, 1.0 - tail, tail)
    return values * below, below + values * bell * 0.3989422804014327


def expert_kernel_body(
    experts,
    sources,
    limit,
    meta_ref,
    sent_all,
    cot_all,
    gate_all,
    up_near,
    up_far,
    down_near,
    down_far,
    back_all,
    made_all,
    dots_all,
    near_out,
    far_out,
    table,
    x_ref,
    c_ref,
    g_ref,
    column_ref,
    up_ref,
    down_ref,
    gu_ref,
    gd_ref,
    pack_ref,
    zero_ref,
    weight_sem,
    in_sem,
    out_sem,
    grad_sem,
    zero_sem,
):
    rows, width = sent_all.shape[1:]
    half = up_near.shape[2]
    own = meta_ref[0]
    spots = sources * experts

    base = 0
    ends = [0] * sources
    for e in range(experts):
        at = base
        for s in range(sources):
            size = meta_ref[1 + s * experts + e]
            table[0, e * sources + s] = size
            table[1, e * sources + s] = ends[s]
            table[2, e * sources + s] = at
            ends[s] = ends[s] + size
            at = at + size
        number = (at - base + (TILE - 1)) // TILE
        table[3, e] = base
        table[4, e] = number
        base = base + number * TILE
    for s in range(sources):
        table[5, s] = ends[s]

    bits = [1 << b for b in range(limit.bit_length()) if ALIGN <= (1 << b)]

    def move(k, act, outward):
        s, e = lax.rem(k, sources), lax.div(k, sources)
        size = table[0, k]
        for piece in bits:
            @pl.when((size & piece) != 0)
            def _(piece=piece):
                offset = size & (piece - 1)
                src = pl.ds(pl.multiple_of(table[1, k] + offset, ALIGN), piece)
                dst = pl.ds(pl.multiple_of(table[2, k] + offset, ALIGN), piece)
                if outward:
                    act(pltpu.make_async_copy(x_ref.at[dst], made_all.at[s, src], out_sem.at[0]))
                    act(pltpu.make_async_copy(c_ref.at[dst], back_all.at[s, src], out_sem.at[1]))
                else:
                    act(pltpu.make_async_copy(sent_all.at[s, src], x_ref.at[dst], in_sem.at[e, 0]))
                    act(pltpu.make_async_copy(cot_all.at[s, src], c_ref.at[dst], in_sem.at[e, 1]))

    def each(low, high, act):
        def one(i, _):
            act(i)
            return 0
        lax.fori_loop(low, high, one, 0)

    def begin(copy):
        copy.start()

    def end(copy):
        copy.wait()

    def move_weights(e, act):
        slot = e - own + experts - 1
        for j, (ups, downs) in enumerate(((up_near, down_near), (up_far, down_far))):
            part = pl.ds(j * half, half)
            act(pltpu.make_async_copy(ups.at[slot], up_ref.at[e, :, part], weight_sem.at[e, j, 0]))
            act(pltpu.make_async_copy(downs.at[slot], down_ref.at[e, part], weight_sem.at[e, j, 1]))

    zero_ref[...] = jnp.zeros_like(zero_ref)

    def bring(e):
        @pl.when(table[4, e] > 0)
        def _():
            last = pl.ds(pl.multiple_of(table[3, e] + (table[4, e] - 1) * TILE, TILE), TILE)
            x_ref[last, :] = jnp.zeros((TILE, width), jnp.bfloat16)
            c_ref[last, :] = jnp.zeros((TILE, width), jnp.bfloat16)
            g_ref[last, :] = jnp.zeros((TILE, 128), jnp.float32)

        move_weights(e, begin)
        each(e * sources, (e + 1) * sources, lambda k: move(k, begin, False))

    each(0, experts, bring)

    chunks = experts + 1

    def tail(k, act):
        s, i = lax.div(k, chunks), lax.rem(k, chunks) + rows // ALIGN - chunks

        @pl.when(i * ALIGN >= table[5, s])
        def _():
            dst = pl.ds(pl.multiple_of(i * ALIGN, ALIGN), ALIGN)
            act(pltpu.make_async_copy(zero_ref, made_all.at[s, dst], zero_sem.at[0]))
            act(pltpu.make_async_copy(zero_ref, back_all.at[s, dst], zero_sem.at[1]))

    each(0, sources * chunks, lambda k: tail(k, begin))

    def shift(s, outward):
        def segment(e):
            k = e * sources + s

            def one(i):
                src = pl.ds(pl.multiple_of(table[1, k] + i * ALIGN, ALIGN), ALIGN)
                dst = pl.ds(pl.multiple_of(table[2, k] + i * ALIGN, ALIGN), ALIGN)
                if outward:
                    column_ref[src, :] = g_ref[dst, :]
                else:
                    g_ref[dst, :] = column_ref[src, :]

            each(0, table[0, k] // ALIGN, one)

        each(0, experts, segment)

    def gates_in(s):
        column_ref[...] = jnp.transpose(jnp.broadcast_to(gate_all[s, 0:1, :], (128, rows)))
        shift(s, False)

    each(0, sources, gates_in)

    def grads(e):
        slot = lax.rem(e, 2)
        return [
            pltpu.make_async_copy(pack_ref.at[slot, j], ref.at[e], grad_sem.at[slot, j])
            for j, ref in enumerate((near_out, far_out))
        ]

    def work(e):
        move_weights(e, end)
        each(e * sources, (e + 1) * sources, lambda k: move(k, end, False))
        gu_ref[...] = jnp.zeros_like(gu_ref)
        gd_ref[...] = jnp.zeros_like(gd_ref)

        def tile(t):
            at = pl.ds(pl.multiple_of(table[3, e] + t * TILE, TILE), TILE)
            x, c, gate = x_ref[at, :], c_ref[at, :], g_ref[at, 0:1]
            before = jnp.dot(x, up_ref[e], preferred_element_type=jnp.float32)
            active, slope = gelu_pair(before)
            through = lax.dot_general(c, down_ref[e], NT, preferred_element_type=jnp.float32)
            grad = (through * (slope * gate)).astype(jnp.bfloat16)
            gated = (active * gate).astype(jnp.bfloat16)
            made = jnp.dot(active.astype(jnp.bfloat16), down_ref[e], preferred_element_type=jnp.float32)
            g_ref[at, :] = jnp.broadcast_to(
                jnp.sum(made * c.astype(jnp.float32), axis=1, keepdims=True), (TILE, 128)
            )
            gd_ref[...] += lax.dot_general(gated, c, TN, preferred_element_type=jnp.float32)
            gu_ref[...] += lax.dot_general(x, grad, TN, preferred_element_type=jnp.float32)
            back = lax.dot_general(grad, up_ref[e], NT, preferred_element_type=jnp.float32)
            x_ref[at, :] = made.astype(jnp.bfloat16)
            c_ref[at, :] = back.astype(jnp.bfloat16)

        each(0, table[4, e], tile)
        each(e * sources, (e + 1) * sources, lambda k: move(k, begin, True))

        @pl.when(e >= 2)
        def _():
            for copy in grads(e - 2):
                copy.wait()

        slot = lax.rem(e, 2)
        for j in range(2):
            pack_ref[slot, j, 0:width, :] = gu_ref[:, j * half : (j + 1) * half].astype(jnp.bfloat16)
            for part in range(2):
                pack_ref[slot, j, width + part * half : width + (part + 1) * half, :] = gd_ref[
                    j * half : (j + 1) * half, part * half : (part + 1) * half
                ].astype(jnp.bfloat16)
        for copy in grads(e):
            copy.start()

    each(0, experts, work)

    def sums_out(s):
        shift(s, True)
        dots_all[s] = jnp.transpose(column_ref[...])[0:8, :]

    each(0, sources, sums_out)
    each(0, spots, lambda k: move(k, end, True))
    each(0, sources * chunks, lambda k: tail(k, end))
    for e in range(max(0, experts - 2), experts):
        for copy in grads(e):
            copy.wait()


def expert_stage(meta, sent, cot, gates, weights, experts, limit):
    sources, rows, width = sent.shape
    half = weights[0].shape[2]
    hidden = 2 * half
    joined = -(-(sources * rows + experts * (TILE - 1)) // TILE) * TILE
    limit = -(-limit // ALIGN) * ALIGN
    anywhere = pl.BlockSpec(memory_space=pl.ANY)
    local = pl.BlockSpec(memory_space=pltpu.VMEM)
    dma = pltpu.SemaphoreType.DMA
    packed = (width + hidden, half)
    return pl.pallas_call(
        partial(expert_kernel_body, experts, sources, limit),
        out_shape=(
            jax.ShapeDtypeStruct((sources, rows, width), jnp.bfloat16),
            jax.ShapeDtypeStruct((sources, rows, width), jnp.bfloat16),
            jax.ShapeDtypeStruct((sources, 8, rows), jnp.float32),
            jax.ShapeDtypeStruct((experts,) + packed, jnp.bfloat16),
            jax.ShapeDtypeStruct((experts,) + packed, jnp.bfloat16),
        ),
        in_specs=[pl.BlockSpec(memory_space=pltpu.SMEM)] + [anywhere] * 2 + [local] + [anywhere] * 4,
        out_specs=(anywhere, anywhere, local, anywhere, anywhere),
        scratch_shapes=[
            pltpu.SMEM((6, sources * experts), jnp.int32),
            pltpu.VMEM((joined, width), jnp.bfloat16),
            pltpu.VMEM((joined, width), jnp.bfloat16),
            pltpu.VMEM((joined, 128), jnp.float32),
            pltpu.VMEM((rows, 128), jnp.float32),
            pltpu.VMEM((experts, width, hidden), jnp.bfloat16),
            pltpu.VMEM((experts, hidden, width), jnp.bfloat16),
            pltpu.VMEM((width, hidden), jnp.float32),
            pltpu.VMEM((hidden, width), jnp.float32),
            pltpu.VMEM((2, 2) + packed, jnp.bfloat16),
            pltpu.VMEM((ALIGN, width), jnp.bfloat16),
            dma((experts, 2, 2)),
            dma((experts, 2)),
            dma((2,)),
            dma((2, 2)),
            dma((2,)),
        ],
        compiler_params=pltpu.CompilerParams(vmem_limit_bytes=VMEM_LIMIT),
        cost_estimate=pl.CostEstimate(
            flops=12 * sources * rows * width * hidden, bytes_accessed=100_000_000, transcendentals=sources * rows * hidden
        ),
    )(meta, sent, cot, gates, *weights)


def arrange(shared, layer, token, vectors, up, down, experts):
    count, width = layer.shape
    third, half = width // 3, width // 2
    steps = 6

    def kernel(shared_ref, layer_ref, token_ref, vectors_ref, up_ref, down_ref, *outs):
        mixing_out, projection_out, layer_out, token_out, up_out, down_out, *vector_outs, centroids_out, balance_out = outs
        mixing_out[...] = shared_ref[0].astype(jnp.float32)
        for k in range(3):
            for c in range(3):
                at = k * width + c * third
                projection_out[:, at : at + third] = shared_ref[1 + c, :, k * third : (k + 1) * third].astype(jnp.float32)
        layer_out[...] = layer_ref[...]
        token_out[...] = token_ref[...]
        up_out[0] = up_ref[...]
        down_out[0] = down_ref[...]
        for i, out in enumerate(vector_outs):
            out[...] = vectors_ref[i]
        centroids_out[...] = vectors_ref[8 : 8 + experts, :]
        balance_out[...] = vectors_ref[4:5, 0:128]

    f32 = jnp.float32
    shape = jax.ShapeDtypeStruct
    rows = lambda n, m: pl.BlockSpec((n // steps, m), lambda i: (i, 0))
    slab = lambda n, m: pl.BlockSpec((1, n // steps, m), lambda i: (0, i, 0))
    whole = lambda *dims: pl.BlockSpec(dims, lambda i: (0,) * len(dims))
    return pl.pallas_call(
        kernel,
        out_shape=[
            shape((width, width), f32),
            shape((width, 3 * width), f32),
            shape((count, width), jnp.bfloat16),
            shape((count, width), f32),
            shape((1, width, half), f32),
            shape((1, half, width), f32),
        ]
        + [shape((width,), f32)] * 4
        + [shape((experts, width), f32), shape((1, 128), f32)],
        grid=(steps,),
        in_specs=[
            pl.BlockSpec((4, width // steps, width), lambda i: (0, i, 0)),
            rows(count, width),
            rows(count, width),
            whole(16, width),
            rows(width, half),
            rows(half, width),
        ],
        out_specs=[
            rows(width, width),
            rows(width, 3 * width),
            rows(count, width),
            rows(count, width),
            slab(width, half),
            slab(half, width),
        ]
        + [whole(width)] * 4
        + [whole(experts, width), whole(1, 128)],
        compiler_params=pltpu.CompilerParams(vmem_limit_bytes=VMEM_LIMIT),
    )(shared, layer, token, vectors, up, down)


def per_device(
    tokens,
    gains,
    shifts,
    projection,
    mixing,
    factors,
    biases,
    centroids,
    expanding,
    contracting,
    routes,
    lengths,
    cotangent,
):
    count, width = tokens.shape
    experts = centroids.shape[0]
    groups = lax.axis_size("expert")
    slabs = groups // experts
    limit = 2 * count // experts
    total_tokens = count * groups * lax.axis_size("tensor")

    norms = jnp.stack((gains, shifts, factors, biases))
    flipped, joint, mixed, logs, residual, place, loads, sent, cot, gates, *weights = front_stage(
        tokens, norms, projection, mixing, centroids, expanding, contracting, routes, lengths, cotangent, experts, slabs
    )
    meta = jnp.concatenate(
        [lax.div(lax.axis_index("expert"), slabs)[None], gates[:, 1, :experts].reshape(-1).astype(jnp.int32)]
    )
    back, made, dots, near, far = expert_stage(meta, sent, cot, gates, weights, experts, limit)
    layer, token, vectors, up, down, shared, *_ = rear_stage(
        tokens, norms, projection, mixing, centroids, routes, lengths, cotangent,
        flipped, joint, mixed, logs, residual, place, loads, dots, back, made, near, far, experts, slabs, total_tokens,
    )
    (
        mixing_grad, projection_grad, layer_output, token_grad, up_grad, down_grad,
        gain_grad, shift_grad, factor_grad, bias_grad, centroid_grad, balance,
    ) = arrange(shared, layer, token, vectors, up, down, experts)
    return (
        layer_output,
        balance[0, 0],
        token_grad,
        gain_grad,
        shift_grad,
        projection_grad,
        mixing_grad,
        factor_grad,
        bias_grad,
        centroid_grad,
        up_grad,
        down_grad,
    )


def solution(mesh):
    placed = (
        P(("expert", "tensor"), None),
        P(),
        P(),
        P(),
        P(),
        P(),
        P(),
        P(),
        P("expert", None, "tensor"),
        P("expert", "tensor", None),
        P(("expert", "tensor"), None),
        P(("expert", "tensor"), None),
        P(("expert", "tensor"), None),
    )
    near = mesh.shape["expert"] == 16 and mesh.shape["tensor"] == 2
    return jax.shard_map(
        per_device if near else moving_tokens,
        mesh=mesh,
        in_specs=placed,
        out_specs=(
            P(("expert", "tensor"), None),
            P(),
            P(("expert", "tensor"), None),
            P(),
            P(),
            P(),
            P(),
            P(),
            P(),
            P(),
            P("expert", None, "tensor"),
            P("expert", "tensor", None),
        ),
        check_vma=False,
    )
```
